32 devices in a mesh: dp: 4 (over x, core), seq: 4 (over z), mp: 2 (over y).
Axes of the slice: x: 2, y: 2, z: 4, core: 2. Of those that a mesh axis runs over, the one named last changes fastest.
Arguments:
- tokens_in: bfloat16 [2, 4, 704, 2048], P(None, 'dp', 'seq'), may hold values from -6 to 6
- cotangent: bfloat16 [2, 4, 704, 2048], P(None, 'dp', 'seq'), may hold values from -6 to 6
- seq_source: int32 [2, 4], P(None, 'dp'), may hold values from 0 to 7
- source_weight: float32 [8], replicated, may hold values from 0.5 to 2
- input_weight: bfloat16 [2048, 2560], P(('dp', 'seq'), 'mp'), may hold values from -0.125 to 0.125
- gelu_weight: bfloat16 [2048, 2560], P(('dp', 'seq'), 'mp'), may hold values from -0.125 to 0.125
- decay_gates: bfloat16 [16, 25600], P('mp', ('dp', 'seq')), may hold values from -0.5 to 0.5
- input_gates: bfloat16 [16, 25600], P('mp', ('dp', 'seq')), may hold values from -0.5 to 0.5
- channel_params: bfloat16 [8, 2, 1280], P(None, 'mp', ('dp', 'seq')), may hold values from -3 to 14, as said below
- norm_gains: bfloat16 [2, 2048], P(None, ('dp', 'seq')), may hold values from 0.099609375 to 1.8984375
- output_weight: bfloat16 [2560, 2048], P('mp', ('dp', 'seq')), may hold values from -0.5 to 0.5
- mlp_gate: bfloat16 [2048, 6144], P(('dp', 'seq'), 'mp'), may hold values from -0.125 to 0.125
- mlp_up: bfloat16 [2048, 6144], P(('dp', 'seq'), 'mp'), may hold values from -0.125 to 0.125
- mlp_down: bfloat16 [6144, 2048], P('mp', ('dp', 'seq')), may hold values from -0.15625 to 0.15625
Outputs:
- block_out: bfloat16 [2, 4, 704, 2048], P(None, 'dp', 'seq')
- grad_tokens: float32 [2, 4, 704, 2048], P(None, 'dp', 'seq')
- grad_input_weight: float32 [2048, 2560], P(('dp', 'seq'), 'mp')
- grad_gelu_weight: float32 [2048, 2560], P(('dp', 'seq'), 'mp')
- grad_decay_gates: float32 [16, 25600], P('mp', ('dp', 'seq'))
- grad_input_gates: float32 [16, 25600], P('mp', ('dp', 'seq'))
- grad_channel_params: float32 [8, 2, 1280], P(None, 'mp', ('dp', 'seq'))
- grad_norm_gains: float32 [2, 2048], P(None, ('dp', 'seq'))
- grad_output_weight: float32 [2560, 2048], P('mp', ('dp', 'seq'))
- grad_mlp_gate: float32 [2048, 6144], P(('dp', 'seq'), 'mp')
- grad_mlp_up: float32 [2048, 6144], P(('dp', 'seq'), 'mp')
- grad_mlp_down: float32 [6144, 2048], P('mp', ('dp', 'seq'))
The draws below stay inside these ranges and needn't reach their ends.
Inputs may be any that keep to these rules, and one draw needn't show every extreme that they name: `channel_params`: row 0 (the decay parameters) lies between 4 and 14 and differs per channel; rows 1 to 7 are of order one.
All inputs are finite; a program needn't handle non-finite values.
Results may differ from the reference program's by a relative error of at most 0.011.
Values may be sent and summed in bfloat16 or wider, within the bound.
A program may use at most 1.9375 GiB of HBM per device.

```python
import math
import jax
import jax.numpy as jnp
from jax import lax

D = 2048
WIDTH = 2560
HEADS = 16
FF = 6144
BW = 160
MB = 2
SOURCES = 8
SEQS = 4
LENGTH = 704
N_MP = 2


def draw_channel_params(key, part):
    key_list = jax.random.split(key, 4)
    lambdas = jax.random.uniform(key_list[0], (1, WIDTH), jnp.float32, 4.0, 14.0)
    biases = jnp.clip(jax.random.normal(key_list[1], (2, WIDTH), jnp.float32), -3.0, 3.0)
    conv_bias = 0.3 * jnp.clip(jax.random.normal(key_list[2], (1, WIDTH), jnp.float32), -3.0, 3.0)
    conv_taps = 0.5 * jnp.clip(jax.random.normal(key_list[3], (4, WIDTH), jnp.float32), -3.0, 3.0)
    stacked_rows = jnp.concatenate([lambdas, biases, conv_bias, conv_taps], axis=0)
    return stacked_rows.reshape(8, N_MP, WIDTH // N_MP).astype(jnp.bfloat16)


def touch_ends(entries, key, smallest, high):
    longest = entries.shape.index(max(entries.shape))
    spots = []
    for shift in (0, 1):
        where = [jax.random.randint(jax.random.fold_in(key, axis), (), 0, length) for axis, length in enumerate(entries.shape)]
        where[longest] = (where[longest] + shift) % entries.shape[longest]
        spots.append(tuple(where))
    return entries.at[spots[0]].set(smallest).at[spots[1]].set(high)


def levels(rng, extent, cuts, least, largest):
    def one(dim, parts):
        heights = jax.random.uniform(jax.random.fold_in(jax.random.fold_in(rng, 6), dim), (parts,), jnp.float32, least / len(cuts), largest / len(cuts))
        return jnp.repeat(jnp.exp(heights), extent[dim] // parts).reshape((-1,) + (1,) * (len(extent) - dim - 1))

    level = one(*cuts[0])
    for cut in cuts[1:]:
        level = level * one(*cut)
    return level


def noise(own_key, shape, width, most, pieces=(), held_as=jnp.bfloat16):
    drawn = width * jax.random.normal(own_key, shape, jnp.float32)
    if pieces:
        drawn = drawn * levels(own_key, shape, pieces, -0.22, 0.18)
    return jnp.clip(drawn, -most, most).astype(held_as)


def setup_inputs(seed: int = 0) -> dict:
    key_of = jax.random.split(jax.random.key(seed), 15)
    return {
        "tokens_in": noise(key_of[0], (MB, SEQS, LENGTH, D), 1.0, 6.0, ((1, 4), (2, 4))),
        "cotangent": noise(key_of[1], (MB, SEQS, LENGTH, D), 1.0, 6.0, ((1, 4), (2, 4))),
        "seq_source": touch_ends(jax.random.randint(key_of[2], (MB, SEQS), 0, SOURCES), jax.random.fold_in(key_of[2], 1), 0, SOURCES - 1).astype(jnp.int32),
        "source_weight": jnp.clip(jnp.exp(jax.random.uniform(key_of[3], (SOURCES,), jnp.float32, math.log(0.5), math.log(2.0))), 0.5, 2.0),
        "input_weight": noise(key_of[4], (D, WIDTH), D ** -0.5, 0.125, ((0, 16), (1, 2))),
        "gelu_weight": noise(key_of[5], (D, WIDTH), D ** -0.5, 0.125, ((0, 16), (1, 2))),
        "decay_gates": noise(key_of[6], (HEADS, BW * BW), BW ** -0.5, 0.5, ((0, 2), (1, 16))),
        "input_gates": noise(key_of[7], (HEADS, BW * BW), BW ** -0.5, 0.5, ((0, 2), (1, 16))),
        "channel_params": draw_channel_params(jax.random.fold_in(key_of[14], 71), 0),
        "norm_gains": jnp.clip(1.0 + 0.18 * jax.random.normal(key_of[9], (2, D), jnp.float32), 0.099609375, 1.8984375).astype(jnp.bfloat16),
        "output_weight": noise(key_of[10], (WIDTH, D), (WIDTH // 16) ** -0.5, 0.5, ((0, 2), (1, 16))),
        "mlp_gate": noise(key_of[11], (D, FF), D ** -0.5, 0.125, ((0, 16), (1, 2))),
        "mlp_up": noise(key_of[12], (D, FF), D ** -0.5, 0.125, ((0, 16), (1, 2))),
        "mlp_down": noise(key_of[13], (FF, D), (FF // 4) ** -0.5, 0.15625, ((0, 2), (1, 16))),
    }


@jax.custom_vjp
def low(v):
    return lax.optimization_barrier(v.astype(jnp.bfloat16)).astype(jnp.float32)

@jax.custom_vjp
def low_back(v):
    return v

def low_keep(v):
    return (low(v), None)

def low_pass(kept, grad):
    return (grad,)

def back_keep(v):
    return (v, None)

def back_low(kept, grad):
    return (low(grad),)
low.defvjp(low_keep, low_pass)
low_back.defvjp(back_keep, back_low)
EPSILON = 1e-06
DECAY_SCALE = 8.0
HIGHEST = lax.Precision.HIGHEST

def normalize(values, gain_vec):
    return values * lax.rsqrt(lax.optimization_barrier(jnp.mean(values * values, axis=-1, keepdims=True)) + EPSILON) * gain_vec

def smooth_gate(values):
    return jax.nn.gelu(values, approximate=True)

def coefficients(inputs, logit_a, logit_i, lambda_param):
    log_decay = -DECAY_SCALE * jax.nn.sigmoid(logit_a) * jax.nn.softplus(-lambda_param)
    decay_rate = jnp.exp(log_decay)
    drive_term = jnp.sqrt(-jnp.expm1(2.0 * log_decay)) * jax.nn.sigmoid(logit_i) * inputs
    return (decay_rate, drive_term)

def combine(earlier, later_pair):
    return (earlier[0] * later_pair[0], later_pair[1] + later_pair[0] * earlier[1])

def gated_product(gate_in, up_in):
    return smooth_gate(gate_in) * up_in

def product_hi(left, right):
    return jnp.dot(left, right, precision=HIGHEST)

def block_forward(params, sequence):
    input_weight, gelu_weight, decay_gates, input_gates, channel_params, norm_gains, output_weight, mlp_gate, mlp_up, mlp_down = params
    normed = low(normalize(sequence, norm_gains[0]))
    branch_x = low_back(low(product_hi(normed, input_weight)))
    branch_y = low_back(product_hi(normed, gelu_weight))
    padded = jnp.concatenate([jnp.zeros((3, WIDTH), jnp.float32), branch_x], axis=0)
    conv_sum = channel_params[3]
    for offset in range(4):
        conv_sum = conv_sum + channel_params[4 + offset] * padded[3 - offset:3 - offset + LENGTH]
    inputs = low(conv_sum)
    split_in = inputs.reshape(LENGTH, HEADS, BW)
    logit_a = low_back(jnp.einsum('thi,hij->thj', split_in, decay_gates, precision=HIGHEST).reshape(LENGTH, WIDTH) + channel_params[1])
    logit_i = low_back(jnp.einsum('thi,hij->thj', split_in, input_gates, precision=HIGHEST).reshape(LENGTH, WIDTH) + channel_params[2])
    decay_rate, drive_term = coefficients(inputs, logit_a, logit_i, channel_params[0])
    states = lax.associative_scan(combine, (decay_rate, drive_term), axis=0)[1]
    mixed = low(smooth_gate(branch_y) * states)
    middle = sequence + low_back(product_hi(mixed, output_weight))
    normed_two = low(normalize(middle, norm_gains[1]))
    gate_pre = low_back(product_hi(normed_two, mlp_gate))
    up_pre = low_back(product_hi(normed_two, mlp_up))
    hidden = low(gated_product(gate_pre, up_pre))
    return middle + low_back(product_hi(hidden, mlp_down))

def reference(tokens_in, cotangent, seq_source, source_weight, input_weight, gelu_weight, decay_gates, input_gates, channel_params, norm_gains, output_weight, mlp_gate, mlp_up, mlp_down):
    params = (input_weight.astype(jnp.float32), gelu_weight.astype(jnp.float32), decay_gates.astype(jnp.float32).reshape(HEADS, BW, BW), input_gates.astype(jnp.float32).reshape(HEADS, BW, BW), channel_params.astype(jnp.float32).reshape(8, WIDTH), norm_gains.astype(jnp.float32), output_weight.astype(jnp.float32), mlp_gate.astype(jnp.float32), mlp_up.astype(jnp.float32), mlp_down.astype(jnp.float32))
    loss_scale = source_weight[seq_source].reshape(MB * SEQS).astype(jnp.float32)
    flat_tokens = tokens_in.astype(jnp.float32).reshape(MB * SEQS, LENGTH, D)
    flat_cot = cotangent.astype(jnp.float32).reshape(MB * SEQS, LENGTH, D)

    def one_sequence(totals, scan_item):
        sequence, upstream, scale_one = scan_item
        result, pullback = jax.vjp(block_forward, params, sequence)
        param_grads, token_grad = pullback(upstream * scale_one)
        return (jax.tree.map(jnp.add, totals, param_grads), (result.astype(jnp.bfloat16), token_grad))
    totals, (results, token_grads) = lax.scan(one_sequence, jax.tree.map(jnp.zeros_like, params), (flat_tokens, flat_cot, loss_scale))
    return (results.reshape(MB, SEQS, LENGTH, D), token_grads.reshape(MB, SEQS, LENGTH, D), totals[0], totals[1], totals[2].reshape(HEADS, BW * BW), totals[3].reshape(HEADS, BW * BW), totals[4].reshape(8, N_MP, WIDTH // N_MP), totals[5], totals[6], totals[7], totals[8], totals[9])
```

```python
import jax
import jax.numpy as jnp
import numpy as np
from jax import lax
from jax.experimental import pallas as pl
from jax.experimental.pallas import tpu as pltpu
from jax.sharding import Mesh, PartitionSpec as P

WIDTH = 2560
HEADS = 16
BLOCK = WIDTH // HEADS
EPSILON = 1e-06
DECAY_SCALE = 8.0
AXES = ("dx", "dc", "zh", "zl", "mp")
BF = jnp.bfloat16
F32 = jnp.float32


def swap_pairs(sizes, partner):
    pairs = []
    for flat in range(int(np.prod(sizes))):
        coords = np.unravel_index(flat, sizes)
        pairs.append((flat, int(np.ravel_multi_index(partner(*map(int, coords)), sizes))))
    return pairs


def gather_blocks(x, axis, dim):
    if lax.axis_size(axis) != 2:
        return lax.all_gather(x, axis, axis=dim, tiled=False)
    here = lax.axis_index(axis)
    other = lax.ppermute(x, axis, [(0, 1), (1, 0)])
    low = jnp.where(here == 0, x, other)
    high = jnp.where(here == 0, other, x)
    return jnp.stack([low, high], axis=dim)


def scatter_blocks(x, axis, dim):
    if lax.axis_size(axis) != 2:
        n = x.shape[dim]
        out = lax.psum_scatter(x.astype(BF), axis, scatter_dimension=dim, tiled=True)
        return lax.squeeze(out, [dim]).astype(F32)
    here = lax.axis_index(axis)
    mine = lax.dynamic_index_in_dim(x, here, dim, keepdims=False)
    theirs = lax.dynamic_index_in_dim(x, 1 - here, dim, keepdims=False)
    got = lax.ppermute(theirs.astype(BF), axis, [(0, 1), (1, 0)])
    return mine.astype(F32) + got.astype(F32)


def fetch_weight(shard, parts):
    rows, cols = shard[0].shape[0], None
    pieces = [s.reshape(rows, parts, -1) for s in shard]
    joined = jnp.concatenate(pieces, axis=2) if len(pieces) > 1 else pieces[0]
    cols = joined.shape[2]
    x = jnp.transpose(joined, (1, 0, 2))
    x = lax.all_to_all(x, ("dc", "zl"), 0, 0, tiled=True)
    x = x.reshape(2, 2, rows, cols)
    x = gather_blocks(x, "zh", 1)
    x = gather_blocks(x, "dx", 0)
    return x.reshape(-1, cols)


def return_grad(grad, rows):
    cols = grad.shape[1]
    dxn, zhn = lax.axis_size("dx"), lax.axis_size("zh")
    g = grad.reshape(dxn, 2, zhn, 2, rows, cols)
    g = scatter_blocks(g, "dx", 0)
    g = scatter_blocks(g, "zh", 1)
    g = g.astype(BF).reshape(4, rows, cols)
    return lax.all_to_all(g, ("dc", "zl"), 0, 0, tiled=True)


class Tokens:
    def __init__(self, sizes):
        self.core = swap_pairs(sizes, lambda a, b, c, d, e: (a, 1 - b, c, d, e))
        self.first = swap_pairs(
            sizes, lambda a, b, c, d, e: (a, b, c, d, 1 - e) if b == 0 else (a, b, c, 1 - d, e)
        )
        self.second = swap_pairs(
            sizes, lambda a, b, c, d, e: (a, b, c, 1 - d, e) if b == 0 else (a, b, c, d, 1 - e)
        )
        self.dc, self.zl, self.mp = (lax.axis_index(n) for n in ("dc", "zl", "mp"))

    def order(self, dc):
        mp, zl = self.mp, self.zl
        own = mp * 2 + zl
        by_mp = (1 - mp) * 2 + zl
        by_zl = mp * 2 + 1 - zl
        both = (1 - mp) * 2 + 1 - zl
        one = jnp.where(dc == 0, by_mp, by_zl)
        two = jnp.where(dc == 0, by_zl, by_mp)
        return own, one, two, both

    def gather(self, x):
        rows, width = x.shape
        one = lax.ppermute(x, AXES, self.first)
        two = lax.ppermute(jnp.stack([x, one]), AXES, self.second)
        far = [lax.ppermute(v, AXES, self.core) for v in (x, one, two)]
        out = jnp.zeros((8, rows, width), x.dtype)
        for dc, blocks in (
            (self.dc, (x, one, two[0], two[1])),
            (1 - self.dc, (far[0], far[1], far[2][0], far[2][1])),
        ):
            for at, block in zip(self.order(dc), blocks):
                out = lax.dynamic_update_index_in_dim(out, block, dc * 4 + at, 0)
        return out.reshape(8 * rows, width)

    def scatter(self, x):
        rows, width = x.shape[0] // 8, x.shape[1]
        x = x.reshape(2, 4, rows, width)
        theirs = lax.dynamic_index_in_dim(x, 1 - self.dc, 0, keepdims=False).astype(BF)
        mine = lax.dynamic_index_in_dim(x, self.dc, 0, keepdims=False)
        total = mine.astype(F32) + lax.ppermute(theirs, AXES, self.core).astype(F32)
        own, one, two, both = self.order(self.dc)
        pick = lambda at: lax.dynamic_index_in_dim(total, at, 0, keepdims=False)
        got = lax.ppermute(jnp.stack([pick(two), pick(both)]).astype(BF), AXES, self.second)
        keep_own = pick(own) + got[0].astype(F32)
        keep_one = pick(one) + got[1].astype(F32)
        got = lax.ppermute(keep_one.astype(BF), AXES, self.first)
        return keep_own + got.astype(F32)


def scan_body(reverse, a_ref, b_ref, p_ref, h_ref):
    length, width = a_ref.shape[1], a_ref.shape[2]
    row = lax.broadcasted_iota(jnp.int32, (8, width), 0)

    def tile(i, carry):
        ca, ch = carry
        at = (length // 8 - 1 - i if reverse else i) * 8
        at = pl.multiple_of(at, 8)
        a = a_ref[0, pl.ds(at, 8), :]
        b = b_ref[0, pl.ds(at, 8), :]
        for step in (1, 2, 4):
            if reverse:
                inside = row < 8 - step
                shift = 8 - step
            else:
                inside = row >= step
                shift = step
            sa = jnp.where(inside, pltpu.roll(a, shift, 0), 1.0)
            sb = jnp.where(inside, pltpu.roll(b, shift, 0), 0.0)
            b = b + a * sb
            a = a * sa
        h = b + a * ch
        p = a * ca
        h_ref[0, pl.ds(at, 8), :] = h
        p_ref[0, pl.ds(at, 8), :] = p
        last = 0 if reverse else 7
        return p[last : last + 1, :], h[last : last + 1, :]

    lax.fori_loop(
        0,
        length // 8,
        tile,
        (jnp.ones((1, width), F32), jnp.zeros((1, width), F32)),
    )


def local_scan(a, b, reverse):
    segs, length, width = a.shape
    spec = pl.BlockSpec((1, length, width), lambda s: (s, 0, 0))
    return pl.pallas_call(
        lambda *refs: scan_body(reverse, *refs),
        grid=(segs,),
        in_specs=[spec, spec],
        out_specs=[spec, spec],
        out_shape=[jax.ShapeDtypeStruct(a.shape, F32)] * 2,
        cost_estimate=pl.CostEstimate(
            flops=20 * a.size, bytes_accessed=16 * a.size, transcendentals=0
        ),
    )(a, b)


def carried(product, state, reverse):
    count = lax.axis_size("zh")
    if count == 2:
        return lax.ppermute(state, "zh", [(1, 0)] if reverse else [(0, 1)])
    here = lax.axis_index("zh")
    pairs = lax.all_gather(jnp.stack([product, state]), "zh")
    total = jnp.zeros_like(state)
    for k in range(count):
        at = count - 1 - k if reverse else k
        reached = at > here if reverse else at < here
        total = jnp.where(reached, pairs[at, 1] + pairs[at, 0] * total, total)
    return total


def from_behind(x, by):
    count = lax.axis_size("zh")
    return lax.ppermute(
        x, "zh", [(i, i + by) for i in range(count) if 0 <= i + by < count]
    )


def inverse_rms(values):
    return lax.rsqrt(jnp.mean(values * values, axis=-1, keepdims=True) + EPSILON)


def norm_grad(values, gain, upstream):
    inv = inverse_rms(values)
    scaled = values * inv
    up = upstream * gain
    inner = jnp.mean(up * scaled, axis=-1, keepdims=True)
    return inv * (up - scaled * inner), jnp.sum(upstream * scaled, axis=0)


def gelu(v):
    return jax.nn.gelu(v, approximate=True)


def gelu_both(v):
    c = 0.7978845608028654
    t = jnp.tanh(c * (v + 0.044715 * v * v * v))
    value = 0.5 * v * (1.0 + t)
    slope = 0.5 * (1.0 + t) + 0.5 * v * (1.0 - t * t) * c * (1.0 + 3 * 0.044715 * v * v)
    return value, slope


def dot(a, b, dims, out=F32):
    r = lax.dot_general(a, b, (dims, ((), ())), preferred_element_type=F32)
    return r.astype(out)


NN = ((1,), (0,))
NT = ((1,), (1,))
TN = ((0,), (0,))


def on_device(
    tokens_in,
    cotangent,
    seq_source,
    source_weight,
    input_weight,
    gelu_weight,
    decay_gates,
    input_gates,
    channel_params,
    norm_gains,
    output_weight,
    mlp_gate,
    mlp_up,
    mlp_down,
):
    sizes = tuple(lax.axis_size(n) for n in AXES)
    dxn, _, zhn, _, _ = sizes
    group = dxn * 2 * zhn * 2
    dc, zl, mp = (lax.axis_index(n) for n in ("dc", "zl", "mp"))
    slot = dc * 2 + zl
    exchange = Tokens(sizes)
    length = tokens_in.shape[2]
    width = tokens_in.shape[3]
    local = input_weight.shape[1] // 4
    heads = decay_gates.shape[0] // 4
    drows = input_weight.shape[0]
    piece = decay_gates.shape[1]

    own = lax.dynamic_index_in_dim(tokens_in[:, 0], mp, 0, keepdims=False)
    own_cot = lax.dynamic_index_in_dim(cotangent[:, 0], mp, 0, keepdims=False).astype(F32)
    source = lax.dynamic_index_in_dim(seq_source[:, 0], mp, 0, keepdims=False)
    scale = jnp.sum(
        jnp.where(jnp.arange(source_weight.shape[0], dtype=jnp.int32) == source, source_weight, 0.0)
    )
    dout = own_cot * scale
    tokens = exchange.gather(own)
    dm = exchange.gather(dout.astype(BF))

    small = jnp.concatenate([channel_params.reshape(-1), norm_gains.reshape(-1)])
    small = lax.all_gather(small, ("dx", "dc", "zh", "zl"))
    nch = channel_params.size
    channels = small[:, :nch].reshape(group, 8, -1).transpose(1, 0, 2).reshape(8, -1)
    channels = lax.dynamic_slice_in_dim(channels, slot * local, local, 1).astype(F32)
    gains = small[:, nch:].reshape(group, 2, -1).transpose(1, 0, 2).reshape(2, -1).astype(F32)

    w_ig = fetch_weight([input_weight, gelu_weight], 4)
    gates = jnp.stack([decay_gates, input_gates]).reshape(2, 4, heads, piece)
    gates = gates.transpose(1, 0, 2, 3)
    gates = lax.all_to_all(gates, ("dc", "zl"), 0, 0, tiled=True).reshape(2, 2, 2 * heads * piece)
    gates = gather_blocks(gather_blocks(gates, "zh", 1), "dx", 0)
    gates = gates.reshape(group, 2 * heads, piece).transpose(1, 0, 2)
    gates = gates.reshape(2, heads, BLOCK, BLOCK)
    w_o = fetch_weight([output_weight.T], 4)
    ff = mlp_gate.shape[1] // 4
    half = ff // 2

    gate4, up4, down4 = (v.reshape(drows, 4, ff) for v in (mlp_gate, mlp_up, mlp_down.T))
    w_gu = []
    for k in range(2):
        cut = slice(k * half, (k + 1) * half)
        w_gu.append(
            fetch_weight(
                [gate4[:, :, cut].reshape(drows, -1), up4[:, :, cut].reshape(drows, -1)], 4
            )
        )
    w_d = fetch_weight([down4.reshape(drows, -1)], 4)

    wide = tokens.astype(F32)
    n1 = (wide * inverse_rms(wide) * gains[0]).astype(BF)
    both = dot(n1, w_ig, NN)
    xb = both[:, :local].astype(BF).reshape(4, 2 * length, local)
    gy = both[:, local:].reshape(4, 2 * length, local)
    rim = from_behind(xb[:, -3:], 1)
    padded = jnp.concatenate([rim, xb], axis=1).astype(F32)
    conv = channels[3]
    for k in range(4):
        conv = conv + channels[4 + k] * padded[:, 3 - k : 3 - k + 2 * length]
    u = conv.astype(BF)
    zero = jnp.zeros((BLOCK, BLOCK), BF)
    blocks = jnp.concatenate(
        [
            jnp.concatenate(
                [gates[g, h] if k == h else zero for g in range(2) for k in range(heads)], axis=1
            )
            for h in range(heads)
        ],
        axis=0,
    )
    u2 = u.reshape(-1, local)
    logits = dot(u2, blocks, NN).reshape(4, 2 * length, 2 * local)
    sig_a = jax.nn.sigmoid(logits[..., :local] + channels[1])
    sig_i = jax.nn.sigmoid(logits[..., local:] + channels[2])
    soft = jax.nn.softplus(-channels[0])
    log_decay = -DECAY_SCALE * sig_a * soft
    decay = jnp.exp(log_decay)
    root = jnp.sqrt(-jnp.expm1(2.0 * log_decay))
    uf = u.astype(F32)
    drive = root * sig_i * uf
    running, state = local_scan(decay, drive, False)
    incoming = carried(running[:, -1], state[:, -1], False)
    states = state + running * incoming[:, None]
    gelu_y, slope_y = gelu_both(gy)
    mixed = (gelu_y * states).astype(BF).reshape(-1, local)
    middle = own.astype(F32) + exchange.scatter(dot(mixed, w_o, NT))
    n2_own = (middle * inverse_rms(middle) * gains[1]).astype(BF)
    n2 = exchange.gather(n2_own)

    hidden, gates_pre = [], []
    for k in range(2):
        pre = dot(n2, w_gu[k], NN)
        gm, up = pre[:, :half], pre[:, half:]
        gates_pre.append((gm, up))
        hidden.append((gelu(gm) * up).astype(BF))
    hidden = jnp.concatenate(hidden, axis=1)
    g_down = dot(dm, hidden, TN, BF)
    share_down = return_grad(g_down, drows)
    dhm = dot(dm, w_d, NN)
    pair_grads, g_gu, dn2 = [], [], None
    for k in range(2):
        gm, up = gates_pre[k]
        value, slope = gelu_both(gm)
        d = dhm[:, k * half : (k + 1) * half]
        pair = jnp.concatenate([(d * up * slope).astype(BF), (d * value).astype(BF)], axis=1)
        pair_grads.append(pair)
        term = dot(pair, w_gu[k], NT)
        dn2 = term if dn2 is None else dn2 + term
    share_gu = [return_grad(dot(n2, pair_grads[k], TN, BF), drows) for k in range(2)]
    dn2_own = exchange.scatter(dn2)
    part, gain_two = norm_grad(middle, gains[1], dn2_own)
    dr1 = dout + part
    do = exchange.gather(dr1.astype(BF))

    result = middle + exchange.scatter(dot(hidden, w_d, NT))
    result = result.astype(BF)

    share_o = return_grad(dot(do, mixed, TN, BF), drows)
    dz = dot(do, w_o, NN).reshape(4, 2 * length, local)
    dh = dz * gelu_y
    dgy = (dz * states * slope_y).astype(BF)
    ones = jnp.ones_like(decay[:, :1])
    after, adjoint = local_scan(jnp.concatenate([decay[:, 1:], ones], axis=1), dh, True)
    later = carried(running[:, -1], decay[:, 0] * adjoint[:, 0], True)
    adjoint = adjoint + after * later[:, None]
    previous = jnp.concatenate([incoming[:, None], states[:, :-1]], axis=1)
    d_root = adjoint * sig_i * uf
    d_sig_i = adjoint * root * uf
    du0 = adjoint * root * sig_i
    d_log = adjoint * previous * decay - d_root * decay * decay / root
    dra = (d_log * (-DECAY_SCALE * soft) * sig_a * (1.0 - sig_a)).astype(BF)
    dri = (d_sig_i * sig_i * (1.0 - sig_i)).astype(BF)
    dlam = jnp.sum(d_log * sig_a, axis=(0, 1)) * DECAY_SCALE * jax.nn.sigmoid(-channels[0])
    dlogits = jnp.concatenate([dra, dri], axis=2).reshape(-1, 2 * local)
    g_blocks = dot(u2, dlogits, TN)
    du = du0 + dot(dlogits, blocks, NT).reshape(4, 2 * length, local)
    zeros = jnp.zeros((4, 3, local), F32)
    spread = jnp.concatenate([zeros, du, zeros], axis=1)
    dpad = jnp.zeros((4, 2 * length + 3, local), F32)
    taps = []
    for k in range(4):
        dpad = dpad + channels[4 + k] * spread[:, k : k + 2 * length + 3]
        taps.append(jnp.sum(du * padded[:, 3 - k : 3 - k + 2 * length], axis=(0, 1)))
    back = from_behind(dpad[:, :3], -1)
    dxb = dpad[:, 3:] + jnp.concatenate(
        [jnp.zeros((4, 2 * length - 3, local), F32), back], axis=1
    )
    dboth = jnp.concatenate([dxb.astype(BF), dgy], axis=2).reshape(-1, 2 * local)
    share_ig = return_grad(dot(n1, dboth, TN, BF), drows)
    dn1_own = exchange.scatter(dot(dboth, w_ig, NT))
    part, gain_one = norm_grad(own.astype(F32), gains[0], dn1_own)
    dx_own = dr1 + part

    g_gates = jnp.stack(
        [
            jnp.stack(
                [
                    g_blocks[
                        h * BLOCK : (h + 1) * BLOCK,
                        g * local + h * BLOCK : g * local + (h + 1) * BLOCK,
                    ]
                    for h in range(heads)
                ]
            )
            for g in range(2)
        ]
    )
    g_gates = g_gates.reshape(2 * heads, group, piece).transpose(1, 0, 2)
    g_gates = g_gates.reshape(dxn, 2, zhn, 2, 2 * heads * piece)
    g_gates = scatter_blocks(scatter_blocks(g_gates, "dx", 0), "zh", 1)
    g_gates = g_gates.reshape(4, 2, heads, piece).astype(BF)
    g_gates = lax.all_to_all(g_gates, ("dc", "zl"), 0, 0, tiled=True).astype(F32)
    g_gates = g_gates.transpose(1, 0, 2, 3).reshape(2, 4 * heads, piece)

    channel_grad = jnp.stack(
        [
            dlam,
            jnp.sum(dra.astype(F32), axis=(0, 1)),
            jnp.sum(dri.astype(F32), axis=(0, 1)),
            jnp.sum(du, axis=(0, 1)),
        ]
        + taps
    )
    spot = (mp * 4 + slot).astype(jnp.int32)
    table = jnp.where(
        jnp.arange(8, dtype=jnp.int32)[:, None, None] == spot, channel_grad[None], 0.0
    )
    sums = jnp.concatenate([table.reshape(-1), gain_one, gain_two])
    sums = lax.psum(sums, AXES)
    share = lax.axis_index(("dx", "dc", "zh", "zl"))
    table = sums[: table.size].reshape(2, 4, 8, local).transpose(0, 2, 1, 3)
    table = lax.dynamic_index_in_dim(table.reshape(2, 8, 4 * local), mp, 0, keepdims=False)
    per = 4 * local // group
    g_channels = lax.dynamic_slice_in_dim(table, share * per, per, 1).reshape(8, 1, per)
    g_gains = sums[-2 * width :].reshape(2, width)
    g_gains = lax.dynamic_slice_in_dim(g_gains, share * drows, drows, 1)

    def both_batches(rows):
        other = lax.ppermute(rows, "mp", [(0, 1), (1, 0)])
        return jnp.stack([jnp.where(mp == 0, rows, other), jnp.where(mp == 0, other, rows)])

    block_out = both_batches(result)[:, None]
    grad_tokens = both_batches(dx_own)[:, None]

    def columns(share, at, count):
        return (
            share[:, :, at : at + count].astype(F32).transpose(1, 0, 2).reshape(drows, 4 * count)
        )

    g_gate = jnp.stack([s[:, :, :half] for s in share_gu], axis=2)
    g_up = jnp.stack([s[:, :, half:] for s in share_gu], axis=2)
    g_gate, g_up = (
        v.astype(F32).transpose(1, 0, 2, 3).reshape(drows, 4 * ff) for v in (g_gate, g_up)
    )
    return (
        block_out,
        grad_tokens,
        columns(share_ig, 0, local),
        columns(share_ig, local, local),
        g_gates[0],
        g_gates[1],
        g_channels,
        g_gains,
        columns(share_o, 0, local).T,
        g_gate,
        g_up,
        columns(share_down, 0, ff).T,
    )


def solution(mesh):
    dpn, seqn, mpn = (mesh.shape[n] for n in ("dp", "seq", "mp"))
    fine = Mesh(mesh.devices.reshape(dpn // 2, 2, seqn // 2, 2, mpn), AXES)
    dp, seq = ("dx", "dc"), ("zh", "zl")
    shards = dp + seq
    weights = (
        P(shards, "mp"),
        P(shards, "mp"),
        P("mp", shards),
        P("mp", shards),
        P(None, "mp", shards),
        P(None, shards),
        P("mp", shards),
        P(shards, "mp"),
        P(shards, "mp"),
        P("mp", shards),
    )
    rows = P(None, dp, seq, None)
    return jax.shard_map(
        on_device,
        mesh=fine,
        in_specs=(rows, rows, P(None, dp), P()) + weights,
        out_specs=(rows, rows) + weights,
        check_vma=False,
    )
```

```python
import jax
import jax.numpy as jnp
import numpy as np
from jax import lax
from jax.experimental import pallas as pl
from jax.experimental.pallas import tpu as pltpu
from jax.sharding import Mesh, PartitionSpec as P

WIDTH = 2560
HEADS = 16
BLOCK = WIDTH // HEADS
EPSILON = 1e-06
DECAY_SCALE = 8.0
AXES = ("dx", "dc", "zh", "zl", "mp")
BF = jnp.bfloat16
F32 = jnp.float32


def swap_pairs(sizes, partner):
    pairs = []
    for flat in range(int(np.prod(sizes))):
        coords = np.unravel_index(flat, sizes)
        pairs.append((flat, int(np.ravel_multi_index(partner(*map(int, coords)), sizes))))
    return pairs


def gather_blocks(x, axis, dim):
    if lax.axis_size(axis) != 2:
        return lax.all_gather(x, axis, axis=dim, tiled=False)
    here = lax.axis_index(axis)
    other = lax.ppermute(x, axis, [(0, 1), (1, 0)])
    low = jnp.where(here == 0, x, other)
    high = jnp.where(here == 0, other, x)
    return jnp.stack([low, high], axis=dim)


def scatter_blocks(x, axis, dim):
    if lax.axis_size(axis) != 2:
        n = x.shape[dim]
        out = lax.psum_scatter(x.astype(BF), axis, scatter_dimension=dim, tiled=True)
        return lax.squeeze(out, [dim]).astype(F32)
    here = lax.axis_index(axis)
    mine = lax.dynamic_index_in_dim(x, here, dim, keepdims=False)
    theirs = lax.dynamic_index_in_dim(x, 1 - here, dim, keepdims=False)
    got = lax.ppermute(theirs.astype(BF), axis, [(0, 1), (1, 0)])
    return mine.astype(F32) + got.astype(F32)


def fetch_weight(shard, parts):
    rows, cols = shard[0].shape[0], None
    pieces = [s.reshape(rows, parts, -1) for s in shard]
    joined = jnp.concatenate(pieces, axis=2) if len(pieces) > 1 else pieces[0]
    cols = joined.shape[2]
    x = jnp.transpose(joined, (1, 0, 2))
    x = lax.all_to_all(x, ("dc", "zl"), 0, 0, tiled=True)
    x = x.reshape(2, 2, rows, cols)
    x = gather_blocks(x, "zh", 1)
    x = gather_blocks(x, "dx", 0)
    return x.reshape(-1, cols)


def return_grad(grad, rows):
    cols = grad.shape[1]
    dxn, zhn = lax.axis_size("dx"), lax.axis_size("zh")
    g = grad.reshape(dxn, 2, zhn, 2, rows, cols)
    g = scatter_blocks(g, "dx", 0)
    g = scatter_blocks(g, "zh", 1)
    g = g.astype(BF).reshape(4, rows, cols)
    return lax.all_to_all(g, ("dc", "zl"), 0, 0, tiled=True)


class Tokens:
    def __init__(self):
        sizes = tuple(lax.axis_size(n) for n in AXES)
        self.core = swap_pairs(sizes, lambda a, b, c, d, e: (a, 1 - b, c, d, e))
        self.first = swap_pairs(
            sizes, lambda a, b, c, d, e: (a, b, c, d, 1 - e) if b == 0 else (a, b, c, 1 - d, e)
        )
        self.second = swap_pairs(
            sizes, lambda a, b, c, d, e: (a, b, c, 1 - d, e) if b == 0 else (a, b, c, d, 1 - e)
        )
        self.dc, self.zl, self.mp = (lax.axis_index(n) for n in ("dc", "zl", "mp"))

    def order(self, dc):
        mp, zl = self.mp, self.zl
        own = mp * 2 + zl
        by_mp = (1 - mp) * 2 + zl
        by_zl = mp * 2 + 1 - zl
        both = (1 - mp) * 2 + 1 - zl
        one = jnp.where(dc == 0, by_mp, by_zl)
        two = jnp.where(dc == 0, by_zl, by_mp)
        return own, one, two, both

    def gather(self, x):
        rows, width = x.shape
        one = lax.ppermute(x, AXES, self.first)
        two = lax.ppermute(jnp.stack([x, one]), AXES, self.second)
        far = [lax.ppermute(v, AXES, self.core) for v in (x, one, two)]
        out = jnp.zeros((8, rows, width), x.dtype)
        for dc, blocks in (
            (self.dc, (x, one, two[0], two[1])),
            (1 - self.dc, (far[0], far[1], far[2][0], far[2][1])),
        ):
            for at, block in zip(self.order(dc), blocks):
                out = lax.dynamic_update_index_in_dim(out, block, dc * 4 + at, 0)
        return out.reshape(8 * rows, width)

    def scatter(self, x):
        rows, width = x.shape[0] // 8, x.shape[1]
        x = x.reshape(2, 4, rows, width)
        theirs = lax.dynamic_index_in_dim(x, 1 - self.dc, 0, keepdims=False).astype(BF)
        mine = lax.dynamic_index_in_dim(x, self.dc, 0, keepdims=False)
        total = mine.astype(F32) + lax.ppermute(theirs, AXES, self.core).astype(F32)
        own, one, two, both = self.order(self.dc)
        pick = lambda at: lax.dynamic_index_in_dim(total, at, 0, keepdims=False)
        got = lax.ppermute(jnp.stack([pick(two), pick(both)]).astype(BF), AXES, self.second)
        keep_own = pick(own) + got[0].astype(F32)
        keep_one = pick(one) + got[1].astype(F32)
        got = lax.ppermute(keep_one.astype(BF), AXES, self.first)
        return keep_own + got.astype(F32)


MESH = pl.DeviceIdType.MESH
ANY = pl.BlockSpec(memory_space=pl.ANY)
VMEM = pl.BlockSpec(memory_space=pltpu.VMEM)
VMEM_BYTES = 40 * 1024 * 1024


def flip(index, by):
    return 1 - index if by else index


class Place:
    def __init__(self):
        self.dx, self.dc, self.zh, self.zl, self.mp = (lax.axis_index(n) for n in AXES)

    def peer(self, dx=0, dc=0, zh=0, zl=0, mp=0):
        return (
            flip(self.dx, dx),
            flip(self.dc, dc),
            flip(self.zh, zh),
            flip(self.zl, zl),
            flip(self.mp, mp),
        )

    def block(self, dx=0, dc=0, zh=0, zl=0):
        a, b, c, d, _ = self.peer(dx, dc, zh, zl)
        return ((a * 2 + b) * 2 + c) * 2 + d

    def slot(self, dc=0, zl=0):
        return flip(self.dc, dc) * 2 + flip(self.zl, zl)

    def rows(self, dc=0, mp=0, zl=0):
        return (flip(self.dc, dc) * 2 + flip(self.mp, mp)) * 2 + flip(self.zl, zl)


def greet(peers):
    barrier = pltpu.get_barrier_semaphore()
    for device in peers:
        pl.semaphore_signal(barrier, inc=1, device_id=device, device_id_type=MESH)
    pl.semaphore_wait(barrier, len(peers))


class Links:
    def __init__(self, send, recv, local):
        self.send, self.recv, self.local = send, recv, local
        self.n, self.m = 0, 0
        self.sent, self.copies = [], []

    def pair(self):
        self.n += 1
        return self.n - 1

    def start(self, src, dst, at, device):
        copy = pltpu.make_async_remote_copy(
            src_ref=src,
            dst_ref=dst,
            send_sem=self.send.at[at],
            recv_sem=self.recv.at[at],
            device_id=device,
            device_id_type=MESH,
        )
        copy.start()
        self.sent.append(copy)

    def arrived(self, ref, at):
        pltpu.make_async_copy(ref, ref, self.recv.at[at]).wait()

    def keep(self, src, dst):
        copy = pltpu.make_async_copy(src, dst, self.local.at[self.m])
        self.m += 1
        copy.start()
        return copy

    def finish(self):
        for copy in self.sent:
            copy.wait_send()


FLIPS = [(zh, dc, zl) for zh in (1, 0) for dc in (0, 1) for zl in (0, 1)]


class WeightGather:
    def __init__(self, place, links, source, target, unit):
        self.place, self.links, self.target = place, links, target
        self.at = {f: links.pair() for f in FLIPS}
        self.cross = {(zh, dc): links.pair() for zh in (0, 1) for dc in (0, 1)}
        self.source = source
        self.kept = None

    def begin(self, zhs=(1, 0)):
        p = self.place
        mine = p.block()
        for f in FLIPS:
            zh, dc, zl = f
            if zh not in zhs:
                continue
            src, dst = self.source(p.slot(dc, zl)), self.target(mine, 1)
            if f == (0, 0, 0):
                self.kept = self.links.keep(src, dst)
            else:
                self.links.start(src, dst, self.at[f], p.peer(dc=dc, zh=zh, zl=zl))

    def onward(self, zh):
        p = self.place
        for dc in (0, 1):
            for zl in (0, 1):
                if (zh, dc, zl) == (0, 0, 0):
                    self.kept.wait()
                else:
                    self.links.arrived(
                        self.target(p.block(dc=dc, zh=zh, zl=zl), 1), self.at[zh, dc, zl]
                    )
            two = self.target(p.block(dc=dc, zh=zh) // 2 * 2, 2)
            self.links.start(two, two, self.cross[zh, dc], p.peer(dx=1))

    def end(self):
        p = self.place
        for zh in (0, 1):
            for dc in (0, 1):
                two = self.target(p.block(dx=1, dc=dc, zh=zh) // 2 * 2, 2)
                self.links.arrived(two, self.cross[zh, dc])


def row_blocks(ref, unit, cols=None):
    def target(first, count):
        rows = pl.ds(pl.multiple_of(first * unit, unit), count * unit)
        return ref.at[rows] if cols is None else ref.at[rows, cols]

    return target


def column_blocks(ref, unit):
    return lambda first, count: ref.at[:, pl.ds(pl.multiple_of(first * unit, unit), count * unit)]


def first_kernel(tok_ref, ig_ref, o_ref, all_ref, wig_ref, wo_ref, send, recv, local):
    p = Place()
    links = Links(send, recv, local)
    drows = ig_ref.shape[1]
    crows = wo_ref.shape[0]
    greet(weight_peers(p))
    gather = TokenGatherTwice(p, links, tok_ref, all_ref)
    gather.begin()
    w_ig = WeightGather(p, links, lambda j: ig_ref.at[j], row_blocks(wig_ref, drows), drows)
    w_o = WeightGather(
        p,
        links,
        lambda j: o_ref.at[pl.ds(pl.multiple_of(j * crows, 16), crows)],
        column_blocks(wo_ref, o_ref.shape[1]),
        drows,
    )
    w_ig.begin((0,))
    w_ig.begin((1,))
    w_o.begin((0,))
    w_ig.onward(0)
    w_o.begin((1,))
    w_o.onward(0)
    gather.forward()
    gather.forward_core()
    w_ig.onward(1)
    w_o.onward(1)
    gather.end()
    w_ig.end()
    w_o.end()
    links.finish()


class TokenGatherTwice:
    def __init__(self, place, links, source, target):
        self.place, self.links, self.source, self.target = place, links, source, target
        self.z, self.y = links.pair(), links.pair()
        self.core = {(mp, zl): links.pair() for mp in (0, 1) for zl in (0, 1)}

    def begin(self):
        p = self.place
        self.kept = []
        for mp in (0, 1):
            at = p.rows(mp=mp)
            src = self.source.at[flip(p.mp, mp)]
            if mp == 0:
                self.links.start(src, self.target.at[at], self.z, p.peer(zl=1))
            self.links.start(src, self.target.at[at], self.core[mp, 0], p.peer(dc=1))
            self.kept.append(self.links.keep(src, self.target.at[at]))

    def forward(self):
        p = self.place
        far = self.target.at[p.rows(zl=1)]
        self.links.arrived(far, self.z)
        self.links.start(far, far, self.y, p.peer(mp=1))
        self.links.start(far, far, self.core[0, 1], p.peer(dc=1))

    def forward_core(self):
        p = self.place
        far = self.target.at[p.rows(mp=1, zl=1)]
        self.links.arrived(far, self.y)
        self.links.start(far, far, self.core[1, 1], p.peer(dc=1))

    def end(self):
        p = self.place
        for (mp, zl), at in self.core.items():
            self.links.arrived(self.target.at[p.rows(dc=1, mp=mp, zl=zl)], at)
        for copy in self.kept:
            copy.wait()


class TokenGather:
    def __init__(self, place, links, source, target):
        self.place, self.links, self.source, self.target = place, links, source, target
        self.z, self.y0, self.y1 = links.pair(), links.pair(), links.pair()
        self.core = {(mp, zl): links.pair() for mp in (0, 1) for zl in (0, 1)}

    def begin(self):
        p = self.place
        at = self.target.at[p.rows()]
        self.links.start(self.source, at, self.z, p.peer(zl=1))
        self.links.start(self.source, at, self.y0, p.peer(mp=1))
        self.links.start(self.source, at, self.core[0, 0], p.peer(dc=1))
        self.kept = self.links.keep(self.source, at)

    def forward(self):
        p = self.place
        far = self.target.at[p.rows(zl=1)]
        self.links.arrived(far, self.z)
        self.links.start(far, far, self.y1, p.peer(mp=1))
        self.links.start(far, far, self.core[0, 1], p.peer(dc=1))

    def forward_core(self):
        p = self.place
        far = self.target.at[p.rows(mp=1)]
        self.links.arrived(far, self.y0)
        self.links.start(far, far, self.core[1, 0], p.peer(dc=1))
        far = self.target.at[p.rows(mp=1, zl=1)]
        self.links.arrived(far, self.y1)
        self.links.start(far, far, self.core[1, 1], p.peer(dc=1))

    def end(self):
        p = self.place
        for (mp, zl), at in self.core.items():
            self.links.arrived(self.target.at[p.rows(dc=1, mp=mp, zl=zl)], at)
        self.kept.wait()


CHUNK = 16


def chunks(count, body):
    def step(i, carry):
        body(pl.ds(pl.multiple_of(i * CHUNK, CHUNK), CHUNK))
        return carry

    lax.fori_loop(0, count // CHUNK, step, 0)


class RowScatter:
    def __init__(self, place, links, source, buffers):
        self.place, self.links, self.source = place, links, source
        self.mine, self.from_core, self.from_y, self.from_z, self.out = buffers
        self.core = {(mp, zl): links.pair() for mp in (1, 0) for zl in (1, 0)}
        self.y = {zl: links.pair() for zl in (1, 0)}
        self.z = links.pair()

    def begin(self):
        p = self.place
        self.kept = {}
        for (mp, zl), at in self.core.items():
            src = self.source.at[p.rows(dc=1, mp=mp, zl=zl)]
            self.links.start(src, self.from_core.at[mp * 2 + zl], at, p.peer(dc=1))
        for mp, zl in self.core:
            src = self.source.at[p.rows(mp=mp, zl=zl)]
            self.kept[mp, zl] = self.links.keep(src, self.mine.at[mp * 2 + zl])

    def ready(self, mp, zl):
        i = mp * 2 + zl
        self.kept[mp, zl].wait()
        self.links.arrived(self.from_core.at[i], self.core[mp, zl])
        return i

    def across_y(self):
        p = self.place
        for zl in (1, 0):
            i = self.ready(1, zl)

            def add(rows, i=i, zl=zl):
                total = self.mine[i, rows, :].astype(F32) + self.from_core[i, rows, :].astype(F32)
                self.out[zl, rows, :] = total.astype(BF)

            chunks(self.mine.shape[1], add)
            self.links.start(self.out.at[zl], self.from_y.at[zl], self.y[zl], p.peer(mp=1))

    def across_z(self):
        p = self.place
        i = self.ready(0, 1)
        self.links.arrived(self.from_y.at[1], self.y[1])

        def add(rows):
            total = self.mine[i, rows, :].astype(F32) + self.from_core[i, rows, :].astype(F32)
            self.out[2, rows, :] = (total + self.from_y[1, rows, :].astype(F32)).astype(BF)

        chunks(self.mine.shape[1], add)
        self.links.start(self.out.at[2], self.from_z, self.z, p.peer(zl=1))

    def arrive(self):
        self.ready(0, 0)
        self.links.arrived(self.from_y.at[0], self.y[0])
        self.links.arrived(self.from_z, self.z)

    def total(self, rows):
        a = self.mine[0, rows, :].astype(F32) + self.from_core[0, rows, :].astype(F32)
        b = self.from_y[0, rows, :].astype(F32) + self.from_z[rows, :].astype(F32)
        return a + b


def scatter_buffers(rows, width):
    return [
        pltpu.VMEM((4, rows, width), BF),
        pltpu.VMEM((4, rows, width), BF),
        pltpu.VMEM((2, rows, width), BF),
        pltpu.VMEM((rows, width), BF),
        pltpu.VMEM((3, rows, width), BF),
    ]


def group_peers(p):
    return [p.peer(dc=1), p.peer(zl=1), p.peer(mp=1)]


def weight_peers(p):
    return [p.peer(dc=dc, zh=zh, zl=zl) for zh, dc, zl in FLIPS if (zh, dc, zl) != (0, 0, 0)] + [
        p.peer(dx=1),
        p.peer(mp=1),
    ]


def second_kernel(
    part_ref, own_ref, gain_ref, cot_ref, gate_ref, up_ref, down_ref,
    mid_ref, all_ref, dm_ref, wgu_ref, wd_ref,
    mine, from_core, from_y, from_z, out, normed, send, recv, local,
):
    p = Place()
    links = Links(send, recv, local)
    drows, ff = gate_ref.shape[0], wd_ref.shape[0]
    greet(weight_peers(p))
    scatter = RowScatter(p, links, part_ref, (mine, from_core, from_y, from_z, out))
    scatter.begin()

    def wide(ref, at):
        return WeightGather(
            p,
            links,
            lambda j: ref.at[:, pl.ds(pl.multiple_of(j * ff, 128), ff)],
            row_blocks(wgu_ref, drows, pl.ds(at, ff)),
            drows,
        )

    w_g, w_u = wide(gate_ref, 0), wide(up_ref, ff)
    w_d = WeightGather(
        p,
        links,
        lambda j: down_ref.at[pl.ds(pl.multiple_of(j * ff, 16), ff)],
        column_blocks(wd_ref, down_ref.shape[1]),
        drows,
    )
    w_g.begin((0,))
    w_g.begin((1,))
    w_u.begin((0,))
    w_d.begin((0,))
    scatter.across_y()
    w_u.begin((1,))
    w_g.onward(0)
    w_u.onward(0)
    w_d.onward(0)
    scatter.across_z()
    scatter.arrive()

    def normalise(rows):
        value = own_ref[rows, :].astype(F32) + scatter.total(rows)
        mid_ref[rows, :] = value
        inv = lax.rsqrt(jnp.mean(value * value, axis=-1, keepdims=True) + EPSILON)
        normed[rows, :] = (value * inv * gain_ref[...]).astype(BF)

    chunks(own_ref.shape[0], normalise)
    gather = TokenGather(p, links, normed, all_ref)
    gather.begin()
    w_d.begin((1,))
    w_g.onward(1)
    gather.forward()
    adjoint = TokenGatherTwice(p, links, cot_ref, dm_ref)
    adjoint.begin()
    gather.forward_core()
    w_u.onward(1)
    adjoint.forward()
    adjoint.forward_core()
    w_d.onward(1)
    gather.end()
    adjoint.end()
    w_g.end()
    w_u.end()
    w_d.end()
    links.finish()


class GradScatter:
    def __init__(self, place, links, source, result, by_rows, buffers):
        self.place, self.links, self.source, self.result = place, links, source, result
        self.by_rows = by_rows
        self.mine, self.from_x, self.to_z, self.from_z, self.sums = buffers
        self.x = {(zh, dc): links.pair() for zh in (1, 0) for dc in (0, 1)}
        self.z = {dc: links.pair() for dc in (0, 1)}
        self.at = {(dc, zl): links.pair() for dc in (0, 1) for zl in (0, 1)}
        self.kept = {}

    def begin(self, zh):
        p = self.place
        for dc in (0, 1):
            i = zh * 2 + dc
            theirs = self.source(p.block(dx=1, dc=dc, zh=zh) // 2 * 2, 2)
            self.links.start(theirs, self.from_x.at[i], self.x[zh, dc], p.peer(dx=1))
            mine = self.source(p.block(dc=dc, zh=zh) // 2 * 2, 2)
            self.kept[zh, dc] = self.links.keep(mine, self.mine.at[i])

    def ready(self, zh, dc):
        self.kept[zh, dc].wait()
        self.links.arrived(self.from_x.at[zh * 2 + dc], self.x[zh, dc])
        return zh * 2 + dc

    def across(self, dc):
        i = self.ready(1, dc)

        def add(rows):
            total = self.mine[i, rows, :].astype(F32) + self.from_x[i, rows, :].astype(F32)
            self.to_z[dc, rows, :] = total.astype(BF)

        chunks(self.mine.shape[1], add)
        self.links.start(self.to_z.at[dc], self.from_z.at[dc], self.z[dc], self.place.peer(zh=1))

    def last(self, dc):
        p = self.place
        i = self.ready(0, dc)
        self.links.arrived(self.from_z.at[dc], self.z[dc])

        def add(rows):
            total = self.mine[i, rows, :].astype(F32) + self.from_x[i, rows, :].astype(F32)
            self.sums[dc, rows, :] = (total + self.from_z[dc, rows, :].astype(F32)).astype(BF)

        chunks(self.mine.shape[1], add)
        for zl in (1, 0):
            src = self.one(dc, flip(p.zl, zl))
            dst = self.result.at[p.slot()]
            if (dc, zl) == (0, 0):
                self.own = self.links.keep(src, dst)
            else:
                self.links.start(src, dst, self.at[dc, zl], p.peer(dc=dc, zl=zl))

    def one(self, dc, zl):
        unit = self.result.shape[1] if self.by_rows else self.result.shape[2]
        span = pl.ds(pl.multiple_of(zl * unit, unit), unit)
        return self.sums.at[dc, span] if self.by_rows else self.sums.at[dc, :, span]

    def end(self):
        p = self.place
        for (dc, zl), at in self.at.items():
            if (dc, zl) == (0, 0):
                self.own.wait()
            else:
                self.links.arrived(self.result.at[p.slot(dc, zl)], at)


def grad_buffers(rows, columns):
    return [
        pltpu.VMEM((n, rows, columns), BF)
        for n in (4, 4, 2, 2, 2)
    ]


def norm_back(value, gain, upstream):
    inv = lax.rsqrt(jnp.mean(value * value, axis=-1, keepdims=True) + EPSILON)
    scaled = value * inv
    up = upstream * gain
    inner = jnp.mean(up * scaled, axis=-1, keepdims=True)
    return inv * (up - scaled * inner), upstream * scaled


def fold(rows):
    return rows[:8] + rows[8:]


def third_kernel(
    part_ref, mid_ref, dout_ref, gain_ref, gd_ref, ggu_ref,
    dr1_ref, gain_out, all_ref, sd_ref, sgu_ref,
    *scratch,
):
    p = Place()
    links = Links(*scratch[-3:])
    do = scratch[-4]
    unit = sgu_ref.shape[1]
    greet(weight_peers(p))
    scatter = RowScatter(p, links, part_ref, scratch[:5])
    down = GradScatter(p, links, column_blocks(gd_ref, unit), sd_ref, False, scratch[5:10])
    wide = GradScatter(p, links, row_blocks(ggu_ref, unit), sgu_ref, True, scratch[10:15])
    scatter.begin()
    down.begin(1)
    wide.begin(1)
    scatter.across_y()
    down.across(0)
    down.across(1)
    down.begin(0)
    wide.across(0)
    scatter.across_z()
    scatter.arrive()
    gain_out[...] = jnp.zeros_like(gain_out)

    def back(rows):
        part, gain = norm_back(mid_ref[rows, :], gain_ref[...], scatter.total(rows))
        value = dout_ref[rows, :] + part
        dr1_ref[rows, :] = value
        do[rows, :] = value.astype(BF)
        gain_out[...] += fold(gain)

    chunks(mid_ref.shape[0], back)
    gather = TokenGather(p, links, do, all_ref)
    gather.begin()
    wide.across(1)
    wide.begin(0)
    gather.forward()
    down.last(0)
    down.last(1)
    gather.forward_core()
    wide.last(0)
    wide.last(1)
    gather.end()
    down.end()
    wide.end()
    links.finish()


def fourth_kernel(
    part_ref, own_ref, dr1_ref, gain_ref, go_ref, gig_ref, gg_ref,
    dx_ref, gain_out, so_ref, sig_ref, sg_ref,
    *scratch,
):
    p = Place()
    links = Links(*scratch[-3:])
    greet(weight_peers(p))
    scatter = RowScatter(p, links, part_ref, scratch[:5])
    out = GradScatter(
        p, links, column_blocks(go_ref, so_ref.shape[2]), so_ref, False, scratch[5:10]
    )
    wide = GradScatter(
        p, links, row_blocks(gig_ref, sig_ref.shape[1]), sig_ref, True, scratch[10:15]
    )
    gates = GradScatter(p, links, row_blocks(gg_ref, sg_ref.shape[1]), sg_ref, True, scratch[15:20])
    grads = (out, wide, gates)
    for g in grads:
        g.begin(1)
    scatter.begin()
    for g in grads:
        g.across(0)
        g.across(1)
        g.begin(0)
    scatter.across_y()
    for g in (out, gates):
        g.last(0)
        g.last(1)
    scatter.across_z()
    wide.last(0)
    wide.last(1)
    scatter.arrive()
    gain_out[...] = jnp.zeros_like(gain_out)

    def back(rows):
        value = own_ref[rows, :].astype(F32)
        part, gain = norm_back(value, gain_ref[...], scatter.total(rows))
        dx_ref[rows, :] = dr1_ref[rows, :] + part
        gain_out[...] += fold(gain)

    chunks(own_ref.shape[0], back)
    for g in grads:
        g.end()
    links.finish()


def semaphores(pairs, local):
    return [
        pltpu.SemaphoreType.DMA((pairs,)),
        pltpu.SemaphoreType.DMA((pairs,)),
        pltpu.SemaphoreType.DMA((local,)),
    ]


def run_kernel(body, name, outs, out_specs, in_specs, scratch, ident, args):
    return pl.pallas_call(
        body,
        name=name,
        out_shape=[jax.ShapeDtypeStruct(*o) for o in outs],
        in_specs=in_specs,
        out_specs=out_specs,
        scratch_shapes=scratch,
        compiler_params=pltpu.CompilerParams(
            collective_id=ident, has_side_effects=True, vmem_limit_bytes=VMEM_BYTES
        ),
    )(*args)


def fetch_first(tokens, input_weight, gelu_weight, output_weight):
    if not shape_fits():
        return plain_fetch_first(tokens, input_weight, gelu_weight, output_weight)
    rows, width = tokens.shape[1:]
    drows, local = input_weight.shape[0], input_weight.shape[1] // 4
    pairs = [v.reshape(drows, 4, local) for v in (input_weight, gelu_weight)]
    ig = jnp.concatenate(pairs, axis=2).transpose(1, 0, 2)
    return run_kernel(
        first_kernel,
        "fetch_first",
        [((8, rows, width), BF), ((width, 2 * local), BF), ((local, width), BF)],
        [ANY] * 3,
        [ANY] * 3,
        semaphores(32, 8),
        1,
        (tokens, ig, output_weight),
    )


def reduce_and_fetch(part, own, gain, dm, mlp_gate, mlp_up, mlp_down):
    if not shape_fits():
        return plain_reduce_and_fetch(part, own, gain, dm, mlp_gate, mlp_up, mlp_down)
    rows, width = own.shape
    ff = mlp_gate.shape[1] // 4
    return run_kernel(
        second_kernel,
        "reduce_and_fetch",
        [
            ((rows, width), F32),
            ((8, rows, width), BF),
            ((8, rows, width), BF),
            ((width, 2 * ff), BF),
            ((ff, width), BF),
        ],
        [VMEM] + [ANY] * 4,
        [ANY, VMEM, VMEM] + [ANY] * 4,
        scatter_buffers(rows, width) + [pltpu.VMEM((rows, width), BF)] + semaphores(64, 16),
        2,
        (part.reshape(8, rows, width), own, gain, dm, mlp_gate, mlp_up, mlp_down),
    )


def reduce_and_return(part, middle, dout, gain, g_down, g_wide, drows):
    if not shape_fits():
        return plain_reduce_and_return(part, middle, dout, gain, g_down, g_wide, drows)
    rows, width = middle.shape
    ff = g_down.shape[0]
    return run_kernel(
        third_kernel,
        "reduce_and_return",
        [
            ((rows, width), F32),
            ((8, width), F32),
            ((8, rows, width), BF),
            ((4, ff, drows), BF),
            ((4, drows, g_wide.shape[1]), BF),
        ],
        [VMEM, VMEM] + [ANY] * 3,
        [ANY] + [VMEM] * 3 + [ANY] * 2,
        scatter_buffers(rows, width)
        + grad_buffers(ff, 2 * drows)
        + grad_buffers(2 * drows, g_wide.shape[1])
        + [pltpu.VMEM((rows, width), BF)]
        + semaphores(40, 24),
        3,
        (part.reshape(8, rows, width), middle, dout, gain, g_down, g_wide),
    )


def return_last(part, own, dr1, gain, g_out, g_wide, g_gates, drows):
    if not shape_fits():
        return plain_return_last(part, own, dr1, gain, g_out, g_wide, g_gates, drows)
    rows, width = own.shape
    local, unit = g_out.shape[0], g_gates.shape[0] // 16
    return run_kernel(
        fourth_kernel,
        "return_last",
        [
            ((rows, width), F32),
            ((8, width), F32),
            ((4, local, drows), BF),
            ((4, drows, g_wide.shape[1]), BF),
            ((4, unit, 128), BF),
        ],
        [VMEM, VMEM] + [ANY] * 3,
        [ANY] + [VMEM] * 3 + [ANY] * 3,
        scatter_buffers(rows, width)
        + grad_buffers(local, 2 * drows)
        + grad_buffers(2 * drows, g_wide.shape[1])
        + grad_buffers(2 * unit, 128)
        + semaphores(48, 32),
        4,
        (part.reshape(8, rows, width), own, dr1, gain, g_out, g_wide, g_gates),
    )


def shape_fits():
    return all(lax.axis_size(n) == 2 for n in AXES)


def plain_fetch_first(tokens, input_weight, gelu_weight, output_weight):
    exchange = Tokens()
    own = lax.dynamic_index_in_dim(tokens, exchange.mp, 0, keepdims=False)
    return (
        exchange.gather(own).reshape((8,) + own.shape),
        fetch_weight([input_weight, gelu_weight], 4),
        fetch_weight([output_weight.T], 4).T,
    )


def plain_reduce_and_fetch(part, own, gain, dm, mlp_gate, mlp_up, mlp_down):
    exchange = Tokens()
    middle = own.astype(F32) + exchange.scatter(part)
    normed = (middle * inverse_rms(middle) * gain).astype(BF)
    dm = lax.dynamic_index_in_dim(dm, exchange.mp, 0, keepdims=False)
    return (
        middle,
        exchange.gather(normed).reshape((8,) + own.shape),
        exchange.gather(dm).reshape((8,) + own.shape),
        fetch_weight([mlp_gate, mlp_up], 4),
        fetch_weight([mlp_down.T], 4).T,
    )


def plain_reduce_and_return(part, middle, dout, gain, g_down, g_wide, drows):
    exchange = Tokens()
    change, gain_rows = norm_back(middle, gain, exchange.scatter(part))
    dr1 = dout + change
    return (
        dr1,
        jnp.sum(gain_rows, axis=0, keepdims=True),
        exchange.gather(dr1.astype(BF)).reshape((8,) + dr1.shape),
        return_grad(g_down.T, drows).transpose(0, 2, 1),
        return_grad(g_wide, drows),
    )


def plain_return_last(part, own, dr1, gain, g_out, g_wide, g_gates, drows):
    exchange = Tokens()
    change, gain_rows = norm_back(own.astype(F32), gain, exchange.scatter(part))
    group = g_wide.shape[0] // drows
    return (
        dr1 + change,
        jnp.sum(gain_rows, axis=0, keepdims=True),
        return_grad(g_out.T, drows).transpose(0, 2, 1),
        return_grad(g_wide, drows),
        return_grad(g_gates, g_gates.shape[0] // group),
    )


def scan_body(reverse, a_ref, b_ref, p_ref, h_ref):
    length, width = a_ref.shape[1], a_ref.shape[2]
    row = lax.broadcasted_iota(jnp.int32, (8, width), 0)

    def tile(i, carry):
        ca, ch = carry
        at = (length // 8 - 1 - i if reverse else i) * 8
        at = pl.multiple_of(at, 8)
        a = a_ref[0, pl.ds(at, 8), :]
        b = b_ref[0, pl.ds(at, 8), :]
        for step in (1, 2, 4):
            if reverse:
                inside = row < 8 - step
                shift = 8 - step
            else:
                inside = row >= step
                shift = step
            sa = jnp.where(inside, pltpu.roll(a, shift, 0), 1.0)
            sb = jnp.where(inside, pltpu.roll(b, shift, 0), 0.0)
            b = b + a * sb
            a = a * sa
        h = b + a * ch
        p = a * ca
        h_ref[0, pl.ds(at, 8), :] = h
        p_ref[0, pl.ds(at, 8), :] = p
        last = 0 if reverse else 7
        return p[last : last + 1, :], h[last : last + 1, :]

    lax.fori_loop(
        0,
        length // 8,
        tile,
        (jnp.ones((1, width), F32), jnp.zeros((1, width), F32)),
    )


def local_scan(a, b, reverse):
    segs, length, width = a.shape
    spec = pl.BlockSpec((1, length, width), lambda s: (s, 0, 0))
    return pl.pallas_call(
        lambda *refs: scan_body(reverse, *refs),
        grid=(segs,),
        in_specs=[spec, spec],
        out_specs=[spec, spec],
        out_shape=[jax.ShapeDtypeStruct(a.shape, F32)] * 2,
        cost_estimate=pl.CostEstimate(
            flops=20 * a.size, bytes_accessed=16 * a.size, transcendentals=0
        ),
    )(a, b)


def carried(product, state, reverse):
    count = lax.axis_size("zh")
    if count == 2:
        return lax.ppermute(state, "zh", [(1, 0)] if reverse else [(0, 1)])
    here = lax.axis_index("zh")
    pairs = lax.all_gather(jnp.stack([product, state]), "zh")
    total = jnp.zeros_like(state)
    for k in range(count):
        at = count - 1 - k if reverse else k
        reached = at > here if reverse else at < here
        total = jnp.where(reached, pairs[at, 1] + pairs[at, 0] * total, total)
    return total


def from_behind(x, by):
    count = lax.axis_size("zh")
    return lax.ppermute(
        x, "zh", [(i, i + by) for i in range(count) if 0 <= i + by < count]
    )


def inverse_rms(values):
    return lax.rsqrt(jnp.mean(values * values, axis=-1, keepdims=True) + EPSILON)


def gelu(v):
    return jax.nn.gelu(v, approximate=True)


def gelu_both(v):
    c = 0.7978845608028654
    t = jnp.tanh(c * (v + 0.044715 * v * v * v))
    value = 0.5 * v * (1.0 + t)
    slope = 0.5 * (1.0 + t) + 0.5 * v * (1.0 - t * t) * c * (1.0 + 3 * 0.044715 * v * v)
    return value, slope


def dot(a, b, dims, out=F32):
    r = lax.dot_general(a, b, (dims, ((), ())), preferred_element_type=F32)
    return r.astype(out)


NN = ((1,), (0,))
NT = ((1,), (1,))
TN = ((0,), (0,))


def on_device(
    tokens_in,
    cotangent,
    seq_source,
    source_weight,
    input_weight,
    gelu_weight,
    decay_gates,
    input_gates,
    channel_params,
    norm_gains,
    output_weight,
    mlp_gate,
    mlp_up,
    mlp_down,
):
    sizes = tuple(lax.axis_size(n) for n in AXES)
    dxn, _, zhn, _, _ = sizes
    group = dxn * 2 * zhn * 2
    dc, zl, mp = (lax.axis_index(n) for n in ("dc", "zl", "mp"))
    slot = dc * 2 + zl
    exchange = Tokens()
    length = tokens_in.shape[2]
    width = tokens_in.shape[3]
    local = input_weight.shape[1] // 4
    heads = decay_gates.shape[0] // 4
    drows = input_weight.shape[0]
    piece = decay_gates.shape[1]

    own = lax.dynamic_index_in_dim(tokens_in[:, 0], mp, 0, keepdims=False)
    scales = jnp.stack(
        [
            jnp.sum(
                jnp.where(
                    jnp.arange(source_weight.shape[0], dtype=jnp.int32) == seq_source[m, 0],
                    source_weight,
                    0.0,
                )
            )
            for m in range(2)
        ]
    )
    douts = cotangent[:, 0].astype(F32) * scales[:, None, None]
    dout = lax.dynamic_index_in_dim(douts, mp, 0, keepdims=False)

    small = jnp.concatenate([channel_params.reshape(-1), norm_gains.reshape(-1)])
    shards = ("dx", "dc", "zh", "zl")
    small = lax.all_to_all(
        jnp.broadcast_to(small[None], (group, small.size)), shards, 0, 0, tiled=True
    )
    nch = channel_params.size
    channels = small[:, :nch].reshape(group, 8, -1).transpose(1, 0, 2).reshape(8, -1)
    channels = lax.dynamic_slice_in_dim(channels, slot * local, local, 1).astype(F32)
    gains = small[:, nch:].reshape(group, 2, -1).transpose(1, 0, 2).reshape(2, -1).astype(F32)

    ff = mlp_gate.shape[1] // 4
    tokens, w_ig, w_o = fetch_first(tokens_in[:, 0], input_weight, gelu_weight, output_weight)
    tokens = tokens.reshape(-1, width)

    gates = jnp.stack([decay_gates, input_gates]).reshape(2, 4, heads, piece)
    gates = gates.transpose(1, 0, 2, 3).reshape(2, 1, 2, 1, 2 * heads * piece)
    gates = jnp.broadcast_to(gates, (2, zhn, 2, dxn, 2 * heads * piece))
    gates = gates.transpose(3, 0, 1, 2, 4).reshape(group, 2 * heads * piece)
    gates = lax.all_to_all(gates, shards, 0, 0, tiled=True)
    gates = gates.reshape(group, 2 * heads, piece).transpose(1, 0, 2)
    gates = gates.reshape(2, heads, BLOCK, BLOCK)

    wide = tokens.astype(F32)
    n1 = (wide * inverse_rms(wide) * gains[0]).astype(BF)
    both = dot(n1, w_ig, NN)
    xb = both[:, :local].astype(BF).reshape(4, 2 * length, local)
    gy = both[:, local:].reshape(4, 2 * length, local)
    rim = from_behind(xb[:, -3:], 1)
    padded = jnp.concatenate([rim, xb], axis=1).astype(F32)
    conv = channels[3]
    for k in range(4):
        conv = conv + channels[4 + k] * padded[:, 3 - k : 3 - k + 2 * length]
    u = conv.astype(BF)
    zero = jnp.zeros((BLOCK, BLOCK), BF)
    blocks = jnp.concatenate(
        [
            jnp.concatenate(
                [gates[g, h] if k == h else zero for g in range(2) for k in range(heads)], axis=1
            )
            for h in range(heads)
        ],
        axis=0,
    )
    u2 = u.reshape(-1, local)
    logits = dot(u2, blocks, NN).reshape(4, 2 * length, 2 * local)
    sig_a = jax.nn.sigmoid(logits[..., :local] + channels[1])
    sig_i = jax.nn.sigmoid(logits[..., local:] + channels[2])
    soft = jax.nn.softplus(-channels[0])
    log_decay = -DECAY_SCALE * sig_a * soft
    decay = jnp.exp(log_decay)
    root = jnp.sqrt(-jnp.expm1(2.0 * log_decay))
    uf = u.astype(F32)
    drive = root * sig_i * uf
    running, state = local_scan(decay, drive, False)
    incoming = carried(running[:, -1], state[:, -1], False)
    states = state + running * incoming[:, None]
    gelu_y, slope_y = gelu_both(gy)
    mixed = (gelu_y * states).astype(BF).reshape(-1, local)
    middle, n2, dm, w_gu, w_d = reduce_and_fetch(
        dot(mixed, w_o, NN, BF), own, gains[1:2], douts.astype(BF), mlp_gate, mlp_up, mlp_down
    )
    n2 = n2.reshape(-1, width)
    dm = dm.reshape(-1, width)

    pre = dot(n2, w_gu, NN)
    gm, up = pre[:, :ff], pre[:, ff:]
    value, slope = gelu_both(gm)
    hidden = (value * up).astype(BF)
    g_down = dot(hidden, dm, TN, BF)
    dhm = dot(dm, w_d, NT)
    dgm, dup = (dhm * up * slope).astype(BF), (dhm * value).astype(BF)
    pair = jnp.concatenate([dgm, dup], axis=1)
    g_wide = dot(n2, pair, TN, BF)
    dr1, gain_two, do, share_down, share_wide = reduce_and_return(
        dot(pair, w_gu, NT, BF), middle, dout, gains[1:2], g_down, g_wide, drows
    )
    gain_two = jnp.sum(gain_two, axis=0)
    do = do.reshape(-1, width)

    result = middle + exchange.scatter(dot(hidden, w_d, NN))
    result = result.astype(BF)

    g_out = dot(mixed, do, TN, BF)
    dz = dot(do, w_o, NT).reshape(4, 2 * length, local)
    dh = dz * gelu_y
    dgy = (dz * states * slope_y).astype(BF)
    ones = jnp.ones_like(decay[:, :1])
    after, adjoint = local_scan(jnp.concatenate([decay[:, 1:], ones], axis=1), dh, True)
    later = carried(running[:, -1], decay[:, 0] * adjoint[:, 0], True)
    adjoint = adjoint + after * later[:, None]
    previous = jnp.concatenate([incoming[:, None], states[:, :-1]], axis=1)
    d_root = adjoint * sig_i * uf
    d_sig_i = adjoint * root * uf
    du0 = adjoint * root * sig_i
    d_log = adjoint * previous * decay - d_root * decay * decay / root
    dra = (d_log * (-DECAY_SCALE * soft) * sig_a * (1.0 - sig_a)).astype(BF)
    dri = (d_sig_i * sig_i * (1.0 - sig_i)).astype(BF)
    dlam = jnp.sum(d_log * sig_a, axis=(0, 1)) * DECAY_SCALE * jax.nn.sigmoid(-channels[0])
    dlogits = jnp.concatenate([dra, dri], axis=2).reshape(-1, 2 * local)
    g_blocks = dot(u2, dlogits, TN)
    du = du0 + dot(dlogits, blocks, NT).reshape(4, 2 * length, local)
    zeros = jnp.zeros((4, 3, local), F32)
    spread = jnp.concatenate([zeros, du, zeros], axis=1)
    dpad = jnp.zeros((4, 2 * length + 3, local), F32)
    taps = []
    for k in range(4):
        dpad = dpad + channels[4 + k] * spread[:, k : k + 2 * length + 3]
        taps.append(jnp.sum(du * padded[:, 3 - k : 3 - k + 2 * length], axis=(0, 1)))
    back = from_behind(dpad[:, :3], -1)
    dxb = dpad[:, 3:] + jnp.concatenate(
        [jnp.zeros((4, 2 * length - 3, local), F32), back], axis=1
    )
    dboth = jnp.concatenate([dxb.astype(BF), dgy], axis=2).reshape(-1, 2 * local)
    g_wide_ig = dot(n1, dboth, TN, BF)
    dn1 = dot(dboth, w_ig, NT, BF)

    g_gates = jnp.stack(
        [
            jnp.stack(
                [
                    g_blocks[
                        h * BLOCK : (h + 1) * BLOCK,
                        g * local + h * BLOCK : g * local + (h + 1) * BLOCK,
                    ]
                    for h in range(heads)
                ]
            )
            for g in range(2)
        ]
    )
    g_gates = g_gates.reshape(2 * heads, group, piece).transpose(1, 0, 2).reshape(group, -1)
    count = g_gates.shape[1]
    unit = (count + 2047) // 2048 * 16
    g_gates = jnp.pad(g_gates, ((0, 0), (0, unit * 128 - count))).astype(BF)
    dx_own, gain_one, share_o, share_ig, share_gates = return_last(
        dn1,
        own,
        dr1,
        gains[0:1],
        g_out,
        g_wide_ig,
        g_gates.reshape(group * unit, 128),
        drows,
    )
    gain_one = jnp.sum(gain_one, axis=0)
    g_gates = share_gates.reshape(4, -1)[:, :count].astype(F32).reshape(4, 2, heads, piece)
    g_gates = g_gates.transpose(1, 0, 2, 3).reshape(2, 4 * heads, piece)

    channel_grad = jnp.stack(
        [
            dlam,
            jnp.sum(dra.astype(F32), axis=(0, 1)),
            jnp.sum(dri.astype(F32), axis=(0, 1)),
            jnp.sum(du, axis=(0, 1)),
        ]
        + taps
    )
    per = 4 * local // group
    mine = channel_grad.reshape(8, group // 4, per).transpose(1, 0, 2)
    mine = jnp.where(
        jnp.arange(4, dtype=jnp.int32)[:, None, None, None] == slot, mine[None], 0.0
    ).reshape(group, 8 * per)
    both_gains = jnp.stack([gain_one, gain_two]).reshape(2, group, -1).transpose(1, 0, 2)
    sums = jnp.concatenate([both_gains.reshape(group, -1), mine], axis=1)
    sums = jnp.sum(lax.all_to_all(sums, shards, 0, 0, tiled=True), axis=0)
    g_gains = sums[: 2 * drows].reshape(2, drows)
    g_gains = g_gains + lax.ppermute(g_gains, "mp", [(0, 1), (1, 0)])
    g_channels = sums[2 * drows :].reshape(8, 1, per)

    def both_batches(rows):
        other = lax.ppermute(rows, "mp", [(0, 1), (1, 0)])
        return jnp.stack([jnp.where(mp == 0, rows, other), jnp.where(mp == 0, other, rows)])

    block_out = both_batches(result)[:, None]
    grad_tokens = both_batches(dx_own)[:, None]

    def columns(share, at, count):
        return (
            share[:, :, at : at + count].astype(F32).transpose(1, 0, 2).reshape(drows, 4 * count)
        )

    return (
        block_out,
        grad_tokens,
        columns(share_ig, 0, local),
        columns(share_ig, local, local),
        g_gates[0],
        g_gates[1],
        g_channels,
        g_gains,
        share_o.astype(F32).reshape(-1, drows),
        columns(share_wide, 0, ff),
        columns(share_wide, ff, ff),
        share_down.astype(F32).reshape(-1, drows),
    )


def solution(mesh):
    dpn, seqn, mpn = (mesh.shape[n] for n in ("dp", "seq", "mp"))
    fine = Mesh(mesh.devices.reshape(dpn // 2, 2, seqn // 2, 2, mpn), AXES)
    dp, seq = ("dx", "dc"), ("zh", "zl")
    shards = dp + seq
    weights = (
        P(shards, "mp"),
        P(shards, "mp"),
        P("mp", shards),
        P("mp", shards),
        P(None, "mp", shards),
        P(None, shards),
        P("mp", shards),
        P(shards, "mp"),
        P(shards, "mp"),
        P("mp", shards),
    )
    rows = P(None, dp, seq, None)
    return jax.shard_map(
        on_device,
        mesh=fine,
        in_specs=(rows, rows, P(None, dp), P()) + weights,
        out_specs=(rows, rows) + weights,
        check_vma=False,
    )
```

```python
import functools

import jax
import jax.numpy as jnp
import numpy as np
from jax import lax
from jax.experimental import pallas as pl
from jax.experimental.pallas import tpu as pltpu
from jax.sharding import Mesh, PartitionSpec as P

WIDTH = 2560
HEADS = 16
BLOCK = WIDTH // HEADS
EPSILON = 1e-06
DECAY_SCALE = 8.0
AXES = ("dx", "dc", "zh", "zl", "mp")
BF = jnp.bfloat16
F32 = jnp.float32


def swap_pairs(sizes, partner):
    pairs = []
    for flat in range(int(np.prod(sizes))):
        coords = np.unravel_index(flat, sizes)
        pairs.append((flat, int(np.ravel_multi_index(partner(*map(int, coords)), sizes))))
    return pairs


def gather_blocks(x, axis, dim):
    if lax.axis_size(axis) != 2:
        return lax.all_gather(x, axis, axis=dim, tiled=False)
    here = lax.axis_index(axis)
    other = lax.ppermute(x, axis, [(0, 1), (1, 0)])
    low = jnp.where(here == 0, x, other)
    high = jnp.where(here == 0, other, x)
    return jnp.stack([low, high], axis=dim)


def scatter_blocks(x, axis, dim):
    if lax.axis_size(axis) != 2:
        n = x.shape[dim]
        out = lax.psum_scatter(x.astype(BF), axis, scatter_dimension=dim, tiled=True)
        return lax.squeeze(out, [dim]).astype(F32)
    here = lax.axis_index(axis)
    mine = lax.dynamic_index_in_dim(x, here, dim, keepdims=False)
    theirs = lax.dynamic_index_in_dim(x, 1 - here, dim, keepdims=False)
    got = lax.ppermute(theirs.astype(BF), axis, [(0, 1), (1, 0)])
    return mine.astype(F32) + got.astype(F32)


def fetch_weight(shard, parts):
    rows, cols = shard[0].shape[0], None
    pieces = [s.reshape(rows, parts, -1) for s in shard]
    joined = jnp.concatenate(pieces, axis=2) if len(pieces) > 1 else pieces[0]
    cols = joined.shape[2]
    x = jnp.transpose(joined, (1, 0, 2))
    x = lax.all_to_all(x, ("dc", "zl"), 0, 0, tiled=True)
    x = x.reshape(2, 2, rows, cols)
    x = gather_blocks(x, "zh", 1)
    x = gather_blocks(x, "dx", 0)
    return x.reshape(-1, cols)


def return_grad(grad, rows):
    cols = grad.shape[1]
    dxn, zhn = lax.axis_size("dx"), lax.axis_size("zh")
    g = grad.reshape(dxn, 2, zhn, 2, rows, cols)
    g = scatter_blocks(g, "dx", 0)
    g = scatter_blocks(g, "zh", 1)
    g = g.astype(BF).reshape(4, rows, cols)
    return lax.all_to_all(g, ("dc", "zl"), 0, 0, tiled=True)


class Tokens:
    def __init__(self):
        sizes = tuple(lax.axis_size(n) for n in AXES)
        self.core = swap_pairs(sizes, lambda a, b, c, d, e: (a, 1 - b, c, d, e))
        self.first = swap_pairs(
            sizes, lambda a, b, c, d, e: (a, b, c, d, 1 - e) if b == 0 else (a, b, c, 1 - d, e)
        )
        self.second = swap_pairs(
            sizes, lambda a, b, c, d, e: (a, b, c, 1 - d, e) if b == 0 else (a, b, c, d, 1 - e)
        )
        self.dc, self.zl, self.mp = (lax.axis_index(n) for n in ("dc", "zl", "mp"))

    def order(self, dc):
        mp, zl = self.mp, self.zl
        own = mp * 2 + zl
        by_mp = (1 - mp) * 2 + zl
        by_zl = mp * 2 + 1 - zl
        both = (1 - mp) * 2 + 1 - zl
        one = jnp.where(dc == 0, by_mp, by_zl)
        two = jnp.where(dc == 0, by_zl, by_mp)
        return own, one, two, both

    def gather(self, x):
        rows, width = x.shape
        one = lax.ppermute(x, AXES, self.first)
        two = lax.ppermute(jnp.stack([x, one]), AXES, self.second)
        far = [lax.ppermute(v, AXES, self.core) for v in (x, one, two)]
        out = jnp.zeros((8, rows, width), x.dtype)
        for dc, blocks in (
            (self.dc, (x, one, two[0], two[1])),
            (1 - self.dc, (far[0], far[1], far[2][0], far[2][1])),
        ):
            for at, block in zip(self.order(dc), blocks):
                out = lax.dynamic_update_index_in_dim(out, block, dc * 4 + at, 0)
        return out.reshape(8 * rows, width)

    def scatter(self, x):
        rows, width = x.shape[0] // 8, x.shape[1]
        x = x.reshape(2, 4, rows, width)
        theirs = lax.dynamic_index_in_dim(x, 1 - self.dc, 0, keepdims=False).astype(BF)
        mine = lax.dynamic_index_in_dim(x, self.dc, 0, keepdims=False)
        total = mine.astype(F32) + lax.ppermute(theirs, AXES, self.core).astype(F32)
        own, one, two, both = self.order(self.dc)
        pick = lambda at: lax.dynamic_index_in_dim(total, at, 0, keepdims=False)
        got = lax.ppermute(jnp.stack([pick(two), pick(both)]).astype(BF), AXES, self.second)
        keep_own = pick(own) + got[0].astype(F32)
        keep_one = pick(one) + got[1].astype(F32)
        got = lax.ppermute(keep_one.astype(BF), AXES, self.first)
        return keep_own + got.astype(F32)


MESH = pl.DeviceIdType.MESH
ANY = pl.BlockSpec(memory_space=pl.ANY)
VMEM = pl.BlockSpec(memory_space=pltpu.VMEM)


def flip(index, by):
    return 1 - index if by else index


class Place:
    def __init__(self):
        self.dx, self.dc, self.zh, self.zl, self.mp = (lax.axis_index(n) for n in AXES)

    def peer(self, dx=0, dc=0, zh=0, zl=0, mp=0):
        return (
            flip(self.dx, dx),
            flip(self.dc, dc),
            flip(self.zh, zh),
            flip(self.zl, zl),
            flip(self.mp, mp),
        )

    def block(self, dx=0, dc=0, zh=0, zl=0):
        a, b, c, d, _ = self.peer(dx, dc, zh, zl)
        return ((a * 2 + b) * 2 + c) * 2 + d

    def slot(self, dc=0, zl=0):
        return flip(self.dc, dc) * 2 + flip(self.zl, zl)

    def rows(self, dc=0, mp=0, zl=0):
        return (flip(self.dc, dc) * 2 + flip(self.mp, mp)) * 2 + flip(self.zl, zl)


def greet(peers):
    barrier = pltpu.get_barrier_semaphore()
    for device in peers:
        pl.semaphore_signal(barrier, inc=1, device_id=device, device_id_type=MESH)
    pl.semaphore_wait(barrier, len(peers))


class Links:
    def __init__(self, send, recv, local):
        self.send, self.recv, self.local = send, recv, local
        self.n, self.m = 0, 0
        self.sent, self.copies = [], []

    def pair(self):
        self.n += 1
        return self.n - 1

    def start(self, src, dst, at, device):
        copy = pltpu.make_async_remote_copy(
            src_ref=src,
            dst_ref=dst,
            send_sem=self.send.at[at],
            recv_sem=self.recv.at[at],
            device_id=device,
            device_id_type=MESH,
        )
        copy.start()
        self.sent.append(copy)

    def arrived(self, ref, at):
        pltpu.make_async_copy(ref, ref, self.recv.at[at]).wait()

    def keep(self, src, dst):
        copy = pltpu.make_async_copy(src, dst, self.local.at[self.m])
        self.m += 1
        copy.start()
        return copy

    def finish(self):
        for copy in self.sent:
            copy.wait_send()


FLIPS = [(zh, dc, zl) for zh in (1, 0) for dc in (0, 1) for zl in (0, 1)]


class WeightGather:
    def __init__(self, place, links, source, target, unit):
        self.place, self.links, self.target = place, links, target
        self.at = {f: links.pair() for f in FLIPS}
        self.cross = {(zh, dc): links.pair() for zh in (0, 1) for dc in (0, 1)}
        self.source = source
        self.kept = None

    def begin(self, zhs=(1, 0), dcs=(0, 1)):
        p = self.place
        mine = p.block()
        for f in FLIPS:
            zh, dc, zl = f
            if zh not in zhs or dc not in dcs:
                continue
            src, dst = self.source(p.slot(dc, zl)), self.target(mine, 1)
            if f == (0, 0, 0):
                self.kept = self.links.keep(src, dst)
            else:
                self.links.start(src, dst, self.at[f], p.peer(dc=dc, zh=zh, zl=zl))

    def onward(self, zh, dcs=(0, 1)):
        p = self.place
        for dc in dcs:
            for zl in (0, 1):
                if (zh, dc, zl) == (0, 0, 0):
                    self.kept.wait()
                else:
                    self.links.arrived(
                        self.target(p.block(dc=dc, zh=zh, zl=zl), 1), self.at[zh, dc, zl]
                    )
            two = self.target(p.block(dc=dc, zh=zh) // 2 * 2, 2)
            self.links.start(two, two, self.cross[zh, dc], p.peer(dx=1))

    def end(self):
        p = self.place
        for zh in (0, 1):
            for dc in (0, 1):
                two = self.target(p.block(dx=1, dc=dc, zh=zh) // 2 * 2, 2)
                self.links.arrived(two, self.cross[zh, dc])


def row_blocks(ref, unit, cols=None):
    def target(first, count):
        rows = pl.ds(pl.multiple_of(first * unit, unit), count * unit)
        return ref.at[rows] if cols is None else ref.at[rows, cols]

    return target


def column_blocks(ref, unit):
    return lambda first, count: ref.at[:, pl.ds(pl.multiple_of(first * unit, unit), count * unit)]


def first_kernel(tok_ref, ig_ref, o_ref, all_ref, wig_ref, wo_ref, send, recv, local):
    p = Place()
    links = Links(send, recv, local)
    drows = ig_ref.shape[1]
    crows = wo_ref.shape[0]
    greet(weight_peers(p))
    gather = TokenGatherTwice(p, links, tok_ref, all_ref)
    w_ig = WeightGather(p, links, lambda j: ig_ref.at[j], row_blocks(wig_ref, drows), drows)
    w_o = WeightGather(
        p,
        links,
        lambda j: o_ref.at[pl.ds(pl.multiple_of(j * crows, 16), crows)],
        column_blocks(wo_ref, o_ref.shape[1]),
        drows,
    )
    w_ig.begin((1,))
    w_ig.begin((0,))
    w_o.begin((0,))
    gather.begin()
    w_ig.onward(0)
    w_o.onward(0)
    w_o.begin((1,))
    w_ig.onward(1)
    gather.forward()
    gather.forward_core()
    w_o.onward(1)
    gather.end()
    w_ig.end()
    w_o.end()
    links.finish()


class TokenGatherTwice:
    def __init__(self, place, links, source, target):
        self.place, self.links, self.source, self.target = place, links, source, target
        self.z, self.y = links.pair(), links.pair()
        self.core = {(mp, zl): links.pair() for mp in (0, 1) for zl in (0, 1)}

    def begin(self):
        p = self.place
        self.kept = []
        for mp in (0, 1):
            at = p.rows(mp=mp)
            src = self.source.at[flip(p.mp, mp)]
            if mp == 0:
                self.links.start(src, self.target.at[at], self.z, p.peer(zl=1))
            self.links.start(src, self.target.at[at], self.core[mp, 0], p.peer(dc=1))
            self.kept.append(self.links.keep(src, self.target.at[at]))

    def forward(self):
        p = self.place
        far = self.target.at[p.rows(zl=1)]
        self.links.arrived(far, self.z)
        self.links.start(far, far, self.y, p.peer(mp=1))
        self.links.start(far, far, self.core[0, 1], p.peer(dc=1))

    def forward_core(self):
        p = self.place
        far = self.target.at[p.rows(mp=1, zl=1)]
        self.links.arrived(far, self.y)
        self.links.start(far, far, self.core[1, 1], p.peer(dc=1))

    def end(self):
        p = self.place
        for (mp, zl), at in self.core.items():
            self.links.arrived(self.target.at[p.rows(dc=1, mp=mp, zl=zl)], at)
        for copy in self.kept:
            copy.wait()


class TokenGather:
    def __init__(self, place, links, source, target, span):
        self.place, self.links = place, links
        self.span = pl.ds(*span)
        self.source, self.target = source.at[self.span], target
        self.z, self.y0, self.y1 = links.pair(), links.pair(), links.pair()
        self.core = {(mp, zl): links.pair() for mp in (0, 1) for zl in (0, 1)}

    def block(self, **where):
        return self.target.at[self.place.rows(**where), self.span]

    def begin(self):
        p = self.place
        at = self.block()
        self.links.start(self.source, at, self.z, p.peer(zl=1))
        self.links.start(self.source, at, self.y0, p.peer(mp=1))
        self.links.start(self.source, at, self.core[0, 0], p.peer(dc=1))
        self.kept = self.links.keep(self.source, at)

    def forward(self):
        p = self.place
        far = self.block(zl=1)
        self.links.arrived(far, self.z)
        self.links.start(far, far, self.y1, p.peer(mp=1))
        self.links.start(far, far, self.core[0, 1], p.peer(dc=1))

    def forward_core(self):
        p = self.place
        far = self.block(mp=1)
        self.links.arrived(far, self.y0)
        self.links.start(far, far, self.core[1, 0], p.peer(dc=1))
        far = self.block(mp=1, zl=1)
        self.links.arrived(far, self.y1)
        self.links.start(far, far, self.core[1, 1], p.peer(dc=1))

    def end(self):
        for (mp, zl), at in self.core.items():
            self.links.arrived(self.block(dc=1, mp=mp, zl=zl), at)
        self.kept.wait()


CHUNK = 16


def chunks(count, body, most=11, first=0):
    n = count // CHUNK
    per = max(k for k in range(1, most + 1) if n % k == 0)

    def step(i, carry):
        for k in range(per):
            body(pl.ds(pl.multiple_of(first + (i * per + k) * CHUNK, CHUNK), CHUNK))
        return carry

    if n == per:
        step(0, 0)
    else:
        lax.fori_loop(0, n // per, step, 0)


def halves(rows):
    first = (rows // 2 + CHUNK - 1) // CHUNK * CHUNK
    return [(0, first), (first, rows - first)]


class RowScatter:
    def __init__(self, place, links, source, buffers, parts=None):
        self.place, self.links, self.source = place, links, source
        self.mine, self.from_core, self.from_y, self.from_z, self.out = buffers[:5]
        self.to_core = buffers[5] if len(buffers) > 5 else None
        self.parts = parts or [(0, self.mine.shape[1])]
        self.blocks = [(mp, zl) for mp in (1, 0) for zl in (1, 0)]
        n = range(len(self.parts))
        self.core = {(h, block): links.pair() for h in n for block in self.blocks}
        self.y = {(h, zl): links.pair() for h in n for zl in (1, 0)}
        self.z = {h: links.pair() for h in n}

    def begin(self):
        p = self.place
        self.kept = {}
        for mp, zl in self.blocks:
            i, block = mp * 2 + zl, p.rows(dc=1, mp=mp, zl=zl)
            if self.to_core is None:
                src = self.source.at[block]
            else:
                self.to_core[i] = self.source(block).astype(BF)
                src = self.to_core.at[i]
            for h, part in enumerate(self.parts):
                at = pl.ds(*part)
                self.links.start(
                    src.at[at], self.from_core.at[i, at], self.core[h, (mp, zl)], p.peer(dc=1)
                )
        for mp, zl in self.blocks:
            i, block = mp * 2 + zl, p.rows(mp=mp, zl=zl)
            if self.to_core is None:
                self.kept[mp, zl] = self.links.keep(self.source.at[block], self.mine.at[i])
            else:
                self.mine[i] = self.source(block).astype(BF)

    def ready(self, mp, zl, h):
        i = mp * 2 + zl
        if h == 0 and self.kept:
            self.kept[mp, zl].wait()
        at = pl.ds(*self.parts[h])
        self.links.arrived(self.from_core.at[i, at], self.core[h, (mp, zl)])
        return i

    def across_y(self, h=0):
        p = self.place
        first, count = self.parts[h]
        at = pl.ds(first, count)
        for zl in (1, 0):
            i = self.ready(1, zl, h)

            def add(rows, i=i, zl=zl):
                total = self.mine[i, rows, :].astype(F32) + self.from_core[i, rows, :].astype(F32)
                self.out[zl, rows, :] = total.astype(BF)

            chunks(count, add, first=first)
            self.links.start(
                self.out.at[zl, at], self.from_y.at[zl, at], self.y[h, zl], p.peer(mp=1)
            )

    def across_z(self, h=0):
        p = self.place
        first, count = self.parts[h]
        at = pl.ds(first, count)
        i = self.ready(0, 1, h)
        self.links.arrived(self.from_y.at[1, at], self.y[h, 1])

        def add(rows):
            total = self.mine[i, rows, :].astype(F32) + self.from_core[i, rows, :].astype(F32)
            self.out[2, rows, :] = (total + self.from_y[1, rows, :].astype(F32)).astype(BF)

        chunks(count, add, first=first)
        self.links.start(self.out.at[2, at], self.from_z.at[at], self.z[h], p.peer(zl=1))

    def arrive(self, h=0):
        at = pl.ds(*self.parts[h])
        self.ready(0, 0, h)
        self.links.arrived(self.from_y.at[0, at], self.y[h, 0])
        self.links.arrived(self.from_z.at[at], self.z[h])

    def total(self, rows):
        a = self.mine[0, rows, :].astype(F32) + self.from_core[0, rows, :].astype(F32)
        b = self.from_y[0, rows, :].astype(F32) + self.from_z[rows, :].astype(F32)
        return a + b


def scatter_buffers(rows, width, products=False):
    return [
        pltpu.VMEM((4, rows, width), BF),
        pltpu.VMEM((4, rows, width), BF),
        pltpu.VMEM((2, rows, width), BF),
        pltpu.VMEM((rows, width), BF),
        pltpu.VMEM((3, rows, width), BF),
    ] + ([pltpu.VMEM((4, rows, width), BF)] if products else [])


def group_peers(p):
    return [p.peer(dc=1), p.peer(zl=1), p.peer(mp=1)]


def weight_peers(p):
    return [p.peer(dc=dc, zh=zh, zl=zl) for zh, dc, zl in FLIPS if (zh, dc, zl) != (0, 0, 0)] + [
        p.peer(dx=1),
        p.peer(mp=1),
    ]


def second_kernel(
    mixed_ref, wo_ref, own_ref, gain_ref, up_ref, down_ref,
    mid_ref, all_ref, wu_ref, wd_ref,
    *scratch,
):
    p = Place()
    links = Links(*scratch[-3:])
    normed = scratch[-4]
    rows, channels = own_ref.shape[0], wo_ref.shape[0]
    greet(weight_peers(p))

    def project(b):
        at = pl.ds(pl.multiple_of(b * rows, 16), rows)
        return dot(mixed_ref[at, :channels], wo_ref[...], NN)

    parts = halves(rows)
    scatter = RowScatter(p, links, project, scratch[:6], parts)
    w_u = slot_columns(p, links, up_ref, wu_ref)
    w_d = WeightGather(
        p,
        links,
        lambda j: down_ref.at[pl.ds(pl.multiple_of(j * wd_ref.shape[0], 16), wd_ref.shape[0])],
        column_blocks(wd_ref, down_ref.shape[1]),
        down_ref.shape[1],
    )
    gathers = [TokenGather(p, links, normed, all_ref, part) for part in parts]
    scatter.begin()
    w_u.begin((1,))
    w_u.begin((0,))
    scatter.across_y(0)
    scatter.across_y(1)
    w_d.begin((0,))
    w_u.onward(0)

    def normalise(at):
        value = own_ref[at, :].astype(F32) + scatter.total(at)
        mid_ref[at, :] = value
        inv = lax.rsqrt(jnp.mean(value * value, axis=-1, keepdims=True) + EPSILON)
        normed[at, :] = (value * inv * gain_ref[...]).astype(BF)

    def middle(h):
        scatter.arrive(h)
        chunks(parts[h][1], normalise, first=parts[h][0])
        gathers[h].begin()

    scatter.across_z(0)
    w_d.onward(0)
    scatter.across_z(1)
    middle(0)
    w_d.begin((1,))
    middle(1)
    gathers[0].forward()
    w_u.onward(1)
    gathers[1].forward()
    gathers[0].forward_core()
    gathers[1].forward_core()
    w_d.onward(1)
    for gather in gathers:
        gather.end()
    w_u.end()
    w_d.end()
    links.finish()


def slot_columns(p, links, source, result):
    count = result.shape[1]
    return WeightGather(
        p,
        links,
        lambda j: source.at[:, pl.ds(pl.multiple_of(j * count, 128), count)],
        row_blocks(result, source.shape[0]),
        source.shape[0],
    )


class GradScatter:
    FAR = [(1, 0, 1), (1, 1, 1)], [(1, 0, 0), (1, 1, 0)]
    NEAR = [(0, 0, 1), (0, 1, 1)], [(0, 0, 0), (0, 1, 0)]
    ORDER = FAR[0] + NEAR[0] + FAR[1] + NEAR[1]
    EARLY = FAR[0] + FAR[1] + NEAR[0] + NEAR[1]

    def __init__(self, place, links, left, right, buffers, order=ORDER):
        self.order = order
        self.place, self.links, self.left, self.right = place, links, left, right
        self.to_x, self.from_x, self.to_z, self.from_z, self.sums, self.result = buffers[:6]
        self.columns = buffers[6] if len(buffers) > 6 else None
        self.rows = self.to_x.shape[1]
        self.x = {(zh, dc): links.pair() for zh in (1, 0) for dc in (0, 1)}
        self.z = {dc: links.pair() for dc in (0, 1)}
        self.at = {(dc, zl): links.pair() for dc in (0, 1) for zl in (0, 1)}
        self.count = 0
        self.load()

    def load(self):
        if self.count < 8 and self.columns is not None:
            dx, dc, zh = self.order[self.count]
            first = self.place.block(dx=dx, dc=dc, zh=zh) // 2
            columns = pl.ds(pl.multiple_of(first * self.rows, self.rows), self.rows)
            self.loading = self.links.keep(
                self.left.at[:, columns], self.columns.at[self.count % 2]
            )

    def product(self, dx=0, dc=0, zh=0):
        assert self.order[self.count] == (dx, dc, zh)
        self.loading.wait()
        self.count += 1
        self.load()
        return dot(self.columns[(self.count - 1) % 2], self.right[...], TN)

    def begin(self, zh):
        for dc in (0, 1):
            i = zh * 2 + dc
            self.to_x[i] = self.product(dx=1, dc=dc, zh=zh).astype(BF)
            self.links.start(
                self.to_x.at[i], self.from_x.at[i], self.x[zh, dc], self.place.peer(dx=1)
            )

    def across(self, dc):
        mine = self.product(dc=dc, zh=1)
        self.links.arrived(self.from_x.at[2 + dc], self.x[1, dc])
        self.to_z[dc] = (mine + self.from_x[2 + dc].astype(F32)).astype(BF)
        self.links.start(self.to_z.at[dc], self.from_z.at[dc], self.z[dc], self.place.peer(zh=1))

    def last(self, dc):
        p = self.place
        mine = self.product(dc=dc, zh=0)
        self.links.arrived(self.from_x.at[dc], self.x[0, dc])
        self.links.arrived(self.from_z.at[dc], self.z[dc])
        total = mine + self.from_x[dc].astype(F32) + self.from_z[dc].astype(F32)
        self.sums[dc] = total.astype(BF)
        unit = self.rows // 2
        for zl in (1, 0):
            src = self.sums.at[dc, pl.ds(pl.multiple_of(flip(p.zl, zl) * unit, unit), unit)]
            dst = self.result.at[p.slot()]
            if (dc, zl) == (0, 0):
                self.own = self.links.keep(src, dst)
            else:
                self.links.start(src, dst, self.at[dc, zl], p.peer(dc=dc, zl=zl))

    def end(self):
        p = self.place
        for (dc, zl), at in self.at.items():
            if (dc, zl) == (0, 0):
                self.own.wait()
            else:
                self.links.arrived(self.result.at[p.slot(dc, zl)], at)


class Ready(GradScatter):
    def product(self, dx=0, dc=0, zh=0):
        first = self.place.block(dx=dx, dc=dc, zh=zh) // 2
        return self.left[pl.ds(pl.multiple_of(first * self.rows, self.rows), self.rows), :].astype(
            F32
        )


def grad_buffers(rows, columns, tokens=None):
    return (
        [pltpu.VMEM((n, rows, columns), BF) for n in (4, 4, 2, 2, 2)]
        + [pltpu.VMEM((4, rows // 2, columns), BF)]
        + ([pltpu.VMEM((2, tokens, rows), BF)] if tokens else [])
    )


def norm_back(value, gain, upstream):
    inv = lax.rsqrt(jnp.mean(value * value, axis=-1, keepdims=True) + EPSILON)
    scaled = value * inv
    up = upstream * gain
    inner = jnp.mean(up * scaled, axis=-1, keepdims=True)
    return inv * (up - scaled * inner), upstream * scaled


def fold(rows):
    return rows[:8] + rows[8:]


def third_kernel(
    wg_ref, wu_ref, wd_ref, mid_ref, dout_ref, gain_ref, dm_ref, hidden_ref, n2_ref, dgm_ref,
    dup_ref,
    dr1_ref, gain_out, all_ref, gate_out, down_out, part_out,
    *scratch,
):
    p = Place()
    links = Links(*scratch[-3:])
    do = scratch[-4]
    rows_of = mid_ref.shape[0]
    greet(weight_peers(p))

    def product(b):
        at = pl.ds(pl.multiple_of(b * rows_of, 16), rows_of)
        return dot(dgm_ref[at, :], wg_ref[...], NT) + dot(dup_ref[at, :], wu_ref[...], NT)

    parts = halves(rows_of)
    scatter = RowScatter(p, links, product, scratch[:6], parts)
    down = GradScatter(p, links, dm_ref, hidden_ref, scratch[6:13])
    gate = GradScatter(p, links, n2_ref, dgm_ref, scratch[13:20])
    gathers = [TokenGather(p, links, do, all_ref, part) for part in parts]
    scatter.begin()
    down.begin(1)
    scatter.across_y(0)
    scatter.across_y(1)
    gate.begin(1)
    down.across(0)
    down.across(1)
    gain_out[...] = jnp.zeros_like(gain_out)

    def back(rows):
        part, gain = norm_back(mid_ref[rows, :], gain_ref[...], scatter.total(rows))
        value = dout_ref[rows, :] + part
        dr1_ref[rows, :] = value
        do[rows, :] = value.astype(BF)
        gain_out[...] += fold(gain)

    def middle(h):
        scatter.arrive(h)
        chunks(parts[h][1], back, first=parts[h][0])
        gathers[h].begin()

    scatter.across_z(0)
    down.begin(0)
    gate.across(0)
    scatter.across_z(1)
    middle(0)
    gate.across(1)
    gate.begin(0)
    middle(1)
    gathers[0].forward()
    gathers[1].forward()
    out = scratch[0]
    writes = []
    for b in range(8):
        if b >= 4:
            writes[b - 4].wait()
        at = pl.ds(b * rows_of, rows_of)
        out[b % 4] = dot(hidden_ref[at, :], wd_ref[...], NN, BF)
        writes.append(links.keep(out.at[b % 4], part_out.at[b]))
    down.last(0)
    down.last(1)
    gathers[0].forward_core()
    gate.last(0)
    gathers[1].forward_core()
    gate.last(1)
    for gather in gathers:
        gather.end()
    down.end()
    ff = down.result.shape[2]
    for j in range(4):
        down_out[j * ff : (j + 1) * ff, :] = down.result[j].astype(F32).T
    gate.end()
    for j in range(4):
        gate_out[:, j * ff : (j + 1) * ff] = gate.result[j].astype(F32)
    for write in writes[4:]:
        write.wait()
    links.finish()


def fourth_kernel(
    wig_ref, own_ref, dr1_ref, gain_ref, do_ref, mixed_ref, n1_ref, dboth_ref, gg_ref,
    dx_ref, gain_out, in_out, gelu_out, out_out, gates_out,
    *scratch,
):
    p = Place()
    links = Links(*scratch[-3:])
    dx_send, dx_recv = scratch[-5:-3]
    greet(weight_peers(p))
    rows_of = own_ref.shape[0]

    def product(b):
        at = pl.ds(pl.multiple_of(b * rows_of, 16), rows_of)
        return dot(dboth_ref[at, :], wig_ref[...], NT)

    parts = halves(rows_of)
    scatter = RowScatter(p, links, product, scratch[:6], parts)
    out = GradScatter(p, links, do_ref, mixed_ref, scratch[6:13])
    wide = GradScatter(p, links, n1_ref, dboth_ref, scratch[13:20])
    gates = Ready(p, links, gg_ref, None, scratch[20:26])
    out.begin(1)
    scatter.begin()
    wide.begin(1)
    scatter.across_y(0)
    gates.begin(1)
    scatter.across_y(1)
    for g in (out, wide, gates):
        g.across(0)
        g.across(1)
        g.begin(0)
    gain_out[...] = jnp.zeros_like(gain_out)

    def back(rows):
        value = own_ref[rows, :].astype(F32)
        part, gain = norm_back(value, gain_ref[...], scatter.total(rows))
        total = dr1_ref[rows, :] + part
        dx_ref[p.mp, rows, :] = total
        dx_send[rows, :] = total.astype(BF)
        gain_out[...] += fold(gain)

    sent = []

    def middle(h):
        scatter.arrive(h)
        chunks(parts[h][1], back, first=parts[h][0])
        span, at = pl.ds(*parts[h]), links.pair()
        links.start(dx_send.at[span], dx_recv.at[span], at, p.peer(mp=1))
        sent.append((span, at))

    scatter.across_z(0)
    scatter.across_z(1)
    middle(0)
    for g in (out, gates):
        g.last(0)
        g.last(1)
    middle(1)
    wide.last(0)
    wide.last(1)
    local = out.result.shape[2]
    out.end()
    for j in range(4):
        out_out[j * out_out.shape[0] // 4 : (j + 1) * out_out.shape[0] // 4, :] = (
            out.result[j].astype(F32).T[: out_out.shape[0] // 4]
        )
    gates.end()
    gates_out[...] = gates.result[...]
    wide.end()
    two = wide.result.shape[2]
    left = lax.broadcasted_iota(jnp.int32, (1, two), 1) < two // 2
    for j in (0, 2):
        a, b = (wide.result[j + i].astype(F32) for i in (0, 1))
        span = slice(j * two // 2, (j + 2) * two // 2)
        in_out[:, span] = jnp.where(left, a, pltpu.roll(b, two // 2, 1))
        gelu_out[:, span] = jnp.where(left, pltpu.roll(a, two // 2, 1), b)
    for span, at in sent:
        links.arrived(dx_recv.at[span], at)
    dx_ref[1 - p.mp] = dx_recv[...].astype(F32)
    links.finish()


def mlp_kernel(
    n2_ref, dm_ref, wg_ref, wu_ref, wd_ref, hidden_ref, dgm_ref, dup_ref, pre, upp, dhm
):
    count, rows, width = n2_ref.shape
    n2 = n2_ref[...].reshape(count * rows, width)
    pre[...] = dot(n2, wg_ref[...], NN)
    upp[...] = dot(n2, wu_ref[...], NN)
    dhm[...] = dot(dm_ref[...].reshape(count * rows, width), wd_ref[...], NT)

    def body(at):
        up, d = upp[at, :], dhm[at, :]
        value, slope = gelu_both(pre[at, :])
        hidden_ref[at, :] = (value * up).astype(BF)
        dgm_ref[at, :] = (d * up * slope).astype(BF)
        dup_ref[at, :] = (d * value).astype(BF)

    chunks(count * rows, body)


def feed_forward(n2, dm, w_g, w_u, w_d):
    blocks, rows, width = n2.shape
    ff = w_d.shape[0]
    if not shape_fits():
        n2, dm = n2.reshape(-1, width), dm.reshape(-1, width)
        pre, d = dot(n2, w_g, NN), dot(dm, w_d, NT)
        gm, up = pre, dot(n2, w_u, NN)
        value, slope = gelu_both(gm)
        return (value * up).astype(BF), (d * up * slope).astype(BF), (d * value).astype(BF)
    two = pl.BlockSpec((2, rows, width), lambda i: (i, 0, 0))
    flat = pl.BlockSpec((2 * rows, ff), lambda i: (i, 0))
    whole = lambda v: pl.BlockSpec(v.shape, lambda i: (0, 0))
    total = blocks * rows
    return pl.pallas_call(
        mlp_kernel,
        name="feed_forward",
        grid=(blocks // 2,),
        in_specs=[two, two, whole(w_g), whole(w_u), whole(w_d)],
        out_specs=[flat] * 3,
        out_shape=[jax.ShapeDtypeStruct((total, ff), BF)] * 3,
        scratch_shapes=[pltpu.VMEM((2 * rows, ff), F32)] * 3,
        compiler_params=pltpu.CompilerParams(vmem_limit_bytes=48 * 1024 * 1024),
        cost_estimate=pl.CostEstimate(
            flops=2 * total * width * ff * 3, bytes_accessed=total * width * 4, transcendentals=0
        ),
    )(n2, dm, w_g, w_u, w_d)


def semaphores(pairs, local):
    return [
        pltpu.SemaphoreType.DMA((pairs,)),
        pltpu.SemaphoreType.DMA((pairs,)),
        pltpu.SemaphoreType.DMA((local,)),
    ]


def run_kernel(body, name, outs, out_specs, in_specs, scratch, ident, args, mib=40):
    return pl.pallas_call(
        body,
        name=name,
        out_shape=[jax.ShapeDtypeStruct(*o) for o in outs],
        in_specs=in_specs,
        out_specs=out_specs,
        scratch_shapes=scratch,
        compiler_params=pltpu.CompilerParams(
            collective_id=ident, has_side_effects=True, vmem_limit_bytes=mib * 1024 * 1024
        ),
    )(*args)


def fetch_first(tokens, input_weight, gelu_weight, output_weight):
    if not shape_fits():
        return plain_fetch_first(tokens, input_weight, gelu_weight, output_weight)
    rows, width = tokens.shape[1:]
    drows, local = input_weight.shape[0], input_weight.shape[1] // 4
    pairs = [v.reshape(drows, 4, local) for v in (input_weight, gelu_weight)]
    ig = jnp.concatenate(pairs, axis=2).transpose(1, 0, 2)
    return run_kernel(
        first_kernel,
        "fetch_first",
        [((8, rows, width), BF), ((width, 2 * local), BF), ((local, width), BF)],
        [ANY] * 3,
        [ANY] * 3,
        semaphores(32, 8),
        1,
        (tokens, ig, output_weight),
    )


def reduce_and_fetch(mixed, w_o, own, gain, mlp_up, mlp_down):
    if not shape_fits():
        return plain_reduce_and_fetch(mixed, w_o, own, gain, mlp_up, mlp_down)
    rows, width = own.shape
    ff = mlp_up.shape[1] // 4
    return run_kernel(
        second_kernel,
        "reduce_and_fetch",
        [((rows, width), F32), ((8, rows, width), BF), ((width, ff), BF), ((ff, width), BF)],
        [VMEM] + [ANY] * 3,
        [VMEM] * 4 + [ANY] * 2,
        scatter_buffers(rows, width, True) + [pltpu.VMEM((rows, width), BF)] + semaphores(64, 16),
        2,
        (mixed, w_o, own, gain, mlp_up, mlp_down),
    )


def reduce_and_return(weights, middle, dout, gain, dm, hidden, n2, dgm, dup, drows):
    if not shape_fits():
        return plain_reduce_and_return(
            weights, middle, dout, gain, dm, hidden, n2, dgm, dup, drows
        )
    rows, width = middle.shape
    ff = hidden.shape[1]
    return run_kernel(
        third_kernel,
        "reduce_and_return",
        [
            ((rows, width), F32),
            ((8, width), F32),
            ((8, rows, width), BF),
            ((drows, 4 * ff), F32),
            ((4 * ff, drows), F32),
            ((8, rows, width), BF),
        ],
        [VMEM, VMEM, ANY] + [VMEM] * 2 + [ANY],
        [VMEM] * 6 + [ANY, VMEM] * 2 + [VMEM],
        scatter_buffers(rows, width, True)
        + grad_buffers(2 * drows, ff, 8 * rows) * 2
        + [pltpu.VMEM((rows, width), BF)]
        + semaphores(56, 48),
        3,
        (*weights, middle, dout, gain, dm, hidden, n2, dgm, dup),
        61,
    )


def return_last(w_ig, own, dr1, gain, do, mixed, n1, dboth, g_gates, drows):
    if not shape_fits():
        return plain_return_last(w_ig, own, dr1, gain, do, mixed, n1, dboth, g_gates, drows)
    rows, width = own.shape
    local, unit = dboth.shape[1] // 2, g_gates.shape[0] // 16
    return run_kernel(
        fourth_kernel,
        "return_last",
        [
            ((2, rows, width), F32),
            ((8, width), F32),
            ((drows, 4 * local), F32),
            ((drows, 4 * local), F32),
            ((4 * local, drows), F32),
            ((4, unit, 128), BF),
        ],
        [VMEM] * 6,
        [VMEM] * 4 + [ANY, VMEM] * 2 + [VMEM],
        scatter_buffers(rows, width, True)
        + grad_buffers(2 * drows, mixed.shape[1], 8 * rows)
        + grad_buffers(2 * drows, 2 * local, 8 * rows)
        + grad_buffers(2 * unit, 128)
        + [pltpu.VMEM((rows, width), BF)] * 2
        + semaphores(64, 48),
        4,
        (w_ig, own, dr1, gain, do, mixed, n1, dboth, g_gates),
        60,
    )


def shape_fits():
    return all(lax.axis_size(n) == 2 for n in AXES)


def plain_fetch_first(tokens, input_weight, gelu_weight, output_weight):
    exchange = Tokens()
    own = lax.dynamic_index_in_dim(tokens, exchange.mp, 0, keepdims=False)
    return (
        exchange.gather(own).reshape((8,) + own.shape),
        fetch_weight([input_weight, gelu_weight], 4),
        fetch_weight([output_weight.T], 4).T,
    )


def plain_reduce_and_fetch(mixed, w_o, own, gain, mlp_up, mlp_down):
    exchange = Tokens()
    middle = own.astype(F32) + exchange.scatter(dot(mixed, w_o, NN, BF))
    normed = (middle * inverse_rms(middle) * gain).astype(BF)
    return (
        middle,
        exchange.gather(normed).reshape((8,) + own.shape),
        fetch_weight([mlp_up], 4),
        fetch_weight([mlp_down.T], 4).T,
    )


def columns(share, at, count):
    return share[:, :, at : at + count].astype(F32).transpose(1, 0, 2).reshape(-1, 4 * count)


def both_batches(rows):
    mp = lax.axis_index("mp")
    other = lax.ppermute(rows, "mp", [(0, 1), (1, 0)])
    return jnp.stack([jnp.where(mp == 0, rows, other), jnp.where(mp == 0, other, rows)])


def plain_reduce_and_return(weights, middle, dout, gain, dm, hidden, n2, dgm, dup, drows):
    exchange = Tokens()
    w_g, w_u, w_d = weights
    ff = hidden.shape[1]
    total = exchange.scatter((dot(dgm, w_g, NT) + dot(dup, w_u, NT)).astype(BF))
    change, gain_rows = norm_back(middle, gain, total)
    dr1 = dout + change
    gate = return_grad(dot(n2, dgm, TN, BF), drows)
    down = return_grad(dot(dm, hidden, TN, BF), drows)
    return (
        dr1,
        jnp.sum(gain_rows, axis=0, keepdims=True),
        exchange.gather(dr1.astype(BF)).reshape((8,) + dr1.shape),
        columns(gate, 0, ff),
        columns(down, 0, ff).T,
        dot(hidden, w_d, NN, BF).reshape((8,) + dr1.shape),
    )


def plain_return_last(w_ig, own, dr1, gain, do, mixed, n1, dboth, g_gates, drows):
    exchange = Tokens()
    local = dboth.shape[1] // 2
    total = exchange.scatter(dot(dboth, w_ig, NT, BF))
    change, gain_rows = norm_back(own.astype(F32), gain, total)
    group = n1.shape[1] // drows
    wide = return_grad(dot(n1, dboth, TN, BF), drows)
    out = return_grad(dot(do, mixed, TN, BF), drows)
    return (
        both_batches(dr1 + change),
        jnp.sum(gain_rows, axis=0, keepdims=True),
        columns(wide, 0, local),
        columns(wide, local, local),
        columns(out, 0, local).T,
        return_grad(g_gates, g_gates.shape[0] // group),
    )


def scan_body(reverse, a_ref, b_ref, p_ref, h_ref):
    length, width = a_ref.shape[1], a_ref.shape[2]
    row = lax.broadcasted_iota(jnp.int32, (8, width), 0)

    def tile(i, carry):
        ca, ch = carry
        at = (length // 8 - 1 - i if reverse else i) * 8
        at = pl.multiple_of(at, 8)
        a = a_ref[0, pl.ds(at, 8), :]
        b = b_ref[0, pl.ds(at, 8), :]
        for step in (1, 2, 4):
            if reverse:
                inside = row < 8 - step
                shift = 8 - step
            else:
                inside = row >= step
                shift = step
            sa = jnp.where(inside, pltpu.roll(a, shift, 0), 1.0)
            sb = jnp.where(inside, pltpu.roll(b, shift, 0), 0.0)
            b = b + a * sb
            a = a * sa
        h = b + a * ch
        p = a * ca
        h_ref[0, pl.ds(at, 8), :] = h
        p_ref[0, pl.ds(at, 8), :] = p
        last = 0 if reverse else 7
        return p[last : last + 1, :], h[last : last + 1, :]

    lax.fori_loop(
        0,
        length // 8,
        tile,
        (jnp.ones((1, width), F32), jnp.zeros((1, width), F32)),
    )


def local_scan(a, b, reverse):
    segs, length, width = a.shape
    spec = pl.BlockSpec((1, length, width), lambda s: (s, 0, 0))
    return pl.pallas_call(
        lambda *refs: scan_body(reverse, *refs),
        grid=(segs,),
        in_specs=[spec, spec],
        out_specs=[spec, spec],
        out_shape=[jax.ShapeDtypeStruct(a.shape, F32)] * 2,
        cost_estimate=pl.CostEstimate(
            flops=20 * a.size, bytes_accessed=16 * a.size, transcendentals=0
        ),
    )(a, b)


def carried(product, state, reverse):
    count = lax.axis_size("zh")
    if count == 2:
        return lax.ppermute(state, "zh", [(1, 0)] if reverse else [(0, 1)])
    here = lax.axis_index("zh")
    pairs = lax.all_gather(jnp.stack([product, state]), "zh")
    total = jnp.zeros_like(state)
    for k in range(count):
        at = count - 1 - k if reverse else k
        reached = at > here if reverse else at < here
        total = jnp.where(reached, pairs[at, 1] + pairs[at, 0] * total, total)
    return total


def from_behind(x, by):
    count = lax.axis_size("zh")
    return lax.ppermute(
        x, "zh", [(i, i + by) for i in range(count) if 0 <= i + by < count]
    )


def inverse_rms(values):
    return lax.rsqrt(jnp.mean(values * values, axis=-1, keepdims=True) + EPSILON)


def gelu(v):
    return jax.nn.gelu(v, approximate=True)


def gelu_both(v):
    c = 0.7978845608028654
    t = jnp.tanh(c * (v + 0.044715 * v * v * v))
    value = 0.5 * v * (1.0 + t)
    slope = 0.5 * (1.0 + t) + 0.5 * v * (1.0 - t * t) * c * (1.0 + 3 * 0.044715 * v * v)
    return value, slope


def dot(a, b, dims, out=F32):
    r = lax.dot_general(a, b, (dims, ((), ())), preferred_element_type=F32)
    return r.astype(out)


NN = ((1,), (0,))
NT = ((1,), (1,))
TN = ((0,), (0,))


LANES = 384


def minus_expm1(v):
    series = 1.0 + v / 8.0
    for k in (7.0, 6.0, 5.0, 4.0, 3.0, 2.0):
        series = 1.0 + v * (1.0 / k) * series
    return jnp.where(v > -0.4, -v * series, 1.0 - jnp.exp(v))


def pad_lanes(v, fill=0.0):
    return jnp.pad(v, ((0, 0), (0, LANES - v.shape[1])), constant_values=fill)


def loop(count, body, unroll=1):
    def step(i, carry):
        body(i)
        return carry

    lax.fori_loop(0, count, step, 0, unroll=unroll)


def tile_scan(a, b, row, reverse):
    for step in (1, 2, 4):
        inside = row < 8 - step if reverse else row >= step
        shift = 8 - step if reverse else step
        sa = jnp.where(inside, pltpu.roll(a, shift, 0), 1.0)
        sb = jnp.where(inside, pltpu.roll(b, shift, 0), 0.0)
        b = b + a * sb
        a = a * sa
    return a, b


def eight(i):
    return pl.multiple_of(i * 8, 8)


def recur_forward_kernel(
    tok_ref, wig_ref, blocks_ref, ch_ref, gain_ref, cot_ref, gate_ref,
    n1_out, xs, gy, u, siga, sigi, decay, states, mixed, dm_ref, wg_ref,
    run, logits, n1, both, halo, ends, inc, tok, sems, send, recv, local_sems,
):
    p = Place()
    links = Links(send, recv, local_sems)
    rows, local = tok_ref.shape[1], wig_ref.shape[1] // 2
    zh = p.zh
    greet(weight_peers(p))
    w_g = slot_columns(p, links, gate_ref, wg_ref)
    adjoint = TokenGatherTwice(p, links, cot_ref, dm_ref)
    w_g.begin((1,), (0,))
    w_g.begin((0,))
    adjoint.begin()

    def read(b):
        return pltpu.make_async_copy(tok_ref.at[b], tok.at[b % 2], sems.at[4 + b % 2])

    read(0).start()
    lane = lax.broadcasted_iota(jnp.int32, (1, LANES), 1)
    real = lane < local

    def project(b):
        read(b).wait()

        @pl.when(b < 7)
        def _():
            read(b + 1).start()

        def normalise(at):
            value = tok[b % 2, at, :].astype(F32)
            inv = lax.rsqrt(jnp.mean(value * value, axis=-1, keepdims=True) + EPSILON)
            n1[b % 2, at, :] = (value * inv * gain_ref[...]).astype(BF)

        def write(i, at):
            return pltpu.make_async_copy(n1.at[i], n1_out.at[at], sems.at[i])

        @pl.when(b >= 2)
        def _():
            write(b % 2, b - 2).wait()

        chunks(rows, normalise)
        write(b % 2, b).start()
        both[...] = dot(n1[b % 2], wig_ref[...], NN)
        seg, zl = b // 2, b % 2

        def split(at):
            v = both[at, :]
            xb = jnp.where(real, v[:, :LANES], 0.0).astype(BF).astype(F32)
            xs[seg, pl.ds(pl.multiple_of(8 + zl * rows + at.start, 8), CHUNK), :] = xb
            rest = pltpu.roll(v, v.shape[1] - local, 1)[:, :LANES]
            gy[b, at, :] = jnp.where(real, rest, 0.0)

        chunks(rows, split)

    loop(8, project)
    for b in (6, 7):
        pltpu.make_async_copy(n1.at[b % 2], n1_out.at[b], sems.at[b % 2]).wait()

    def to_partner(src, dst):
        at = links.pair()
        links.start(src, dst, at, p.peer(zh=1))
        return at

    at = to_partner(xs.at[:, pl.ds(2 * rows, 8)], halo)
    w_g.onward(0)
    adjoint.forward()
    links.arrived(halo, at)
    w_g.begin((1,), (1,))
    row = lax.broadcasted_iota(jnp.int32, (8, LANES), 0)
    soft = ch_ref[0:1, :]

    def head(seg):
        xs[seg, 0:8, :] = jnp.where(zh == 1, halo[seg], 0.0)

    loop(4, head)

    def convolve(b):
        seg, zl = b // 2, b % 2

        def body(at):
            v = xs[seg, pl.ds(pl.multiple_of(zl * rows + at.start, 8), CHUNK + 8), :]
            total = ch_ref[3:4, :] + ch_ref[4:5, :] * v[8:]
            for k in (1, 2, 3):
                total = total + ch_ref[4 + k : 5 + k, :] * pltpu.roll(v, k, 0)[8:]
            u[b, at, :] = total.astype(BF)

        chunks(rows, body)
        logits[b] = dot(u[b], blocks_ref[...], NN)

    loop(8, convolve)

    def tile(i, carry, zl):
        at = pl.ds(eight(i), 8)
        out = []
        for seg in range(4):
            b = seg * 2 + zl
            cp, ch = carry[seg]
            sa = jax.nn.sigmoid(logits[b, at, :LANES] + ch_ref[1:2, :])
            si = jax.nn.sigmoid(logits[b, at, LANES:] + ch_ref[2:3, :])
            log_decay = -DECAY_SCALE * sa * soft
            a = jnp.exp(log_decay)
            drive = jnp.sqrt(minus_expm1(2.0 * log_decay)) * si * u[b, at, :].astype(F32)
            siga[b, at, :] = sa
            sigi[b, at, :] = si
            decay[b, at, :] = a
            pa, h = tile_scan(a, drive, row, False)
            h = h + pa * ch
            pa = pa * cp
            run[b, at, :] = pa
            states[seg, pl.ds(pl.multiple_of(8 + zl * rows + i * 8, 8), 8), :] = h
            out.append((pa[7:8, :], h[7:8, :]))
        return tuple(out)

    carry = ((jnp.ones((1, LANES), F32), jnp.zeros((1, LANES), F32)),) * 4
    for zl in range(2):
        carry = lax.fori_loop(0, rows // 8, functools.partial(tile, zl=zl), carry)
    ends[...] = jnp.zeros_like(ends)
    for seg in range(4):
        ends[seg : seg + 1, :] = carry[seg][1]
    at = to_partner(ends, inc)
    adjoint.forward_core()
    w_g.onward(1, (0,))
    links.arrived(inc, at)

    def finish(b):
        seg, zl = b // 2, b % 2
        start = jnp.where(zh == 1, inc[pl.ds(seg, 1), :], 0.0)

        @pl.when(zl == 0)
        def _():
            states[seg, 0:8, :] = jnp.broadcast_to(start, (8, LANES))

        def state(at):
            there = pl.ds(pl.multiple_of(8 + zl * rows + at.start, 8), CHUNK)
            h = states[seg, there, :] + run[b, at, :] * start
            states[seg, there, :] = h
            v = gy[b, at, :]
            t = jnp.tanh(0.7978845608028654 * (v + 0.044715 * v * v * v))
            mixed[b, at, :] = (0.5 * v * (1.0 + t) * h).astype(BF)

        chunks(rows, state)

    loop(8, finish)
    w_g.onward(1, (1,))
    adjoint.end()
    w_g.end()
    links.finish()


def recur_backward_kernel(
    do_ref, wo_ref, blocks_ref, ch_ref,
    xs, gy, u, siga, sigi, decay, states, rows_ref, mid_ref, n2_ref, dup_ref,
    dboth_out, gb_out, ch_out, block_out, up_out,
    dh, after, dgy, dlog_ref, du, dboth, halo, ends, inc, do, final, sems,
    *scratch,
):
    p = Place()
    links = Links(*scratch[-3:])
    rows, local = do_ref.shape[1], wo_ref.shape[0]
    zh = p.zh
    greet(weight_peers(p))
    scatter = RowScatter(p, links, rows_ref, scratch[:5])
    up = GradScatter(p, links, n2_ref, dup_ref, scratch[5:12], GradScatter.EARLY)

    def read(b):
        return pltpu.make_async_copy(do_ref.at[b], do.at[b % 2], sems.at[4 + b % 2])

    read(0).start()
    up.begin(1)
    scatter.begin()
    ch_out[...] = jnp.zeros_like(ch_out)
    gb_out[...] = jnp.zeros_like(gb_out)
    soft = ch_ref[0:1, :]

    def to_partner(src, dst):
        at = links.pair()
        links.start(src, dst, at, p.peer(zh=1))
        return at

    def upstream(b):
        seg, zl = b // 2, b % 2
        dh[b, :, local:] = jnp.zeros((rows, LANES - local), F32)
        read(b).wait()

        @pl.when(b < 7)
        def _():
            read(b + 1).start()

        dh[b, :, :local] = dot(do[b % 2], wo_ref[...], NT)

        def split(at):
            value, slope = gelu_both(gy[b, at, :])
            dz = dh[b, at, :]
            h = states[seg, pl.ds(pl.multiple_of(8 + zl * rows + at.start, 8), CHUNK), :]
            dh[b, at, :] = dz * value
            dgy[b, at, :] = (dz * h * slope).astype(BF)

        chunks(rows, split)

    loop(8, upstream)
    scatter.across_y()
    up.begin(0)
    row = lax.broadcasted_iota(jnp.int32, (8, LANES), 0)
    one = jnp.ones((1, LANES), F32)
    ends[...] = jnp.zeros_like(ends)

    def tile(i, carry, zl):
        at = pl.ds(eight(rows // 8 - 1 - i), 8)
        out = []
        for seg in range(4):
            b = seg * 2 + zl
            cp, cg, following = carry[seg]
            a = decay[b, at, :]
            shifted = jnp.where(row == 7, following, pltpu.roll(a, 7, 0))
            pa, g = tile_scan(shifted, dh[b, at, :], row, True)
            g = g + pa * cg
            pa = pa * cp
            dh[b, at, :] = g
            after[b, at, :] = pa
            out.append((pa[0:1, :], g[0:1, :], a[0:1, :]))
        return tuple(out)

    carry = ((one, jnp.zeros((1, LANES), F32), one),) * 4
    for zl in (1, 0):
        carry = lax.fori_loop(0, rows // 8, functools.partial(tile, zl=zl), carry)
    for seg in range(4):
        ends[seg : seg + 1, :] = carry[seg][1] * carry[seg][2]
    at = to_partner(ends, inc)
    links.arrived(inc, at)
    up.across(0)
    scatter.across_z()

    def gradients(b):
        seg, zl = b // 2, b % 2
        later = jnp.where(zh == 0, inc[pl.ds(seg, 1), :], 0.0)

        def body(at):
            window = states[seg, pl.ds(pl.multiple_of(zl * rows + at.start, 8), CHUNK + 8), :]
            previous = pltpu.roll(window, 1, 0)[8:]
            g = dh[b, at, :] + after[b, at, :] * later
            sa, si, a = siga[b, at, :], sigi[b, at, :], decay[b, at, :]
            uf = u[b, at, :].astype(F32)
            root = jnp.sqrt(minus_expm1((-2.0 * DECAY_SCALE) * sa * soft))
            gu = g * uf
            gr = g * root
            d_log = a * (g * previous - gu * si * a / root)
            d_log = jnp.where(real, d_log, 0.0)
            dra = (d_log * (-DECAY_SCALE * soft) * sa * (1.0 - sa)).astype(BF)
            dri = (gr * uf * si * (1.0 - si)).astype(BF)
            du[seg, pl.ds(pl.multiple_of(zl * rows + at.start, 8), CHUNK), :] = gr * si
            dlog_ref[at, :LANES] = dra
            dlog_ref[at, LANES:] = dri
            for k, v in enumerate((d_log * sa, dra.astype(F32), dri.astype(F32))):
                sums[k] = sums[k] + fold(v)

        sums = [jnp.zeros((8, LANES), F32) for _ in range(3)]
        chunks(rows, body)
        for k in range(3):
            ch_out[k] += sums[k]
        d = dlog_ref[...]
        there = pl.ds(pl.multiple_of(zl * rows, 8), rows)
        du[seg, there, :] += dot(d, blocks_ref[...], NT)
        gb_out[...] += dot(u[b], d, TN)

    lane = lax.broadcasted_iota(jnp.int32, (1, LANES), 1)
    real = lane < local
    loop(8, gradients)
    at = to_partner(du.at[:, pl.ds(0, 8)], halo)
    up.across(1)

    def write(i, at, src, dst, base):
        return pltpu.make_async_copy(src.at[i], dst.at[at], sems.at[base + i])

    def convolve(i, zl):
        seg = i
        b = i * 2 + zl
        slot = i % 2

        @pl.when(i >= 2)
        def _():
            write(slot, b - 4, dboth, dboth_out, 0).wait()

        def body(at):
            start = pl.multiple_of(zl * rows + at.start, 8)
            v = du[seg, pl.ds(start, CHUNK + 8), :]
            x = xs[seg, pl.ds(start, CHUNK + 8), :]
            here = v[:CHUNK]
            total = ch_ref[4:5, :] * here
            sums[0] = sums[0] + fold(here)
            sums[1] = sums[1] + fold(here * x[8:])
            for k in (1, 2, 3):
                total = total + ch_ref[4 + k : 5 + k, :] * pltpu.roll(v, CHUNK + 8 - k, 0)[:CHUNK]
                sums[1 + k] = sums[1 + k] + fold(here * pltpu.roll(x, k, 0)[8:])
            wide = 2 * local - LANES
            zeros = jnp.zeros((CHUNK, wide), F32)
            left = jnp.concatenate([total, zeros], axis=1)
            right = jnp.concatenate([dgy[b, at, :].astype(F32), zeros], axis=1)
            dboth[slot, at, :] = (left + pltpu.roll(right, local, 1)).astype(BF)

        sums = [jnp.zeros((8, LANES), F32) for _ in range(5)]
        chunks(rows, body)
        for k in range(5):
            ch_out[3 + k] += sums[k]
        write(slot, b, dboth, dboth_out, 0).start()

    def drain(zl):
        for i in (2, 3):
            write(i % 2, i * 2 + zl, dboth, dboth_out, 0).wait()

    loop(4, functools.partial(convolve, zl=0))
    drain(0)
    up.last(0)
    links.arrived(halo, at)

    def tail(seg):
        du[seg, pl.ds(2 * rows, 8), :] = jnp.where(zh == 0, halo[seg], 0.0)

    loop(4, tail)
    loop(4, functools.partial(convolve, zl=1))
    drain(1)
    up.last(1)
    scatter.arrive()

    def add(at):
        final[at, :] = (mid_ref[at, :] + scatter.total(at)).astype(BF)

    chunks(rows, add)
    at = links.pair()
    links.start(final, block_out.at[p.mp], at, p.peer(mp=1))
    kept = links.keep(final, block_out.at[p.mp])
    up.end()
    ff = up.result.shape[2]
    for j in range(4):
        up_out[:, j * ff : (j + 1) * ff] = up.result[j].astype(F32)
    kept.wait()
    links.arrived(block_out.at[1 - p.mp], at)
    links.finish()


def recur_forward(tokens, w_ig, blocks, channels, gain, dm, mlp_gate):
    if not shape_fits():
        return plain_recur_forward(tokens, w_ig, blocks, channels, gain, dm, mlp_gate)
    ff, drows = mlp_gate.shape[1] // 4, mlp_gate.shape[0]
    rows, width = tokens.shape[1:]
    local = w_ig.shape[1] // 2
    soft = jax.nn.softplus(-channels[0:1])
    table = jnp.concatenate([soft, channels[1:]], axis=0)
    table = pad_lanes(table)
    wide = jnp.concatenate(
        [jnp.pad(blocks[:, g * local : (g + 1) * local], ((0, LANES - local),) * 2) for g in (0, 1)],
        axis=1,
    )
    f, h = (8, rows, LANES), (4, 2 * rows + 8, LANES)
    n1, *saved = run_kernel(
        recur_forward_kernel,
        "recur_forward",
        [(tokens.shape, BF), (h, F32), (f, F32), (f, BF)]
        + [(f, F32)] * 3
        + [(h, F32), (f, BF), (tokens.shape, BF), ((width, ff), BF)],
        [ANY] + [VMEM] * 8 + [ANY] * 2,
        [ANY] + [VMEM] * 4 + [ANY] * 2,
        [
            pltpu.VMEM(f, F32),
            pltpu.VMEM((8, rows, 2 * LANES), F32),
            pltpu.VMEM((2, rows, width), BF),
            pltpu.VMEM((rows, 2 * local), F32),
            pltpu.VMEM((4, 8, LANES), F32),
            pltpu.VMEM((8, LANES), F32),
            pltpu.VMEM((8, LANES), F32),
            pltpu.VMEM((2, rows, width), BF),
        ]
        + semaphores(6, 2)[:1]
        + semaphores(24, 8),
        5,
        (tokens, w_ig, wide, table, gain, dm, mlp_gate),
        56,
    )
    *saved, mixed, dm, w_g = saved
    return n1.reshape(-1, width), mixed.reshape(-1, LANES), (table, wide, *saved), dm, w_g


def recur_backward(do, saved, w_o, channels, out_part, middle, n2, dup, drows):
    if not shape_fits():
        return plain_recur_backward(do, saved, w_o, channels, out_part, middle, n2, dup, drows)
    ff = dup.shape[1]
    table, wide, xs, gy, u, siga, sigi, decay, states = saved
    rows, width = do.shape[1:]
    local = w_o.shape[0]
    f, h = (8, rows, LANES), (4, 2 * rows + 8, LANES)
    dboth, g_blocks, sums, block_out, g_up = run_kernel(
        recur_backward_kernel,
        "recur_backward",
        [
            ((8, rows, 2 * local), BF),
            ((LANES, 2 * LANES), F32),
            ((8, 8, LANES), F32),
            ((2, rows, width), BF),
            ((drows, 4 * ff), F32),
        ],
        [ANY] + [VMEM] * 2 + [ANY, VMEM],
        [ANY] + [VMEM] * 10 + [ANY, VMEM, ANY, VMEM],
        [
            pltpu.VMEM(f, F32),
            pltpu.VMEM(f, F32),
            pltpu.VMEM(f, BF),
            pltpu.VMEM((rows, 2 * LANES), BF),
            pltpu.VMEM(h, F32),
            pltpu.VMEM((2, rows, 2 * local), BF),
            pltpu.VMEM((4, 8, LANES), F32),
            pltpu.VMEM((8, LANES), F32),
            pltpu.VMEM((8, LANES), F32),
            pltpu.VMEM((2, rows, width), BF),
            pltpu.VMEM((rows, width), BF),
        ]
        + semaphores(6, 2)[:1]
        + scatter_buffers(rows, width)
        + grad_buffers(2 * drows, ff, 8 * rows)
        + semaphores(32, 24),
        6,
        (do, w_o, wide, table, xs, gy, u, siga, sigi, decay, states)
        + (out_part, middle, n2, dup),
        61,
    )
    sums = jnp.sum(sums, axis=1)[:, :local]
    dlam = sums[0] * DECAY_SCALE * jax.nn.sigmoid(-channels[0])
    g_blocks = jnp.concatenate(
        [g_blocks[:local, g * LANES : g * LANES + local] for g in (0, 1)], axis=1
    )
    return (
        dboth.reshape(-1, 2 * local),
        g_blocks,
        jnp.concatenate([dlam[None], sums[1:]], axis=0),
        block_out,
        g_up,
    )


def plain_recur_forward(tokens, w_ig, blocks, channels, gain, dm, mlp_gate):
    length, local, width = tokens.shape[1], w_ig.shape[1] // 2, tokens.shape[2]
    wide = tokens.reshape(-1, width).astype(F32)
    n1 = (wide * inverse_rms(wide) * gain).astype(BF)
    both = dot(n1, w_ig, NN)
    xb = both[:, :local].astype(BF).reshape(4, 2 * length, local)
    gy = both[:, local:].reshape(4, 2 * length, local)
    rim = from_behind(xb[:, -3:], 1)
    padded = jnp.concatenate([rim, xb], axis=1).astype(F32)
    conv = channels[3]
    for k in range(4):
        conv = conv + channels[4 + k] * padded[:, 3 - k : 3 - k + 2 * length]
    u = conv.astype(BF)
    logits = dot(u.reshape(-1, local), blocks, NN).reshape(4, 2 * length, 2 * local)
    sig_a = jax.nn.sigmoid(logits[..., :local] + channels[1])
    sig_i = jax.nn.sigmoid(logits[..., local:] + channels[2])
    log_decay = -DECAY_SCALE * sig_a * jax.nn.softplus(-channels[0])
    decay = jnp.exp(log_decay)
    root = jnp.sqrt(-jnp.expm1(2.0 * log_decay))
    running, state = local_scan(decay, root * sig_i * u.astype(F32), False)
    incoming = carried(running[:, -1], state[:, -1], False)
    states = state + running * incoming[:, None]
    gelu_y, slope_y = gelu_both(gy)
    mixed = (gelu_y * states).astype(BF).reshape(-1, local)
    saved = (blocks, padded, u, sig_a, sig_i, decay, root, running, incoming, states)
    exchange = Tokens()
    dm = exchange.gather(lax.dynamic_index_in_dim(dm, exchange.mp, 0, keepdims=False))
    return (
        n1,
        mixed,
        saved + (gelu_y, slope_y),
        dm.reshape(8, length, width),
        fetch_weight([mlp_gate], 4),
    )


def plain_recur_backward(do, saved, w_o, channels, out_part, middle, n2, dup, drows):
    blocks, padded, u, sig_a, sig_i, decay, root, running, incoming, states = saved[:10]
    gelu_y, slope_y = saved[10:]
    length, local, width = do.shape[1], w_o.shape[0], do.shape[2]
    dz = dot(do.reshape(-1, width), w_o, NT).reshape(4, 2 * length, local)
    dh = dz * gelu_y
    dgy = (dz * states * slope_y).astype(BF)
    ones = jnp.ones_like(decay[:, :1])
    after, adjoint = local_scan(jnp.concatenate([decay[:, 1:], ones], axis=1), dh, True)
    later = carried(running[:, -1], decay[:, 0] * adjoint[:, 0], True)
    adjoint = adjoint + after * later[:, None]
    previous = jnp.concatenate([incoming[:, None], states[:, :-1]], axis=1)
    soft, uf = jax.nn.softplus(-channels[0]), u.astype(F32)
    d_root = adjoint * sig_i * uf
    d_log = adjoint * previous * decay - d_root * decay * decay / root
    dra = (d_log * (-DECAY_SCALE * soft) * sig_a * (1.0 - sig_a)).astype(BF)
    dri = (adjoint * root * uf * sig_i * (1.0 - sig_i)).astype(BF)
    dlam = jnp.sum(d_log * sig_a, axis=(0, 1)) * DECAY_SCALE * jax.nn.sigmoid(-channels[0])
    dlogits = jnp.concatenate([dra, dri], axis=2).reshape(-1, 2 * local)
    g_blocks = dot(u.reshape(-1, local), dlogits, TN)
    du = adjoint * root * sig_i + dot(dlogits, blocks, NT).reshape(4, 2 * length, local)
    zeros = jnp.zeros((4, 3, local), F32)
    spread = jnp.concatenate([zeros, du, zeros], axis=1)
    dpad = jnp.zeros((4, 2 * length + 3, local), F32)
    taps = []
    for k in range(4):
        dpad = dpad + channels[4 + k] * spread[:, k : k + 2 * length + 3]
        taps.append(jnp.sum(du * padded[:, 3 - k : 3 - k + 2 * length], axis=(0, 1)))
    back = from_behind(dpad[:, :3], -1)
    dxb = dpad[:, 3:] + jnp.concatenate(
        [jnp.zeros((4, 2 * length - 3, local), F32), back], axis=1
    )
    dboth = jnp.concatenate([dxb.astype(BF), dgy], axis=2).reshape(-1, 2 * local)
    sums = [jnp.sum(v.astype(F32), axis=(0, 1)) for v in (dra, dri, du)]
    result = (middle + Tokens().scatter(out_part.reshape(-1, width))).astype(BF)
    g_up = columns(return_grad(dot(n2, dup, TN, BF), drows), 0, dup.shape[1])
    small = jnp.stack([dlam] + sums + taps)
    return dboth, g_blocks, small, both_batches(result), g_up


def on_device(
    tokens_in,
    cotangent,
    seq_source,
    source_weight,
    input_weight,
    gelu_weight,
    decay_gates,
    input_gates,
    channel_params,
    norm_gains,
    output_weight,
    mlp_gate,
    mlp_up,
    mlp_down,
):
    sizes = tuple(lax.axis_size(n) for n in AXES)
    dxn, _, zhn, _, _ = sizes
    group = dxn * 2 * zhn * 2
    dc, zl, mp = (lax.axis_index(n) for n in ("dc", "zl", "mp"))
    slot = dc * 2 + zl
    width = tokens_in.shape[3]
    local = input_weight.shape[1] // 4
    heads = decay_gates.shape[0] // 4
    drows = input_weight.shape[0]
    piece = decay_gates.shape[1]

    own = lax.dynamic_index_in_dim(tokens_in[:, 0], mp, 0, keepdims=False)
    scales = jnp.stack(
        [
            jnp.sum(
                jnp.where(
                    jnp.arange(source_weight.shape[0], dtype=jnp.int32) == seq_source[m, 0],
                    source_weight,
                    0.0,
                )
            )
            for m in range(2)
        ]
    )
    douts = cotangent[:, 0].astype(F32) * scales[:, None, None]
    dout = lax.dynamic_index_in_dim(douts, mp, 0, keepdims=False)

    small = jnp.concatenate([channel_params.reshape(-1), norm_gains.reshape(-1)])
    shards = ("dx", "dc", "zh", "zl")
    small = lax.all_to_all(
        jnp.broadcast_to(small[None], (group, small.size)), shards, 0, 0, tiled=True
    )
    nch = channel_params.size
    channels = small[:, :nch].reshape(group, 8, -1).transpose(1, 0, 2).reshape(8, -1)
    channels = lax.dynamic_slice_in_dim(channels, slot * local, local, 1).astype(F32)
    gains = small[:, nch:].reshape(group, 2, -1).transpose(1, 0, 2).reshape(2, -1).astype(F32)

    ff = mlp_gate.shape[1] // 4
    tokens, w_ig, w_o = fetch_first(tokens_in[:, 0], input_weight, gelu_weight, output_weight)

    gates = jnp.stack([decay_gates, input_gates]).reshape(2, 4, heads, piece)
    gates = gates.transpose(1, 0, 2, 3).reshape(2, 1, 2, 1, 2 * heads * piece)
    gates = jnp.broadcast_to(gates, (2, zhn, 2, dxn, 2 * heads * piece))
    gates = gates.transpose(3, 0, 1, 2, 4).reshape(group, 2 * heads * piece)
    gates = lax.all_to_all(gates, shards, 0, 0, tiled=True)
    gates = gates.reshape(group, 2 * heads, piece).transpose(1, 0, 2)
    gates = gates.reshape(2, heads, BLOCK, BLOCK)

    zero = jnp.zeros((BLOCK, BLOCK), BF)
    blocks = jnp.concatenate(
        [
            jnp.concatenate(
                [gates[g, h] if k == h else zero for g in range(2) for k in range(heads)], axis=1
            )
            for h in range(heads)
        ],
        axis=0,
    )
    n1, mixed, saved, dm, w_g = recur_forward(
        tokens, w_ig, blocks, channels, gains[0:1], douts.astype(BF), mlp_gate
    )
    middle, n2, w_u, w_d = reduce_and_fetch(mixed, w_o, own, gains[1:2], mlp_up, mlp_down)

    hidden, dgm, dup = feed_forward(n2, dm, w_g, w_u, w_d)
    n2, dm = n2.reshape(-1, width), dm.reshape(-1, width)
    dr1, gain_two, do, g_gate, g_down, out_part = reduce_and_return(
        (w_g, w_u, w_d), middle, dout, gains[1:2], dm, hidden, n2, dgm, dup, drows
    )
    gain_two = jnp.sum(gain_two, axis=0)

    dboth, g_blocks, channel_grad, block_out, g_up = recur_backward(
        do, saved, w_o, channels, out_part, middle, n2, dup, drows
    )

    g_gates = jnp.stack(
        [
            jnp.stack(
                [
                    g_blocks[
                        h * BLOCK : (h + 1) * BLOCK,
                        g * local + h * BLOCK : g * local + (h + 1) * BLOCK,
                    ]
                    for h in range(heads)
                ]
            )
            for g in range(2)
        ]
    )
    g_gates = g_gates.reshape(2 * heads, group, piece).transpose(1, 0, 2).reshape(group, -1)
    count = g_gates.shape[1]
    unit = (count + 2047) // 2048 * 16
    g_gates = jnp.pad(g_gates, ((0, 0), (0, unit * 128 - count))).astype(BF)
    grad_tokens, gain_one, g_input, g_gelu, g_output, share_gates = return_last(
        w_ig,
        own,
        dr1,
        gains[0:1],
        do.reshape(-1, width),
        mixed,
        n1,
        dboth,
        g_gates.reshape(group * unit, 128),
        drows,
    )
    gain_one = jnp.sum(gain_one, axis=0)
    g_gates = share_gates.reshape(4, -1)[:, :count].astype(F32).reshape(4, 2, heads, piece)
    g_gates = g_gates.transpose(1, 0, 2, 3).reshape(2, 4 * heads, piece)

    per = 4 * local // group
    mine = channel_grad.reshape(8, group // 4, per).transpose(1, 0, 2)
    mine = jnp.where(
        jnp.arange(4, dtype=jnp.int32)[:, None, None, None] == slot, mine[None], 0.0
    ).reshape(group, 1, 8 * per)
    mine = jnp.where(jnp.arange(2, dtype=jnp.int32)[None, :, None] == mp, mine, 0.0)
    both_gains = jnp.stack([gain_one, gain_two]).reshape(2, group, -1).transpose(1, 0, 2)
    both_gains = jnp.broadcast_to(both_gains.reshape(group, 1, -1), (group, 2, 2 * drows))
    sums = jnp.concatenate([both_gains, mine], axis=2).reshape(2 * group, -1)
    sums = jnp.sum(lax.all_to_all(sums, AXES, 0, 0, tiled=True), axis=0)
    g_gains = sums[: 2 * drows].reshape(2, drows)
    g_channels = sums[2 * drows :].reshape(8, 1, per)
    return (
        block_out[:, None],
        grad_tokens[:, None],
        g_input,
        g_gelu,
        g_gates[0],
        g_gates[1],
        g_channels,
        g_gains,
        g_output,
        g_gate,
        g_up,
        g_down,
    )


def solution(mesh):
    dpn, seqn, mpn = (mesh.shape[n] for n in ("dp", "seq", "mp"))
    fine = Mesh(mesh.devices.reshape(dpn // 2, 2, seqn // 2, 2, mpn), AXES)
    dp, seq = ("dx", "dc"), ("zh", "zl")
    shards = dp + seq
    weights = (
        P(shards, "mp"),
        P(shards, "mp"),
        P("mp", shards),
        P("mp", shards),
        P(None, "mp", shards),
        P(None, shards),
        P("mp", shards),
        P(shards, "mp"),
        P(shards, "mp"),
        P("mp", shards),
    )
    rows = P(None, dp, seq, None)
    return jax.shard_map(
        on_device,
        mesh=fine,
        in_specs=(rows, rows, P(None, dp), P()) + weights,
        out_specs=(rows, rows) + weights,
        check_vma=False,
    )
```

```python
import functools

import jax
import jax.numpy as jnp
import numpy as np
from jax import lax
from jax.experimental import pallas as pl
from jax.experimental.pallas import tpu as pltpu
from jax.sharding import Mesh, PartitionSpec as P

WIDTH = 2560
HEADS = 16
BLOCK = WIDTH // HEADS
EPSILON = 1e-06
DECAY_SCALE = 8.0
AXES = ("dx", "dc", "zh", "zl", "mp")
BF = jnp.bfloat16
F32 = jnp.float32
LANES = 384


def swap_pairs(sizes, partner):
    pairs = []
    for flat in range(int(np.prod(sizes))):
        coords = np.unravel_index(flat, sizes)
        pairs.append((flat, int(np.ravel_multi_index(partner(*map(int, coords)), sizes))))
    return pairs


def gather_blocks(x, axis, dim):
    if lax.axis_size(axis) != 2:
        return lax.all_gather(x, axis, axis=dim, tiled=False)
    here = lax.axis_index(axis)
    other = lax.ppermute(x, axis, [(0, 1), (1, 0)])
    low = jnp.where(here == 0, x, other)
    high = jnp.where(here == 0, other, x)
    return jnp.stack([low, high], axis=dim)


def scatter_blocks(x, axis, dim):
    if lax.axis_size(axis) != 2:
        n = x.shape[dim]
        out = lax.psum_scatter(x.astype(BF), axis, scatter_dimension=dim, tiled=True)
        return lax.squeeze(out, [dim]).astype(F32)
    here = lax.axis_index(axis)
    mine = lax.dynamic_index_in_dim(x, here, dim, keepdims=False)
    theirs = lax.dynamic_index_in_dim(x, 1 - here, dim, keepdims=False)
    got = lax.ppermute(theirs.astype(BF), axis, [(0, 1), (1, 0)])
    return mine.astype(F32) + got.astype(F32)


def fetch_weight(shard, parts):
    rows, cols = shard[0].shape[0], None
    pieces = [s.reshape(rows, parts, -1) for s in shard]
    joined = jnp.concatenate(pieces, axis=2) if len(pieces) > 1 else pieces[0]
    cols = joined.shape[2]
    x = jnp.transpose(joined, (1, 0, 2))
    x = lax.all_to_all(x, ("dc", "zl"), 0, 0, tiled=True)
    x = x.reshape(2, 2, rows, cols)
    x = gather_blocks(x, "zh", 1)
    x = gather_blocks(x, "dx", 0)
    return x.reshape(-1, cols)


def return_grad(grad, rows):
    cols = grad.shape[1]
    dxn, zhn = lax.axis_size("dx"), lax.axis_size("zh")
    g = grad.reshape(dxn, 2, zhn, 2, rows, cols)
    g = scatter_blocks(g, "dx", 0)
    g = scatter_blocks(g, "zh", 1)
    g = g.astype(BF).reshape(4, rows, cols)
    return lax.all_to_all(g, ("dc", "zl"), 0, 0, tiled=True)


class Tokens:
    def __init__(self):
        sizes = tuple(lax.axis_size(n) for n in AXES)
        self.core = swap_pairs(sizes, lambda a, b, c, d, e: (a, 1 - b, c, d, e))
        self.first = swap_pairs(
            sizes, lambda a, b, c, d, e: (a, b, c, d, 1 - e) if b == 0 else (a, b, c, 1 - d, e)
        )
        self.second = swap_pairs(
            sizes, lambda a, b, c, d, e: (a, b, c, 1 - d, e) if b == 0 else (a, b, c, d, 1 - e)
        )
        self.dc, self.zl, self.mp = (lax.axis_index(n) for n in ("dc", "zl", "mp"))

    def order(self, dc):
        mp, zl = self.mp, self.zl
        own = mp * 2 + zl
        by_mp = (1 - mp) * 2 + zl
        by_zl = mp * 2 + 1 - zl
        both = (1 - mp) * 2 + 1 - zl
        one = jnp.where(dc == 0, by_mp, by_zl)
        two = jnp.where(dc == 0, by_zl, by_mp)
        return own, one, two, both

    def gather(self, x):
        rows, width = x.shape
        one = lax.ppermute(x, AXES, self.first)
        two = lax.ppermute(jnp.stack([x, one]), AXES, self.second)
        far = [lax.ppermute(v, AXES, self.core) for v in (x, one, two)]
        out = jnp.zeros((8, rows, width), x.dtype)
        for dc, blocks in (
            (self.dc, (x, one, two[0], two[1])),
            (1 - self.dc, (far[0], far[1], far[2][0], far[2][1])),
        ):
            for at, block in zip(self.order(dc), blocks):
                out = lax.dynamic_update_index_in_dim(out, block, dc * 4 + at, 0)
        return out.reshape(8 * rows, width)

    def scatter(self, x):
        rows, width = x.shape[0] // 8, x.shape[1]
        x = x.reshape(2, 4, rows, width)
        theirs = lax.dynamic_index_in_dim(x, 1 - self.dc, 0, keepdims=False).astype(BF)
        mine = lax.dynamic_index_in_dim(x, self.dc, 0, keepdims=False)
        total = mine.astype(F32) + lax.ppermute(theirs, AXES, self.core).astype(F32)
        own, one, two, both = self.order(self.dc)
        pick = lambda at: lax.dynamic_index_in_dim(total, at, 0, keepdims=False)
        got = lax.ppermute(jnp.stack([pick(two), pick(both)]).astype(BF), AXES, self.second)
        keep_own = pick(own) + got[0].astype(F32)
        keep_one = pick(one) + got[1].astype(F32)
        got = lax.ppermute(keep_one.astype(BF), AXES, self.first)
        return keep_own + got.astype(F32)


MESH = pl.DeviceIdType.MESH
ANY = pl.BlockSpec(memory_space=pl.ANY)
VMEM = pl.BlockSpec(memory_space=pltpu.VMEM)


def flip(index, by):
    return 1 - index if by else index


class Place:
    def __init__(self):
        self.dx, self.dc, self.zh, self.zl, self.mp = (lax.axis_index(n) for n in AXES)

    def peer(self, dx=0, dc=0, zh=0, zl=0, mp=0):
        return (
            flip(self.dx, dx),
            flip(self.dc, dc),
            flip(self.zh, zh),
            flip(self.zl, zl),
            flip(self.mp, mp),
        )

    def block(self, dx=0, dc=0, zh=0, zl=0):
        a, b, c, d, _ = self.peer(dx, dc, zh, zl)
        return ((a * 2 + b) * 2 + c) * 2 + d

    def slot(self, dc=0, zl=0):
        return flip(self.dc, dc) * 2 + flip(self.zl, zl)

    def rows(self, dc=0, mp=0, zl=0):
        return (flip(self.dc, dc) * 2 + flip(self.mp, mp)) * 2 + flip(self.zl, zl)


def greet(peers):
    barrier = pltpu.get_barrier_semaphore()
    for device in peers:
        pl.semaphore_signal(barrier, inc=1, device_id=device, device_id_type=MESH)
    pl.semaphore_wait(barrier, len(peers))


class Links:
    def __init__(self, send, recv, local):
        self.send, self.recv, self.local = send, recv, local
        self.n, self.m = 0, 0
        self.sent, self.copies = [], []

    def pair(self):
        self.n += 1
        return self.n - 1

    def start(self, src, dst, at, device):
        copy = pltpu.make_async_remote_copy(
            src_ref=src,
            dst_ref=dst,
            send_sem=self.send.at[at],
            recv_sem=self.recv.at[at],
            device_id=device,
            device_id_type=MESH,
        )
        copy.start()
        self.sent.append(copy)

    def arrived(self, ref, at):
        pltpu.make_async_copy(ref, ref, self.recv.at[at]).wait()

    def keep(self, src, dst):
        copy = pltpu.make_async_copy(src, dst, self.local.at[self.m])
        self.m += 1
        copy.start()
        return copy

    def finish(self):
        for copy in self.sent:
            copy.wait_send()


FLIPS = [(zh, dc, zl) for zh in (1, 0) for dc in (0, 1) for zl in (0, 1)]


class WeightGather:
    def __init__(self, place, links, source, target, unit):
        self.place, self.links, self.target = place, links, target
        self.at = {f: links.pair() for f in FLIPS}
        self.cross = {(zh, dc): links.pair() for zh in (0, 1) for dc in (0, 1)}
        self.source = source
        self.kept = None

    def begin(self, zhs=(1, 0), dcs=(0, 1)):
        p = self.place
        mine = p.block()
        for f in FLIPS:
            zh, dc, zl = f
            if zh not in zhs or dc not in dcs:
                continue
            src, dst = self.source(p.slot(dc, zl)), self.target(mine, 1)
            if f == (0, 0, 0):
                self.kept = self.links.keep(src, dst)
            else:
                self.links.start(src, dst, self.at[f], p.peer(dc=dc, zh=zh, zl=zl))

    def onward(self, zh, dcs=(0, 1)):
        p = self.place
        for dc in dcs:
            for zl in (0, 1):
                if (zh, dc, zl) == (0, 0, 0):
                    self.kept.wait()
                else:
                    self.links.arrived(
                        self.target(p.block(dc=dc, zh=zh, zl=zl), 1), self.at[zh, dc, zl]
                    )
            two = self.target(p.block(dc=dc, zh=zh) // 2 * 2, 2)
            self.links.start(two, two, self.cross[zh, dc], p.peer(dx=1))

    def end(self):
        p = self.place
        for zh in (0, 1):
            for dc in (0, 1):
                two = self.target(p.block(dx=1, dc=dc, zh=zh) // 2 * 2, 2)
                self.links.arrived(two, self.cross[zh, dc])


def row_blocks(ref, unit, cols=None):
    def target(first, count):
        rows = pl.ds(pl.multiple_of(first * unit, unit), count * unit)
        return ref.at[rows] if cols is None else ref.at[rows, cols]

    return target


def column_blocks(ref, unit):
    return lambda first, count: ref.at[:, pl.ds(pl.multiple_of(first * unit, unit), count * unit)]


def first_kernel(
    weight_ref, source_ref, tok_ref, cot_ref, ig_ref, o_ref, gates_ref, small_ref, gate_ref,
    all_ref, wig_ref, wo_ref, wide_ref, ch_ref, gains_ref, dms_ref, dout_ref, own_ref, wg_ref,
    pieces, smalls, dm, send, recv, local,
):
    p = Place()
    links = Links(send, recv, local)
    drows = ig_ref.shape[1]
    crows = wo_ref.shape[0]
    greet(weight_peers(p))
    gather = TokenGatherTwice(p, links, tok_ref, all_ref)
    w_ig = WeightGather(p, links, lambda j: ig_ref.at[j], row_blocks(wig_ref, drows), drows)
    w_o = WeightGather(
        p,
        links,
        lambda j: o_ref.at[pl.ds(pl.multiple_of(j * crows, 16), crows)],
        column_blocks(wo_ref, o_ref.shape[1]),
        drows,
    )
    unit = gates_ref.shape[1]
    w_g = WeightGather(p, links, lambda j: gates_ref.at[j], row_blocks(pieces, unit), unit)
    w_s = WeightGather(p, links, lambda j: small_ref, row_blocks(smalls, 16), 16)
    w_gate = slot_columns(p, links, gate_ref, wg_ref)
    adjoint = TokenGatherTwice(p, links, dm, dms_ref)
    w_s.begin()
    w_ig.begin((1,))
    w_ig.begin((0,))
    w_g.begin((0,))
    w_o.begin((0,))
    gather.begin()
    own = links.keep(tok_ref.at[p.mp], own_ref)
    scales = [weight_ref[source_ref[m, 0]] for m in range(2)]
    for m in range(2):

        def scale(rows, m=m):
            value = cot_ref[m, rows, :].astype(F32) * scales[m]
            dm[m, rows, :] = value.astype(BF)

            @pl.when(p.mp == m)
            def _():
                dout_ref[rows, :] = value

        chunks(cot_ref.shape[1], scale, 1)
    w_ig.onward(0)
    w_s.onward(0)
    w_g.onward(0)
    w_o.onward(0)
    w_g.begin((1,))
    w_o.begin((1,))
    w_gate.begin((0,))
    w_s.onward(1)
    gather.forward()
    w_ig.onward(1)
    w_gate.begin((1,))
    adjoint.begin()
    gather.forward_core()
    w_gate.onward(0)
    w_g.onward(1)
    w_o.onward(1)
    adjoint.forward()
    w_gate.onward(1, (0,))
    adjoint.forward_core()
    w_s.end()
    count = small_channels(local_channels=crows)
    table = jnp.zeros((8, LANES), F32)
    for k in range(4):
        at = pl.ds(pl.multiple_of((p.slot() * 4 + k) * 16, 16), 16)
        rows = smalls[at, :].astype(F32)[:8]
        rows = jnp.concatenate([rows, jnp.zeros((8, LANES - 128), F32)], axis=1)
        table = table + (pltpu.roll(rows, k * count, 1) if k else rows)
    ch_ref[...] = table
    for k in range(16):
        rows = smalls[k * 16 : (k + 1) * 16, :].astype(F32)
        gains_ref[:, k * 128 : (k + 1) * 128] = rows[8:10]
    w_g.end()
    size = crows // 2
    per = size // 16
    total = jnp.zeros(wide_ref.shape, F32)
    row = lax.broadcasted_iota(jnp.int32, (LANES, pieces.shape[0]), 0)
    column = lax.broadcasted_iota(jnp.int32, (LANES, pieces.shape[0]), 1)
    source = lax.broadcasted_iota(jnp.int32, (LANES, 2 * LANES), 0)
    target = lax.broadcasted_iota(jnp.int32, (LANES, 2 * LANES), 1)
    for h in range(2):
        r = column % 32 - h * 16
        wanted = (r >= 0) & (r < per) & (row == h * size + column // 32 * per + r)
        rows = dot(jnp.where(wanted, 1.0, 0.0).astype(BF), pieces[...], NN, BF)
        gate = target // LANES
        wanted = (source == target - gate * LANES - h * size + gate * size) & (
            (source >= gate * size) & (source < (gate + 1) * size)
        )
        total = total + dot(rows, jnp.where(wanted, 1.0, 0.0).astype(BF), NN)
    wide_ref[...] = total.astype(BF)
    w_gate.onward(1, (1,))
    own.wait()
    gather.end()
    adjoint.end()
    w_gate.end()
    w_ig.end()
    w_o.end()
    links.finish()


def small_channels(local_channels):
    return local_channels // 4


class TokenGatherTwice:
    def __init__(self, place, links, source, target):
        self.place, self.links, self.source, self.target = place, links, source, target
        self.z, self.y = links.pair(), links.pair()
        self.core = {(mp, zl): links.pair() for mp in (0, 1) for zl in (0, 1)}

    def begin(self):
        p = self.place
        self.kept = []
        for mp in (0, 1):
            at = p.rows(mp=mp)
            src = self.source.at[flip(p.mp, mp)]
            if mp == 0:
                self.links.start(src, self.target.at[at], self.z, p.peer(zl=1))
            self.links.start(src, self.target.at[at], self.core[mp, 0], p.peer(dc=1))
            self.kept.append(self.links.keep(src, self.target.at[at]))

    def forward(self):
        p = self.place
        far = self.target.at[p.rows(zl=1)]
        self.links.arrived(far, self.z)
        self.links.start(far, far, self.y, p.peer(mp=1))
        self.links.start(far, far, self.core[0, 1], p.peer(dc=1))

    def forward_core(self):
        p = self.place
        far = self.target.at[p.rows(mp=1, zl=1)]
        self.links.arrived(far, self.y)
        self.links.start(far, far, self.core[1, 1], p.peer(dc=1))

    def end(self):
        p = self.place
        for (mp, zl), at in self.core.items():
            self.links.arrived(self.target.at[p.rows(dc=1, mp=mp, zl=zl)], at)
        for copy in self.kept:
            copy.wait()


class TokenGather:
    def __init__(self, place, links, source, target, span):
        self.place, self.links = place, links
        self.span = pl.ds(*span)
        self.source, self.target = source.at[self.span], target
        self.z, self.y0, self.y1 = links.pair(), links.pair(), links.pair()
        self.core = {(mp, zl): links.pair() for mp in (0, 1) for zl in (0, 1)}

    def block(self, **where):
        return self.target.at[self.place.rows(**where), self.span]

    def begin(self):
        p = self.place
        at = self.block()
        self.links.start(self.source, at, self.z, p.peer(zl=1))
        self.links.start(self.source, at, self.y0, p.peer(mp=1))
        self.links.start(self.source, at, self.core[0, 0], p.peer(dc=1))
        self.kept = self.links.keep(self.source, at)

    def forward(self):
        p = self.place
        far = self.block(zl=1)
        self.links.arrived(far, self.z)
        self.links.start(far, far, self.y1, p.peer(mp=1))
        self.links.start(far, far, self.core[0, 1], p.peer(dc=1))

    def forward_core(self):
        p = self.place
        far = self.block(mp=1)
        self.links.arrived(far, self.y0)
        self.links.start(far, far, self.core[1, 0], p.peer(dc=1))
        far = self.block(mp=1, zl=1)
        self.links.arrived(far, self.y1)
        self.links.start(far, far, self.core[1, 1], p.peer(dc=1))

    def end(self):
        for (mp, zl), at in self.core.items():
            self.links.arrived(self.block(dc=1, mp=mp, zl=zl), at)
        self.kept.wait()


CHUNK = 16


def chunks(count, body, most=11, first=0):
    n = count // CHUNK
    per = max(k for k in range(1, most + 1) if n % k == 0)

    def step(i, carry):
        for k in range(per):
            body(pl.ds(pl.multiple_of(first + (i * per + k) * CHUNK, CHUNK), CHUNK))
        return carry

    if n == per:
        step(0, 0)
    else:
        lax.fori_loop(0, n // per, step, 0)


def halves(rows):
    first = (rows // 2 + CHUNK - 1) // CHUNK * CHUNK
    return [(0, first), (first, rows - first)]


class RowScatter:
    def __init__(self, place, links, source, buffers, parts=None):
        self.place, self.links, self.source = place, links, source
        self.mine, self.from_core, self.from_y, self.from_z, self.out = buffers[:5]
        self.to_core = buffers[5] if len(buffers) > 5 else None
        self.parts = parts or [(0, self.mine.shape[1])]
        self.blocks = [(mp, zl) for mp in (1, 0) for zl in (1, 0)]
        self.kept = {}
        n = range(len(self.parts))
        self.core = {(h, block): links.pair() for h in n for block in self.blocks}
        self.y = {(h, zl): links.pair() for h in n for zl in (1, 0)}
        self.z = {h: links.pair() for h in n}

    def begin(self, mps=(1, 0)):
        p = self.place
        for mp, zl in self.blocks:
            if mp not in mps:
                continue
            i, block = mp * 2 + zl, p.rows(dc=1, mp=mp, zl=zl)
            if self.to_core is None:
                src = self.source.at[block]
            else:
                self.to_core[i] = self.source(block).astype(BF)
                src = self.to_core.at[i]
            for h, part in enumerate(self.parts):
                at = pl.ds(*part)
                self.links.start(
                    src.at[at], self.from_core.at[i, at], self.core[h, (mp, zl)], p.peer(dc=1)
                )
            block = p.rows(mp=mp, zl=zl)
            if self.to_core is None:
                self.kept[mp, zl] = self.links.keep(self.source.at[block], self.mine.at[i])
            else:
                self.mine[i] = self.source(block).astype(BF)

    def ready(self, mp, zl, h):
        i = mp * 2 + zl
        if h == 0 and self.kept:
            self.kept[mp, zl].wait()
        at = pl.ds(*self.parts[h])
        self.links.arrived(self.from_core.at[i, at], self.core[h, (mp, zl)])
        return i

    def across_y(self, h=0):
        p = self.place
        first, count = self.parts[h]
        at = pl.ds(first, count)
        for zl in (1, 0):
            i = self.ready(1, zl, h)

            def add(rows, i=i, zl=zl):
                total = self.mine[i, rows, :].astype(F32) + self.from_core[i, rows, :].astype(F32)
                self.out[zl, rows, :] = total.astype(BF)

            chunks(count, add, first=first)
            self.links.start(
                self.out.at[zl, at], self.from_y.at[zl, at], self.y[h, zl], p.peer(mp=1)
            )

    def across_z(self, h=0):
        p = self.place
        first, count = self.parts[h]
        at = pl.ds(first, count)
        i = self.ready(0, 1, h)
        self.links.arrived(self.from_y.at[1, at], self.y[h, 1])

        def add(rows):
            total = self.mine[i, rows, :].astype(F32) + self.from_core[i, rows, :].astype(F32)
            self.out[2, rows, :] = (total + self.from_y[1, rows, :].astype(F32)).astype(BF)

        chunks(count, add, first=first)
        self.links.start(self.out.at[2, at], self.from_z.at[at], self.z[h], p.peer(zl=1))

    def arrive(self, h=0):
        at = pl.ds(*self.parts[h])
        self.ready(0, 0, h)
        self.links.arrived(self.from_y.at[0, at], self.y[h, 0])
        self.links.arrived(self.from_z.at[at], self.z[h])

    def total(self, rows):
        a = self.mine[0, rows, :].astype(F32) + self.from_core[0, rows, :].astype(F32)
        b = self.from_y[0, rows, :].astype(F32) + self.from_z[rows, :].astype(F32)
        return a + b


def scatter_buffers(rows, width, products=False):
    return [
        pltpu.VMEM((4, rows, width), BF),
        pltpu.VMEM((4, rows, width), BF),
        pltpu.VMEM((2, rows, width), BF),
        pltpu.VMEM((rows, width), BF),
        pltpu.VMEM((3, rows, width), BF),
    ] + ([pltpu.VMEM((4, rows, width), BF)] if products else [])


def group_peers(p):
    return [p.peer(dc=1), p.peer(zl=1), p.peer(mp=1)]


def weight_peers(p):
    return [p.peer(dc=dc, zh=zh, zl=zl) for zh, dc, zl in FLIPS if (zh, dc, zl) != (0, 0, 0)] + [
        p.peer(dx=1),
        p.peer(mp=1),
    ]


def second_kernel(
    mixed_ref, wo_ref, own_ref, gain_ref, up_ref, down_ref,
    mid_ref, all_ref, wu_ref, wd_ref,
    *scratch,
):
    p = Place()
    links = Links(*scratch[-3:])
    normed = scratch[-4]
    rows, channels = own_ref.shape[0], wo_ref.shape[0]
    greet(weight_peers(p))

    def project(b):
        at = pl.ds(pl.multiple_of(b * rows, 16), rows)
        return dot(mixed_ref[at, :channels], wo_ref[...], NN)

    parts = halves(rows)
    scatter = RowScatter(p, links, project, scratch[:6], parts)
    w_u = slot_columns(p, links, up_ref, wu_ref)
    w_d = WeightGather(
        p,
        links,
        lambda j: down_ref.at[pl.ds(pl.multiple_of(j * wd_ref.shape[0], 16), wd_ref.shape[0])],
        column_blocks(wd_ref, down_ref.shape[1]),
        down_ref.shape[1],
    )
    gathers = [TokenGather(p, links, normed, all_ref, part) for part in parts]
    w_u.begin((1,))
    scatter.begin((1,))
    w_u.begin((0,))
    scatter.across_y(0)
    scatter.across_y(1)
    scatter.begin((0,))
    w_d.begin((0,))
    w_u.onward(0)

    def normalise(at):
        value = own_ref[at, :].astype(F32) + scatter.total(at)
        mid_ref[at, :] = value
        inv = lax.rsqrt(jnp.mean(value * value, axis=-1, keepdims=True) + EPSILON)
        normed[at, :] = (value * inv * gain_ref[...]).astype(BF)

    def middle(h):
        scatter.arrive(h)
        chunks(parts[h][1], normalise, first=parts[h][0])
        gathers[h].begin()

    scatter.across_z(0)
    w_d.onward(0)
    scatter.across_z(1)
    middle(0)
    w_d.begin((1,))
    middle(1)
    gathers[0].forward()
    w_u.onward(1)
    gathers[1].forward()
    gathers[0].forward_core()
    gathers[1].forward_core()
    w_d.onward(1)
    for gather in gathers:
        gather.end()
    w_u.end()
    w_d.end()
    links.finish()


def slot_columns(p, links, source, result):
    count = result.shape[1]
    return WeightGather(
        p,
        links,
        lambda j: source.at[:, pl.ds(pl.multiple_of(j * count, 128), count)],
        row_blocks(result, source.shape[0]),
        source.shape[0],
    )


class GradScatter:
    FAR = [(1, 0, 1), (1, 1, 1)], [(1, 0, 0), (1, 1, 0)]
    NEAR = [(0, 0, 1), (0, 1, 1)], [(0, 0, 0), (0, 1, 0)]
    ORDER = FAR[0] + NEAR[0] + FAR[1] + NEAR[1]
    EARLY = FAR[0] + FAR[1] + NEAR[0] + NEAR[1]

    def __init__(self, place, links, left, right, buffers, order=ORDER):
        self.order = order
        self.place, self.links, self.left, self.right = place, links, left, right
        self.to_x, self.from_x, self.to_z, self.from_z, self.sums, self.result = buffers[:6]
        self.columns = buffers[6] if len(buffers) > 6 else None
        self.rows = self.to_x.shape[1]
        self.x = {(zh, dc): links.pair() for zh in (1, 0) for dc in (0, 1)}
        self.z = {dc: links.pair() for dc in (0, 1)}
        self.at = {(dc, zl): links.pair() for dc in (0, 1) for zl in (0, 1)}
        self.count = 0
        self.load()

    def load(self):
        if self.count < 8 and self.columns is not None:
            dx, dc, zh = self.order[self.count]
            first = self.place.block(dx=dx, dc=dc, zh=zh) // 2
            columns = pl.ds(pl.multiple_of(first * self.rows, self.rows), self.rows)
            self.loading = self.links.keep(
                self.left.at[:, columns], self.columns.at[self.count % 2]
            )

    def product(self, dx=0, dc=0, zh=0):
        assert self.order[self.count] == (dx, dc, zh)
        self.loading.wait()
        self.count += 1
        self.load()
        return dot(self.columns[(self.count - 1) % 2], self.right[...], TN)

    def begin(self, zh):
        for dc in (0, 1):
            i = zh * 2 + dc
            self.to_x[i] = self.product(dx=1, dc=dc, zh=zh).astype(BF)
            self.links.start(
                self.to_x.at[i], self.from_x.at[i], self.x[zh, dc], self.place.peer(dx=1)
            )

    def across(self, dc):
        mine = self.product(dc=dc, zh=1)
        self.links.arrived(self.from_x.at[2 + dc], self.x[1, dc])
        self.to_z[dc] = (mine + self.from_x[2 + dc].astype(F32)).astype(BF)
        self.links.start(self.to_z.at[dc], self.from_z.at[dc], self.z[dc], self.place.peer(zh=1))

    def last(self, dc):
        p = self.place
        mine = self.product(dc=dc, zh=0)
        self.links.arrived(self.from_x.at[dc], self.x[0, dc])
        self.links.arrived(self.from_z.at[dc], self.z[dc])
        total = mine + self.from_x[dc].astype(F32) + self.from_z[dc].astype(F32)
        self.sums[dc] = total.astype(BF)
        unit = self.rows // 2
        for zl in (1, 0):
            src = self.sums.at[dc, pl.ds(pl.multiple_of(flip(p.zl, zl) * unit, unit), unit)]
            dst = self.result.at[p.slot()]
            if (dc, zl) == (0, 0):
                self.own = self.links.keep(src, dst)
            else:
                self.links.start(src, dst, self.at[dc, zl], p.peer(dc=dc, zl=zl))

    def end(self):
        p = self.place
        for (dc, zl), at in self.at.items():
            if (dc, zl) == (0, 0):
                self.own.wait()
            else:
                self.links.arrived(self.result.at[p.slot(dc, zl)], at)


class Ready(GradScatter):
    def product(self, dx=0, dc=0, zh=0):
        first = self.place.block(dx=dx, dc=dc, zh=zh) // 2
        return self.left[pl.ds(pl.multiple_of(first * self.rows, self.rows), self.rows), :].astype(
            F32
        )


def grad_buffers(rows, columns, tokens=None):
    return (
        [pltpu.VMEM((n, rows, columns), BF) for n in (4, 4, 2, 2, 2)]
        + [pltpu.VMEM((4, rows // 2, columns), BF)]
        + ([pltpu.VMEM((2, tokens, rows), BF)] if tokens else [])
    )


def norm_back(value, gain, upstream):
    inv = lax.rsqrt(jnp.mean(value * value, axis=-1, keepdims=True) + EPSILON)
    scaled = value * inv
    up = upstream * gain
    inner = jnp.mean(up * scaled, axis=-1, keepdims=True)
    return inv * (up - scaled * inner), upstream * scaled


def fold(rows):
    return rows[:8] + rows[8:]


def third_kernel(
    wg_ref, wu_ref, wd_in, mid_in, dout_in, gain_ref, dm_ref, hidden_ref, n2_ref, dgm_ref,
    dup_ref,
    dr1_ref, gain_out, all_ref, gate_out, down_out, part_out,
    *scratch,
):
    p = Place()
    links = Links(*scratch[-3:])
    do, wd_ref, mid_ref, dout_ref = scratch[-7:-3]
    rows_of = mid_ref.shape[0]
    staged = [
        links.keep(src, dst)
        for src, dst in ((mid_in, mid_ref), (dout_in, dout_ref), (wd_in, wd_ref))
    ]
    greet(weight_peers(p))

    def product(b):
        at = pl.ds(pl.multiple_of(b * rows_of, 16), rows_of)
        return dot(dgm_ref[at, :], wg_ref[...], NT) + dot(dup_ref[at, :], wu_ref[...], NT)

    parts = halves(rows_of)
    scatter = RowScatter(p, links, product, scratch[:6], parts)
    down = GradScatter(p, links, dm_ref, hidden_ref, scratch[6:13])
    gate = GradScatter(p, links, n2_ref, dgm_ref, scratch[13:20])
    gathers = [TokenGather(p, links, do, all_ref, part) for part in parts]
    scatter.begin((1,))
    down.begin(1)
    scatter.across_y(0)
    scatter.across_y(1)
    scatter.begin((0,))
    gate.begin(1)
    down.across(0)
    down.across(1)
    gain_out[...] = jnp.zeros_like(gain_out)
    for copy in staged:
        copy.wait()

    def back(rows):
        part, gain = norm_back(mid_ref[rows, :], gain_ref[...], scatter.total(rows))
        value = dout_ref[rows, :] + part
        dr1_ref[rows, :] = value
        do[rows, :] = value.astype(BF)
        gain_out[...] += fold(gain)

    def middle(h):
        scatter.arrive(h)
        chunks(parts[h][1], back, first=parts[h][0])
        gathers[h].begin()

    scatter.across_z(0)
    down.begin(0)
    gate.across(0)
    scatter.across_z(1)
    middle(0)
    gate.across(1)
    gate.begin(0)
    middle(1)
    gathers[0].forward()
    gathers[1].forward()
    out = scratch[0]
    writes = []
    for b in range(8):
        if b >= 4:
            writes[b - 4].wait()
        at = pl.ds(b * rows_of, rows_of)
        out[b % 4] = dot(hidden_ref[at, :], wd_ref[...], NN, BF)
        writes.append(links.keep(out.at[b % 4], part_out.at[b]))
    down.last(0)
    down.last(1)
    gathers[0].forward_core()
    gate.last(0)
    gathers[1].forward_core()
    gate.last(1)
    for gather in gathers:
        gather.end()
    down.end()
    ff = down.result.shape[2]
    for j in range(4):
        down_out[j * ff : (j + 1) * ff, :] = down.result[j].astype(F32).T
    gate.end()
    for j in range(4):
        gate_out[:, j * ff : (j + 1) * ff] = gate.result[j].astype(F32)
    for write in writes[4:]:
        write.wait()
    links.finish()


def fourth_kernel(
    wig_ref, own_ref, dr1_ref, gain_ref, do_ref, mixed_ref, n1_ref, dboth_ref, gg_ref,
    dx_ref, gain_out, in_out, gelu_out, out_out, gates_out,
    *scratch,
):
    p = Place()
    links = Links(*scratch[-3:])
    dx_send, dx_recv = scratch[-5:-3]
    greet(weight_peers(p))
    rows_of = own_ref.shape[0]

    def product(b):
        at = pl.ds(pl.multiple_of(b * rows_of, 16), rows_of)
        return dot(dboth_ref[at, :], wig_ref[...], NT)

    parts = halves(rows_of)
    scatter = RowScatter(p, links, product, scratch[:6], parts)
    out = GradScatter(p, links, do_ref, mixed_ref, scratch[6:13])
    wide = GradScatter(p, links, n1_ref, dboth_ref, scratch[13:20])
    gates = Ready(p, links, gg_ref, None, scratch[20:26])
    scatter.begin((1,))
    out.begin(1)
    scatter.across_y(0)
    scatter.across_y(1)
    wide.begin(1)
    scatter.begin((0,))
    gates.begin(1)
    for g in (out, wide, gates):
        g.across(0)
        g.across(1)
        g.begin(0)
    gain_out[...] = jnp.zeros_like(gain_out)

    def back(rows):
        value = own_ref[rows, :].astype(F32)
        part, gain = norm_back(value, gain_ref[...], scatter.total(rows))
        total = dr1_ref[rows, :] + part
        dx_ref[p.mp, rows, :] = total
        dx_send[rows, :] = total.astype(BF)
        gain_out[...] += fold(gain)

    sent = []

    def middle(h):
        scatter.arrive(h)
        chunks(parts[h][1], back, first=parts[h][0])
        span, at = pl.ds(*parts[h]), links.pair()
        links.start(dx_send.at[span], dx_recv.at[span], at, p.peer(mp=1))
        sent.append((span, at))

    scatter.across_z(0)
    scatter.across_z(1)
    middle(0)
    for g in (out, gates):
        g.last(0)
        g.last(1)
    middle(1)
    wide.last(0)
    wide.last(1)
    local = out.result.shape[2]
    out.end()
    for j in range(4):
        out_out[j * out_out.shape[0] // 4 : (j + 1) * out_out.shape[0] // 4, :] = (
            out.result[j].astype(F32).T[: out_out.shape[0] // 4]
        )
    gates.end()
    gates_out[...] = gates.result[...]
    wide.end()
    two = wide.result.shape[2]
    left = lax.broadcasted_iota(jnp.int32, (1, two), 1) < two // 2
    for j in (0, 2):
        a, b = (wide.result[j + i].astype(F32) for i in (0, 1))
        span = slice(j * two // 2, (j + 2) * two // 2)
        in_out[:, span] = jnp.where(left, a, pltpu.roll(b, two // 2, 1))
        gelu_out[:, span] = jnp.where(left, pltpu.roll(a, two // 2, 1), b)
    for span, at in sent:
        links.arrived(dx_recv.at[span], at)
    dx_ref[1 - p.mp] = dx_recv[...].astype(F32)
    links.finish()


def mlp_kernel(
    n2_ref, dm_ref, wg_ref, wu_ref, wd_ref, hidden_ref, dgm_ref, dup_ref, pre, upp, dhm
):
    count, rows, width = n2_ref.shape
    n2 = n2_ref[...].reshape(count * rows, width)
    pre[...] = dot(n2, wg_ref[...], NN)
    upp[...] = dot(n2, wu_ref[...], NN)
    dhm[...] = dot(dm_ref[...].reshape(count * rows, width), wd_ref[...], NT)

    def body(at):
        up, d = upp[at, :], dhm[at, :]
        value, slope = gelu_both(pre[at, :])
        hidden_ref[at, :] = (value * up).astype(BF)
        dgm_ref[at, :] = (d * up * slope).astype(BF)
        dup_ref[at, :] = (d * value).astype(BF)

    chunks(count * rows, body)


def feed_forward(n2, dm, w_g, w_u, w_d):
    blocks, rows, width = n2.shape
    ff = w_d.shape[0]
    if not shape_fits():
        n2, dm = n2.reshape(-1, width), dm.reshape(-1, width)
        pre, d = dot(n2, w_g, NN), dot(dm, w_d, NT)
        gm, up = pre, dot(n2, w_u, NN)
        value, slope = gelu_both(gm)
        return (value * up).astype(BF), (d * up * slope).astype(BF), (d * value).astype(BF)
    two = pl.BlockSpec((2, rows, width), lambda i: (i, 0, 0))
    flat = pl.BlockSpec((2 * rows, ff), lambda i: (i, 0))
    whole = lambda v: pl.BlockSpec(v.shape, lambda i: (0, 0))
    total = blocks * rows
    return pl.pallas_call(
        mlp_kernel,
        name="feed_forward",
        grid=(blocks // 2,),
        in_specs=[two, two, whole(w_g), whole(w_u), whole(w_d)],
        out_specs=[flat] * 3,
        out_shape=[jax.ShapeDtypeStruct((total, ff), BF)] * 3,
        scratch_shapes=[pltpu.VMEM((2 * rows, ff), F32)] * 3,
        compiler_params=pltpu.CompilerParams(vmem_limit_bytes=48 * 1024 * 1024),
        cost_estimate=pl.CostEstimate(
            flops=2 * total * width * ff * 3, bytes_accessed=total * width * 4, transcendentals=0
        ),
    )(n2, dm, w_g, w_u, w_d)


def semaphores(pairs, local):
    return [
        pltpu.SemaphoreType.DMA((pairs,)),
        pltpu.SemaphoreType.DMA((pairs,)),
        pltpu.SemaphoreType.DMA((local,)),
    ]


def run_kernel(body, name, outs, out_specs, in_specs, scratch, ident, args, mib=40):
    return pl.pallas_call(
        body,
        name=name,
        out_shape=[jax.ShapeDtypeStruct(*o) for o in outs],
        in_specs=in_specs,
        out_specs=out_specs,
        scratch_shapes=scratch,
        compiler_params=pltpu.CompilerParams(
            collective_id=ident, has_side_effects=True, vmem_limit_bytes=mib * 1024 * 1024
        ),
    )(*args)


def fetch_first(
    tokens, cotangent, seq_source, source_weight, input_weight, gelu_weight, output_weight,
    decay_gates, input_gates, channel_params, norm_gains, mlp_gate,
):
    args = (
        tokens, cotangent, seq_source, source_weight, input_weight, gelu_weight, output_weight,
        decay_gates, input_gates, channel_params, norm_gains, mlp_gate,
    )
    if not shape_fits():
        return plain_fetch_first(*args)
    rows, width = tokens.shape[1:]
    drows, local = input_weight.shape[0], input_weight.shape[1] // 4
    pairs = [v.reshape(drows, 4, local) for v in (input_weight, gelu_weight)]
    ig = jnp.concatenate(pairs, axis=2).transpose(1, 0, 2)
    per = decay_gates.shape[1] // BLOCK
    gates = [v.reshape(8, per, BLOCK) for v in (decay_gates, input_gates)]
    gates = jnp.concatenate(gates, axis=2)
    gates = jnp.pad(gates, ((0, 0), (0, 16 - per), (0, LANES - 2 * BLOCK))).reshape(4, 32, LANES)
    small = jnp.pad(channel_params[:, 0], ((0, 0), (0, drows - channel_params.shape[2])))
    small = jnp.pad(jnp.concatenate([small, norm_gains], axis=0), ((0, 6), (0, 0)))
    smem = pl.BlockSpec(memory_space=pltpu.SMEM)
    return run_kernel(
        first_kernel,
        "fetch_first",
        [
            ((8, rows, width), BF),
            ((width, 2 * local), BF),
            ((local, width), BF),
            ((LANES, 2 * LANES), BF),
            ((8, LANES), F32),
            ((2, width), F32),
            ((8, rows, width), BF),
            ((rows, width), F32),
            ((rows, width), BF),
            ((width, mlp_gate.shape[1] // 4), BF),
        ],
        [ANY] * 3 + [VMEM] * 3 + [ANY, VMEM, ANY, ANY],
        [smem, smem, ANY, VMEM] + [ANY] * 5,
        [
            pltpu.VMEM((512, LANES), BF),
            pltpu.VMEM((256, 128), BF),
            pltpu.VMEM((2, rows, width), BF),
        ]
        + semaphores(80, 16),
        1,
        (source_weight, seq_source, tokens, cotangent, ig, output_weight, gates, small, mlp_gate),
        61,
    )


def reduce_and_fetch(mixed, w_o, own, gain, mlp_up, mlp_down):
    if not shape_fits():
        return plain_reduce_and_fetch(mixed, w_o, own, gain, mlp_up, mlp_down)
    rows, width = own.shape
    ff = mlp_up.shape[1] // 4
    return run_kernel(
        second_kernel,
        "reduce_and_fetch",
        [((rows, width), F32), ((8, rows, width), BF), ((width, ff), BF), ((ff, width), BF)],
        [VMEM] + [ANY] * 3,
        [VMEM] * 4 + [ANY] * 2,
        scatter_buffers(rows, width, True) + [pltpu.VMEM((rows, width), BF)] + semaphores(64, 16),
        2,
        (mixed, w_o, own, gain, mlp_up, mlp_down),
    )


def reduce_and_return(weights, middle, dout, gain, dm, hidden, n2, dgm, dup, drows):
    if not shape_fits():
        return plain_reduce_and_return(
            weights, middle, dout, gain, dm, hidden, n2, dgm, dup, drows
        )
    rows, width = middle.shape
    ff = hidden.shape[1]
    return run_kernel(
        third_kernel,
        "reduce_and_return",
        [
            ((rows, width), F32),
            ((8, width), F32),
            ((8, rows, width), BF),
            ((drows, 4 * ff), F32),
            ((4 * ff, drows), F32),
            ((8, rows, width), BF),
        ],
        [VMEM, VMEM, ANY] + [VMEM] * 2 + [ANY],
        [VMEM] * 2 + [ANY] * 3 + [VMEM] + [ANY, VMEM] * 2 + [VMEM],
        scatter_buffers(rows, width, True)
        + grad_buffers(2 * drows, ff, 8 * rows) * 2
        + [pltpu.VMEM((rows, width), BF), pltpu.VMEM((ff, width), BF)]
        + [pltpu.VMEM((rows, width), F32)] * 2
        + semaphores(56, 56),
        3,
        (*weights, middle, dout, gain, dm, hidden, n2, dgm, dup),
        61,
    )


def return_last(w_ig, own, dr1, gain, do, mixed, n1, dboth, g_gates, drows):
    if not shape_fits():
        return plain_return_last(w_ig, own, dr1, gain, do, mixed, n1, dboth, g_gates, drows)
    rows, width = own.shape
    local, unit = dboth.shape[1] // 2, g_gates.shape[0] // 16
    return run_kernel(
        fourth_kernel,
        "return_last",
        [
            ((2, rows, width), F32),
            ((8, width), F32),
            ((drows, 4 * local), F32),
            ((drows, 4 * local), F32),
            ((4 * local, drows), F32),
            ((4, unit, 128), BF),
        ],
        [VMEM] * 6,
        [VMEM] * 4 + [ANY, VMEM] * 2 + [VMEM],
        scatter_buffers(rows, width, True)
        + grad_buffers(2 * drows, mixed.shape[1], 8 * rows)
        + grad_buffers(2 * drows, 2 * local, 8 * rows)
        + grad_buffers(2 * unit, 128)
        + [pltpu.VMEM((rows, width), BF)] * 2
        + semaphores(64, 48),
        4,
        (w_ig, own, dr1, gain, do, mixed, n1, dboth, g_gates),
        60,
    )


def shape_fits():
    return all(lax.axis_size(n) == 2 for n in AXES)


def plain_fetch_first(
    tokens, cotangent, seq_source, source_weight, input_weight, gelu_weight, output_weight,
    decay_gates, input_gates, channel_params, norm_gains, mlp_gate,
):
    exchange = Tokens()
    dxn, zhn, mp = lax.axis_size("dx"), lax.axis_size("zh"), exchange.mp
    group = dxn * 2 * zhn * 2
    local = input_weight.shape[1] // 4
    heads, piece = decay_gates.shape[0] // 4, decay_gates.shape[1]
    shards = ("dx", "dc", "zh", "zl")
    own = lax.dynamic_index_in_dim(tokens, mp, 0, keepdims=False)
    sources = jnp.arange(source_weight.shape[0], dtype=jnp.int32)
    scales = jnp.sum(jnp.where(seq_source == sources[None], source_weight[None], 0.0), axis=1)
    douts = cotangent.astype(F32) * scales[:, None, None]
    small = jnp.concatenate([channel_params.reshape(-1), norm_gains.reshape(-1)])
    small = lax.all_to_all(
        jnp.broadcast_to(small[None], (group, small.size)), shards, 0, 0, tiled=True
    )
    nch = channel_params.size
    channels = small[:, :nch].reshape(group, 8, -1).transpose(1, 0, 2).reshape(8, -1)
    slot = exchange.dc * 2 + exchange.zl
    channels = lax.dynamic_slice_in_dim(channels, slot * local, local, 1).astype(F32)
    gains = small[:, nch:].reshape(group, 2, -1).transpose(1, 0, 2).reshape(2, -1).astype(F32)
    gates = jnp.stack([decay_gates, input_gates]).reshape(2, 4, heads, piece)
    gates = gates.transpose(1, 0, 2, 3).reshape(2, 1, 2, 1, 2 * heads * piece)
    gates = jnp.broadcast_to(gates, (2, zhn, 2, dxn, 2 * heads * piece))
    gates = gates.transpose(3, 0, 1, 2, 4).reshape(group, 2 * heads * piece)
    gates = lax.all_to_all(gates, shards, 0, 0, tiled=True)
    gates = gates.reshape(group, 2 * heads, piece).transpose(1, 0, 2)
    gates = gates.reshape(2, heads, BLOCK, BLOCK)
    zero = jnp.zeros((BLOCK, BLOCK), BF)
    blocks = [
        [gates[g, h] if k == h else zero for g in range(2) for k in range(heads)]
        for h in range(heads)
    ]
    return (
        exchange.gather(own).reshape((8,) + own.shape),
        fetch_weight([input_weight, gelu_weight], 4),
        fetch_weight([output_weight.T], 4).T,
        jnp.concatenate([jnp.concatenate(v, axis=1) for v in blocks], axis=0),
        channels,
        gains,
        exchange.gather(lax.dynamic_index_in_dim(douts, mp, 0, keepdims=False).astype(BF)).reshape(
            (8,) + own.shape
        ),
        lax.dynamic_index_in_dim(douts, mp, 0, keepdims=False),
        own,
        fetch_weight([mlp_gate], 4),
    )


def plain_reduce_and_fetch(mixed, w_o, own, gain, mlp_up, mlp_down):
    exchange = Tokens()
    middle = own.astype(F32) + exchange.scatter(dot(mixed, w_o, NN, BF))
    normed = (middle * inverse_rms(middle) * gain).astype(BF)
    return (
        middle,
        exchange.gather(normed).reshape((8,) + own.shape),
        fetch_weight([mlp_up], 4),
        fetch_weight([mlp_down.T], 4).T,
    )


def columns(share, at, count):
    return share[:, :, at : at + count].astype(F32).transpose(1, 0, 2).reshape(-1, 4 * count)


def both_batches(rows):
    mp = lax.axis_index("mp")
    other = lax.ppermute(rows, "mp", [(0, 1), (1, 0)])
    return jnp.stack([jnp.where(mp == 0, rows, other), jnp.where(mp == 0, other, rows)])


def plain_reduce_and_return(weights, middle, dout, gain, dm, hidden, n2, dgm, dup, drows):
    exchange = Tokens()
    w_g, w_u, w_d = weights
    ff = hidden.shape[1]
    total = exchange.scatter((dot(dgm, w_g, NT) + dot(dup, w_u, NT)).astype(BF))
    change, gain_rows = norm_back(middle, gain, total)
    dr1 = dout + change
    gate = return_grad(dot(n2, dgm, TN, BF), drows)
    down = return_grad(dot(dm, hidden, TN, BF), drows)
    return (
        dr1,
        jnp.sum(gain_rows, axis=0, keepdims=True),
        exchange.gather(dr1.astype(BF)).reshape((8,) + dr1.shape),
        columns(gate, 0, ff),
        columns(down, 0, ff).T,
        dot(hidden, w_d, NN, BF).reshape((8,) + dr1.shape),
    )


def plain_return_last(w_ig, own, dr1, gain, do, mixed, n1, dboth, g_gates, drows):
    exchange = Tokens()
    local = dboth.shape[1] // 2
    total = exchange.scatter(dot(dboth, w_ig, NT, BF))
    change, gain_rows = norm_back(own.astype(F32), gain, total)
    group = n1.shape[1] // drows
    wide = return_grad(dot(n1, dboth, TN, BF), drows)
    out = return_grad(dot(do, mixed, TN, BF), drows)
    return (
        both_batches(dr1 + change),
        jnp.sum(gain_rows, axis=0, keepdims=True),
        columns(wide, 0, local),
        columns(wide, local, local),
        columns(out, 0, local).T,
        return_grad(g_gates, g_gates.shape[0] // group),
    )


def scan_body(reverse, a_ref, b_ref, p_ref, h_ref):
    length, width = a_ref.shape[1], a_ref.shape[2]
    row = lax.broadcasted_iota(jnp.int32, (8, width), 0)

    def tile(i, carry):
        ca, ch = carry
        at = (length // 8 - 1 - i if reverse else i) * 8
        at = pl.multiple_of(at, 8)
        a = a_ref[0, pl.ds(at, 8), :]
        b = b_ref[0, pl.ds(at, 8), :]
        for step in (1, 2, 4):
            if reverse:
                inside = row < 8 - step
                shift = 8 - step
            else:
                inside = row >= step
                shift = step
            sa = jnp.where(inside, pltpu.roll(a, shift, 0), 1.0)
            sb = jnp.where(inside, pltpu.roll(b, shift, 0), 0.0)
            b = b + a * sb
            a = a * sa
        h = b + a * ch
        p = a * ca
        h_ref[0, pl.ds(at, 8), :] = h
        p_ref[0, pl.ds(at, 8), :] = p
        last = 0 if reverse else 7
        return p[last : last + 1, :], h[last : last + 1, :]

    lax.fori_loop(
        0,
        length // 8,
        tile,
        (jnp.ones((1, width), F32), jnp.zeros((1, width), F32)),
    )


def local_scan(a, b, reverse):
    segs, length, width = a.shape
    spec = pl.BlockSpec((1, length, width), lambda s: (s, 0, 0))
    return pl.pallas_call(
        lambda *refs: scan_body(reverse, *refs),
        grid=(segs,),
        in_specs=[spec, spec],
        out_specs=[spec, spec],
        out_shape=[jax.ShapeDtypeStruct(a.shape, F32)] * 2,
        cost_estimate=pl.CostEstimate(
            flops=20 * a.size, bytes_accessed=16 * a.size, transcendentals=0
        ),
    )(a, b)


def carried(product, state, reverse):
    count = lax.axis_size("zh")
    if count == 2:
        return lax.ppermute(state, "zh", [(1, 0)] if reverse else [(0, 1)])
    here = lax.axis_index("zh")
    pairs = lax.all_gather(jnp.stack([product, state]), "zh")
    total = jnp.zeros_like(state)
    for k in range(count):
        at = count - 1 - k if reverse else k
        reached = at > here if reverse else at < here
        total = jnp.where(reached, pairs[at, 1] + pairs[at, 0] * total, total)
    return total


def from_behind(x, by):
    count = lax.axis_size("zh")
    return lax.ppermute(
        x, "zh", [(i, i + by) for i in range(count) if 0 <= i + by < count]
    )


def inverse_rms(values):
    return lax.rsqrt(jnp.mean(values * values, axis=-1, keepdims=True) + EPSILON)


def gelu(v):
    return jax.nn.gelu(v, approximate=True)


def gelu_both(v):
    c = 0.7978845608028654
    t = jnp.tanh(c * (v + 0.044715 * v * v * v))
    value = 0.5 * v * (1.0 + t)
    slope = 0.5 * (1.0 + t) + 0.5 * v * (1.0 - t * t) * c * (1.0 + 3 * 0.044715 * v * v)
    return value, slope


def dot(a, b, dims, out=F32):
    r = lax.dot_general(a, b, (dims, ((), ())), preferred_element_type=F32)
    return r.astype(out)


NN = ((1,), (0,))
NT = ((1,), (1,))
TN = ((0,), (0,))


def minus_expm1(v):
    series = 1.0 + v / 8.0
    for k in (7.0, 6.0, 5.0, 4.0, 3.0, 2.0):
        series = 1.0 + v * (1.0 / k) * series
    return jnp.where(v > -0.4, -v * series, 1.0 - jnp.exp(v))


def loop(count, body, unroll=1):
    def step(i, carry):
        body(i)
        return carry

    lax.fori_loop(0, count, step, 0, unroll=unroll)


def tile_scan(a, b, row, reverse):
    for step in (1, 2, 4):
        inside = row < 8 - step if reverse else row >= step
        shift = 8 - step if reverse else step
        sa = jnp.where(inside, pltpu.roll(a, shift, 0), 1.0)
        sb = jnp.where(inside, pltpu.roll(b, shift, 0), 0.0)
        b = b + a * sb
        a = a * sa
    return a, b


def eight(i):
    return pl.multiple_of(i * 8, 8)


def recur_forward_kernel(
    tok_ref, wig_ref, blocks_ref, ch_ref, gain_ref,
    n1_out, xs_out, gy_out, u_out, siga_out, sigi_out, decay_out, states, mixed,
    xs, gy, u, siga, sigi, decay, run, logits, n1, both, halo, ends, inc, tok, sems,
    send, recv, local_sems,
):
    p = Place()
    links = Links(send, recv, local_sems)
    rows, local = tok_ref.shape[1], wig_ref.shape[1] // 2
    zh = p.zh
    greet([p.peer(zh=1)])

    def read(b):
        return pltpu.make_async_copy(tok_ref.at[b], tok.at[b % 2], sems.at[4 + b % 2])

    read(0).start()
    lane = lax.broadcasted_iota(jnp.int32, (1, LANES), 1)
    real = lane < local

    def project(b):
        read(b).wait()

        @pl.when(b < 7)
        def _():
            read(b + 1).start()

        def normalise(at):
            value = tok[b % 2, at, :].astype(F32)
            inv = lax.rsqrt(jnp.mean(value * value, axis=-1, keepdims=True) + EPSILON)
            n1[b % 2, at, :] = (value * inv * gain_ref[...]).astype(BF)

        def write(i, at):
            return pltpu.make_async_copy(n1.at[i], n1_out.at[at], sems.at[i])

        @pl.when(b >= 2)
        def _():
            write(b % 2, b - 2).wait()

        chunks(rows, normalise)
        write(b % 2, b).start()
        both[...] = dot(n1[b % 2], wig_ref[...], NN)
        seg, zl = b // 2, b % 2

        def split(at):
            v = both[at, :]
            xb = jnp.where(real, v[:, :LANES], 0.0).astype(BF).astype(F32)
            xs[seg, pl.ds(pl.multiple_of(8 + zl * rows + at.start, 8), CHUNK), :] = xb
            rest = pltpu.roll(v, v.shape[1] - local, 1)[:, :LANES]
            gy[b, at, :] = jnp.where(real, rest, 0.0)

        chunks(rows, split)

    loop(8, project)
    for b in (6, 7):
        pltpu.make_async_copy(n1.at[b % 2], n1_out.at[b], sems.at[b % 2]).wait()

    def to_partner(src, dst):
        at = links.pair()
        links.start(src, dst, at, p.peer(zh=1))
        return at

    at = to_partner(xs.at[:, pl.ds(2 * rows, 8)], halo)
    kept = [links.keep(gy, gy_out)]
    links.arrived(halo, at)
    row = lax.broadcasted_iota(jnp.int32, (8, LANES), 0)
    soft = ch_ref[0:1, :]

    def head(seg):
        xs[seg, 0:8, :] = jnp.where(zh == 1, halo[seg], 0.0)

    loop(4, head)

    def convolve(b):
        seg, zl = b // 2, b % 2

        def body(at):
            v = xs[seg, pl.ds(pl.multiple_of(zl * rows + at.start, 8), CHUNK + 8), :]
            total = ch_ref[3:4, :] + ch_ref[4:5, :] * v[8:]
            for k in (1, 2, 3):
                total = total + ch_ref[4 + k : 5 + k, :] * pltpu.roll(v, k, 0)[8:]
            u[b, at, :] = total.astype(BF)

        chunks(rows, body)
        logits[b] = dot(u[b], blocks_ref[...], NN)

    loop(8, convolve)

    def tile(i, carry, zl):
        at = pl.ds(pl.multiple_of(i * CHUNK, CHUNK), CHUNK)
        out = []
        for seg in range(4):
            b = seg * 2 + zl
            cp, ch = carry[seg]
            sa = jax.nn.sigmoid(logits[b, at, :LANES] + ch_ref[1:2, :])
            si = jax.nn.sigmoid(logits[b, at, LANES:] + ch_ref[2:3, :])
            log_decay = -DECAY_SCALE * sa * soft
            a = jnp.exp(log_decay)
            drive = jnp.sqrt(minus_expm1(2.0 * log_decay)) * si * u[b, at, :].astype(F32)
            siga[b, at, :] = sa
            sigi[b, at, :] = si
            decay[b, at, :] = a
            for k in range(2):
                pa, h = tile_scan(a[k * 8 : k * 8 + 8], drive[k * 8 : k * 8 + 8], row, False)
                h = h + pa * ch
                pa = pa * cp
                run[b, pl.ds(eight(i * 2 + k), 8), :] = pa
                there = pl.ds(pl.multiple_of(8 + zl * rows + i * CHUNK + k * 8, 8), 8)
                states[seg, there, :] = h
                cp, ch = pa[7:8, :], h[7:8, :]
            out.append((cp, ch))
        return tuple(out)

    kept += [links.keep(xs, xs_out), links.keep(u, u_out)]
    carry = ((jnp.ones((1, LANES), F32), jnp.zeros((1, LANES), F32)),) * 4
    for zl in range(2):
        carry = lax.fori_loop(0, rows // CHUNK, functools.partial(tile, zl=zl), carry)
    ends[...] = jnp.zeros_like(ends)
    for seg in range(4):
        ends[seg : seg + 1, :] = carry[seg][1]
    at = to_partner(ends, inc)
    kept += [links.keep(siga, siga_out), links.keep(sigi, sigi_out), links.keep(decay, decay_out)]
    links.arrived(inc, at)

    def finish(b):
        seg, zl = b // 2, b % 2
        start = jnp.where(zh == 1, inc[pl.ds(seg, 1), :], 0.0)

        @pl.when(zl == 0)
        def _():
            states[seg, 0:8, :] = jnp.broadcast_to(start, (8, LANES))

        def state(at):
            there = pl.ds(pl.multiple_of(8 + zl * rows + at.start, 8), CHUNK)
            h = states[seg, there, :] + run[b, at, :] * start
            states[seg, there, :] = h
            v = gy[b, at, :]
            t = jnp.tanh(0.7978845608028654 * (v + 0.044715 * v * v * v))
            mixed[b, at, :] = (0.5 * v * (1.0 + t) * h).astype(BF)

        chunks(rows, state)

    loop(8, finish)
    for copy in kept:
        copy.wait()
    links.finish()


def recur_backward_kernel(
    do_ref, wo_ref, blocks_ref, ch_ref,
    xs_in, gy, u_in, siga_in, sigi_in, decay_in, states, rows_ref, mid_in, n2_ref, dup_ref,
    dboth_out, gb_out, ch_out, block_out, up_out,
    xs, u, siga, sigi, decay, mid_ref,
    dh, after, dgy, dlog_ref, du, dboth, halo, ends, inc, do, final, sems,
    *scratch,
):
    p = Place()
    links = Links(*scratch[-3:])
    rows, local = do_ref.shape[1], wo_ref.shape[0]
    zh = p.zh
    greet(weight_peers(p))
    scatter = RowScatter(p, links, rows_ref, scratch[:5])
    up = GradScatter(p, links, n2_ref, dup_ref, scratch[5:12], GradScatter.EARLY)

    def read(b):
        return pltpu.make_async_copy(do_ref.at[b], do.at[b % 2], sems.at[4 + b % 2])

    read(0).start()
    kept = {
        name: links.keep(src, dst)
        for name, src, dst in (
            ("decay", decay_in, decay),
            ("siga", siga_in, siga),
            ("sigi", sigi_in, sigi),
            ("u", u_in, u),
            ("xs", xs_in, xs),
            ("mid", mid_in, mid_ref),
        )
    }
    up.begin(1)
    scatter.begin()
    ch_out[...] = jnp.zeros_like(ch_out)
    gb_out[...] = jnp.zeros_like(gb_out)
    soft = ch_ref[0:1, :]

    def to_partner(src, dst):
        at = links.pair()
        links.start(src, dst, at, p.peer(zh=1))
        return at

    def upstream(b):
        seg, zl = b // 2, b % 2
        dh[b, :, local:] = jnp.zeros((rows, LANES - local), F32)
        read(b).wait()

        @pl.when(b < 7)
        def _():
            read(b + 1).start()

        dh[b, :, :local] = dot(do[b % 2], wo_ref[...], NT)

        def split(at):
            value, slope = gelu_both(gy[b, at, :])
            dz = dh[b, at, :]
            h = states[seg, pl.ds(pl.multiple_of(8 + zl * rows + at.start, 8), CHUNK), :]
            dh[b, at, :] = dz * value
            dgy[b, at, :] = (dz * h * slope).astype(BF)

        chunks(rows, split)

    loop(8, upstream)
    scatter.across_y()
    up.begin(0)
    row = lax.broadcasted_iota(jnp.int32, (8, LANES), 0)
    one = jnp.ones((1, LANES), F32)
    ends[...] = jnp.zeros_like(ends)

    def tile(i, carry, zl):
        at = pl.ds(eight(rows // 8 - 1 - i), 8)
        out = []
        for seg in range(4):
            b = seg * 2 + zl
            cp, cg, following = carry[seg]
            a = decay[b, at, :]
            shifted = jnp.where(row == 7, following, pltpu.roll(a, 7, 0))
            pa, g = tile_scan(shifted, dh[b, at, :], row, True)
            g = g + pa * cg
            pa = pa * cp
            dh[b, at, :] = g
            after[b, at, :] = pa
            out.append((pa[0:1, :], g[0:1, :], a[0:1, :]))
        return tuple(out)

    carry = ((one, jnp.zeros((1, LANES), F32), one),) * 4
    kept["decay"].wait()
    for zl in (1, 0):
        carry = lax.fori_loop(0, rows // 8, functools.partial(tile, zl=zl), carry)
    for seg in range(4):
        ends[seg : seg + 1, :] = carry[seg][1] * carry[seg][2]
    at = to_partner(ends, inc)
    links.arrived(inc, at)
    up.across(0)

    def gradients(b):
        seg, zl = b // 2, b % 2
        later = jnp.where(zh == 0, inc[pl.ds(seg, 1), :], 0.0)

        def body(at):
            window = states[seg, pl.ds(pl.multiple_of(zl * rows + at.start, 8), CHUNK + 8), :]
            previous = pltpu.roll(window, 1, 0)[8:]
            g = dh[b, at, :] + after[b, at, :] * later
            sa, si, a = siga[b, at, :], sigi[b, at, :], decay[b, at, :]
            uf = u[b, at, :].astype(F32)
            root = jnp.sqrt(minus_expm1((-2.0 * DECAY_SCALE) * sa * soft))
            gu = g * uf
            gr = g * root
            d_log = a * (g * previous - gu * si * a / root)
            d_log = jnp.where(real, d_log, 0.0)
            dra = (d_log * (-DECAY_SCALE * soft) * sa * (1.0 - sa)).astype(BF)
            dri = (gr * uf * si * (1.0 - si)).astype(BF)
            du[seg, pl.ds(pl.multiple_of(zl * rows + at.start, 8), CHUNK), :] = gr * si
            dlog_ref[at, :LANES] = dra
            dlog_ref[at, LANES:] = dri
            for k, v in enumerate((d_log * sa, dra.astype(F32), dri.astype(F32))):
                sums[k] = sums[k] + fold(v)

        sums = [jnp.zeros((8, LANES), F32) for _ in range(3)]
        chunks(rows, body)
        for k in range(3):
            ch_out[k] += sums[k]
        d = dlog_ref[...]
        there = pl.ds(pl.multiple_of(zl * rows, 8), rows)
        du[seg, there, :] += dot(d, blocks_ref[...], NT)
        gb_out[...] += dot(u[b], d, TN)

    lane = lax.broadcasted_iota(jnp.int32, (1, LANES), 1)
    real = lane < local
    for name in ("siga", "sigi", "u"):
        kept[name].wait()
    loop(8, gradients)
    at = to_partner(du.at[:, pl.ds(0, 8)], halo)
    scatter.across_z()
    up.across(1)

    def write(i, at, src, dst, base):
        return pltpu.make_async_copy(src.at[i], dst.at[at], sems.at[base + i])

    def convolve(i, zl):
        seg = i
        b = i * 2 + zl
        slot = i % 2

        @pl.when(i >= 2)
        def _():
            write(slot, b - 4, dboth, dboth_out, 0).wait()

        def body(at):
            start = pl.multiple_of(zl * rows + at.start, 8)
            v = du[seg, pl.ds(start, CHUNK + 8), :]
            x = xs[seg, pl.ds(start, CHUNK + 8), :]
            here = v[:CHUNK]
            total = ch_ref[4:5, :] * here
            sums[0] = sums[0] + fold(here)
            sums[1] = sums[1] + fold(here * x[8:])
            for k in (1, 2, 3):
                total = total + ch_ref[4 + k : 5 + k, :] * pltpu.roll(v, CHUNK + 8 - k, 0)[:CHUNK]
                sums[1 + k] = sums[1 + k] + fold(here * pltpu.roll(x, k, 0)[8:])
            wide = 2 * local - LANES
            zeros = jnp.zeros((CHUNK, wide), F32)
            left = jnp.concatenate([total, zeros], axis=1)
            right = jnp.concatenate([dgy[b, at, :].astype(F32), zeros], axis=1)
            dboth[slot, at, :] = (left + pltpu.roll(right, local, 1)).astype(BF)

        sums = [jnp.zeros((8, LANES), F32) for _ in range(5)]
        chunks(rows, body)
        for k in range(5):
            ch_out[3 + k] += sums[k]
        write(slot, b, dboth, dboth_out, 0).start()

    def drain(zl):
        for i in (2, 3):
            write(i % 2, i * 2 + zl, dboth, dboth_out, 0).wait()

    kept["xs"].wait()
    kept["mid"].wait()
    loop(4, functools.partial(convolve, zl=0))
    drain(0)
    links.arrived(halo, at)

    def tail(seg):
        du[seg, pl.ds(2 * rows, 8), :] = jnp.where(zh == 0, halo[seg], 0.0)

    loop(4, tail)
    loop(2, functools.partial(convolve, zl=1))
    scatter.arrive()

    def add(at):
        final[at, :] = (mid_ref[at, :] + scatter.total(at)).astype(BF)

    chunks(rows, add)
    at = links.pair()
    links.start(final, block_out.at[p.mp], at, p.peer(mp=1))
    own = links.keep(final, block_out.at[p.mp])
    loop(2, lambda i: convolve(i + 2, 1))
    up.last(0)
    drain(1)
    up.last(1)
    up.end()
    ff = up.result.shape[2]
    for j in range(4):
        up_out[:, j * ff : (j + 1) * ff] = up.result[j].astype(F32)
    own.wait()
    links.arrived(block_out.at[1 - p.mp], at)
    links.finish()


def recur_forward(tokens, w_ig, blocks, channels, gain):
    if not shape_fits():
        return plain_recur_forward(tokens, w_ig, blocks, channels, gain)
    rows, width = tokens.shape[1:]
    local = w_ig.shape[1] // 2
    table = jnp.concatenate([jax.nn.softplus(-channels[0:1]), channels[1:]], axis=0)
    f, h = (8, rows, LANES), (4, 2 * rows + 8, LANES)
    n1, *saved = run_kernel(
        recur_forward_kernel,
        "recur_forward",
        [(tokens.shape, BF), (h, F32), (f, F32), (f, BF)]
        + [(f, F32)] * 3
        + [(h, F32), (f, BF)],
        [ANY] * 7 + [VMEM] * 2,
        [ANY] + [VMEM] * 4,
        [
            pltpu.VMEM(h, F32),
            pltpu.VMEM(f, F32),
            pltpu.VMEM(f, BF),
            pltpu.VMEM(f, F32),
            pltpu.VMEM(f, F32),
            pltpu.VMEM(f, F32),
            pltpu.VMEM(f, F32),
            pltpu.VMEM((8, rows, 2 * LANES), F32),
            pltpu.VMEM((2, rows, width), BF),
            pltpu.VMEM((rows, 2 * local), F32),
            pltpu.VMEM((4, 8, LANES), F32),
            pltpu.VMEM((8, LANES), F32),
            pltpu.VMEM((8, LANES), F32),
            pltpu.VMEM((2, rows, width), BF),
        ]
        + semaphores(6, 2)[:1]
        + semaphores(2, 6),
        5,
        (tokens, w_ig, blocks, table, gain),
        61,
    )
    *saved, mixed = saved
    return n1.reshape(-1, width), mixed.reshape(-1, LANES), (table, blocks, *saved)


def recur_backward(do, saved, w_o, channels, out_part, middle, n2, dup, drows):
    if not shape_fits():
        return plain_recur_backward(do, saved, w_o, channels, out_part, middle, n2, dup, drows)
    ff = dup.shape[1]
    table, wide, xs, gy, u, siga, sigi, decay, states = saved
    rows, width = do.shape[1:]
    local = w_o.shape[0]
    f, h = (8, rows, LANES), (4, 2 * rows + 8, LANES)
    dboth, g_blocks, sums, block_out, g_up = run_kernel(
        recur_backward_kernel,
        "recur_backward",
        [
            ((8, rows, 2 * local), BF),
            ((LANES, 2 * LANES), F32),
            ((8, 8, LANES), F32),
            ((2, rows, width), BF),
            ((drows, 4 * ff), F32),
        ],
        [ANY] + [VMEM] * 2 + [ANY, VMEM],
        [ANY] + [VMEM] * 3 + [ANY, VMEM] + [ANY] * 4 + [VMEM] + [ANY] * 3 + [VMEM],
        [
            pltpu.VMEM(h, F32),
            pltpu.VMEM(f, BF),
            pltpu.VMEM(f, F32),
            pltpu.VMEM(f, F32),
            pltpu.VMEM(f, F32),
            pltpu.VMEM((rows, width), F32),
            pltpu.VMEM(f, F32),
            pltpu.VMEM(f, F32),
            pltpu.VMEM(f, BF),
            pltpu.VMEM((rows, 2 * LANES), BF),
            pltpu.VMEM(h, F32),
            pltpu.VMEM((2, rows, 2 * local), BF),
            pltpu.VMEM((4, 8, LANES), F32),
            pltpu.VMEM((8, LANES), F32),
            pltpu.VMEM((8, LANES), F32),
            pltpu.VMEM((2, rows, width), BF),
            pltpu.VMEM((rows, width), BF),
        ]
        + semaphores(6, 2)[:1]
        + scatter_buffers(rows, width)
        + grad_buffers(2 * drows, ff, 8 * rows)
        + semaphores(32, 32),
        6,
        (do, w_o, wide, table, xs, gy, u, siga, sigi, decay, states)
        + (out_part, middle, n2, dup),
        61,
    )
    sums = jnp.sum(sums, axis=1)[:, :local]
    dlam = sums[0] * DECAY_SCALE * jax.nn.sigmoid(-channels[0, :local])
    g_blocks = jnp.concatenate(
        [g_blocks[:local, g * LANES : g * LANES + local] for g in (0, 1)], axis=1
    )
    return (
        dboth.reshape(-1, 2 * local),
        g_blocks,
        jnp.concatenate([dlam[None], sums[1:]], axis=0),
        block_out,
        g_up,
    )


def plain_recur_forward(tokens, w_ig, blocks, channels, gain):
    length, local, width = tokens.shape[1], w_ig.shape[1] // 2, tokens.shape[2]
    wide = tokens.reshape(-1, width).astype(F32)
    n1 = (wide * inverse_rms(wide) * gain).astype(BF)
    both = dot(n1, w_ig, NN)
    xb = both[:, :local].astype(BF).reshape(4, 2 * length, local)
    gy = both[:, local:].reshape(4, 2 * length, local)
    rim = from_behind(xb[:, -3:], 1)
    padded = jnp.concatenate([rim, xb], axis=1).astype(F32)
    conv = channels[3]
    for k in range(4):
        conv = conv + channels[4 + k] * padded[:, 3 - k : 3 - k + 2 * length]
    u = conv.astype(BF)
    logits = dot(u.reshape(-1, local), blocks, NN).reshape(4, 2 * length, 2 * local)
    sig_a = jax.nn.sigmoid(logits[..., :local] + channels[1])
    sig_i = jax.nn.sigmoid(logits[..., local:] + channels[2])
    log_decay = -DECAY_SCALE * sig_a * jax.nn.softplus(-channels[0])
    decay = jnp.exp(log_decay)
    root = jnp.sqrt(-jnp.expm1(2.0 * log_decay))
    running, state = local_scan(decay, root * sig_i * u.astype(F32), False)
    incoming = carried(running[:, -1], state[:, -1], False)
    states = state + running * incoming[:, None]
    gelu_y, slope_y = gelu_both(gy)
    mixed = (gelu_y * states).astype(BF).reshape(-1, local)
    saved = (blocks, padded, u, sig_a, sig_i, decay, root, running, incoming, states)
    return n1, mixed, saved + (gelu_y, slope_y)


def plain_recur_backward(do, saved, w_o, channels, out_part, middle, n2, dup, drows):
    blocks, padded, u, sig_a, sig_i, decay, root, running, incoming, states = saved[:10]
    gelu_y, slope_y = saved[10:]
    length, local, width = do.shape[1], w_o.shape[0], do.shape[2]
    dz = dot(do.reshape(-1, width), w_o, NT).reshape(4, 2 * length, local)
    dh = dz * gelu_y
    dgy = (dz * states * slope_y).astype(BF)
    ones = jnp.ones_like(decay[:, :1])
    after, adjoint = local_scan(jnp.concatenate([decay[:, 1:], ones], axis=1), dh, True)
    later = carried(running[:, -1], decay[:, 0] * adjoint[:, 0], True)
    adjoint = adjoint + after * later[:, None]
    previous = jnp.concatenate([incoming[:, None], states[:, :-1]], axis=1)
    soft, uf = jax.nn.softplus(-channels[0]), u.astype(F32)
    d_root = adjoint * sig_i * uf
    d_log = adjoint * previous * decay - d_root * decay * decay / root
    dra = (d_log * (-DECAY_SCALE * soft) * sig_a * (1.0 - sig_a)).astype(BF)
    dri = (adjoint * root * uf * sig_i * (1.0 - sig_i)).astype(BF)
    dlam = jnp.sum(d_log * sig_a, axis=(0, 1)) * DECAY_SCALE * jax.nn.sigmoid(-channels[0])
    dlogits = jnp.concatenate([dra, dri], axis=2).reshape(-1, 2 * local)
    g_blocks = dot(u.reshape(-1, local), dlogits, TN)
    du = adjoint * root * sig_i + dot(dlogits, blocks, NT).reshape(4, 2 * length, local)
    zeros = jnp.zeros((4, 3, local), F32)
    spread = jnp.concatenate([zeros, du, zeros], axis=1)
    dpad = jnp.zeros((4, 2 * length + 3, local), F32)
    taps = []
    for k in range(4):
        dpad = dpad + channels[4 + k] * spread[:, k : k + 2 * length + 3]
        taps.append(jnp.sum(du * padded[:, 3 - k : 3 - k + 2 * length], axis=(0, 1)))
    back = from_behind(dpad[:, :3], -1)
    dxb = dpad[:, 3:] + jnp.concatenate(
        [jnp.zeros((4, 2 * length - 3, local), F32), back], axis=1
    )
    dboth = jnp.concatenate([dxb.astype(BF), dgy], axis=2).reshape(-1, 2 * local)
    sums = [jnp.sum(v.astype(F32), axis=(0, 1)) for v in (dra, dri, du)]
    result = (middle + Tokens().scatter(out_part.reshape(-1, width))).astype(BF)
    g_up = columns(return_grad(dot(n2, dup, TN, BF), drows), 0, dup.shape[1])
    small = jnp.stack([dlam] + sums + taps)
    return dboth, g_blocks, small, both_batches(result), g_up


def on_device(
    tokens_in,
    cotangent,
    seq_source,
    source_weight,
    input_weight,
    gelu_weight,
    decay_gates,
    input_gates,
    channel_params,
    norm_gains,
    output_weight,
    mlp_gate,
    mlp_up,
    mlp_down,
):
    sizes = tuple(lax.axis_size(n) for n in AXES)
    dxn, _, zhn, _, _ = sizes
    group = dxn * 2 * zhn * 2
    dc, zl, mp = (lax.axis_index(n) for n in ("dc", "zl", "mp"))
    slot = dc * 2 + zl
    width = tokens_in.shape[3]
    local = input_weight.shape[1] // 4
    heads = decay_gates.shape[0] // 4
    drows = input_weight.shape[0]
    piece = decay_gates.shape[1]

    tokens, w_ig, w_o, blocks, channels, gains, dm, dout, own, w_g = fetch_first(
        tokens_in[:, 0],
        cotangent[:, 0],
        seq_source,
        source_weight,
        input_weight,
        gelu_weight,
        output_weight,
        decay_gates,
        input_gates,
        channel_params,
        norm_gains,
        mlp_gate,
    )

    n1, mixed, saved = recur_forward(tokens, w_ig, blocks, channels, gains[0:1])
    middle, n2, w_u, w_d = reduce_and_fetch(mixed, w_o, own, gains[1:2], mlp_up, mlp_down)

    hidden, dgm, dup = feed_forward(n2, dm, w_g, w_u, w_d)
    n2, dm = n2.reshape(-1, width), dm.reshape(-1, width)
    dr1, gain_two, do, g_gate, g_down, out_part = reduce_and_return(
        (w_g, w_u, w_d), middle, dout, gains[1:2], dm, hidden, n2, dgm, dup, drows
    )
    gain_two = jnp.sum(gain_two, axis=0)

    dboth, g_blocks, channel_grad, block_out, g_up = recur_backward(
        do, saved, w_o, channels, out_part, middle, n2, dup, drows
    )

    g_gates = jnp.stack(
        [
            jnp.stack(
                [
                    g_blocks[
                        h * BLOCK : (h + 1) * BLOCK,
                        g * local + h * BLOCK : g * local + (h + 1) * BLOCK,
                    ]
                    for h in range(heads)
                ]
            )
            for g in range(2)
        ]
    )
    g_gates = g_gates.reshape(2 * heads, group, piece).transpose(1, 0, 2).reshape(group, -1)
    count = g_gates.shape[1]
    unit = (count + 2047) // 2048 * 16
    g_gates = jnp.pad(g_gates, ((0, 0), (0, unit * 128 - count))).astype(BF)
    grad_tokens, gain_one, g_input, g_gelu, g_output, share_gates = return_last(
        w_ig,
        own,
        dr1,
        gains[0:1],
        do.reshape(-1, width),
        mixed,
        n1,
        dboth,
        g_gates.reshape(group * unit, 128),
        drows,
    )
    gain_one = jnp.sum(gain_one, axis=0)
    g_gates = share_gates.reshape(4, -1)[:, :count].astype(F32).reshape(4, 2, heads, piece)
    g_gates = g_gates.transpose(1, 0, 2, 3).reshape(2, 4 * heads, piece)

    per = 4 * local // group
    mine = channel_grad.reshape(8, group // 4, per).transpose(1, 0, 2)
    mine = jnp.where(
        jnp.arange(4, dtype=jnp.int32)[:, None, None, None] == slot, mine[None], 0.0
    ).reshape(group, 1, 8 * per)
    mine = jnp.where(jnp.arange(2, dtype=jnp.int32)[None, :, None] == mp, mine, 0.0)
    both_gains = jnp.stack([gain_one, gain_two]).reshape(2, group, -1).transpose(1, 0, 2)
    both_gains = jnp.broadcast_to(both_gains.reshape(group, 1, -1), (group, 2, 2 * drows))
    sums = jnp.concatenate([both_gains, mine], axis=2).reshape(2 * group, -1)
    sums = jnp.sum(lax.all_to_all(sums, AXES, 0, 0, tiled=True), axis=0)
    g_gains = sums[: 2 * drows].reshape(2, drows)
    g_channels = sums[2 * drows :].reshape(8, 1, per)
    return (
        block_out[:, None],
        grad_tokens[:, None],
        g_input,
        g_gelu,
        g_gates[0],
        g_gates[1],
        g_channels,
        g_gains,
        g_output,
        g_gate,
        g_up,
        g_down,
    )


def solution(mesh):
    dpn, seqn, mpn = (mesh.shape[n] for n in ("dp", "seq", "mp"))
    fine = Mesh(mesh.devices.reshape(dpn // 2, 2, seqn // 2, 2, mpn), AXES)
    dp, seq = ("dx", "dc"), ("zh", "zl")
    shards = dp + seq
    weights = (
        P(shards, "mp"),
        P(shards, "mp"),
        P("mp", shards),
        P("mp", shards),
        P(None, "mp", shards),
        P(None, shards),
        P("mp", shards),
        P(shards, "mp"),
        P(shards, "mp"),
        P("mp", shards),
    )
    rows = P(None, dp, seq, None)
    return jax.shard_map(
        on_device,
        mesh=fine,
        in_specs=(rows, rows, P(None, dp), P()) + weights,
        out_specs=(rows, rows) + weights,
        check_vma=False,
    )
```

```python
import functools

import jax
import jax.numpy as jnp
import numpy as np
from jax import lax
from jax.experimental import pallas as pl
from jax.experimental.pallas import tpu as pltpu
from jax.sharding import Mesh, PartitionSpec as P

WIDTH = 2560
HEADS = 16
BLOCK = WIDTH // HEADS
EPSILON = 1e-06
DECAY_SCALE = 8.0
AXES = ("dx", "dc", "zh", "zl", "mp")
BF = jnp.bfloat16
F32 = jnp.float32
LANES = 384


def swap_pairs(sizes, partner):
    pairs = []
    for flat in range(int(np.prod(sizes))):
        coords = np.unravel_index(flat, sizes)
        pairs.append((flat, int(np.ravel_multi_index(partner(*map(int, coords)), sizes))))
    return pairs


def gather_blocks(x, axis, dim):
    if lax.axis_size(axis) != 2:
        return lax.all_gather(x, axis, axis=dim, tiled=False)
    here = lax.axis_index(axis)
    other = lax.ppermute(x, axis, [(0, 1), (1, 0)])
    low = jnp.where(here == 0, x, other)
    high = jnp.where(here == 0, other, x)
    return jnp.stack([low, high], axis=dim)


def scatter_blocks(x, axis, dim):
    if lax.axis_size(axis) != 2:
        n = x.shape[dim]
        out = lax.psum_scatter(x.astype(BF), axis, scatter_dimension=dim, tiled=True)
        return lax.squeeze(out, [dim]).astype(F32)
    here = lax.axis_index(axis)
    mine = lax.dynamic_index_in_dim(x, here, dim, keepdims=False)
    theirs = lax.dynamic_index_in_dim(x, 1 - here, dim, keepdims=False)
    got = lax.ppermute(theirs.astype(BF), axis, [(0, 1), (1, 0)])
    return mine.astype(F32) + got.astype(F32)


def fetch_weight(shard, parts):
    rows, cols = shard[0].shape[0], None
    pieces = [s.reshape(rows, parts, -1) for s in shard]
    joined = jnp.concatenate(pieces, axis=2) if len(pieces) > 1 else pieces[0]
    cols = joined.shape[2]
    x = jnp.transpose(joined, (1, 0, 2))
    x = lax.all_to_all(x, ("dc", "zl"), 0, 0, tiled=True)
    x = x.reshape(2, 2, rows, cols)
    x = gather_blocks(x, "zh", 1)
    x = gather_blocks(x, "dx", 0)
    return x.reshape(-1, cols)


def return_grad(grad, rows):
    cols = grad.shape[1]
    dxn, zhn = lax.axis_size("dx"), lax.axis_size("zh")
    g = grad.reshape(dxn, 2, zhn, 2, rows, cols)
    g = scatter_blocks(g, "dx", 0)
    g = scatter_blocks(g, "zh", 1)
    g = g.astype(BF).reshape(4, rows, cols)
    return lax.all_to_all(g, ("dc", "zl"), 0, 0, tiled=True)


class Tokens:
    def __init__(self):
        sizes = tuple(lax.axis_size(n) for n in AXES)
        self.core = swap_pairs(sizes, lambda a, b, c, d, e: (a, 1 - b, c, d, e))
        self.first = swap_pairs(
            sizes, lambda a, b, c, d, e: (a, b, c, d, 1 - e) if b == 0 else (a, b, c, 1 - d, e)
        )
        self.second = swap_pairs(
            sizes, lambda a, b, c, d, e: (a, b, c, 1 - d, e) if b == 0 else (a, b, c, d, 1 - e)
        )
        self.dc, self.zl, self.mp = (lax.axis_index(n) for n in ("dc", "zl", "mp"))

    def order(self, dc):
        mp, zl = self.mp, self.zl
        own = mp * 2 + zl
        by_mp = (1 - mp) * 2 + zl
        by_zl = mp * 2 + 1 - zl
        both = (1 - mp) * 2 + 1 - zl
        one = jnp.where(dc == 0, by_mp, by_zl)
        two = jnp.where(dc == 0, by_zl, by_mp)
        return own, one, two, both

    def gather(self, x):
        rows, width = x.shape
        one = lax.ppermute(x, AXES, self.first)
        two = lax.ppermute(jnp.stack([x, one]), AXES, self.second)
        far = [lax.ppermute(v, AXES, self.core) for v in (x, one, two)]
        out = jnp.zeros((8, rows, width), x.dtype)
        for dc, blocks in (
            (self.dc, (x, one, two[0], two[1])),
            (1 - self.dc, (far[0], far[1], far[2][0], far[2][1])),
        ):
            for at, block in zip(self.order(dc), blocks):
                out = lax.dynamic_update_index_in_dim(out, block, dc * 4 + at, 0)
        return out.reshape(8 * rows, width)

    def scatter(self, x):
        rows, width = x.shape[0] // 8, x.shape[1]
        x = x.reshape(2, 4, rows, width)
        theirs = lax.dynamic_index_in_dim(x, 1 - self.dc, 0, keepdims=False).astype(BF)
        mine = lax.dynamic_index_in_dim(x, self.dc, 0, keepdims=False)
        total = mine.astype(F32) + lax.ppermute(theirs, AXES, self.core).astype(F32)
        own, one, two, both = self.order(self.dc)
        pick = lambda at: lax.dynamic_index_in_dim(total, at, 0, keepdims=False)
        got = lax.ppermute(jnp.stack([pick(two), pick(both)]).astype(BF), AXES, self.second)
        keep_own = pick(own) + got[0].astype(F32)
        keep_one = pick(one) + got[1].astype(F32)
        got = lax.ppermute(keep_one.astype(BF), AXES, self.first)
        return keep_own + got.astype(F32)


MESH = pl.DeviceIdType.MESH
ANY = pl.BlockSpec(memory_space=pl.ANY)
VMEM = pl.BlockSpec(memory_space=pltpu.VMEM)


def flip(index, by):
    return 1 - index if by else index


class Place:
    def __init__(self):
        self.dx, self.dc, self.zh, self.zl, self.mp = (lax.axis_index(n) for n in AXES)

    def peer(self, dx=0, dc=0, zh=0, zl=0, mp=0):
        return (
            flip(self.dx, dx),
            flip(self.dc, dc),
            flip(self.zh, zh),
            flip(self.zl, zl),
            flip(self.mp, mp),
        )

    def block(self, dx=0, dc=0, zh=0, zl=0):
        a, b, c, d, _ = self.peer(dx, dc, zh, zl)
        return ((a * 2 + b) * 2 + c) * 2 + d

    def slot(self, dc=0, zl=0):
        return flip(self.dc, dc) * 2 + flip(self.zl, zl)

    def rows(self, dc=0, mp=0, zl=0):
        return (flip(self.dc, dc) * 2 + flip(self.mp, mp)) * 2 + flip(self.zl, zl)


def greet(peers):
    barrier = pltpu.get_barrier_semaphore()
    for device in peers:
        pl.semaphore_signal(barrier, inc=1, device_id=device, device_id_type=MESH)
    pl.semaphore_wait(barrier, len(peers))


class Links:
    def __init__(self, send, recv, local):
        self.send, self.recv, self.local = send, recv, local
        self.n, self.m = 0, 0
        self.sent, self.copies = [], []

    def pair(self):
        self.n += 1
        return self.n - 1

    def start(self, src, dst, at, device):
        copy = pltpu.make_async_remote_copy(
            src_ref=src,
            dst_ref=dst,
            send_sem=self.send.at[at],
            recv_sem=self.recv.at[at],
            device_id=device,
            device_id_type=MESH,
        )
        copy.start()
        self.sent.append(copy)

    def arrived(self, ref, at):
        pltpu.make_async_copy(ref, ref, self.recv.at[at]).wait()

    def keep(self, src, dst):
        copy = pltpu.make_async_copy(src, dst, self.local.at[self.m])
        self.m += 1
        copy.start()
        return copy

    def finish(self):
        for copy in self.sent:
            copy.wait_send()


FLIPS = [(zh, dc, zl) for zh in (1, 0) for dc in (0, 1) for zl in (0, 1)]


class WeightGather:
    def __init__(self, place, links, source, target, unit):
        self.place, self.links, self.target = place, links, target
        self.at = {f: links.pair() for f in FLIPS}
        self.cross = {(zh, dc): links.pair() for zh in (0, 1) for dc in (0, 1)}
        self.source = source
        self.kept = None

    def begin(self, zhs=(1, 0), dcs=(0, 1)):
        p = self.place
        mine = p.block()
        for f in FLIPS:
            zh, dc, zl = f
            if zh not in zhs or dc not in dcs:
                continue
            src, dst = self.source(p.slot(dc, zl)), self.target(mine, 1)
            if f == (0, 0, 0):
                self.kept = self.links.keep(src, dst)
            else:
                self.links.start(src, dst, self.at[f], p.peer(dc=dc, zh=zh, zl=zl))

    def onward(self, zh, dcs=(0, 1)):
        p = self.place
        for dc in dcs:
            for zl in (0, 1):
                if (zh, dc, zl) == (0, 0, 0):
                    self.kept.wait()
                else:
                    self.links.arrived(
                        self.target(p.block(dc=dc, zh=zh, zl=zl), 1), self.at[zh, dc, zl]
                    )
            two = self.target(p.block(dc=dc, zh=zh) // 2 * 2, 2)
            self.links.start(two, two, self.cross[zh, dc], p.peer(dx=1))

    def end(self):
        p = self.place
        for zh in (0, 1):
            for dc in (0, 1):
                two = self.target(p.block(dx=1, dc=dc, zh=zh) // 2 * 2, 2)
                self.links.arrived(two, self.cross[zh, dc])


def row_blocks(ref, unit, cols=None):
    def target(first, count):
        rows = pl.ds(pl.multiple_of(first * unit, unit), count * unit)
        return ref.at[rows] if cols is None else ref.at[rows, cols]

    return target


def column_blocks(ref, unit):
    return lambda first, count: ref.at[:, pl.ds(pl.multiple_of(first * unit, unit), count * unit)]


def first_kernel(
    weight_ref, source_ref, tok_ref, cot_ref, ig_ref, o_ref, gates_ref, small_ref, gate_ref,
    all_ref, wig_ref, wo_ref, wide_ref, ch_ref, gains_ref, dms_ref, dout_ref, own_ref, wg_ref,
    pieces, smalls, dm, send, recv, local,
):
    p = Place()
    links = Links(send, recv, local)
    drows = ig_ref.shape[1]
    crows = wo_ref.shape[0]
    greet(weight_peers(p))
    gather = TokenGatherTwice(p, links, tok_ref, all_ref)
    w_ig = WeightGather(p, links, lambda j: ig_ref.at[j], row_blocks(wig_ref, drows), drows)
    w_o = WeightGather(
        p,
        links,
        lambda j: o_ref.at[pl.ds(pl.multiple_of(j * crows, 16), crows)],
        column_blocks(wo_ref, o_ref.shape[1]),
        drows,
    )
    unit = gates_ref.shape[1]
    w_g = WeightGather(p, links, lambda j: gates_ref.at[j], row_blocks(pieces, unit), unit)
    w_s = WeightGather(p, links, lambda j: small_ref, row_blocks(smalls, 16), 16)
    w_gate = slot_columns(p, links, gate_ref, wg_ref)
    adjoint = TokenGatherTwice(p, links, dm, dms_ref)
    w_s.begin()
    w_ig.begin((1,))
    w_ig.begin((0,))
    w_g.begin((0,))
    w_o.begin((0,))
    gather.begin()
    own = links.keep(tok_ref.at[p.mp], own_ref)
    scales = [weight_ref[source_ref[m, 0]] for m in range(2)]
    for m in range(2):

        def scale(rows, m=m):
            value = cot_ref[m, rows, :].astype(F32) * scales[m]
            dm[m, rows, :] = value.astype(BF)

            @pl.when(p.mp == m)
            def _():
                dout_ref[rows, :] = value

        chunks(cot_ref.shape[1], scale, 1)
    adjoint.begin()
    w_ig.onward(0)
    w_g.onward(0)
    w_o.onward(0)
    w_s.onward(0)
    w_gate.begin((0,))
    w_o.begin((1,))
    w_g.begin((1,))
    w_ig.onward(1)
    w_gate.begin((1,), (0,))
    w_s.onward(1)
    gather.forward()
    w_o.onward(1)
    w_g.onward(1)
    w_gate.begin((1,), (1,))
    gather.forward_core()
    w_gate.onward(0)
    adjoint.forward()
    w_gate.onward(1, (0,))
    adjoint.forward_core()
    w_s.end()
    count = small_channels(local_channels=crows)
    table = jnp.zeros((8, LANES), F32)
    for k in range(4):
        at = pl.ds(pl.multiple_of((p.slot() * 4 + k) * 16, 16), 16)
        rows = smalls[at, :].astype(F32)[:8]
        rows = jnp.concatenate([rows, jnp.zeros((8, LANES - 128), F32)], axis=1)
        table = table + (pltpu.roll(rows, k * count, 1) if k else rows)
    ch_ref[...] = table
    for k in range(16):
        rows = smalls[k * 16 : (k + 1) * 16, :].astype(F32)
        gains_ref[:, k * 128 : (k + 1) * 128] = rows[8:10]
    w_g.end()
    size = crows // 2
    per = size // 16
    total = jnp.zeros(wide_ref.shape, F32)
    row = lax.broadcasted_iota(jnp.int32, (LANES, pieces.shape[0]), 0)
    column = lax.broadcasted_iota(jnp.int32, (LANES, pieces.shape[0]), 1)
    source = lax.broadcasted_iota(jnp.int32, (LANES, 2 * LANES), 0)
    target = lax.broadcasted_iota(jnp.int32, (LANES, 2 * LANES), 1)
    for h in range(2):
        r = column % 32 - h * 16
        wanted = (r >= 0) & (r < per) & (row == h * size + column // 32 * per + r)
        rows = dot(jnp.where(wanted, 1.0, 0.0).astype(BF), pieces[...], NN, BF)
        gate = target // LANES
        wanted = (source == target - gate * LANES - h * size + gate * size) & (
            (source >= gate * size) & (source < (gate + 1) * size)
        )
        total = total + dot(rows, jnp.where(wanted, 1.0, 0.0).astype(BF), NN)
    wide_ref[...] = total.astype(BF)
    w_gate.onward(1, (1,))
    own.wait()
    gather.end()
    adjoint.end()
    w_gate.end()
    w_ig.end()
    w_o.end()
    links.finish()


def small_channels(local_channels):
    return local_channels // 4


class TokenGatherTwice:
    def __init__(self, place, links, source, target):
        self.place, self.links, self.source, self.target = place, links, source, target
        self.z, self.y = links.pair(), links.pair()
        self.core = {(mp, zl): links.pair() for mp in (0, 1) for zl in (0, 1)}

    def begin(self):
        p = self.place
        self.kept = []
        for mp in (0, 1):
            at = p.rows(mp=mp)
            src = self.source.at[flip(p.mp, mp)]
            if mp == 0:
                self.links.start(src, self.target.at[at], self.z, p.peer(zl=1))
            self.links.start(src, self.target.at[at], self.core[mp, 0], p.peer(dc=1))
            self.kept.append(self.links.keep(src, self.target.at[at]))

    def forward(self):
        p = self.place
        far = self.target.at[p.rows(zl=1)]
        self.links.arrived(far, self.z)
        self.links.start(far, far, self.y, p.peer(mp=1))
        self.links.start(far, far, self.core[0, 1], p.peer(dc=1))

    def forward_core(self):
        p = self.place
        far = self.target.at[p.rows(mp=1, zl=1)]
        self.links.arrived(far, self.y)
        self.links.start(far, far, self.core[1, 1], p.peer(dc=1))

    def end(self):
        p = self.place
        for (mp, zl), at in self.core.items():
            self.links.arrived(self.target.at[p.rows(dc=1, mp=mp, zl=zl)], at)
        for copy in self.kept:
            copy.wait()


class TokenGather:
    def __init__(self, place, links, source, target, span):
        self.place, self.links = place, links
        self.span = pl.ds(*span)
        self.source, self.target = source.at[self.span], target
        self.z, self.y0, self.y1 = links.pair(), links.pair(), links.pair()
        self.core = {(mp, zl): links.pair() for mp in (0, 1) for zl in (0, 1)}

    def block(self, **where):
        return self.target.at[self.place.rows(**where), self.span]

    def begin(self):
        p = self.place
        at = self.block()
        self.links.start(self.source, at, self.z, p.peer(zl=1))
        self.links.start(self.source, at, self.y0, p.peer(mp=1))
        self.links.start(self.source, at, self.core[0, 0], p.peer(dc=1))
        self.kept = self.links.keep(self.source, at)

    def forward(self):
        p = self.place
        far = self.block(zl=1)
        self.links.arrived(far, self.z)
        self.links.start(far, far, self.y1, p.peer(mp=1))
        self.links.start(far, far, self.core[0, 1], p.peer(dc=1))

    def forward_core(self):
        p = self.place
        far = self.block(mp=1)
        self.links.arrived(far, self.y0)
        self.links.start(far, far, self.core[1, 0], p.peer(dc=1))
        far = self.block(mp=1, zl=1)
        self.links.arrived(far, self.y1)
        self.links.start(far, far, self.core[1, 1], p.peer(dc=1))

    def end(self):
        for (mp, zl), at in self.core.items():
            self.links.arrived(self.block(dc=1, mp=mp, zl=zl), at)
        self.kept.wait()


CHUNK = 16


def chunks(count, body, most=11, first=0):
    n = count // CHUNK
    per = max(k for k in range(1, most + 1) if n % k == 0)

    def step(i, carry):
        for k in range(per):
            body(pl.ds(pl.multiple_of(first + (i * per + k) * CHUNK, CHUNK), CHUNK))
        return carry

    if n == per:
        step(0, 0)
    else:
        lax.fori_loop(0, n // per, step, 0)


def halves(rows):
    first = (rows // 2 + CHUNK - 1) // CHUNK * CHUNK
    return [(0, first), (first, rows - first)]


class RowScatter:
    def __init__(self, place, links, source, buffers, parts=None):
        self.place, self.links, self.source = place, links, source
        self.mine, self.from_core, self.from_y, self.from_z, self.out = buffers[:5]
        self.to_core = buffers[5] if len(buffers) > 5 else None
        self.parts = parts or [(0, self.mine.shape[1])]
        self.blocks = [(mp, zl) for mp in (1, 0) for zl in (1, 0)]
        self.kept = {}
        n = range(len(self.parts))
        self.core = {(h, block): links.pair() for h in n for block in self.blocks}
        self.y = {(h, zl): links.pair() for h in n for zl in (1, 0)}
        self.z = {h: links.pair() for h in n}

    def begin(self, mps=(1, 0)):
        p = self.place
        for mp, zl in self.blocks:
            if mp not in mps:
                continue
            i, block = mp * 2 + zl, p.rows(dc=1, mp=mp, zl=zl)
            if self.to_core is None:
                src = self.source.at[block]
            else:
                self.to_core[i] = self.source(block).astype(BF)
                src = self.to_core.at[i]
            for h, part in enumerate(self.parts):
                at = pl.ds(*part)
                self.links.start(
                    src.at[at], self.from_core.at[i, at], self.core[h, (mp, zl)], p.peer(dc=1)
                )
            block = p.rows(mp=mp, zl=zl)
            if self.to_core is None:
                self.kept[mp, zl] = self.links.keep(self.source.at[block], self.mine.at[i])
            else:
                self.mine[i] = self.source(block).astype(BF)

    def ready(self, mp, zl, h):
        i = mp * 2 + zl
        if h == 0 and self.kept:
            self.kept[mp, zl].wait()
        at = pl.ds(*self.parts[h])
        self.links.arrived(self.from_core.at[i, at], self.core[h, (mp, zl)])
        return i

    def across_y(self, h=0):
        p = self.place
        first, count = self.parts[h]
        at = pl.ds(first, count)
        for zl in (1, 0):
            i = self.ready(1, zl, h)

            def add(rows, i=i, zl=zl):
                total = self.mine[i, rows, :].astype(F32) + self.from_core[i, rows, :].astype(F32)
                self.out[zl, rows, :] = total.astype(BF)

            chunks(count, add, first=first)
            self.links.start(
                self.out.at[zl, at], self.from_y.at[zl, at], self.y[h, zl], p.peer(mp=1)
            )

    def across_z(self, h=0):
        p = self.place
        first, count = self.parts[h]
        at = pl.ds(first, count)
        i = self.ready(0, 1, h)
        self.links.arrived(self.from_y.at[1, at], self.y[h, 1])

        def add(rows):
            total = self.mine[i, rows, :].astype(F32) + self.from_core[i, rows, :].astype(F32)
            self.out[2, rows, :] = (total + self.from_y[1, rows, :].astype(F32)).astype(BF)

        chunks(count, add, first=first)
        self.links.start(self.out.at[2, at], self.from_z.at[at], self.z[h], p.peer(zl=1))

    def arrive(self, h=0):
        at = pl.ds(*self.parts[h])
        self.ready(0, 0, h)
        self.links.arrived(self.from_y.at[0, at], self.y[h, 0])
        self.links.arrived(self.from_z.at[at], self.z[h])

    def total(self, rows):
        a = self.mine[0, rows, :].astype(F32) + self.from_core[0, rows, :].astype(F32)
        b = self.from_y[0, rows, :].astype(F32) + self.from_z[rows, :].astype(F32)
        return a + b


def scatter_buffers(rows, width, products=False):
    return [
        pltpu.VMEM((4, rows, width), BF),
        pltpu.VMEM((4, rows, width), BF),
        pltpu.VMEM((2, rows, width), BF),
        pltpu.VMEM((rows, width), BF),
        pltpu.VMEM((3, rows, width), BF),
    ] + ([pltpu.VMEM((4, rows, width), BF)] if products else [])


def group_peers(p):
    return [p.peer(dc=1), p.peer(zl=1), p.peer(mp=1)]


def weight_peers(p):
    return [p.peer(dc=dc, zh=zh, zl=zl) for zh, dc, zl in FLIPS if (zh, dc, zl) != (0, 0, 0)] + [
        p.peer(dx=1),
        p.peer(mp=1),
    ]


def second_kernel(
    mixed_ref, wo_ref, own_ref, gain_ref, up_ref, down_ref,
    mid_ref, all_ref, wu_ref, wd_ref,
    *scratch,
):
    p = Place()
    links = Links(*scratch[-3:])
    normed = scratch[-4]
    rows, channels = own_ref.shape[0], wo_ref.shape[0]
    greet(weight_peers(p))

    def project(b):
        at = pl.ds(pl.multiple_of(b * rows, 16), rows)
        return dot(mixed_ref[at, :channels], wo_ref[...], NN)

    parts = halves(rows)
    scatter = RowScatter(p, links, project, scratch[:6], parts)
    w_u = slot_columns(p, links, up_ref, wu_ref)
    w_d = WeightGather(
        p,
        links,
        lambda j: down_ref.at[pl.ds(pl.multiple_of(j * wd_ref.shape[0], 16), wd_ref.shape[0])],
        column_blocks(wd_ref, down_ref.shape[1]),
        down_ref.shape[1],
    )
    gathers = [TokenGather(p, links, normed, all_ref, part) for part in parts]
    w_u.begin((1,), (0,))
    scatter.begin((1,))
    w_u.begin((0,))
    scatter.across_y(0)
    scatter.across_y(1)
    w_u.begin((1,), (1,))
    scatter.begin((0,))
    w_d.begin((0,))
    w_u.onward(0)

    def normalise(at):
        value = own_ref[at, :].astype(F32) + scatter.total(at)
        mid_ref[at, :] = value
        inv = lax.rsqrt(jnp.mean(value * value, axis=-1, keepdims=True) + EPSILON)
        normed[at, :] = (value * inv * gain_ref[...]).astype(BF)

    def middle(h):
        scatter.arrive(h)
        chunks(parts[h][1], normalise, first=parts[h][0])
        gathers[h].begin()

    scatter.across_z(0)
    w_d.onward(0)
    scatter.across_z(1)
    w_d.begin((1,), (0,))
    middle(0)
    w_u.onward(1, (0,))
    middle(1)
    w_u.onward(1, (1,))
    w_d.begin((1,), (1,))
    gathers[0].forward()
    gathers[1].forward()
    w_d.onward(1, (0,))
    gathers[0].forward_core()
    gathers[1].forward_core()
    w_d.onward(1, (1,))
    for gather in gathers:
        gather.end()
    w_u.end()
    w_d.end()
    links.finish()


def slot_columns(p, links, source, result):
    count = result.shape[1]
    return WeightGather(
        p,
        links,
        lambda j: source.at[:, pl.ds(pl.multiple_of(j * count, 128), count)],
        row_blocks(result, source.shape[0]),
        source.shape[0],
    )


class GradScatter:
    FAR = [(1, 0, 1), (1, 1, 1)], [(1, 0, 0), (1, 1, 0)]
    NEAR = [(0, 0, 1), (0, 1, 1)], [(0, 0, 0), (0, 1, 0)]
    ORDER = FAR[0] + NEAR[0] + FAR[1] + NEAR[1]
    EARLY = FAR[0] + FAR[1] + NEAR[0] + NEAR[1]

    def __init__(self, place, links, left, right, buffers, order=ORDER):
        self.order = order
        self.place, self.links, self.left, self.right = place, links, left, right
        self.to_x, self.from_x, self.to_z, self.from_z, self.sums, self.result = buffers[:6]
        self.columns = buffers[6] if len(buffers) > 6 else None
        self.rows = self.to_x.shape[1]
        self.x = {(zh, dc): links.pair() for zh in (1, 0) for dc in (0, 1)}
        self.z = {dc: links.pair() for dc in (0, 1)}
        self.at = {(dc, zl): links.pair() for dc in (0, 1) for zl in (0, 1)}
        self.count = 0
        self.load()

    def load(self):
        if self.count < 8 and self.columns is not None:
            dx, dc, zh = self.order[self.count]
            first = self.place.block(dx=dx, dc=dc, zh=zh) // 2
            columns = pl.ds(pl.multiple_of(first * self.rows, self.rows), self.rows)
            self.loading = self.links.keep(
                self.left.at[:, columns], self.columns.at[self.count % 2]
            )

    def product(self, dx=0, dc=0, zh=0):
        assert self.order[self.count] == (dx, dc, zh)
        self.loading.wait()
        self.count += 1
        self.load()
        return dot(self.columns[(self.count - 1) % 2], self.right[...], TN)

    def begin(self, zh):
        for dc in (0, 1):
            i = zh * 2 + dc
            self.to_x[i] = self.product(dx=1, dc=dc, zh=zh).astype(BF)
            self.links.start(
                self.to_x.at[i], self.from_x.at[i], self.x[zh, dc], self.place.peer(dx=1)
            )

    def across(self, dc):
        mine = self.product(dc=dc, zh=1)
        self.links.arrived(self.from_x.at[2 + dc], self.x[1, dc])
        self.to_z[dc] = (mine + self.from_x[2 + dc].astype(F32)).astype(BF)
        self.links.start(self.to_z.at[dc], self.from_z.at[dc], self.z[dc], self.place.peer(zh=1))

    def last(self, dc):
        p = self.place
        mine = self.product(dc=dc, zh=0)
        self.links.arrived(self.from_x.at[dc], self.x[0, dc])
        self.links.arrived(self.from_z.at[dc], self.z[dc])
        total = mine + self.from_x[dc].astype(F32) + self.from_z[dc].astype(F32)
        self.sums[dc] = total.astype(BF)
        unit = self.rows // 2
        for zl in (1, 0):
            src = self.sums.at[dc, pl.ds(pl.multiple_of(flip(p.zl, zl) * unit, unit), unit)]
            dst = self.result.at[p.slot()]
            if (dc, zl) == (0, 0):
                self.own = self.links.keep(src, dst)
            else:
                self.links.start(src, dst, self.at[dc, zl], p.peer(dc=dc, zl=zl))

    def end(self):
        p = self.place
        for (dc, zl), at in self.at.items():
            if (dc, zl) == (0, 0):
                self.own.wait()
            else:
                self.links.arrived(self.result.at[p.slot(dc, zl)], at)


class Ready(GradScatter):
    def product(self, dx=0, dc=0, zh=0):
        first = self.place.block(dx=dx, dc=dc, zh=zh) // 2
        return self.left[pl.ds(pl.multiple_of(first * self.rows, self.rows), self.rows), :].astype(
            F32
        )


def grad_buffers(rows, columns, tokens=None):
    return (
        [pltpu.VMEM((n, rows, columns), BF) for n in (4, 4, 2, 2, 2)]
        + [pltpu.VMEM((4, rows // 2, columns), BF)]
        + ([pltpu.VMEM((2, tokens, rows), BF)] if tokens else [])
    )


def norm_back(value, gain, upstream):
    inv = lax.rsqrt(jnp.mean(value * value, axis=-1, keepdims=True) + EPSILON)
    scaled = value * inv
    up = upstream * gain
    inner = jnp.mean(up * scaled, axis=-1, keepdims=True)
    return inv * (up - scaled * inner), upstream * scaled


def fold(rows):
    return rows[:8] + rows[8:]


def third_kernel(
    wg_ref, wu_ref, wd_in, mid_in, dout_in, gain_ref, dm_ref, hidden_ref, n2_ref, dgm_ref,
    dup_ref,
    dr1_ref, gain_out, all_ref, gate_out, down_out, part_out,
    *scratch,
):
    p = Place()
    links = Links(*scratch[-3:])
    do, wd_ref, mid_ref, dout_ref = scratch[-7:-3]
    rows_of = mid_ref.shape[0]
    staged = [
        links.keep(src, dst)
        for src, dst in ((mid_in, mid_ref), (dout_in, dout_ref), (wd_in, wd_ref))
    ]
    greet(weight_peers(p))

    def product(b):
        at = pl.ds(pl.multiple_of(b * rows_of, 16), rows_of)
        return dot(dgm_ref[at, :], wg_ref[...], NT) + dot(dup_ref[at, :], wu_ref[...], NT)

    parts = halves(rows_of)
    scatter = RowScatter(p, links, product, scratch[:6], parts)
    down = GradScatter(p, links, dm_ref, hidden_ref, scratch[6:13])
    gate = GradScatter(p, links, n2_ref, dgm_ref, scratch[13:20])
    gathers = [TokenGather(p, links, do, all_ref, part) for part in parts]
    down.begin(1)
    scatter.begin((1,))
    scatter.across_y(0)
    scatter.across_y(1)
    down.across(0)
    scatter.begin((0,))
    down.across(1)
    gate.begin(1)
    gain_out[...] = jnp.zeros_like(gain_out)
    for copy in staged:
        copy.wait()

    def back(rows):
        part, gain = norm_back(mid_ref[rows, :], gain_ref[...], scatter.total(rows))
        value = dout_ref[rows, :] + part
        dr1_ref[rows, :] = value
        do[rows, :] = value.astype(BF)
        gain_out[...] += fold(gain)

    def middle(h):
        scatter.arrive(h)
        chunks(parts[h][1], back, first=parts[h][0])
        gathers[h].begin()

    scatter.across_z(0)
    down.begin(0)
    gate.across(0)
    scatter.across_z(1)
    middle(0)
    gate.across(1)
    gate.begin(0)
    middle(1)
    gathers[0].forward()
    gathers[1].forward()
    out = scratch[0]
    writes = []
    for b in range(8):
        if b >= 4:
            writes[b - 4].wait()
        at = pl.ds(b * rows_of, rows_of)
        out[b % 4] = dot(hidden_ref[at, :], wd_ref[...], NN, BF)
        writes.append(links.keep(out.at[b % 4], part_out.at[b]))
    down.last(0)
    down.last(1)
    gathers[0].forward_core()
    gate.last(0)
    gathers[1].forward_core()
    gate.last(1)
    for gather in gathers:
        gather.end()
    down.end()
    ff = down.result.shape[2]
    for j in range(4):
        down_out[j * ff : (j + 1) * ff, :] = down.result[j].astype(F32).T
    gate.end()
    for j in range(4):
        gate_out[:, j * ff : (j + 1) * ff] = gate.result[j].astype(F32)
    for write in writes[4:]:
        write.wait()
    links.finish()


def fourth_kernel(
    wig_ref, own_ref, dr1_ref, gain_ref, do_ref, mixed_ref, n1_ref, dboth_ref, gg_ref,
    dx_ref, gain_out, in_out, gelu_out, out_out, gates_out,
    *scratch,
):
    p = Place()
    links = Links(*scratch[-3:])
    dx_send, dx_recv = scratch[-5:-3]
    greet(weight_peers(p))
    rows_of = own_ref.shape[0]

    def product(b):
        at = pl.ds(pl.multiple_of(b * rows_of, 16), rows_of)
        return dot(dboth_ref[at, :], wig_ref[...], NT)

    parts = halves(rows_of)
    scatter = RowScatter(p, links, product, scratch[:6], parts)
    out = GradScatter(p, links, do_ref, mixed_ref, scratch[6:13])
    wide = GradScatter(p, links, n1_ref, dboth_ref, scratch[13:20])
    gates = Ready(p, links, gg_ref, None, scratch[20:26])
    out.begin(1)
    scatter.begin((1,))
    scatter.across_y(0)
    scatter.across_y(1)
    out.across(0)
    out.across(1)
    wide.begin(1)
    scatter.begin((0,))
    gates.begin(1)
    out.begin(0)
    for g in (wide, gates):
        g.across(0)
        g.across(1)
        g.begin(0)
    gain_out[...] = jnp.zeros_like(gain_out)

    def back(rows):
        value = own_ref[rows, :].astype(F32)
        part, gain = norm_back(value, gain_ref[...], scatter.total(rows))
        total = dr1_ref[rows, :] + part
        dx_ref[p.mp, rows, :] = total
        dx_send[rows, :] = total.astype(BF)
        gain_out[...] += fold(gain)

    sent = []

    def middle(h):
        scatter.arrive(h)
        chunks(parts[h][1], back, first=parts[h][0])
        span, at = pl.ds(*parts[h]), links.pair()
        links.start(dx_send.at[span], dx_recv.at[span], at, p.peer(mp=1))
        sent.append((span, at))

    scatter.across_z(0)
    scatter.across_z(1)
    middle(0)
    for g in (out, gates):
        g.last(0)
        g.last(1)
    middle(1)
    wide.last(0)
    wide.last(1)
    local = out.result.shape[2]
    out.end()
    for j in range(4):
        out_out[j * out_out.shape[0] // 4 : (j + 1) * out_out.shape[0] // 4, :] = (
            out.result[j].astype(F32).T[: out_out.shape[0] // 4]
        )
    gates.end()
    gates_out[...] = gates.result[...]
    wide.end()
    two = wide.result.shape[2]
    left = lax.broadcasted_iota(jnp.int32, (1, two), 1) < two // 2
    for j in (0, 2):
        a, b = (wide.result[j + i].astype(F32) for i in (0, 1))
        span = slice(j * two // 2, (j + 2) * two // 2)
        in_out[:, span] = jnp.where(left, a, pltpu.roll(b, two // 2, 1))
        gelu_out[:, span] = jnp.where(left, pltpu.roll(a, two // 2, 1), b)
    for span, at in sent:
        links.arrived(dx_recv.at[span], at)
    dx_ref[1 - p.mp] = dx_recv[...].astype(F32)
    links.finish()


def mlp_kernel(
    n2_ref, dm_ref, wg_ref, wu_ref, wd_ref, hidden_ref, dgm_ref, dup_ref, pre, upp, dhm
):
    count, rows, width = n2_ref.shape
    n2 = n2_ref[...].reshape(count * rows, width)
    pre[...] = dot(n2, wg_ref[...], NN)
    upp[...] = dot(n2, wu_ref[...], NN)
    dhm[...] = dot(dm_ref[...].reshape(count * rows, width), wd_ref[...], NT)

    def body(at):
        up, d = upp[at, :], dhm[at, :]
        value, slope = gelu_both(pre[at, :])
        hidden_ref[at, :] = (value * up).astype(BF)
        dgm_ref[at, :] = (d * up * slope).astype(BF)
        dup_ref[at, :] = (d * value).astype(BF)

    chunks(count * rows, body)


def feed_forward(n2, dm, w_g, w_u, w_d):
    blocks, rows, width = n2.shape
    ff = w_d.shape[0]
    if not shape_fits():
        n2, dm = n2.reshape(-1, width), dm.reshape(-1, width)
        pre, d = dot(n2, w_g, NN), dot(dm, w_d, NT)
        gm, up = pre, dot(n2, w_u, NN)
        value, slope = gelu_both(gm)
        return (value * up).astype(BF), (d * up * slope).astype(BF), (d * value).astype(BF)
    two = pl.BlockSpec((2, rows, width), lambda i: (i, 0, 0))
    flat = pl.BlockSpec((2 * rows, ff), lambda i: (i, 0))
    whole = lambda v: pl.BlockSpec(v.shape, lambda i: (0, 0))
    total = blocks * rows
    return pl.pallas_call(
        mlp_kernel,
        name="feed_forward",
        grid=(blocks // 2,),
        in_specs=[two, two, whole(w_g), whole(w_u), whole(w_d)],
        out_specs=[flat] * 3,
        out_shape=[jax.ShapeDtypeStruct((total, ff), BF)] * 3,
        scratch_shapes=[pltpu.VMEM((2 * rows, ff), F32)] * 3,
        compiler_params=pltpu.CompilerParams(vmem_limit_bytes=48 * 1024 * 1024),
        cost_estimate=pl.CostEstimate(
            flops=2 * total * width * ff * 3, bytes_accessed=total * width * 4, transcendentals=0
        ),
    )(n2, dm, w_g, w_u, w_d)


def semaphores(pairs, local):
    return [
        pltpu.SemaphoreType.DMA((pairs,)),
        pltpu.SemaphoreType.DMA((pairs,)),
        pltpu.SemaphoreType.DMA((local,)),
    ]


def run_kernel(body, name, outs, out_specs, in_specs, scratch, ident, args, mib=40):
    return pl.pallas_call(
        body,
        name=name,
        out_shape=[jax.ShapeDtypeStruct(*o) for o in outs],
        in_specs=in_specs,
        out_specs=out_specs,
        scratch_shapes=scratch,
        compiler_params=pltpu.CompilerParams(
            collective_id=ident, has_side_effects=True, vmem_limit_bytes=mib * 1024 * 1024
        ),
    )(*args)


def fetch_first(
    tokens, cotangent, seq_source, source_weight, input_weight, gelu_weight, output_weight,
    decay_gates, input_gates, channel_params, norm_gains, mlp_gate,
):
    args = (
        tokens, cotangent, seq_source, source_weight, input_weight, gelu_weight, output_weight,
        decay_gates, input_gates, channel_params, norm_gains, mlp_gate,
    )
    if not shape_fits():
        return plain_fetch_first(*args)
    rows, width = tokens.shape[1:]
    drows, local = input_weight.shape[0], input_weight.shape[1] // 4
    pairs = [v.reshape(drows, 4, local) for v in (input_weight, gelu_weight)]
    ig = jnp.concatenate(pairs, axis=2).transpose(1, 0, 2)
    per = decay_gates.shape[1] // BLOCK
    gates = [v.reshape(8, per, BLOCK) for v in (decay_gates, input_gates)]
    gates = jnp.concatenate(gates, axis=2)
    gates = jnp.pad(gates, ((0, 0), (0, 16 - per), (0, LANES - 2 * BLOCK))).reshape(4, 32, LANES)
    small = jnp.pad(channel_params[:, 0], ((0, 0), (0, drows - channel_params.shape[2])))
    small = jnp.pad(jnp.concatenate([small, norm_gains], axis=0), ((0, 6), (0, 0)))
    smem = pl.BlockSpec(memory_space=pltpu.SMEM)
    return run_kernel(
        first_kernel,
        "fetch_first",
        [
            ((8, rows, width), BF),
            ((width, 2 * local), BF),
            ((local, width), BF),
            ((LANES, 2 * LANES), BF),
            ((8, LANES), F32),
            ((2, width), F32),
            ((8, rows, width), BF),
            ((rows, width), F32),
            ((rows, width), BF),
            ((width, mlp_gate.shape[1] // 4), BF),
        ],
        [ANY] * 3 + [VMEM] * 3 + [ANY, VMEM, ANY, ANY],
        [smem, smem, ANY, VMEM] + [ANY] * 5,
        [
            pltpu.VMEM((512, LANES), BF),
            pltpu.VMEM((256, 128), BF),
            pltpu.VMEM((2, rows, width), BF),
        ]
        + semaphores(80, 16),
        1,
        (source_weight, seq_source, tokens, cotangent, ig, output_weight, gates, small, mlp_gate),
        61,
    )


def reduce_and_fetch(mixed, w_o, own, gain, mlp_up, mlp_down):
    if not shape_fits():
        return plain_reduce_and_fetch(mixed, w_o, own, gain, mlp_up, mlp_down)
    rows, width = own.shape
    ff = mlp_up.shape[1] // 4
    return run_kernel(
        second_kernel,
        "reduce_and_fetch",
        [((rows, width), F32), ((8, rows, width), BF), ((width, ff), BF), ((ff, width), BF)],
        [VMEM] + [ANY] * 3,
        [VMEM] * 4 + [ANY] * 2,
        scatter_buffers(rows, width, True) + [pltpu.VMEM((rows, width), BF)] + semaphores(64, 16),
        2,
        (mixed, w_o, own, gain, mlp_up, mlp_down),
    )


def reduce_and_return(weights, middle, dout, gain, dm, hidden, n2, dgm, dup, drows):
    if not shape_fits():
        return plain_reduce_and_return(
            weights, middle, dout, gain, dm, hidden, n2, dgm, dup, drows
        )
    rows, width = middle.shape
    ff = hidden.shape[1]
    return run_kernel(
        third_kernel,
        "reduce_and_return",
        [
            ((rows, width), F32),
            ((8, width), F32),
            ((8, rows, width), BF),
            ((drows, 4 * ff), F32),
            ((4 * ff, drows), F32),
            ((8, rows, width), BF),
        ],
        [VMEM, VMEM, ANY] + [VMEM] * 2 + [ANY],
        [VMEM] * 2 + [ANY] * 3 + [VMEM] + [ANY, VMEM] * 2 + [VMEM],
        scatter_buffers(rows, width, True)
        + grad_buffers(2 * drows, ff, 8 * rows) * 2
        + [pltpu.VMEM((rows, width), BF), pltpu.VMEM((ff, width), BF)]
        + [pltpu.VMEM((rows, width), F32)] * 2
        + semaphores(56, 56),
        3,
        (*weights, middle, dout, gain, dm, hidden, n2, dgm, dup),
        61,
    )


def return_last(w_ig, own, dr1, gain, do, mixed, n1, dboth, g_gates, drows):
    if not shape_fits():
        return plain_return_last(w_ig, own, dr1, gain, do, mixed, n1, dboth, g_gates, drows)
    rows, width = own.shape
    local, unit = dboth.shape[1] // 2, g_gates.shape[0] // 16
    return run_kernel(
        fourth_kernel,
        "return_last",
        [
            ((2, rows, width), F32),
            ((8, width), F32),
            ((drows, 4 * local), F32),
            ((drows, 4 * local), F32),
            ((4 * local, drows), F32),
            ((4, unit, 128), BF),
        ],
        [VMEM] * 6,
        [VMEM] * 4 + [ANY, VMEM] * 2 + [VMEM],
        scatter_buffers(rows, width, True)
        + grad_buffers(2 * drows, mixed.shape[1], 8 * rows)
        + grad_buffers(2 * drows, 2 * local, 8 * rows)
        + grad_buffers(2 * unit, 128)
        + [pltpu.VMEM((rows, width), BF)] * 2
        + semaphores(64, 48),
        4,
        (w_ig, own, dr1, gain, do, mixed, n1, dboth, g_gates),
        60,
    )


def shape_fits():
    return all(lax.axis_size(n) == 2 for n in AXES)


def plain_fetch_first(
    tokens, cotangent, seq_source, source_weight, input_weight, gelu_weight, output_weight,
    decay_gates, input_gates, channel_params, norm_gains, mlp_gate,
):
    exchange = Tokens()
    dxn, zhn, mp = lax.axis_size("dx"), lax.axis_size("zh"), exchange.mp
    group = dxn * 2 * zhn * 2
    local = input_weight.shape[1] // 4
    heads, piece = decay_gates.shape[0] // 4, decay_gates.shape[1]
    shards = ("dx", "dc", "zh", "zl")
    own = lax.dynamic_index_in_dim(tokens, mp, 0, keepdims=False)
    sources = jnp.arange(source_weight.shape[0], dtype=jnp.int32)
    scales = jnp.sum(jnp.where(seq_source == sources[None], source_weight[None], 0.0), axis=1)
    douts = cotangent.astype(F32) * scales[:, None, None]
    small = jnp.concatenate([channel_params.reshape(-1), norm_gains.reshape(-1)])
    small = lax.all_to_all(
        jnp.broadcast_to(small[None], (group, small.size)), shards, 0, 0, tiled=True
    )
    nch = channel_params.size
    channels = small[:, :nch].reshape(group, 8, -1).transpose(1, 0, 2).reshape(8, -1)
    slot = exchange.dc * 2 + exchange.zl
    channels = lax.dynamic_slice_in_dim(channels, slot * local, local, 1).astype(F32)
    gains = small[:, nch:].reshape(group, 2, -1).transpose(1, 0, 2).reshape(2, -1).astype(F32)
    gates = jnp.stack([decay_gates, input_gates]).reshape(2, 4, heads, piece)
    gates = gates.transpose(1, 0, 2, 3).reshape(2, 1, 2, 1, 2 * heads * piece)
    gates = jnp.broadcast_to(gates, (2, zhn, 2, dxn, 2 * heads * piece))
    gates = gates.transpose(3, 0, 1, 2, 4).reshape(group, 2 * heads * piece)
    gates = lax.all_to_all(gates, shards, 0, 0, tiled=True)
    gates = gates.reshape(group, 2 * heads, piece).transpose(1, 0, 2)
    gates = gates.reshape(2, heads, BLOCK, BLOCK)
    zero = jnp.zeros((BLOCK, BLOCK), BF)
    blocks = [
        [gates[g, h] if k == h else zero for g in range(2) for k in range(heads)]
        for h in range(heads)
    ]
    return (
        exchange.gather(own).reshape((8,) + own.shape),
        fetch_weight([input_weight, gelu_weight], 4),
        fetch_weight([output_weight.T], 4).T,
        jnp.concatenate([jnp.concatenate(v, axis=1) for v in blocks], axis=0),
        channels,
        gains,
        exchange.gather(lax.dynamic_index_in_dim(douts, mp, 0, keepdims=False).astype(BF)).reshape(
            (8,) + own.shape
        ),
        lax.dynamic_index_in_dim(douts, mp, 0, keepdims=False),
        own,
        fetch_weight([mlp_gate], 4),
    )


def plain_reduce_and_fetch(mixed, w_o, own, gain, mlp_up, mlp_down):
    exchange = Tokens()
    middle = own.astype(F32) + exchange.scatter(dot(mixed, w_o, NN, BF))
    normed = (middle * inverse_rms(middle) * gain).astype(BF)
    return (
        middle,
        exchange.gather(normed).reshape((8,) + own.shape),
        fetch_weight([mlp_up], 4),
        fetch_weight([mlp_down.T], 4).T,
    )


def columns(share, at, count):
    return share[:, :, at : at + count].astype(F32).transpose(1, 0, 2).reshape(-1, 4 * count)


def both_batches(rows):
    mp = lax.axis_index("mp")
    other = lax.ppermute(rows, "mp", [(0, 1), (1, 0)])
    return jnp.stack([jnp.where(mp == 0, rows, other), jnp.where(mp == 0, other, rows)])


def plain_reduce_and_return(weights, middle, dout, gain, dm, hidden, n2, dgm, dup, drows):
    exchange = Tokens()
    w_g, w_u, w_d = weights
    ff = hidden.shape[1]
    total = exchange.scatter((dot(dgm, w_g, NT) + dot(dup, w_u, NT)).astype(BF))
    change, gain_rows = norm_back(middle, gain, total)
    dr1 = dout + change
    gate = return_grad(dot(n2, dgm, TN, BF), drows)
    down = return_grad(dot(dm, hidden, TN, BF), drows)
    return (
        dr1,
        jnp.sum(gain_rows, axis=0, keepdims=True),
        exchange.gather(dr1.astype(BF)).reshape((8,) + dr1.shape),
        columns(gate, 0, ff),
        columns(down, 0, ff).T,
        dot(hidden, w_d, NN, BF).reshape((8,) + dr1.shape),
    )


def plain_return_last(w_ig, own, dr1, gain, do, mixed, n1, dboth, g_gates, drows):
    exchange = Tokens()
    local = dboth.shape[1] // 2
    total = exchange.scatter(dot(dboth, w_ig, NT, BF))
    change, gain_rows = norm_back(own.astype(F32), gain, total)
    group = n1.shape[1] // drows
    wide = return_grad(dot(n1, dboth, TN, BF), drows)
    out = return_grad(dot(do, mixed, TN, BF), drows)
    return (
        both_batches(dr1 + change),
        jnp.sum(gain_rows, axis=0, keepdims=True),
        columns(wide, 0, local),
        columns(wide, local, local),
        columns(out, 0, local).T,
        return_grad(g_gates, g_gates.shape[0] // group),
    )


def scan_body(reverse, a_ref, b_ref, p_ref, h_ref):
    length, width = a_ref.shape[1], a_ref.shape[2]
    row = lax.broadcasted_iota(jnp.int32, (8, width), 0)

    def tile(i, carry):
        ca, ch = carry
        at = (length // 8 - 1 - i if reverse else i) * 8
        at = pl.multiple_of(at, 8)
        a = a_ref[0, pl.ds(at, 8), :]
        b = b_ref[0, pl.ds(at, 8), :]
        for step in (1, 2, 4):
            if reverse:
                inside = row < 8 - step
                shift = 8 - step
            else:
                inside = row >= step
                shift = step
            sa = jnp.where(inside, pltpu.roll(a, shift, 0), 1.0)
            sb = jnp.where(inside, pltpu.roll(b, shift, 0), 0.0)
            b = b + a * sb
            a = a * sa
        h = b + a * ch
        p = a * ca
        h_ref[0, pl.ds(at, 8), :] = h
        p_ref[0, pl.ds(at, 8), :] = p
        last = 0 if reverse else 7
        return p[last : last + 1, :], h[last : last + 1, :]

    lax.fori_loop(
        0,
        length // 8,
        tile,
        (jnp.ones((1, width), F32), jnp.zeros((1, width), F32)),
    )


def local_scan(a, b, reverse):
    segs, length, width = a.shape
    spec = pl.BlockSpec((1, length, width), lambda s: (s, 0, 0))
    return pl.pallas_call(
        lambda *refs: scan_body(reverse, *refs),
        grid=(segs,),
        in_specs=[spec, spec],
        out_specs=[spec, spec],
        out_shape=[jax.ShapeDtypeStruct(a.shape, F32)] * 2,
        cost_estimate=pl.CostEstimate(
            flops=20 * a.size, bytes_accessed=16 * a.size, transcendentals=0
        ),
    )(a, b)


def carried(product, state, reverse):
    count = lax.axis_size("zh")
    if count == 2:
        return lax.ppermute(state, "zh", [(1, 0)] if reverse else [(0, 1)])
    here = lax.axis_index("zh")
    pairs = lax.all_gather(jnp.stack([product, state]), "zh")
    total = jnp.zeros_like(state)
    for k in range(count):
        at = count - 1 - k if reverse else k
        reached = at > here if reverse else at < here
        total = jnp.where(reached, pairs[at, 1] + pairs[at, 0] * total, total)
    return total


def from_behind(x, by):
    count = lax.axis_size("zh")
    return lax.ppermute(
        x, "zh", [(i, i + by) for i in range(count) if 0 <= i + by < count]
    )


def inverse_rms(values):
    return lax.rsqrt(jnp.mean(values * values, axis=-1, keepdims=True) + EPSILON)


def gelu(v):
    return jax.nn.gelu(v, approximate=True)


def gelu_both(v):
    c = 0.7978845608028654
    t = jnp.tanh(c * (v + 0.044715 * v * v * v))
    value = 0.5 * v * (1.0 + t)
    slope = 0.5 * (1.0 + t) + 0.5 * v * (1.0 - t * t) * c * (1.0 + 3 * 0.044715 * v * v)
    return value, slope


def dot(a, b, dims, out=F32):
    r = lax.dot_general(a, b, (dims, ((), ())), preferred_element_type=F32)
    return r.astype(out)


NN = ((1,), (0,))
NT = ((1,), (1,))
TN = ((0,), (0,))


def minus_expm1(v):
    series = 1.0 + v / 8.0
    for k in (7.0, 6.0, 5.0, 4.0, 3.0, 2.0):
        series = 1.0 + v * (1.0 / k) * series
    return jnp.where(v > -0.4, -v * series, 1.0 - jnp.exp(v))


def loop(count, body, unroll=1):
    def step(i, carry):
        body(i)
        return carry

    lax.fori_loop(0, count, step, 0, unroll=unroll)


def tile_scan(a, b, row, reverse):
    for step in (1, 2, 4):
        inside = row < 8 - step if reverse else row >= step
        shift = 8 - step if reverse else step
        sa = jnp.where(inside, pltpu.roll(a, shift, 0), 1.0)
        sb = jnp.where(inside, pltpu.roll(b, shift, 0), 0.0)
        b = b + a * sb
        a = a * sa
    return a, b


def eight(i):
    return pl.multiple_of(i * 8, 8)


def recur_forward_kernel(
    tok_ref, wig_ref, blocks_ref, ch_ref, gain_ref,
    n1_out, xs_out, gy_out, u_out, siga_out, sigi_out, decay_out, states, mixed,
    xs, gy, u, siga, sigi, decay, run, logits, n1, both, halo, ends, inc, tok, sems,
    send, recv, local_sems,
):
    p = Place()
    links = Links(send, recv, local_sems)
    rows, local = tok_ref.shape[1], wig_ref.shape[1] // 2
    zh = p.zh
    greet([p.peer(zh=1)])

    def read(b):
        return pltpu.make_async_copy(tok_ref.at[b], tok.at[b % 2], sems.at[4 + b % 2])

    read(0).start()
    lane = lax.broadcasted_iota(jnp.int32, (1, LANES), 1)
    real = lane < local

    def project(b):
        read(b).wait()

        @pl.when(b < 7)
        def _():
            read(b + 1).start()

        def normalise(at):
            value = tok[b % 2, at, :].astype(F32)
            inv = lax.rsqrt(jnp.mean(value * value, axis=-1, keepdims=True) + EPSILON)
            n1[b % 2, at, :] = (value * inv * gain_ref[...]).astype(BF)

        def write(i, at):
            return pltpu.make_async_copy(n1.at[i], n1_out.at[at], sems.at[i])

        @pl.when(b >= 2)
        def _():
            write(b % 2, b - 2).wait()

        chunks(rows, normalise)
        write(b % 2, b).start()
        both[...] = dot(n1[b % 2], wig_ref[...], NN)
        seg, zl = b // 2, b % 2

        def split(at):
            v = both[at, :]
            xb = jnp.where(real, v[:, :LANES], 0.0).astype(BF).astype(F32)
            xs[seg, pl.ds(pl.multiple_of(8 + zl * rows + at.start, 8), CHUNK), :] = xb
            rest = pltpu.roll(v, v.shape[1] - local, 1)[:, :LANES]
            gy[b, at, :] = jnp.where(real, rest, 0.0)

        chunks(rows, split)

    loop(8, project)
    for b in (6, 7):
        pltpu.make_async_copy(n1.at[b % 2], n1_out.at[b], sems.at[b % 2]).wait()

    def to_partner(src, dst):
        at = links.pair()
        links.start(src, dst, at, p.peer(zh=1))
        return at

    at = to_partner(xs.at[:, pl.ds(2 * rows, 8)], halo)
    kept = [links.keep(gy, gy_out)]
    links.arrived(halo, at)
    row = lax.broadcasted_iota(jnp.int32, (8, LANES), 0)
    soft = ch_ref[0:1, :]

    def head(seg):
        xs[seg, 0:8, :] = jnp.where(zh == 1, halo[seg], 0.0)

    loop(4, head)

    def convolve(b):
        seg, zl = b // 2, b % 2

        def body(at):
            v = xs[seg, pl.ds(pl.multiple_of(zl * rows + at.start, 8), CHUNK + 8), :]
            total = ch_ref[3:4, :] + ch_ref[4:5, :] * v[8:]
            for k in (1, 2, 3):
                total = total + ch_ref[4 + k : 5 + k, :] * pltpu.roll(v, k, 0)[8:]
            u[b, at, :] = total.astype(BF)

        chunks(rows, body)
        logits[b] = dot(u[b], blocks_ref[...], NN)

    loop(8, convolve)

    def tile(i, carry, zl):
        at = pl.ds(pl.multiple_of(i * CHUNK, CHUNK), CHUNK)
        out = []
        for seg in range(4):
            b = seg * 2 + zl
            cp, ch = carry[seg]
            sa = jax.nn.sigmoid(logits[b, at, :LANES] + ch_ref[1:2, :])
            si = jax.nn.sigmoid(logits[b, at, LANES:] + ch_ref[2:3, :])
            log_decay = -DECAY_SCALE * sa * soft
            a = jnp.exp(log_decay)
            drive = jnp.sqrt(minus_expm1(2.0 * log_decay)) * si * u[b, at, :].astype(F32)
            siga[b, at, :] = sa
            sigi[b, at, :] = si
            decay[b, at, :] = a
            for k in range(2):
                pa, h = tile_scan(a[k * 8 : k * 8 + 8], drive[k * 8 : k * 8 + 8], row, False)
                h = h + pa * ch
                pa = pa * cp
                run[b, pl.ds(eight(i * 2 + k), 8), :] = pa
                there = pl.ds(pl.multiple_of(8 + zl * rows + i * CHUNK + k * 8, 8), 8)
                states[seg, there, :] = h
                cp, ch = pa[7:8, :], h[7:8, :]
            out.append((cp, ch))
        return tuple(out)

    kept += [links.keep(xs, xs_out), links.keep(u, u_out)]
    carry = ((jnp.ones((1, LANES), F32), jnp.zeros((1, LANES), F32)),) * 4
    for zl in range(2):
        carry = lax.fori_loop(0, rows // CHUNK, functools.partial(tile, zl=zl), carry)
    ends[...] = jnp.zeros_like(ends)
    for seg in range(4):
        ends[seg : seg + 1, :] = carry[seg][1]
    at = to_partner(ends, inc)
    kept += [links.keep(siga, siga_out), links.keep(sigi, sigi_out), links.keep(decay, decay_out)]
    links.arrived(inc, at)

    def finish(b):
        seg, zl = b // 2, b % 2
        start = jnp.where(zh == 1, inc[pl.ds(seg, 1), :], 0.0)

        @pl.when(zl == 0)
        def _():
            states[seg, 0:8, :] = jnp.broadcast_to(start, (8, LANES))

        def state(at):
            there = pl.ds(pl.multiple_of(8 + zl * rows + at.start, 8), CHUNK)
            h = states[seg, there, :] + run[b, at, :] * start
            states[seg, there, :] = h
            v = gy[b, at, :]
            t = jnp.tanh(0.7978845608028654 * (v + 0.044715 * v * v * v))
            mixed[b, at, :] = (0.5 * v * (1.0 + t) * h).astype(BF)

        chunks(rows, state)

    loop(8, finish)
    for copy in kept:
        copy.wait()
    links.finish()


def recur_backward_kernel(
    do_ref, wo_ref, blocks_ref, ch_ref,
    xs_in, gy, u_in, siga_in, sigi_in, decay_in, states, rows_ref, mid_in, n2_ref, dup_ref,
    dboth_out, gb_out, ch_out, block_out, up_out,
    xs, u, siga, sigi, decay, mid_ref,
    dh, after, dgy, dlog_ref, du, dboth, halo, ends, inc, do, final, sems,
    *scratch,
):
    p = Place()
    links = Links(*scratch[-3:])
    rows, local = do_ref.shape[1], wo_ref.shape[0]
    zh = p.zh
    greet(weight_peers(p))
    scatter = RowScatter(p, links, rows_ref, scratch[:5])
    up = GradScatter(p, links, n2_ref, dup_ref, scratch[5:12], GradScatter.EARLY)

    def read(b):
        return pltpu.make_async_copy(do_ref.at[b], do.at[b % 2], sems.at[4 + b % 2])

    read(0).start()
    kept = {
        name: links.keep(src, dst)
        for name, src, dst in (
            ("decay", decay_in, decay),
            ("siga", siga_in, siga),
            ("sigi", sigi_in, sigi),
            ("u", u_in, u),
            ("xs", xs_in, xs),
            ("mid", mid_in, mid_ref),
        )
    }
    scatter.begin()
    up.begin(1)
    scatter.across_y()
    ch_out[...] = jnp.zeros_like(ch_out)
    gb_out[...] = jnp.zeros_like(gb_out)
    soft = ch_ref[0:1, :]

    def to_partner(src, dst):
        at = links.pair()
        links.start(src, dst, at, p.peer(zh=1))
        return at

    def upstream(b):
        seg, zl = b // 2, b % 2
        dh[b, :, local:] = jnp.zeros((rows, LANES - local), F32)
        read(b).wait()

        @pl.when(b < 7)
        def _():
            read(b + 1).start()

        dh[b, :, :local] = dot(do[b % 2], wo_ref[...], NT)

        def split(at):
            value, slope = gelu_both(gy[b, at, :])
            dz = dh[b, at, :]
            h = states[seg, pl.ds(pl.multiple_of(8 + zl * rows + at.start, 8), CHUNK), :]
            dh[b, at, :] = dz * value
            dgy[b, at, :] = (dz * h * slope).astype(BF)

        chunks(rows, split)

    loop(8, upstream)
    up.begin(0)
    row = lax.broadcasted_iota(jnp.int32, (8, LANES), 0)
    one = jnp.ones((1, LANES), F32)
    ends[...] = jnp.zeros_like(ends)

    def tile(i, carry, zl):
        at = pl.ds(eight(rows // 8 - 1 - i), 8)
        out = []
        for seg in range(4):
            b = seg * 2 + zl
            cp, cg, following = carry[seg]
            a = decay[b, at, :]
            shifted = jnp.where(row == 7, following, pltpu.roll(a, 7, 0))
            pa, g = tile_scan(shifted, dh[b, at, :], row, True)
            g = g + pa * cg
            pa = pa * cp
            dh[b, at, :] = g
            after[b, at, :] = pa
            out.append((pa[0:1, :], g[0:1, :], a[0:1, :]))
        return tuple(out)

    carry = ((one, jnp.zeros((1, LANES), F32), one),) * 4
    kept["decay"].wait()
    for zl in (1, 0):
        carry = lax.fori_loop(0, rows // 8, functools.partial(tile, zl=zl), carry)
    for seg in range(4):
        ends[seg : seg + 1, :] = carry[seg][1] * carry[seg][2]
    at = to_partner(ends, inc)
    links.arrived(inc, at)
    scatter.across_z()
    up.across(0)

    def gradients(b):
        seg, zl = b // 2, b % 2
        later = jnp.where(zh == 0, inc[pl.ds(seg, 1), :], 0.0)

        def body(at):
            window = states[seg, pl.ds(pl.multiple_of(zl * rows + at.start, 8), CHUNK + 8), :]
            previous = pltpu.roll(window, 1, 0)[8:]
            g = dh[b, at, :] + after[b, at, :] * later
            sa, si, a = siga[b, at, :], sigi[b, at, :], decay[b, at, :]
            uf = u[b, at, :].astype(F32)
            root = jnp.sqrt(minus_expm1((-2.0 * DECAY_SCALE) * sa * soft))
            gu = g * uf
            gr = g * root
            d_log = a * (g * previous - gu * si * a / root)
            d_log = jnp.where(real, d_log, 0.0)
            dra = (d_log * (-DECAY_SCALE * soft) * sa * (1.0 - sa)).astype(BF)
            dri = (gr * uf * si * (1.0 - si)).astype(BF)
            du[seg, pl.ds(pl.multiple_of(zl * rows + at.start, 8), CHUNK), :] = gr * si
            dlog_ref[at, :LANES] = dra
            dlog_ref[at, LANES:] = dri
            for k, v in enumerate((d_log * sa, dra.astype(F32), dri.astype(F32))):
                sums[k] = sums[k] + fold(v)

        sums = [jnp.zeros((8, LANES), F32) for _ in range(3)]
        chunks(rows, body)
        for k in range(3):
            ch_out[k] += sums[k]
        d = dlog_ref[...]
        there = pl.ds(pl.multiple_of(zl * rows, 8), rows)
        du[seg, there, :] += dot(d, blocks_ref[...], NT)
        gb_out[...] += dot(u[b], d, TN)

    lane = lax.broadcasted_iota(jnp.int32, (1, LANES), 1)
    real = lane < local
    for name in ("siga", "sigi", "u"):
        kept[name].wait()
    loop(8, gradients)
    at = to_partner(du.at[:, pl.ds(0, 8)], halo)
    up.across(1)

    def write(i, at, src, dst, base):
        return pltpu.make_async_copy(src.at[i], dst.at[at], sems.at[base + i])

    def convolve(i, zl):
        seg = i
        b = i * 2 + zl
        slot = i % 2

        @pl.when(i >= 2)
        def _():
            write(slot, b - 4, dboth, dboth_out, 0).wait()

        def body(at):
            start = pl.multiple_of(zl * rows + at.start, 8)
            v = du[seg, pl.ds(start, CHUNK + 8), :]
            x = xs[seg, pl.ds(start, CHUNK + 8), :]
            here = v[:CHUNK]
            total = ch_ref[4:5, :] * here
            sums[0] = sums[0] + fold(here)
            sums[1] = sums[1] + fold(here * x[8:])
            for k in (1, 2, 3):
                total = total + ch_ref[4 + k : 5 + k, :] * pltpu.roll(v, CHUNK + 8 - k, 0)[:CHUNK]
                sums[1 + k] = sums[1 + k] + fold(here * pltpu.roll(x, k, 0)[8:])
            wide = 2 * local - LANES
            zeros = jnp.zeros((CHUNK, wide), F32)
            left = jnp.concatenate([total, zeros], axis=1)
            right = jnp.concatenate([dgy[b, at, :].astype(F32), zeros], axis=1)
            dboth[slot, at, :] = (left + pltpu.roll(right, local, 1)).astype(BF)

        sums = [jnp.zeros((8, LANES), F32) for _ in range(5)]
        chunks(rows, body)
        for k in range(5):
            ch_out[3 + k] += sums[k]
        write(slot, b, dboth, dboth_out, 0).start()

    def drain(zl):
        for i in (2, 3):
            write(i % 2, i * 2 + zl, dboth, dboth_out, 0).wait()

    kept["xs"].wait()
    kept["mid"].wait()
    loop(4, functools.partial(convolve, zl=0))
    drain(0)
    links.arrived(halo, at)

    def tail(seg):
        du[seg, pl.ds(2 * rows, 8), :] = jnp.where(zh == 0, halo[seg], 0.0)

    loop(4, tail)
    scatter.arrive()

    def add(at):
        final[at, :] = (mid_ref[at, :] + scatter.total(at)).astype(BF)

    chunks(rows, add)
    at = links.pair()
    links.start(final, block_out.at[p.mp], at, p.peer(mp=1))
    own = links.keep(final, block_out.at[p.mp])
    loop(4, functools.partial(convolve, zl=1))
    up.last(0)
    drain(1)
    up.last(1)
    up.end()
    ff = up.result.shape[2]
    for j in range(4):
        up_out[:, j * ff : (j + 1) * ff] = up.result[j].astype(F32)
    own.wait()
    links.arrived(block_out.at[1 - p.mp], at)
    links.finish()


def recur_forward(tokens, w_ig, blocks, channels, gain):
    if not shape_fits():
        return plain_recur_forward(tokens, w_ig, blocks, channels, gain)
    rows, width = tokens.shape[1:]
    local = w_ig.shape[1] // 2
    table = jnp.concatenate([jax.nn.softplus(-channels[0:1]), channels[1:]], axis=0)
    f, h = (8, rows, LANES), (4, 2 * rows + 8, LANES)
    n1, *saved = run_kernel(
        recur_forward_kernel,
        "recur_forward",
        [(tokens.shape, BF), (h, F32), (f, F32), (f, BF)]
        + [(f, F32)] * 3
        + [(h, F32), (f, BF)],
        [ANY] * 7 + [VMEM] * 2,
        [ANY] + [VMEM] * 4,
        [
            pltpu.VMEM(h, F32),
            pltpu.VMEM(f, F32),
            pltpu.VMEM(f, BF),
            pltpu.VMEM(f, F32),
            pltpu.VMEM(f, F32),
            pltpu.VMEM(f, F32),
            pltpu.VMEM(f, F32),
            pltpu.VMEM((8, rows, 2 * LANES), F32),
            pltpu.VMEM((2, rows, width), BF),
            pltpu.VMEM((rows, 2 * local), F32),
            pltpu.VMEM((4, 8, LANES), F32),
            pltpu.VMEM((8, LANES), F32),
            pltpu.VMEM((8, LANES), F32),
            pltpu.VMEM((2, rows, width), BF),
        ]
        + semaphores(6, 2)[:1]
        + semaphores(2, 6),
        5,
        (tokens, w_ig, blocks, table, gain),
        61,
    )
    *saved, mixed = saved
    return n1.reshape(-1, width), mixed.reshape(-1, LANES), (table, blocks, *saved)


def recur_backward(do, saved, w_o, channels, out_part, middle, n2, dup, drows):
    if not shape_fits():
        return plain_recur_backward(do, saved, w_o, channels, out_part, middle, n2, dup, drows)
    ff = dup.shape[1]
    table, wide, xs, gy, u, siga, sigi, decay, states = saved
    rows, width = do.shape[1:]
    local = w_o.shape[0]
    f, h = (8, rows, LANES), (4, 2 * rows + 8, LANES)
    dboth, g_blocks, sums, block_out, g_up = run_kernel(
        recur_backward_kernel,
        "recur_backward",
        [
            ((8, rows, 2 * local), BF),
            ((LANES, 2 * LANES), F32),
            ((8, 8, LANES), F32),
            ((2, rows, width), BF),
            ((drows, 4 * ff), F32),
        ],
        [ANY] + [VMEM] * 2 + [ANY, VMEM],
        [ANY] + [VMEM] * 3 + [ANY, VMEM] + [ANY] * 4 + [VMEM] + [ANY] * 3 + [VMEM],
        [
            pltpu.VMEM(h, F32),
            pltpu.VMEM(f, BF),
            pltpu.VMEM(f, F32),
            pltpu.VMEM(f, F32),
            pltpu.VMEM(f, F32),
            pltpu.VMEM((rows, width), F32),
            pltpu.VMEM(f, F32),
            pltpu.VMEM(f, F32),
            pltpu.VMEM(f, BF),
            pltpu.VMEM((rows, 2 * LANES), BF),
            pltpu.VMEM(h, F32),
            pltpu.VMEM((2, rows, 2 * local), BF),
            pltpu.VMEM((4, 8, LANES), F32),
            pltpu.VMEM((8, LANES), F32),
            pltpu.VMEM((8, LANES), F32),
            pltpu.VMEM((2, rows, width), BF),
            pltpu.VMEM((rows, width), BF),
        ]
        + semaphores(6, 2)[:1]
        + scatter_buffers(rows, width)
        + grad_buffers(2 * drows, ff, 8 * rows)
        + semaphores(32, 32),
        6,
        (do, w_o, wide, table, xs, gy, u, siga, sigi, decay, states)
        + (out_part, middle, n2, dup),
        61,
    )
    sums = jnp.sum(sums, axis=1)[:, :local]
    dlam = sums[0] * DECAY_SCALE * jax.nn.sigmoid(-channels[0, :local])
    g_blocks = jnp.concatenate(
        [g_blocks[:local, g * LANES : g * LANES + local] for g in (0, 1)], axis=1
    )
    return (
        dboth.reshape(-1, 2 * local),
        g_blocks,
        jnp.concatenate([dlam[None], sums[1:]], axis=0),
        block_out,
        g_up,
    )


def plain_recur_forward(tokens, w_ig, blocks, channels, gain):
    length, local, width = tokens.shape[1], w_ig.shape[1] // 2, tokens.shape[2]
    wide = tokens.reshape(-1, width).astype(F32)
    n1 = (wide * inverse_rms(wide) * gain).astype(BF)
    both = dot(n1, w_ig, NN)
    xb = both[:, :local].astype(BF).reshape(4, 2 * length, local)
    gy = both[:, local:].reshape(4, 2 * length, local)
    rim = from_behind(xb[:, -3:], 1)
    padded = jnp.concatenate([rim, xb], axis=1).astype(F32)
    conv = channels[3]
    for k in range(4):
        conv = conv + channels[4 + k] * padded[:, 3 - k : 3 - k + 2 * length]
    u = conv.astype(BF)
    logits = dot(u.reshape(-1, local), blocks, NN).reshape(4, 2 * length, 2 * local)
    sig_a = jax.nn.sigmoid(logits[..., :local] + channels[1])
    sig_i = jax.nn.sigmoid(logits[..., local:] + channels[2])
    log_decay = -DECAY_SCALE * sig_a * jax.nn.softplus(-channels[0])
    decay = jnp.exp(log_decay)
    root = jnp.sqrt(-jnp.expm1(2.0 * log_decay))
    running, state = local_scan(decay, root * sig_i * u.astype(F32), False)
    incoming = carried(running[:, -1], state[:, -1], False)
    states = state + running * incoming[:, None]
    gelu_y, slope_y = gelu_both(gy)
    mixed = (gelu_y * states).astype(BF).reshape(-1, local)
    saved = (blocks, padded, u, sig_a, sig_i, decay, root, running, incoming, states)
    return n1, mixed, saved + (gelu_y, slope_y)


def plain_recur_backward(do, saved, w_o, channels, out_part, middle, n2, dup, drows):
    blocks, padded, u, sig_a, sig_i, decay, root, running, incoming, states = saved[:10]
    gelu_y, slope_y = saved[10:]
    length, local, width = do.shape[1], w_o.shape[0], do.shape[2]
    dz = dot(do.reshape(-1, width), w_o, NT).reshape(4, 2 * length, local)
    dh = dz * gelu_y
    dgy = (dz * states * slope_y).astype(BF)
    ones = jnp.ones_like(decay[:, :1])
    after, adjoint = local_scan(jnp.concatenate([decay[:, 1:], ones], axis=1), dh, True)
    later = carried(running[:, -1], decay[:, 0] * adjoint[:, 0], True)
    adjoint = adjoint + after * later[:, None]
    previous = jnp.concatenate([incoming[:, None], states[:, :-1]], axis=1)
    soft, uf = jax.nn.softplus(-channels[0]), u.astype(F32)
    d_root = adjoint * sig_i * uf
    d_log = adjoint * previous * decay - d_root * decay * decay / root
    dra = (d_log * (-DECAY_SCALE * soft) * sig_a * (1.0 - sig_a)).astype(BF)
    dri = (adjoint * root * uf * sig_i * (1.0 - sig_i)).astype(BF)
    dlam = jnp.sum(d_log * sig_a, axis=(0, 1)) * DECAY_SCALE * jax.nn.sigmoid(-channels[0])
    dlogits = jnp.concatenate([dra, dri], axis=2).reshape(-1, 2 * local)
    g_blocks = dot(u.reshape(-1, local), dlogits, TN)
    du = adjoint * root * sig_i + dot(dlogits, blocks, NT).reshape(4, 2 * length, local)
    zeros = jnp.zeros((4, 3, local), F32)
    spread = jnp.concatenate([zeros, du, zeros], axis=1)
    dpad = jnp.zeros((4, 2 * length + 3, local), F32)
    taps = []
    for k in range(4):
        dpad = dpad + channels[4 + k] * spread[:, k : k + 2 * length + 3]
        taps.append(jnp.sum(du * padded[:, 3 - k : 3 - k + 2 * length], axis=(0, 1)))
    back = from_behind(dpad[:, :3], -1)
    dxb = dpad[:, 3:] + jnp.concatenate(
        [jnp.zeros((4, 2 * length - 3, local), F32), back], axis=1
    )
    dboth = jnp.concatenate([dxb.astype(BF), dgy], axis=2).reshape(-1, 2 * local)
    sums = [jnp.sum(v.astype(F32), axis=(0, 1)) for v in (dra, dri, du)]
    result = (middle + Tokens().scatter(out_part.reshape(-1, width))).astype(BF)
    g_up = columns(return_grad(dot(n2, dup, TN, BF), drows), 0, dup.shape[1])
    small = jnp.stack([dlam] + sums + taps)
    return dboth, g_blocks, small, both_batches(result), g_up


def on_device(
    tokens_in,
    cotangent,
    seq_source,
    source_weight,
    input_weight,
    gelu_weight,
    decay_gates,
    input_gates,
    channel_params,
    norm_gains,
    output_weight,
    mlp_gate,
    mlp_up,
    mlp_down,
):
    sizes = tuple(lax.axis_size(n) for n in AXES)
    dxn, _, zhn, _, _ = sizes
    group = dxn * 2 * zhn * 2
    dc, zl, mp = (lax.axis_index(n) for n in ("dc", "zl", "mp"))
    slot = dc * 2 + zl
    width = tokens_in.shape[3]
    local = input_weight.shape[1] // 4
    heads = decay_gates.shape[0] // 4
    drows = input_weight.shape[0]
    piece = decay_gates.shape[1]

    tokens, w_ig, w_o, blocks, channels, gains, dm, dout, own, w_g = fetch_first(
        tokens_in[:, 0],
        cotangent[:, 0],
        seq_source,
        source_weight,
        input_weight,
        gelu_weight,
        output_weight,
        decay_gates,
        input_gates,
        channel_params,
        norm_gains,
        mlp_gate,
    )

    n1, mixed, saved = recur_forward(tokens, w_ig, blocks, channels, gains[0:1])
    middle, n2, w_u, w_d = reduce_and_fetch(mixed, w_o, own, gains[1:2], mlp_up, mlp_down)

    hidden, dgm, dup = feed_forward(n2, dm, w_g, w_u, w_d)
    n2, dm = n2.reshape(-1, width), dm.reshape(-1, width)
    dr1, gain_two, do, g_gate, g_down, out_part = reduce_and_return(
        (w_g, w_u, w_d), middle, dout, gains[1:2], dm, hidden, n2, dgm, dup, drows
    )
    gain_two = jnp.sum(gain_two, axis=0)

    dboth, g_blocks, channel_grad, block_out, g_up = recur_backward(
        do, saved, w_o, channels, out_part, middle, n2, dup, drows
    )

    g_gates = jnp.stack(
        [
            jnp.stack(
                [
                    g_blocks[
                        h * BLOCK : (h + 1) * BLOCK,
                        g * local + h * BLOCK : g * local + (h + 1) * BLOCK,
                    ]
                    for h in range(heads)
                ]
            )
            for g in range(2)
        ]
    )
    g_gates = g_gates.reshape(2 * heads, group, piece).transpose(1, 0, 2).reshape(group, -1)
    count = g_gates.shape[1]
    unit = (count + 2047) // 2048 * 16
    g_gates = jnp.pad(g_gates, ((0, 0), (0, unit * 128 - count))).astype(BF)
    grad_tokens, gain_one, g_input, g_gelu, g_output, share_gates = return_last(
        w_ig,
        own,
        dr1,
        gains[0:1],
        do.reshape(-1, width),
        mixed,
        n1,
        dboth,
        g_gates.reshape(group * unit, 128),
        drows,
    )
    gain_one = jnp.sum(gain_one, axis=0)
    g_gates = share_gates.reshape(4, -1)[:, :count].astype(F32).reshape(4, 2, heads, piece)
    g_gates = g_gates.transpose(1, 0, 2, 3).reshape(2, 4 * heads, piece)

    per = 4 * local // group
    mine = channel_grad.reshape(8, group // 4, per).transpose(1, 0, 2)
    mine = jnp.where(
        jnp.arange(4, dtype=jnp.int32)[:, None, None, None] == slot, mine[None], 0.0
    ).reshape(group, 1, 8 * per)
    mine = jnp.where(jnp.arange(2, dtype=jnp.int32)[None, :, None] == mp, mine, 0.0)
    both_gains = jnp.stack([gain_one, gain_two]).reshape(2, group, -1).transpose(1, 0, 2)
    both_gains = jnp.broadcast_to(both_gains.reshape(group, 1, -1), (group, 2, 2 * drows))
    sums = jnp.concatenate([both_gains, mine], axis=2).reshape(2 * group, -1)
    sums = jnp.sum(lax.all_to_all(sums, AXES, 0, 0, tiled=True), axis=0)
    g_gains = sums[: 2 * drows].reshape(2, drows)
    g_channels = sums[2 * drows :].reshape(8, 1, per)
    return (
        block_out[:, None],
        grad_tokens[:, None],
        g_input,
        g_gelu,
        g_gates[0],
        g_gates[1],
        g_channels,
        g_gains,
        g_output,
        g_gate,
        g_up,
        g_down,
    )


def solution(mesh):
    dpn, seqn, mpn = (mesh.shape[n] for n in ("dp", "seq", "mp"))
    fine = Mesh(mesh.devices.reshape(dpn // 2, 2, seqn // 2, 2, mpn), AXES)
    dp, seq = ("dx", "dc"), ("zh", "zl")
    shards = dp + seq
    weights = (
        P(shards, "mp"),
        P(shards, "mp"),
        P("mp", shards),
        P("mp", shards),
        P(None, "mp", shards),
        P(None, shards),
        P("mp", shards),
        P(shards, "mp"),
        P(shards, "mp"),
        P("mp", shards),
    )
    rows = P(None, dp, seq, None)
    return jax.shard_map(
        on_device,
        mesh=fine,
        in_specs=(rows, rows, P(None, dp), P()) + weights,
        out_specs=(rows, rows) + weights,
        check_vma=False,
    )
```

```python
import functools

import jax
import jax.numpy as jnp
import numpy as np
from jax import lax
from jax.experimental import pallas as pl
from jax.experimental.pallas import tpu as pltpu
from jax.sharding import Mesh, PartitionSpec as P

WIDTH = 2560
HEADS = 16
BLOCK = WIDTH // HEADS
EPSILON = 1e-06
DECAY_SCALE = 8.0
AXES = ("dx", "dc", "zh", "zl", "mp")
BF = jnp.bfloat16
F32 = jnp.float32
LANES = 384


def swap_pairs(sizes, partner):
    pairs = []
    for flat in range(int(np.prod(sizes))):
        coords = np.unravel_index(flat, sizes)
        pairs.append((flat, int(np.ravel_multi_index(partner(*map(int, coords)), sizes))))
    return pairs


def gather_blocks(x, axis, dim):
    if lax.axis_size(axis) != 2:
        return lax.all_gather(x, axis, axis=dim, tiled=False)
    here = lax.axis_index(axis)
    other = lax.ppermute(x, axis, [(0, 1), (1, 0)])
    low = jnp.where(here == 0, x, other)
    high = jnp.where(here == 0, other, x)
    return jnp.stack([low, high], axis=dim)


def scatter_blocks(x, axis, dim):
    if lax.axis_size(axis) != 2:
        n = x.shape[dim]
        out = lax.psum_scatter(x.astype(BF), axis, scatter_dimension=dim, tiled=True)
        return lax.squeeze(out, [dim]).astype(F32)
    here = lax.axis_index(axis)
    mine = lax.dynamic_index_in_dim(x, here, dim, keepdims=False)
    theirs = lax.dynamic_index_in_dim(x, 1 - here, dim, keepdims=False)
    got = lax.ppermute(theirs.astype(BF), axis, [(0, 1), (1, 0)])
    return mine.astype(F32) + got.astype(F32)


def fetch_weight(shard, parts):
    rows, cols = shard[0].shape[0], None
    pieces = [s.reshape(rows, parts, -1) for s in shard]
    joined = jnp.concatenate(pieces, axis=2) if len(pieces) > 1 else pieces[0]
    cols = joined.shape[2]
    x = jnp.transpose(joined, (1, 0, 2))
    x = lax.all_to_all(x, ("dc", "zl"), 0, 0, tiled=True)
    x = x.reshape(2, 2, rows, cols)
    x = gather_blocks(x, "zh", 1)
    x = gather_blocks(x, "dx", 0)
    return x.reshape(-1, cols)


def return_grad(grad, rows):
    cols = grad.shape[1]
    dxn, zhn = lax.axis_size("dx"), lax.axis_size("zh")
    g = grad.reshape(dxn, 2, zhn, 2, rows, cols)
    g = scatter_blocks(g, "dx", 0)
    g = scatter_blocks(g, "zh", 1)
    g = g.astype(BF).reshape(4, rows, cols)
    return lax.all_to_all(g, ("dc", "zl"), 0, 0, tiled=True)


class Tokens:
    def __init__(self):
        sizes = tuple(lax.axis_size(n) for n in AXES)
        self.core = swap_pairs(sizes, lambda a, b, c, d, e: (a, 1 - b, c, d, e))
        self.first = swap_pairs(
            sizes, lambda a, b, c, d, e: (a, b, c, d, 1 - e) if b == 0 else (a, b, c, 1 - d, e)
        )
        self.second = swap_pairs(
            sizes, lambda a, b, c, d, e: (a, b, c, 1 - d, e) if b == 0 else (a, b, c, d, 1 - e)
        )
        self.dc, self.zl, self.mp = (lax.axis_index(n) for n in ("dc", "zl", "mp"))

    def order(self, dc):
        mp, zl = self.mp, self.zl
        own = mp * 2 + zl
        by_mp = (1 - mp) * 2 + zl
        by_zl = mp * 2 + 1 - zl
        both = (1 - mp) * 2 + 1 - zl
        one = jnp.where(dc == 0, by_mp, by_zl)
        two = jnp.where(dc == 0, by_zl, by_mp)
        return own, one, two, both

    def gather(self, x):
        rows, width = x.shape
        one = lax.ppermute(x, AXES, self.first)
        two = lax.ppermute(jnp.stack([x, one]), AXES, self.second)
        far = [lax.ppermute(v, AXES, self.core) for v in (x, one, two)]
        out = jnp.zeros((8, rows, width), x.dtype)
        for dc, blocks in (
            (self.dc, (x, one, two[0], two[1])),
            (1 - self.dc, (far[0], far[1], far[2][0], far[2][1])),
        ):
            for at, block in zip(self.order(dc), blocks):
                out = lax.dynamic_update_index_in_dim(out, block, dc * 4 + at, 0)
        return out.reshape(8 * rows, width)

    def scatter(self, x):
        rows, width = x.shape[0] // 8, x.shape[1]
        x = x.reshape(2, 4, rows, width)
        theirs = lax.dynamic_index_in_dim(x, 1 - self.dc, 0, keepdims=False).astype(BF)
        mine = lax.dynamic_index_in_dim(x, self.dc, 0, keepdims=False)
        total = mine.astype(F32) + lax.ppermute(theirs, AXES, self.core).astype(F32)
        own, one, two, both = self.order(self.dc)
        pick = lambda at: lax.dynamic_index_in_dim(total, at, 0, keepdims=False)
        got = lax.ppermute(jnp.stack([pick(two), pick(both)]).astype(BF), AXES, self.second)
        keep_own = pick(own) + got[0].astype(F32)
        keep_one = pick(one) + got[1].astype(F32)
        got = lax.ppermute(keep_one.astype(BF), AXES, self.first)
        return keep_own + got.astype(F32)


MESH = pl.DeviceIdType.MESH
ANY = pl.BlockSpec(memory_space=pl.ANY)
VMEM = pl.BlockSpec(memory_space=pltpu.VMEM)


def flip(index, by):
    return 1 - index if by else index


class Place:
    def __init__(self):
        self.dx, self.dc, self.zh, self.zl, self.mp = (lax.axis_index(n) for n in AXES)

    def peer(self, dx=0, dc=0, zh=0, zl=0, mp=0):
        return (
            flip(self.dx, dx),
            flip(self.dc, dc),
            flip(self.zh, zh),
            flip(self.zl, zl),
            flip(self.mp, mp),
        )

    def block(self, dx=0, dc=0, zh=0, zl=0):
        a, b, c, d, _ = self.peer(dx, dc, zh, zl)
        return ((a * 2 + b) * 2 + c) * 2 + d

    def slot(self, dc=0, zl=0):
        return flip(self.dc, dc) * 2 + flip(self.zl, zl)

    def rows(self, dc=0, mp=0, zl=0):
        return (flip(self.dc, dc) * 2 + flip(self.mp, mp)) * 2 + flip(self.zl, zl)


def greet(peers):
    barrier = pltpu.get_barrier_semaphore()
    for device in peers:
        pl.semaphore_signal(barrier, inc=1, device_id=device, device_id_type=MESH)
    pl.semaphore_wait(barrier, len(peers))


class Links:
    def __init__(self, send, recv, local):
        self.send, self.recv, self.local = send, recv, local
        self.n, self.m = 0, 0
        self.sent, self.copies = [], []

    def pair(self):
        self.n += 1
        return self.n - 1

    def start(self, src, dst, at, device):
        copy = pltpu.make_async_remote_copy(
            src_ref=src,
            dst_ref=dst,
            send_sem=self.send.at[at],
            recv_sem=self.recv.at[at],
            device_id=device,
            device_id_type=MESH,
        )
        copy.start()
        self.sent.append(copy)

    def arrived(self, ref, at):
        pltpu.make_async_copy(ref, ref, self.recv.at[at]).wait()

    def keep(self, src, dst):
        copy = pltpu.make_async_copy(src, dst, self.local.at[self.m])
        self.m += 1
        copy.start()
        return copy

    def finish(self):
        for copy in self.sent:
            copy.wait_send()


FLIPS = [(zh, dc, zl) for zh in (1, 0) for dc in (0, 1) for zl in (0, 1)]


class WeightGather:
    def __init__(self, place, links, source, target, unit):
        self.place, self.links, self.target = place, links, target
        self.at = {f: links.pair() for f in FLIPS}
        self.cross = {(zh, dc): links.pair() for zh in (0, 1) for dc in (0, 1)}
        self.source = source
        self.kept = None

    def begin(self, zhs=(1, 0), dcs=(0, 1)):
        p = self.place
        mine = p.block()
        for f in FLIPS:
            zh, dc, zl = f
            if zh not in zhs or dc not in dcs:
                continue
            src, dst = self.source(p.slot(dc, zl)), self.target(mine, 1)
            if f == (0, 0, 0):
                self.kept = self.links.keep(src, dst)
            else:
                self.links.start(src, dst, self.at[f], p.peer(dc=dc, zh=zh, zl=zl))

    def onward(self, zh, dcs=(0, 1)):
        p = self.place
        for dc in dcs:
            for zl in (0, 1):
                if (zh, dc, zl) == (0, 0, 0):
                    self.kept.wait()
                else:
                    self.links.arrived(
                        self.target(p.block(dc=dc, zh=zh, zl=zl), 1), self.at[zh, dc, zl]
                    )
            two = self.target(p.block(dc=dc, zh=zh) // 2 * 2, 2)
            self.links.start(two, two, self.cross[zh, dc], p.peer(dx=1))

    def end(self):
        p = self.place
        for zh in (0, 1):
            for dc in (0, 1):
                two = self.target(p.block(dx=1, dc=dc, zh=zh) // 2 * 2, 2)
                self.links.arrived(two, self.cross[zh, dc])


def row_blocks(ref, unit, cols=None):
    def target(first, count):
        rows = pl.ds(pl.multiple_of(first * unit, unit), count * unit)
        return ref.at[rows] if cols is None else ref.at[rows, cols]

    return target


def column_blocks(ref, unit):
    return lambda first, count: ref.at[:, pl.ds(pl.multiple_of(first * unit, unit), count * unit)]


def first_kernel(
    weight_ref, source_ref, tok_ref, cot_ref, ig_ref, o_ref, gates_ref, small_ref, gate_ref,
    all_ref, wig_ref, wo_ref, wide_ref, ch_ref, gains_ref, dms_ref, dout_ref, own_ref, wg_ref,
    pieces, smalls, dm, send, recv, local,
):
    p = Place()
    links = Links(send, recv, local)
    drows = ig_ref.shape[1]
    crows = wo_ref.shape[0]
    greet(weight_peers(p))
    gather = TokenGatherTwice(p, links, tok_ref, all_ref)
    w_ig = WeightGather(p, links, lambda j: ig_ref.at[j], row_blocks(wig_ref, drows), drows)
    w_o = WeightGather(
        p,
        links,
        lambda j: o_ref.at[pl.ds(pl.multiple_of(j * crows, 16), crows)],
        column_blocks(wo_ref, o_ref.shape[1]),
        drows,
    )
    unit = gates_ref.shape[1]
    w_g = WeightGather(p, links, lambda j: gates_ref.at[j], row_blocks(pieces, unit), unit)
    w_s = WeightGather(p, links, lambda j: small_ref, row_blocks(smalls, 16), 16)
    w_gate = slot_columns(p, links, gate_ref, wg_ref)
    adjoint = TokenGatherTwice(p, links, dm, dms_ref)
    w_s.begin()
    w_ig.begin((1,))
    w_ig.begin((0,))
    w_g.begin((0,))
    w_o.begin((0,))
    gather.begin()
    own = links.keep(tok_ref.at[p.mp], own_ref)
    scales = [weight_ref[source_ref[m, 0]] for m in range(2)]
    for m in range(2):

        def scale(rows, m=m):
            value = cot_ref[m, rows, :].astype(F32) * scales[m]
            dm[m, rows, :] = value.astype(BF)

            @pl.when(p.mp == m)
            def _():
                dout_ref[rows, :] = value

        chunks(cot_ref.shape[1], scale, 1)
    adjoint.begin()
    w_ig.onward(0)
    w_g.onward(0)
    w_o.onward(0)
    w_s.onward(0)
    w_gate.begin((0,))
    w_o.begin((1,))
    w_g.begin((1,))
    w_ig.onward(1)
    w_gate.begin((1,), (0,))
    w_s.onward(1)
    gather.forward()
    w_o.onward(1)
    w_g.onward(1)
    w_gate.begin((1,), (1,))
    gather.forward_core()
    w_gate.onward(0)
    adjoint.forward()
    w_gate.onward(1, (0,))
    adjoint.forward_core()
    w_s.end()
    count = small_channels(local_channels=crows)
    table = jnp.zeros((8, LANES), F32)
    for k in range(4):
        at = pl.ds(pl.multiple_of((p.slot() * 4 + k) * 16, 16), 16)
        rows = smalls[at, :].astype(F32)[:8]
        rows = jnp.concatenate([rows, jnp.zeros((8, LANES - 128), F32)], axis=1)
        table = table + (pltpu.roll(rows, k * count, 1) if k else rows)
    ch_ref[...] = table
    for k in range(16):
        rows = smalls[k * 16 : (k + 1) * 16, :].astype(F32)
        gains_ref[:, k * 128 : (k + 1) * 128] = rows[8:10]
    w_g.end()
    size = crows // 2
    per = size // 16
    total = jnp.zeros(wide_ref.shape, F32)
    row = lax.broadcasted_iota(jnp.int32, (LANES, pieces.shape[0]), 0)
    column = lax.broadcasted_iota(jnp.int32, (LANES, pieces.shape[0]), 1)
    source = lax.broadcasted_iota(jnp.int32, (LANES, 2 * LANES), 0)
    target = lax.broadcasted_iota(jnp.int32, (LANES, 2 * LANES), 1)
    for h in range(2):
        r = column % 32 - h * 16
        wanted = (r >= 0) & (r < per) & (row == h * size + column // 32 * per + r)
        rows = dot(jnp.where(wanted, 1.0, 0.0).astype(BF), pieces[...], NN, BF)
        gate = target // LANES
        wanted = (source == target - gate * LANES - h * size + gate * size) & (
            (source >= gate * size) & (source < (gate + 1) * size)
        )
        total = total + dot(rows, jnp.where(wanted, 1.0, 0.0).astype(BF), NN)
    wide_ref[...] = total.astype(BF)
    w_gate.onward(1, (1,))
    own.wait()
    gather.end()
    adjoint.end()
    w_gate.end()
    w_ig.end()
    w_o.end()
    links.finish()


def small_channels(local_channels):
    return local_channels // 4


class TokenGatherTwice:
    def __init__(self, place, links, source, target):
        self.place, self.links, self.source, self.target = place, links, source, target
        self.z, self.y = links.pair(), links.pair()
        self.core = {(mp, zl): links.pair() for mp in (0, 1) for zl in (0, 1)}

    def begin(self):
        p = self.place
        self.kept = []
        for mp in (0, 1):
            at = p.rows(mp=mp)
            src = self.source.at[flip(p.mp, mp)]
            if mp == 0:
                self.links.start(src, self.target.at[at], self.z, p.peer(zl=1))
            self.links.start(src, self.target.at[at], self.core[mp, 0], p.peer(dc=1))
            self.kept.append(self.links.keep(src, self.target.at[at]))

    def forward(self):
        p = self.place
        far = self.target.at[p.rows(zl=1)]
        self.links.arrived(far, self.z)
        self.links.start(far, far, self.y, p.peer(mp=1))
        self.links.start(far, far, self.core[0, 1], p.peer(dc=1))

    def forward_core(self):
        p = self.place
        far = self.target.at[p.rows(mp=1, zl=1)]
        self.links.arrived(far, self.y)
        self.links.start(far, far, self.core[1, 1], p.peer(dc=1))

    def end(self):
        p = self.place
        for (mp, zl), at in self.core.items():
            self.links.arrived(self.target.at[p.rows(dc=1, mp=mp, zl=zl)], at)
        for copy in self.kept:
            copy.wait()


class TokenGather:
    def __init__(self, place, links, source, target, span):
        self.place, self.links = place, links
        self.span = pl.ds(*span)
        self.source, self.target = source.at[self.span], target
        self.z, self.y0, self.y1 = links.pair(), links.pair(), links.pair()
        self.core = {(mp, zl): links.pair() for mp in (0, 1) for zl in (0, 1)}

    def block(self, **where):
        return self.target.at[self.place.rows(**where), self.span]

    def begin(self):
        p = self.place
        at = self.block()
        self.links.start(self.source, at, self.z, p.peer(zl=1))
        self.links.start(self.source, at, self.y0, p.peer(mp=1))
        self.links.start(self.source, at, self.core[0, 0], p.peer(dc=1))
        self.kept = self.links.keep(self.source, at)

    def forward(self):
        p = self.place
        far = self.block(zl=1)
        self.links.arrived(far, self.z)
        self.links.start(far, far, self.y1, p.peer(mp=1))
        self.links.start(far, far, self.core[0, 1], p.peer(dc=1))

    def forward_core(self):
        p = self.place
        far = self.block(mp=1)
        self.links.arrived(far, self.y0)
        self.links.start(far, far, self.core[1, 0], p.peer(dc=1))
        far = self.block(mp=1, zl=1)
        self.links.arrived(far, self.y1)
        self.links.start(far, far, self.core[1, 1], p.peer(dc=1))

    def end(self):
        for (mp, zl), at in self.core.items():
            self.links.arrived(self.block(dc=1, mp=mp, zl=zl), at)
        self.kept.wait()


CHUNK = 16


def chunks(count, body, most=11, first=0):
    n = count // CHUNK
    per = max(k for k in range(1, most + 1) if n % k == 0)

    def step(i, carry):
        for k in range(per):
            body(pl.ds(pl.multiple_of(first + (i * per + k) * CHUNK, CHUNK), CHUNK))
        return carry

    if n == per:
        step(0, 0)
    else:
        lax.fori_loop(0, n // per, step, 0)


def halves(rows):
    first = (rows // 2 + CHUNK - 1) // CHUNK * CHUNK
    return [(0, first), (first, rows - first)]


class RowScatter:
    def __init__(self, place, links, source, buffers, parts=None):
        self.place, self.links, self.source = place, links, source
        self.mine, self.from_core, self.from_y, self.from_z, self.out = buffers[:5]
        self.to_core = buffers[5] if len(buffers) > 5 else None
        self.parts = parts or [(0, self.mine.shape[1])]
        self.blocks = [(mp, zl) for mp in (1, 0) for zl in (1, 0)]
        self.kept = {}
        n = range(len(self.parts))
        self.core = {(h, block): links.pair() for h in n for block in self.blocks}
        self.y = {(h, zl): links.pair() for h in n for zl in (1, 0)}
        self.z = {h: links.pair() for h in n}

    def begin(self, mps=(1, 0)):
        p = self.place
        for mp, zl in self.blocks:
            if mp not in mps:
                continue
            i, block = mp * 2 + zl, p.rows(dc=1, mp=mp, zl=zl)
            if self.to_core is None:
                src = self.source.at[block]
            else:
                self.to_core[i] = self.source(block).astype(BF)
                src = self.to_core.at[i]
            for h, part in enumerate(self.parts):
                at = pl.ds(*part)
                self.links.start(
                    src.at[at], self.from_core.at[i, at], self.core[h, (mp, zl)], p.peer(dc=1)
                )
            block = p.rows(mp=mp, zl=zl)
            if self.to_core is None:
                self.kept[mp, zl] = self.links.keep(self.source.at[block], self.mine.at[i])
            else:
                self.mine[i] = self.source(block).astype(BF)

    def ready(self, mp, zl, h):
        i = mp * 2 + zl
        if h == 0 and self.kept:
            self.kept[mp, zl].wait()
        at = pl.ds(*self.parts[h])
        self.links.arrived(self.from_core.at[i, at], self.core[h, (mp, zl)])
        return i

    def across_y(self, h=0):
        p = self.place
        first, count = self.parts[h]
        at = pl.ds(first, count)
        for zl in (1, 0):
            i = self.ready(1, zl, h)

            def add(rows, i=i, zl=zl):
                total = self.mine[i, rows, :].astype(F32) + self.from_core[i, rows, :].astype(F32)
                self.out[zl, rows, :] = total.astype(BF)

            chunks(count, add, first=first)
            self.links.start(
                self.out.at[zl, at], self.from_y.at[zl, at], self.y[h, zl], p.peer(mp=1)
            )

    def across_z(self, h=0):
        p = self.place
        first, count = self.parts[h]
        at = pl.ds(first, count)
        i = self.ready(0, 1, h)
        self.links.arrived(self.from_y.at[1, at], self.y[h, 1])

        def add(rows):
            total = self.mine[i, rows, :].astype(F32) + self.from_core[i, rows, :].astype(F32)
            self.out[2, rows, :] = (total + self.from_y[1, rows, :].astype(F32)).astype(BF)

        chunks(count, add, first=first)
        self.links.start(self.out.at[2, at], self.from_z.at[at], self.z[h], p.peer(zl=1))

    def arrive(self, h=0):
        at = pl.ds(*self.parts[h])
        self.ready(0, 0, h)
        self.links.arrived(self.from_y.at[0, at], self.y[h, 0])
        self.links.arrived(self.from_z.at[at], self.z[h])

    def total(self, rows):
        a = self.mine[0, rows, :].astype(F32) + self.from_core[0, rows, :].astype(F32)
        b = self.from_y[0, rows, :].astype(F32) + self.from_z[rows, :].astype(F32)
        return a + b


def scatter_buffers(rows, width, products=False):
    return [
        pltpu.VMEM((4, rows, width), BF),
        pltpu.VMEM((4, rows, width), BF),
        pltpu.VMEM((2, rows, width), BF),
        pltpu.VMEM((rows, width), BF),
        pltpu.VMEM((3, rows, width), BF),
    ] + ([pltpu.VMEM((4, rows, width), BF)] if products else [])


def group_peers(p):
    return [p.peer(dc=1), p.peer(zl=1), p.peer(mp=1)]


def weight_peers(p):
    return [p.peer(dc=dc, zh=zh, zl=zl) for zh, dc, zl in FLIPS if (zh, dc, zl) != (0, 0, 0)] + [
        p.peer(dx=1),
        p.peer(mp=1),
    ]


def second_kernel(
    mixed_ref, wo_ref, own_ref, gain_ref, up_ref, down_ref,
    mid_ref, all_ref, wu_ref, wd_ref,
    *scratch,
):
    p = Place()
    links = Links(*scratch[-3:])
    normed = scratch[-4]
    rows, channels = own_ref.shape[0], wo_ref.shape[0]
    greet(weight_peers(p))

    def project(b):
        at = pl.ds(pl.multiple_of(b * rows, 16), rows)
        return dot(mixed_ref[at, :channels], wo_ref[...], NN)

    parts = halves(rows)
    scatter = RowScatter(p, links, project, scratch[:6], parts)
    w_u = slot_columns(p, links, up_ref, wu_ref)
    w_d = WeightGather(
        p,
        links,
        lambda j: down_ref.at[pl.ds(pl.multiple_of(j * wd_ref.shape[0], 16), wd_ref.shape[0])],
        column_blocks(wd_ref, down_ref.shape[1]),
        down_ref.shape[1],
    )
    gathers = [TokenGather(p, links, normed, all_ref, part) for part in parts]
    w_u.begin((1,), (0,))
    scatter.begin((1,))
    w_u.begin((0,))
    scatter.across_y(0)
    scatter.across_y(1)
    w_u.begin((1,), (1,))
    scatter.begin((0,))
    w_d.begin((0,))
    w_u.onward(0)

    def normalise(at):
        value = own_ref[at, :].astype(F32) + scatter.total(at)
        mid_ref[at, :] = value
        inv = lax.rsqrt(jnp.mean(value * value, axis=-1, keepdims=True) + EPSILON)
        normed[at, :] = (value * inv * gain_ref[...]).astype(BF)

    def middle(h):
        scatter.arrive(h)
        chunks(parts[h][1], normalise, first=parts[h][0])
        gathers[h].begin()

    scatter.across_z(0)
    w_d.onward(0)
    scatter.across_z(1)
    w_d.begin((1,), (0,))
    middle(0)
    w_u.onward(1, (0,))
    middle(1)
    w_u.onward(1, (1,))
    w_d.begin((1,), (1,))
    gathers[0].forward()
    gathers[1].forward()
    w_d.onward(1, (0,))
    gathers[0].forward_core()
    gathers[1].forward_core()
    w_d.onward(1, (1,))
    for gather in gathers:
        gather.end()
    w_u.end()
    w_d.end()
    links.finish()


def slot_columns(p, links, source, result):
    count = result.shape[1]
    return WeightGather(
        p,
        links,
        lambda j: source.at[:, pl.ds(pl.multiple_of(j * count, 128), count)],
        row_blocks(result, source.shape[0]),
        source.shape[0],
    )


class GradScatter:
    FAR = [(1, 0, 1), (1, 1, 1)], [(1, 0, 0), (1, 1, 0)]
    NEAR = [(0, 0, 1), (0, 1, 1)], [(0, 0, 0), (0, 1, 0)]
    ORDER = FAR[0] + NEAR[0] + FAR[1] + NEAR[1]
    EARLY = FAR[0] + FAR[1] + NEAR[0] + NEAR[1]

    def __init__(self, place, links, left, right, buffers, order=ORDER):
        self.order = order
        self.place, self.links, self.left, self.right = place, links, left, right
        self.to_x, self.from_x, self.to_z, self.from_z, self.sums, self.result = buffers[:6]
        self.columns = buffers[6] if len(buffers) > 6 else None
        self.rows = self.to_x.shape[1]
        self.x = {(zh, dc): links.pair() for zh in (1, 0) for dc in (0, 1)}
        self.z = {dc: links.pair() for dc in (0, 1)}
        self.at = {(dc, zl): links.pair() for dc in (0, 1) for zl in (0, 1)}
        self.count = 0
        self.load()

    def load(self):
        if self.count < 8 and self.columns is not None:
            dx, dc, zh = self.order[self.count]
            first = self.place.block(dx=dx, dc=dc, zh=zh) // 2
            columns = pl.ds(pl.multiple_of(first * self.rows, self.rows), self.rows)
            self.loading = self.links.keep(
                self.left.at[:, columns], self.columns.at[self.count % 2]
            )

    def product(self, dx=0, dc=0, zh=0):
        assert self.order[self.count] == (dx, dc, zh)
        self.loading.wait()
        self.count += 1
        self.load()
        return dot(self.columns[(self.count - 1) % 2], self.right[...], TN)

    def begin(self, zh):
        for dc in (0, 1):
            i = zh * 2 + dc
            self.to_x[i] = self.product(dx=1, dc=dc, zh=zh).astype(BF)
            self.links.start(
                self.to_x.at[i], self.from_x.at[i], self.x[zh, dc], self.place.peer(dx=1)
            )

    def across(self, dc):
        mine = self.product(dc=dc, zh=1)
        self.links.arrived(self.from_x.at[2 + dc], self.x[1, dc])
        self.to_z[dc] = (mine + self.from_x[2 + dc].astype(F32)).astype(BF)
        self.links.start(self.to_z.at[dc], self.from_z.at[dc], self.z[dc], self.place.peer(zh=1))

    def last(self, dc):
        p = self.place
        mine = self.product(dc=dc, zh=0)
        self.links.arrived(self.from_x.at[dc], self.x[0, dc])
        self.links.arrived(self.from_z.at[dc], self.z[dc])
        total = mine + self.from_x[dc].astype(F32) + self.from_z[dc].astype(F32)
        self.sums[dc] = total.astype(BF)
        unit = self.rows // 2
        for zl in (1, 0):
            src = self.sums.at[dc, pl.ds(pl.multiple_of(flip(p.zl, zl) * unit, unit), unit)]
            dst = self.result.at[p.slot()]
            if (dc, zl) == (0, 0):
                self.own = self.links.keep(src, dst)
            else:
                self.links.start(src, dst, self.at[dc, zl], p.peer(dc=dc, zl=zl))

    def end(self):
        p = self.place
        for (dc, zl), at in self.at.items():
            if (dc, zl) == (0, 0):
                self.own.wait()
            else:
                self.links.arrived(self.result.at[p.slot(dc, zl)], at)


class Ready(GradScatter):
    def product(self, dx=0, dc=0, zh=0):
        first = self.place.block(dx=dx, dc=dc, zh=zh) // 2
        return self.left[pl.ds(pl.multiple_of(first * self.rows, self.rows), self.rows), :].astype(
            F32
        )


def grad_buffers(rows, columns, tokens=None):
    return (
        [pltpu.VMEM((n, rows, columns), BF) for n in (4, 4, 2, 2, 2)]
        + [pltpu.VMEM((4, rows // 2, columns), BF)]
        + ([pltpu.VMEM((2, tokens, rows), BF)] if tokens else [])
    )


def norm_back(value, gain, upstream):
    inv = lax.rsqrt(jnp.mean(value * value, axis=-1, keepdims=True) + EPSILON)
    scaled = value * inv
    up = upstream * gain
    inner = jnp.mean(up * scaled, axis=-1, keepdims=True)
    return inv * (up - scaled * inner), upstream * scaled


def fold(rows):
    return rows[:8] + rows[8:]


def third_kernel(
    wg_ref, wu_ref, wd_in, mid_in, dout_in, gain_ref, dm_ref, hidden_ref, n2_ref, dgm_ref,
    dup_ref,
    dr1_ref, gain_out, all_ref, gate_out, down_out, part_out,
    *scratch,
):
    p = Place()
    links = Links(*scratch[-3:])
    do, wd_ref, mid_ref, dout_ref = scratch[-7:-3]
    rows_of = mid_ref.shape[0]
    staged = [
        links.keep(src, dst)
        for src, dst in ((mid_in, mid_ref), (dout_in, dout_ref), (wd_in, wd_ref))
    ]
    greet(weight_peers(p))

    def product(b):
        at = pl.ds(pl.multiple_of(b * rows_of, 16), rows_of)
        return dot(dgm_ref[at, :], wg_ref[...], NT) + dot(dup_ref[at, :], wu_ref[...], NT)

    parts = halves(rows_of)
    scatter = RowScatter(p, links, product, scratch[:6], parts)
    down = GradScatter(p, links, dm_ref, hidden_ref, scratch[6:13])
    gate = GradScatter(p, links, n2_ref, dgm_ref, scratch[13:20])
    gathers = [TokenGather(p, links, do, all_ref, part) for part in parts]
    down.begin(1)
    scatter.begin((1,))
    scatter.across_y(0)
    scatter.across_y(1)
    down.across(0)
    scatter.begin((0,))
    down.across(1)
    gate.begin(1)
    gain_out[...] = jnp.zeros_like(gain_out)
    for copy in staged:
        copy.wait()

    def back(rows):
        part, gain = norm_back(mid_ref[rows, :], gain_ref[...], scatter.total(rows))
        value = dout_ref[rows, :] + part
        dr1_ref[rows, :] = value
        do[rows, :] = value.astype(BF)
        gain_out[...] += fold(gain)

    def middle(h):
        scatter.arrive(h)
        chunks(parts[h][1], back, first=parts[h][0])
        gathers[h].begin()

    scatter.across_z(0)
    down.begin(0)
    gate.across(0)
    scatter.across_z(1)
    middle(0)
    gate.across(1)
    gate.begin(0)
    middle(1)
    gathers[0].forward()
    gathers[1].forward()
    down.last(0)
    down.last(1)
    gathers[0].forward_core()
    gate.last(0)
    out = scratch[0]
    writes = []
    for b in range(8):
        if b >= 4:
            writes[b - 4].wait()
        at = pl.ds(b * rows_of, rows_of)
        out[b % 4] = dot(hidden_ref[at, :], wd_ref[...], NN, BF)
        writes.append(links.keep(out.at[b % 4], part_out.at[b]))
    gathers[1].forward_core()
    gate.last(1)
    for gather in gathers:
        gather.end()
    down.end()
    ff = down.result.shape[2]
    for j in range(4):
        down_out[j * ff : (j + 1) * ff, :] = down.result[j].astype(F32).T.astype(BF)
    gate.end()
    for j in range(4):
        gate_out[:, j * ff : (j + 1) * ff] = gate.result[j]
    for write in writes[4:]:
        write.wait()
    links.finish()


def fourth_kernel(
    wig_ref, own_ref, dr1_ref, gain_ref, do_ref, mixed_ref, n1_ref, dboth_ref, gg_ref,
    dx_ref, gain_out, in_out, gelu_out, out_out, gates_out,
    *scratch,
):
    p = Place()
    links = Links(*scratch[-3:])
    dx_send, dx_recv = scratch[-5:-3]
    greet(weight_peers(p))
    rows_of = own_ref.shape[0]

    def product(b):
        at = pl.ds(pl.multiple_of(b * rows_of, 16), rows_of)
        return dot(dboth_ref[at, :], wig_ref[...], NT)

    parts = halves(rows_of)
    scatter = RowScatter(p, links, product, scratch[:6], parts)
    out = GradScatter(p, links, do_ref, mixed_ref, scratch[6:13])
    wide = GradScatter(p, links, n1_ref, dboth_ref, scratch[13:20])
    gates = Ready(p, links, gg_ref, None, scratch[20:26])
    out.begin(1)
    scatter.begin((1,))
    scatter.across_y(0)
    scatter.across_y(1)
    out.across(0)
    out.across(1)
    wide.begin(1)
    scatter.begin((0,))
    gates.begin(1)
    out.begin(0)
    for g in (wide, gates):
        g.across(0)
        g.across(1)
        g.begin(0)
    gain_out[...] = jnp.zeros_like(gain_out)

    def back(rows):
        value = own_ref[rows, :].astype(F32)
        part, gain = norm_back(value, gain_ref[...], scatter.total(rows))
        total = dr1_ref[rows, :] + part
        dx_ref[p.mp, rows, :] = total
        dx_send[rows, :] = total.astype(BF)
        gain_out[...] += fold(gain)

    sent = []

    def middle(h):
        scatter.arrive(h)
        chunks(parts[h][1], back, first=parts[h][0])
        span, at = pl.ds(*parts[h]), links.pair()
        links.start(dx_send.at[span], dx_recv.at[span], at, p.peer(mp=1))
        sent.append((span, at))

    scatter.across_z(0)
    scatter.across_z(1)
    middle(0)
    for g in (out, gates):
        g.last(0)
        g.last(1)
    middle(1)
    wide.last(0)
    wide.last(1)
    local = out.result.shape[2]
    out.end()
    for j in range(4):
        out_out[j * out_out.shape[0] // 4 : (j + 1) * out_out.shape[0] // 4, :] = (
            out.result[j].astype(F32).T[: out_out.shape[0] // 4].astype(BF)
        )
    gates.end()
    gates_out[...] = gates.result[...]
    wide.end()
    two = wide.result.shape[2]
    left = lax.broadcasted_iota(jnp.int32, (1, two), 1) < two // 2
    for j in (0, 2):
        a, b = (wide.result[j + i].astype(F32) for i in (0, 1))
        span = slice(j * two // 2, (j + 2) * two // 2)
        in_out[:, span] = jnp.where(left, a, pltpu.roll(b, two // 2, 1)).astype(BF)
        gelu_out[:, span] = jnp.where(left, pltpu.roll(a, two // 2, 1), b).astype(BF)
    for span, at in sent:
        links.arrived(dx_recv.at[span], at)
    dx_ref[1 - p.mp] = dx_recv[...].astype(F32)
    links.finish()


def mlp_kernel(
    n2_ref, dm_ref, wg_ref, wu_ref, wd_ref, hidden_ref, dgm_ref, dup_ref, pre, upp, dhm
):
    count, rows, width = n2_ref.shape
    n2 = n2_ref[...].reshape(count * rows, width)
    pre[...] = dot(n2, wg_ref[...], NN)
    upp[...] = dot(n2, wu_ref[...], NN)
    dhm[...] = dot(dm_ref[...].reshape(count * rows, width), wd_ref[...], NT)

    def body(at):
        up, d = upp[at, :], dhm[at, :]
        value, slope = gelu_both(pre[at, :])
        hidden_ref[at, :] = (value * up).astype(BF)
        dgm_ref[at, :] = (d * up * slope).astype(BF)
        dup_ref[at, :] = (d * value).astype(BF)

    chunks(count * rows, body, 22)


def feed_forward(n2, dm, w_g, w_u, w_d):
    blocks, rows, width = n2.shape
    ff = w_d.shape[0]
    if not shape_fits():
        n2, dm = n2.reshape(-1, width), dm.reshape(-1, width)
        pre, d = dot(n2, w_g, NN), dot(dm, w_d, NT)
        gm, up = pre, dot(n2, w_u, NN)
        value, slope = gelu_both(gm)
        return (value * up).astype(BF), (d * up * slope).astype(BF), (d * value).astype(BF)
    two = pl.BlockSpec((2, rows, width), lambda i: (i, 0, 0))
    flat = pl.BlockSpec((2 * rows, ff), lambda i: (i, 0))
    whole = lambda v: pl.BlockSpec(v.shape, lambda i: (0, 0))
    total = blocks * rows
    return pl.pallas_call(
        mlp_kernel,
        name="feed_forward",
        grid=(blocks // 2,),
        in_specs=[two, two, whole(w_g), whole(w_u), whole(w_d)],
        out_specs=[flat] * 3,
        out_shape=[jax.ShapeDtypeStruct((total, ff), BF)] * 3,
        scratch_shapes=[pltpu.VMEM((2 * rows, ff), F32)] * 3,
        compiler_params=pltpu.CompilerParams(vmem_limit_bytes=48 * 1024 * 1024),
        cost_estimate=pl.CostEstimate(
            flops=2 * total * width * ff * 3, bytes_accessed=total * width * 4, transcendentals=0
        ),
    )(n2, dm, w_g, w_u, w_d)


def semaphores(pairs, local):
    return [
        pltpu.SemaphoreType.DMA((pairs,)),
        pltpu.SemaphoreType.DMA((pairs,)),
        pltpu.SemaphoreType.DMA((local,)),
    ]


def run_kernel(body, name, outs, out_specs, in_specs, scratch, ident, args, mib=40):
    return pl.pallas_call(
        body,
        name=name,
        out_shape=[jax.ShapeDtypeStruct(*o) for o in outs],
        in_specs=in_specs,
        out_specs=out_specs,
        scratch_shapes=scratch,
        compiler_params=pltpu.CompilerParams(
            collective_id=ident, has_side_effects=True, vmem_limit_bytes=mib * 1024 * 1024
        ),
    )(*args)


def fetch_first(
    tokens, cotangent, seq_source, source_weight, input_weight, gelu_weight, output_weight,
    decay_gates, input_gates, channel_params, norm_gains, mlp_gate,
):
    args = (
        tokens, cotangent, seq_source, source_weight, input_weight, gelu_weight, output_weight,
        decay_gates, input_gates, channel_params, norm_gains, mlp_gate,
    )
    if not shape_fits():
        return plain_fetch_first(*args)
    rows, width = tokens.shape[1:]
    drows, local = input_weight.shape[0], input_weight.shape[1] // 4
    pairs = [v.reshape(drows, 4, local) for v in (input_weight, gelu_weight)]
    ig = jnp.concatenate(pairs, axis=2).transpose(1, 0, 2)
    per = decay_gates.shape[1] // BLOCK
    gates = [v.reshape(8, per, BLOCK) for v in (decay_gates, input_gates)]
    gates = jnp.concatenate(gates, axis=2)
    gates = jnp.pad(gates, ((0, 0), (0, 16 - per), (0, LANES - 2 * BLOCK))).reshape(4, 32, LANES)
    small = jnp.pad(channel_params[:, 0], ((0, 0), (0, drows - channel_params.shape[2])))
    small = jnp.pad(jnp.concatenate([small, norm_gains], axis=0), ((0, 6), (0, 0)))
    smem = pl.BlockSpec(memory_space=pltpu.SMEM)
    return run_kernel(
        first_kernel,
        "fetch_first",
        [
            ((8, rows, width), BF),
            ((width, 2 * local), BF),
            ((local, width), BF),
            ((LANES, 2 * LANES), BF),
            ((8, LANES), F32),
            ((2, width), F32),
            ((8, rows, width), BF),
            ((rows, width), F32),
            ((rows, width), BF),
            ((width, mlp_gate.shape[1] // 4), BF),
        ],
        [ANY] * 3 + [VMEM] * 3 + [ANY, VMEM, ANY, ANY],
        [smem, smem, ANY, VMEM] + [ANY] * 5,
        [
            pltpu.VMEM((512, LANES), BF),
            pltpu.VMEM((256, 128), BF),
            pltpu.VMEM((2, rows, width), BF),
        ]
        + semaphores(80, 16),
        1,
        (source_weight, seq_source, tokens, cotangent, ig, output_weight, gates, small, mlp_gate),
        61,
    )


def reduce_and_fetch(mixed, w_o, own, gain, mlp_up, mlp_down):
    if not shape_fits():
        return plain_reduce_and_fetch(mixed, w_o, own, gain, mlp_up, mlp_down)
    rows, width = own.shape
    ff = mlp_up.shape[1] // 4
    return run_kernel(
        second_kernel,
        "reduce_and_fetch",
        [((rows, width), F32), ((8, rows, width), BF), ((width, ff), BF), ((ff, width), BF)],
        [VMEM] + [ANY] * 3,
        [VMEM] * 4 + [ANY] * 2,
        scatter_buffers(rows, width, True) + [pltpu.VMEM((rows, width), BF)] + semaphores(64, 16),
        2,
        (mixed, w_o, own, gain, mlp_up, mlp_down),
    )


def reduce_and_return(weights, middle, dout, gain, dm, hidden, n2, dgm, dup, drows):
    if not shape_fits():
        return plain_reduce_and_return(
            weights, middle, dout, gain, dm, hidden, n2, dgm, dup, drows
        )
    rows, width = middle.shape
    ff = hidden.shape[1]
    return run_kernel(
        third_kernel,
        "reduce_and_return",
        [
            ((rows, width), F32),
            ((8, width), F32),
            ((8, rows, width), BF),
            ((drows, 4 * ff), BF),
            ((4 * ff, drows), BF),
            ((8, rows, width), BF),
        ],
        [VMEM, VMEM, ANY] + [VMEM] * 2 + [ANY],
        [VMEM] * 2 + [ANY] * 3 + [VMEM] + [ANY, VMEM] * 2 + [VMEM],
        scatter_buffers(rows, width, True)
        + grad_buffers(2 * drows, ff, 8 * rows) * 2
        + [pltpu.VMEM((rows, width), BF), pltpu.VMEM((ff, width), BF)]
        + [pltpu.VMEM((rows, width), F32)] * 2
        + semaphores(56, 56),
        3,
        (*weights, middle, dout, gain, dm, hidden, n2, dgm, dup),
        61,
    )


def return_last(w_ig, own, dr1, gain, do, mixed, n1, dboth, g_gates, drows):
    if not shape_fits():
        return plain_return_last(w_ig, own, dr1, gain, do, mixed, n1, dboth, g_gates, drows)
    rows, width = own.shape
    local, unit = dboth.shape[1] // 2, g_gates.shape[0] // 16
    return run_kernel(
        fourth_kernel,
        "return_last",
        [
            ((2, rows, width), F32),
            ((8, width), F32),
            ((drows, 4 * local), BF),
            ((drows, 4 * local), BF),
            ((4 * local, drows), BF),
            ((4, unit, 128), BF),
        ],
        [VMEM] * 6,
        [VMEM] * 4 + [ANY, VMEM] * 2 + [VMEM],
        scatter_buffers(rows, width, True)
        + grad_buffers(2 * drows, mixed.shape[1], 8 * rows)
        + grad_buffers(2 * drows, 2 * local, 8 * rows)
        + grad_buffers(2 * unit, 128)
        + [pltpu.VMEM((rows, width), BF)] * 2
        + semaphores(64, 48),
        4,
        (w_ig, own, dr1, gain, do, mixed, n1, dboth, g_gates),
        60,
    )


def shape_fits():
    return all(lax.axis_size(n) == 2 for n in AXES)


def plain_fetch_first(
    tokens, cotangent, seq_source, source_weight, input_weight, gelu_weight, output_weight,
    decay_gates, input_gates, channel_params, norm_gains, mlp_gate,
):
    exchange = Tokens()
    dxn, zhn, mp = lax.axis_size("dx"), lax.axis_size("zh"), exchange.mp
    group = dxn * 2 * zhn * 2
    local = input_weight.shape[1] // 4
    heads, piece = decay_gates.shape[0] // 4, decay_gates.shape[1]
    shards = ("dx", "dc", "zh", "zl")
    own = lax.dynamic_index_in_dim(tokens, mp, 0, keepdims=False)
    sources = jnp.arange(source_weight.shape[0], dtype=jnp.int32)
    scales = jnp.sum(jnp.where(seq_source == sources[None], source_weight[None], 0.0), axis=1)
    douts = cotangent.astype(F32) * scales[:, None, None]
    small = jnp.concatenate([channel_params.reshape(-1), norm_gains.reshape(-1)])
    small = lax.all_to_all(
        jnp.broadcast_to(small[None], (group, small.size)), shards, 0, 0, tiled=True
    )
    nch = channel_params.size
    channels = small[:, :nch].reshape(group, 8, -1).transpose(1, 0, 2).reshape(8, -1)
    slot = exchange.dc * 2 + exchange.zl
    channels = lax.dynamic_slice_in_dim(channels, slot * local, local, 1).astype(F32)
    gains = small[:, nch:].reshape(group, 2, -1).transpose(1, 0, 2).reshape(2, -1).astype(F32)
    gates = jnp.stack([decay_gates, input_gates]).reshape(2, 4, heads, piece)
    gates = gates.transpose(1, 0, 2, 3).reshape(2, 1, 2, 1, 2 * heads * piece)
    gates = jnp.broadcast_to(gates, (2, zhn, 2, dxn, 2 * heads * piece))
    gates = gates.transpose(3, 0, 1, 2, 4).reshape(group, 2 * heads * piece)
    gates = lax.all_to_all(gates, shards, 0, 0, tiled=True)
    gates = gates.reshape(group, 2 * heads, piece).transpose(1, 0, 2)
    gates = gates.reshape(2, heads, BLOCK, BLOCK)
    zero = jnp.zeros((BLOCK, BLOCK), BF)
    blocks = [
        [gates[g, h] if k == h else zero for g in range(2) for k in range(heads)]
        for h in range(heads)
    ]
    return (
        exchange.gather(own).reshape((8,) + own.shape),
        fetch_weight([input_weight, gelu_weight], 4),
        fetch_weight([output_weight.T], 4).T,
        jnp.concatenate([jnp.concatenate(v, axis=1) for v in blocks], axis=0),
        channels,
        gains,
        exchange.gather(lax.dynamic_index_in_dim(douts, mp, 0, keepdims=False).astype(BF)).reshape(
            (8,) + own.shape
        ),
        lax.dynamic_index_in_dim(douts, mp, 0, keepdims=False),
        own,
        fetch_weight([mlp_gate], 4),
    )


def plain_reduce_and_fetch(mixed, w_o, own, gain, mlp_up, mlp_down):
    exchange = Tokens()
    middle = own.astype(F32) + exchange.scatter(dot(mixed, w_o, NN, BF))
    normed = (middle * inverse_rms(middle) * gain).astype(BF)
    return (
        middle,
        exchange.gather(normed).reshape((8,) + own.shape),
        fetch_weight([mlp_up], 4),
        fetch_weight([mlp_down.T], 4).T,
    )


def columns(share, at, count):
    return share[:, :, at : at + count].astype(F32).transpose(1, 0, 2).reshape(-1, 4 * count)


def both_batches(rows):
    mp = lax.axis_index("mp")
    other = lax.ppermute(rows, "mp", [(0, 1), (1, 0)])
    return jnp.stack([jnp.where(mp == 0, rows, other), jnp.where(mp == 0, other, rows)])


def plain_reduce_and_return(weights, middle, dout, gain, dm, hidden, n2, dgm, dup, drows):
    exchange = Tokens()
    w_g, w_u, w_d = weights
    ff = hidden.shape[1]
    total = exchange.scatter((dot(dgm, w_g, NT) + dot(dup, w_u, NT)).astype(BF))
    change, gain_rows = norm_back(middle, gain, total)
    dr1 = dout + change
    gate = return_grad(dot(n2, dgm, TN, BF), drows)
    down = return_grad(dot(dm, hidden, TN, BF), drows)
    return (
        dr1,
        jnp.sum(gain_rows, axis=0, keepdims=True),
        exchange.gather(dr1.astype(BF)).reshape((8,) + dr1.shape),
        columns(gate, 0, ff),
        columns(down, 0, ff).T,
        dot(hidden, w_d, NN, BF).reshape((8,) + dr1.shape),
    )


def plain_return_last(w_ig, own, dr1, gain, do, mixed, n1, dboth, g_gates, drows):
    exchange = Tokens()
    local = dboth.shape[1] // 2
    total = exchange.scatter(dot(dboth, w_ig, NT, BF))
    change, gain_rows = norm_back(own.astype(F32), gain, total)
    group = n1.shape[1] // drows
    wide = return_grad(dot(n1, dboth, TN, BF), drows)
    out = return_grad(dot(do, mixed, TN, BF), drows)
    return (
        both_batches(dr1 + change),
        jnp.sum(gain_rows, axis=0, keepdims=True),
        columns(wide, 0, local),
        columns(wide, local, local),
        columns(out, 0, local).T,
        return_grad(g_gates, g_gates.shape[0] // group),
    )


def scan_body(reverse, a_ref, b_ref, p_ref, h_ref):
    length, width = a_ref.shape[1], a_ref.shape[2]
    row = lax.broadcasted_iota(jnp.int32, (8, width), 0)

    def tile(i, carry):
        ca, ch = carry
        at = (length // 8 - 1 - i if reverse else i) * 8
        at = pl.multiple_of(at, 8)
        a = a_ref[0, pl.ds(at, 8), :]
        b = b_ref[0, pl.ds(at, 8), :]
        for step in (1, 2, 4):
            if reverse:
                inside = row < 8 - step
                shift = 8 - step
            else:
                inside = row >= step
                shift = step
            sa = jnp.where(inside, pltpu.roll(a, shift, 0), 1.0)
            sb = jnp.where(inside, pltpu.roll(b, shift, 0), 0.0)
            b = b + a * sb
            a = a * sa
        h = b + a * ch
        p = a * ca
        h_ref[0, pl.ds(at, 8), :] = h
        p_ref[0, pl.ds(at, 8), :] = p
        last = 0 if reverse else 7
        return p[last : last + 1, :], h[last : last + 1, :]

    lax.fori_loop(
        0,
        length // 8,
        tile,
        (jnp.ones((1, width), F32), jnp.zeros((1, width), F32)),
    )


def local_scan(a, b, reverse):
    segs, length, width = a.shape
    spec = pl.BlockSpec((1, length, width), lambda s: (s, 0, 0))
    return pl.pallas_call(
        lambda *refs: scan_body(reverse, *refs),
        grid=(segs,),
        in_specs=[spec, spec],
        out_specs=[spec, spec],
        out_shape=[jax.ShapeDtypeStruct(a.shape, F32)] * 2,
        cost_estimate=pl.CostEstimate(
            flops=20 * a.size, bytes_accessed=16 * a.size, transcendentals=0
        ),
    )(a, b)


def carried(product, state, reverse):
    count = lax.axis_size("zh")
    if count == 2:
        return lax.ppermute(state, "zh", [(1, 0)] if reverse else [(0, 1)])
    here = lax.axis_index("zh")
    pairs = lax.all_gather(jnp.stack([product, state]), "zh")
    total = jnp.zeros_like(state)
    for k in range(count):
        at = count - 1 - k if reverse else k
        reached = at > here if reverse else at < here
        total = jnp.where(reached, pairs[at, 1] + pairs[at, 0] * total, total)
    return total


def from_behind(x, by):
    count = lax.axis_size("zh")
    return lax.ppermute(
        x, "zh", [(i, i + by) for i in range(count) if 0 <= i + by < count]
    )


def inverse_rms(values):
    return lax.rsqrt(jnp.mean(values * values, axis=-1, keepdims=True) + EPSILON)


def gelu(v):
    return jax.nn.gelu(v, approximate=True)


def gelu_both(v):
    c = 0.7978845608028654
    t = jnp.tanh(c * (v + 0.044715 * v * v * v))
    value = 0.5 * v * (1.0 + t)
    slope = 0.5 * (1.0 + t) + 0.5 * v * (1.0 - t * t) * c * (1.0 + 3 * 0.044715 * v * v)
    return value, slope


def dot(a, b, dims, out=F32):
    r = lax.dot_general(a, b, (dims, ((), ())), preferred_element_type=F32)
    return r.astype(out)


NN = ((1,), (0,))
NT = ((1,), (1,))
TN = ((0,), (0,))


def minus_expm1(v):
    series = 1.0 + v / 8.0
    for k in (7.0, 6.0, 5.0, 4.0, 3.0, 2.0):
        series = 1.0 + v * (1.0 / k) * series
    return jnp.where(v > -0.4, -v * series, 1.0 - jnp.exp(v))


def loop(count, body, unroll=1):
    def step(i, carry):
        body(i)
        return carry

    lax.fori_loop(0, count, step, 0, unroll=unroll)


def tile_scan(a, b, row, reverse):
    for step in (1, 2, 4):
        inside = row < 8 - step if reverse else row >= step
        shift = 8 - step if reverse else step
        sa = jnp.where(inside, pltpu.roll(a, shift, 0), 1.0)
        sb = jnp.where(inside, pltpu.roll(b, shift, 0), 0.0)
        b = b + a * sb
        a = a * sa
    return a, b


def eight(i):
    return pl.multiple_of(i * 8, 8)


def recur_forward_kernel(
    tok_ref, wig_ref, blocks_ref, ch_ref, gain_ref,
    n1_out, xs_out, gy_out, u_out, siga_out, sigi_out, decay_out, states, mixed,
    xs, gy, u, siga, sigi, decay, run, logits, n1, both, halo, ends, inc, tok, sems,
    send, recv, local_sems,
):
    p = Place()
    links = Links(send, recv, local_sems)
    rows, local = tok_ref.shape[1], wig_ref.shape[1] // 2
    zh = p.zh
    greet([p.peer(zh=1)])

    def read(b):
        return pltpu.make_async_copy(tok_ref.at[b], tok.at[b % 2], sems.at[4 + b % 2])

    read(0).start()
    lane = lax.broadcasted_iota(jnp.int32, (1, LANES), 1)
    real = lane < local

    def project(b):
        read(b).wait()

        @pl.when(b < 7)
        def _():
            read(b + 1).start()

        def normalise(at):
            value = tok[b % 2, at, :].astype(F32)
            inv = lax.rsqrt(jnp.mean(value * value, axis=-1, keepdims=True) + EPSILON)
            n1[b % 2, at, :] = (value * inv * gain_ref[...]).astype(BF)

        def write(i, at):
            return pltpu.make_async_copy(n1.at[i], n1_out.at[at], sems.at[i])

        @pl.when(b >= 2)
        def _():
            write(b % 2, b - 2).wait()

        chunks(rows, normalise)
        write(b % 2, b).start()
        both[...] = dot(n1[b % 2], wig_ref[...], NN)
        seg, zl = b // 2, b % 2

        def split(at):
            v = both[at, :]
            xb = jnp.where(real, v[:, :LANES], 0.0).astype(BF).astype(F32)
            xs[seg, pl.ds(pl.multiple_of(8 + zl * rows + at.start, 8), CHUNK), :] = xb
            rest = pltpu.roll(v, v.shape[1] - local, 1)[:, :LANES]
            gy[b, at, :] = jnp.where(real, rest, 0.0)

        chunks(rows, split)

    loop(8, project)
    for b in (6, 7):
        pltpu.make_async_copy(n1.at[b % 2], n1_out.at[b], sems.at[b % 2]).wait()

    def to_partner(src, dst):
        at = links.pair()
        links.start(src, dst, at, p.peer(zh=1))
        return at

    at = to_partner(xs.at[:, pl.ds(2 * rows, 8)], halo)
    kept = [links.keep(gy, gy_out)]
    links.arrived(halo, at)
    row = lax.broadcasted_iota(jnp.int32, (8, LANES), 0)
    soft = ch_ref[0:1, :]

    def head(seg):
        xs[seg, 0:8, :] = jnp.where(zh == 1, halo[seg], 0.0)

    loop(4, head)

    def convolve(b):
        seg, zl = b // 2, b % 2

        def body(at):
            v = xs[seg, pl.ds(pl.multiple_of(zl * rows + at.start, 8), CHUNK + 8), :]
            total = ch_ref[3:4, :] + ch_ref[4:5, :] * v[8:]
            for k in (1, 2, 3):
                total = total + ch_ref[4 + k : 5 + k, :] * pltpu.roll(v, k, 0)[8:]
            u[b, at, :] = total.astype(BF)

        chunks(rows, body)
        logits[b] = dot(u[b], blocks_ref[...], NN)

    loop(8, convolve)

    def tile(i, carry, zl):
        at = pl.ds(pl.multiple_of(i * CHUNK, CHUNK), CHUNK)
        out = []
        for seg in range(4):
            b = seg * 2 + zl
            cp, ch = carry[seg]
            sa = jax.nn.sigmoid(logits[b, at, :LANES] + ch_ref[1:2, :])
            si = jax.nn.sigmoid(logits[b, at, LANES:] + ch_ref[2:3, :])
            log_decay = -DECAY_SCALE * sa * soft
            a = jnp.exp(log_decay)
            drive = jnp.sqrt(minus_expm1(2.0 * log_decay)) * si * u[b, at, :].astype(F32)
            siga[b, at, :] = sa
            sigi[b, at, :] = si
            decay[b, at, :] = a
            for k in range(2):
                pa, h = tile_scan(a[k * 8 : k * 8 + 8], drive[k * 8 : k * 8 + 8], row, False)
                h = h + pa * ch
                pa = pa * cp
                run[b, pl.ds(eight(i * 2 + k), 8), :] = pa
                there = pl.ds(pl.multiple_of(8 + zl * rows + i * CHUNK + k * 8, 8), 8)
                states[seg, there, :] = h
                cp, ch = pa[7:8, :], h[7:8, :]
            out.append((cp, ch))
        return tuple(out)

    kept += [links.keep(xs, xs_out), links.keep(u, u_out)]
    carry = ((jnp.ones((1, LANES), F32), jnp.zeros((1, LANES), F32)),) * 4
    for zl in range(2):
        carry = lax.fori_loop(0, rows // CHUNK, functools.partial(tile, zl=zl), carry)
    ends[...] = jnp.zeros_like(ends)
    for seg in range(4):
        ends[seg : seg + 1, :] = carry[seg][1]
    at = to_partner(ends, inc)
    kept += [links.keep(siga, siga_out), links.keep(sigi, sigi_out), links.keep(decay, decay_out)]
    links.arrived(inc, at)

    def finish(b):
        seg, zl = b // 2, b % 2
        start = jnp.where(zh == 1, inc[pl.ds(seg, 1), :], 0.0)

        @pl.when(zl == 0)
        def _():
            states[seg, 0:8, :] = jnp.broadcast_to(start, (8, LANES))

        def state(at):
            there = pl.ds(pl.multiple_of(8 + zl * rows + at.start, 8), CHUNK)
            h = states[seg, there, :] + run[b, at, :] * start
            states[seg, there, :] = h
            v = gy[b, at, :]
            t = jnp.tanh(0.7978845608028654 * (v + 0.044715 * v * v * v))
            mixed[b, at, :] = (0.5 * v * (1.0 + t) * h).astype(BF)

        chunks(rows, state)

    loop(8, finish)
    for copy in kept:
        copy.wait()
    links.finish()


def recur_backward_kernel(
    do_ref, wo_ref, blocks_ref, ch_ref,
    xs_in, gy, u_in, siga_in, sigi_in, decay_in, states, rows_ref, mid_in, n2_ref, dup_ref,
    dboth_out, gb_out, ch_out, block_out, up_out,
    xs, u, siga, sigi, decay, mid_ref,
    dh, after, dgy, dlog_ref, du, dboth, halo, ends, inc, do, final, sems,
    *scratch,
):
    p = Place()
    links = Links(*scratch[-3:])
    rows, local = do_ref.shape[1], wo_ref.shape[0]
    zh = p.zh
    greet(weight_peers(p))
    scatter = RowScatter(p, links, rows_ref, scratch[:5])
    up = GradScatter(p, links, n2_ref, dup_ref, scratch[5:12], GradScatter.EARLY)

    def read(b):
        return pltpu.make_async_copy(do_ref.at[b], do.at[b % 2], sems.at[4 + b % 2])

    read(0).start()
    kept = {
        name: links.keep(src, dst)
        for name, src, dst in (
            ("decay", decay_in, decay),
            ("siga", siga_in, siga),
            ("sigi", sigi_in, sigi),
            ("u", u_in, u),
            ("xs", xs_in, xs),
            ("mid", mid_in, mid_ref),
        )
    }
    scatter.begin()
    up.begin(1)
    scatter.across_y()
    ch_out[...] = jnp.zeros_like(ch_out)
    gb_out[...] = jnp.zeros_like(gb_out)
    soft = ch_ref[0:1, :]

    def to_partner(src, dst):
        at = links.pair()
        links.start(src, dst, at, p.peer(zh=1))
        return at

    def upstream(b):
        seg, zl = b // 2, b % 2
        dh[b, :, local:] = jnp.zeros((rows, LANES - local), F32)
        read(b).wait()

        @pl.when(b < 7)
        def _():
            read(b + 1).start()

        dh[b, :, :local] = dot(do[b % 2], wo_ref[...], NT)

        def split(at):
            value, slope = gelu_both(gy[b, at, :])
            dz = dh[b, at, :]
            h = states[seg, pl.ds(pl.multiple_of(8 + zl * rows + at.start, 8), CHUNK), :]
            dh[b, at, :] = dz * value
            dgy[b, at, :] = (dz * h * slope).astype(BF)

        chunks(rows, split)

    loop(8, upstream)
    up.begin(0)
    row = lax.broadcasted_iota(jnp.int32, (8, LANES), 0)
    one = jnp.ones((1, LANES), F32)
    ends[...] = jnp.zeros_like(ends)

    def tile(i, carry, zl):
        at = pl.ds(eight(rows // 8 - 1 - i), 8)
        out = []
        for seg in range(4):
            b = seg * 2 + zl
            cp, cg, following = carry[seg]
            a = decay[b, at, :]
            shifted = jnp.where(row == 7, following, pltpu.roll(a, 7, 0))
            pa, g = tile_scan(shifted, dh[b, at, :], row, True)
            g = g + pa * cg
            pa = pa * cp
            dh[b, at, :] = g
            after[b, at, :] = pa
            out.append((pa[0:1, :], g[0:1, :], a[0:1, :]))
        return tuple(out)

    carry = ((one, jnp.zeros((1, LANES), F32), one),) * 4
    kept["decay"].wait()
    for zl in (1, 0):
        carry = lax.fori_loop(0, rows // 8, functools.partial(tile, zl=zl), carry)
    for seg in range(4):
        ends[seg : seg + 1, :] = carry[seg][1] * carry[seg][2]
    at = to_partner(ends, inc)
    links.arrived(inc, at)
    scatter.across_z()
    up.across(0)

    def gradients(b):
        seg, zl = b // 2, b % 2
        later = jnp.where(zh == 0, inc[pl.ds(seg, 1), :], 0.0)

        def body(at):
            window = states[seg, pl.ds(pl.multiple_of(zl * rows + at.start, 8), CHUNK + 8), :]
            previous = pltpu.roll(window, 1, 0)[8:]
            g = dh[b, at, :] + after[b, at, :] * later
            sa, si, a = siga[b, at, :], sigi[b, at, :], decay[b, at, :]
            uf = u[b, at, :].astype(F32)
            root = jnp.sqrt(minus_expm1((-2.0 * DECAY_SCALE) * sa * soft))
            gu = g * uf
            gr = g * root
            d_log = a * (g * previous - gu * si * a / root)
            d_log = jnp.where(real, d_log, 0.0)
            dra = (d_log * (-DECAY_SCALE * soft) * sa * (1.0 - sa)).astype(BF)
            dri = (gr * uf * si * (1.0 - si)).astype(BF)
            du[seg, pl.ds(pl.multiple_of(zl * rows + at.start, 8), CHUNK), :] = gr * si
            dlog_ref[at, :LANES] = dra
            dlog_ref[at, LANES:] = dri
            for k, v in enumerate((d_log * sa, dra.astype(F32), dri.astype(F32))):
                sums[k] = sums[k] + fold(v)

        sums = [jnp.zeros((8, LANES), F32) for _ in range(3)]
        chunks(rows, body)
        for k in range(3):
            ch_out[k] += sums[k]
        d = dlog_ref[...]
        there = pl.ds(pl.multiple_of(zl * rows, 8), rows)
        du[seg, there, :] += dot(d, blocks_ref[...], NT)
        gb_out[...] += dot(u[b], d, TN)

    lane = lax.broadcasted_iota(jnp.int32, (1, LANES), 1)
    real = lane < local
    for name in ("siga", "sigi", "u"):
        kept[name].wait()
    loop(8, gradients)
    at = to_partner(du.at[:, pl.ds(0, 8)], halo)
    up.across(1)

    def write(i, at, src, dst, base):
        return pltpu.make_async_copy(src.at[i], dst.at[at], sems.at[base + i])

    def convolve(i, zl):
        seg = i
        b = i * 2 + zl
        slot = i % 2

        @pl.when(i >= 2)
        def _():
            write(slot, b - 4, dboth, dboth_out, 0).wait()

        def body(at):
            start = pl.multiple_of(zl * rows + at.start, 8)
            v = du[seg, pl.ds(start, CHUNK + 8), :]
            x = xs[seg, pl.ds(start, CHUNK + 8), :]
            here = v[:CHUNK]
            total = ch_ref[4:5, :] * here
            sums[0] = sums[0] + fold(here)
            sums[1] = sums[1] + fold(here * x[8:])
            for k in (1, 2, 3):
                total = total + ch_ref[4 + k : 5 + k, :] * pltpu.roll(v, CHUNK + 8 - k, 0)[:CHUNK]
                sums[1 + k] = sums[1 + k] + fold(here * pltpu.roll(x, k, 0)[8:])
            wide = 2 * local - LANES
            zeros = jnp.zeros((CHUNK, wide), F32)
            left = jnp.concatenate([total, zeros], axis=1)
            right = jnp.concatenate([dgy[b, at, :].astype(F32), zeros], axis=1)
            dboth[slot, at, :] = (left + pltpu.roll(right, local, 1)).astype(BF)

        sums = [jnp.zeros((8, LANES), F32) for _ in range(5)]
        chunks(rows, body)
        for k in range(5):
            ch_out[3 + k] += sums[k]
        write(slot, b, dboth, dboth_out, 0).start()

    def drain(zl):
        for i in (2, 3):
            write(i % 2, i * 2 + zl, dboth, dboth_out, 0).wait()

    kept["xs"].wait()
    kept["mid"].wait()
    loop(4, functools.partial(convolve, zl=0))
    drain(0)
    links.arrived(halo, at)

    def tail(seg):
        du[seg, pl.ds(2 * rows, 8), :] = jnp.where(zh == 0, halo[seg], 0.0)

    loop(4, tail)
    scatter.arrive()

    def add(at):
        final[at, :] = (mid_ref[at, :] + scatter.total(at)).astype(BF)

    chunks(rows, add)
    at = links.pair()
    links.start(final, block_out.at[p.mp], at, p.peer(mp=1))
    own = links.keep(final, block_out.at[p.mp])
    loop(4, functools.partial(convolve, zl=1))
    up.last(0)
    drain(1)
    up.last(1)
    up.end()
    ff = up.result.shape[2]
    for j in range(4):
        up_out[:, j * ff : (j + 1) * ff] = up.result[j]
    own.wait()
    links.arrived(block_out.at[1 - p.mp], at)
    links.finish()


def recur_forward(tokens, w_ig, blocks, channels, gain):
    if not shape_fits():
        return plain_recur_forward(tokens, w_ig, blocks, channels, gain)
    rows, width = tokens.shape[1:]
    local = w_ig.shape[1] // 2
    table = jnp.concatenate([jax.nn.softplus(-channels[0:1]), channels[1:]], axis=0)
    f, h = (8, rows, LANES), (4, 2 * rows + 8, LANES)
    n1, *saved = run_kernel(
        recur_forward_kernel,
        "recur_forward",
        [(tokens.shape, BF), (h, F32), (f, F32), (f, BF)]
        + [(f, F32)] * 3
        + [(h, F32), (f, BF)],
        [ANY] * 7 + [VMEM] * 2,
        [ANY] + [VMEM] * 4,
        [
            pltpu.VMEM(h, F32),
            pltpu.VMEM(f, F32),
            pltpu.VMEM(f, BF),
            pltpu.VMEM(f, F32),
            pltpu.VMEM(f, F32),
            pltpu.VMEM(f, F32),
            pltpu.VMEM(f, F32),
            pltpu.VMEM((8, rows, 2 * LANES), F32),
            pltpu.VMEM((2, rows, width), BF),
            pltpu.VMEM((rows, 2 * local), F32),
            pltpu.VMEM((4, 8, LANES), F32),
            pltpu.VMEM((8, LANES), F32),
            pltpu.VMEM((8, LANES), F32),
            pltpu.VMEM((2, rows, width), BF),
        ]
        + semaphores(6, 2)[:1]
        + semaphores(2, 6),
        5,
        (tokens, w_ig, blocks, table, gain),
        61,
    )
    *saved, mixed = saved
    return n1.reshape(-1, width), mixed.reshape(-1, LANES), (table, blocks, *saved)


def recur_backward(do, saved, w_o, channels, out_part, middle, n2, dup, drows):
    if not shape_fits():
        return plain_recur_backward(do, saved, w_o, channels, out_part, middle, n2, dup, drows)
    ff = dup.shape[1]
    table, wide, xs, gy, u, siga, sigi, decay, states = saved
    rows, width = do.shape[1:]
    local = w_o.shape[0]
    f, h = (8, rows, LANES), (4, 2 * rows + 8, LANES)
    dboth, g_blocks, sums, block_out, g_up = run_kernel(
        recur_backward_kernel,
        "recur_backward",
        [
            ((8, rows, 2 * local), BF),
            ((LANES, 2 * LANES), F32),
            ((8, 8, LANES), F32),
            ((2, rows, width), BF),
            ((drows, 4 * ff), BF),
        ],
        [ANY] + [VMEM] * 2 + [ANY, VMEM],
        [ANY] + [VMEM] * 3 + [ANY, VMEM] + [ANY] * 4 + [VMEM] + [ANY] * 3 + [VMEM],
        [
            pltpu.VMEM(h, F32),
            pltpu.VMEM(f, BF),
            pltpu.VMEM(f, F32),
            pltpu.VMEM(f, F32),
            pltpu.VMEM(f, F32),
            pltpu.VMEM((rows, width), F32),
            pltpu.VMEM(f, F32),
            pltpu.VMEM(f, F32),
            pltpu.VMEM(f, BF),
            pltpu.VMEM((rows, 2 * LANES), BF),
            pltpu.VMEM(h, F32),
            pltpu.VMEM((2, rows, 2 * local), BF),
            pltpu.VMEM((4, 8, LANES), F32),
            pltpu.VMEM((8, LANES), F32),
            pltpu.VMEM((8, LANES), F32),
            pltpu.VMEM((2, rows, width), BF),
            pltpu.VMEM((rows, width), BF),
        ]
        + semaphores(6, 2)[:1]
        + scatter_buffers(rows, width)
        + grad_buffers(2 * drows, ff, 8 * rows)
        + semaphores(32, 32),
        6,
        (do, w_o, wide, table, xs, gy, u, siga, sigi, decay, states)
        + (out_part, middle, n2, dup),
        61,
    )
    sums = jnp.sum(sums, axis=1)[:, :local]
    dlam = sums[0] * DECAY_SCALE * jax.nn.sigmoid(-channels[0, :local])
    g_blocks = jnp.concatenate(
        [g_blocks[:local, g * LANES : g * LANES + local] for g in (0, 1)], axis=1
    )
    return (
        dboth.reshape(-1, 2 * local),
        g_blocks,
        jnp.concatenate([dlam[None], sums[1:]], axis=0),
        block_out,
        g_up,
    )


def plain_recur_forward(tokens, w_ig, blocks, channels, gain):
    length, local, width = tokens.shape[1], w_ig.shape[1] // 2, tokens.shape[2]
    wide = tokens.reshape(-1, width).astype(F32)
    n1 = (wide * inverse_rms(wide) * gain).astype(BF)
    both = dot(n1, w_ig, NN)
    xb = both[:, :local].astype(BF).reshape(4, 2 * length, local)
    gy = both[:, local:].reshape(4, 2 * length, local)
    rim = from_behind(xb[:, -3:], 1)
    padded = jnp.concatenate([rim, xb], axis=1).astype(F32)
    conv = channels[3]
    for k in range(4):
        conv = conv + channels[4 + k] * padded[:, 3 - k : 3 - k + 2 * length]
    u = conv.astype(BF)
    logits = dot(u.reshape(-1, local), blocks, NN).reshape(4, 2 * length, 2 * local)
    sig_a = jax.nn.sigmoid(logits[..., :local] + channels[1])
    sig_i = jax.nn.sigmoid(logits[..., local:] + channels[2])
    log_decay = -DECAY_SCALE * sig_a * jax.nn.softplus(-channels[0])
    decay = jnp.exp(log_decay)
    root = jnp.sqrt(-jnp.expm1(2.0 * log_decay))
    running, state = local_scan(decay, root * sig_i * u.astype(F32), False)
    incoming = carried(running[:, -1], state[:, -1], False)
    states = state + running * incoming[:, None]
    gelu_y, slope_y = gelu_both(gy)
    mixed = (gelu_y * states).astype(BF).reshape(-1, local)
    saved = (blocks, padded, u, sig_a, sig_i, decay, root, running, incoming, states)
    return n1, mixed, saved + (gelu_y, slope_y)


def plain_recur_backward(do, saved, w_o, channels, out_part, middle, n2, dup, drows):
    blocks, padded, u, sig_a, sig_i, decay, root, running, incoming, states = saved[:10]
    gelu_y, slope_y = saved[10:]
    length, local, width = do.shape[1], w_o.shape[0], do.shape[2]
    dz = dot(do.reshape(-1, width), w_o, NT).reshape(4, 2 * length, local)
    dh = dz * gelu_y
    dgy = (dz * states * slope_y).astype(BF)
    ones = jnp.ones_like(decay[:, :1])
    after, adjoint = local_scan(jnp.concatenate([decay[:, 1:], ones], axis=1), dh, True)
    later = carried(running[:, -1], decay[:, 0] * adjoint[:, 0], True)
    adjoint = adjoint + after * later[:, None]
    previous = jnp.concatenate([incoming[:, None], states[:, :-1]], axis=1)
    soft, uf = jax.nn.softplus(-channels[0]), u.astype(F32)
    d_root = adjoint * sig_i * uf
    d_log = adjoint * previous * decay - d_root * decay * decay / root
    dra = (d_log * (-DECAY_SCALE * soft) * sig_a * (1.0 - sig_a)).astype(BF)
    dri = (adjoint * root * uf * sig_i * (1.0 - sig_i)).astype(BF)
    dlam = jnp.sum(d_log * sig_a, axis=(0, 1)) * DECAY_SCALE * jax.nn.sigmoid(-channels[0])
    dlogits = jnp.concatenate([dra, dri], axis=2).reshape(-1, 2 * local)
    g_blocks = dot(u.reshape(-1, local), dlogits, TN)
    du = adjoint * root * sig_i + dot(dlogits, blocks, NT).reshape(4, 2 * length, local)
    zeros = jnp.zeros((4, 3, local), F32)
    spread = jnp.concatenate([zeros, du, zeros], axis=1)
    dpad = jnp.zeros((4, 2 * length + 3, local), F32)
    taps = []
    for k in range(4):
        dpad = dpad + channels[4 + k] * spread[:, k : k + 2 * length + 3]
        taps.append(jnp.sum(du * padded[:, 3 - k : 3 - k + 2 * length], axis=(0, 1)))
    back = from_behind(dpad[:, :3], -1)
    dxb = dpad[:, 3:] + jnp.concatenate(
        [jnp.zeros((4, 2 * length - 3, local), F32), back], axis=1
    )
    dboth = jnp.concatenate([dxb.astype(BF), dgy], axis=2).reshape(-1, 2 * local)
    sums = [jnp.sum(v.astype(F32), axis=(0, 1)) for v in (dra, dri, du)]
    result = (middle + Tokens().scatter(out_part.reshape(-1, width))).astype(BF)
    g_up = columns(return_grad(dot(n2, dup, TN, BF), drows), 0, dup.shape[1])
    small = jnp.stack([dlam] + sums + taps)
    return dboth, g_blocks, small, both_batches(result), g_up


def on_device(
    tokens_in,
    cotangent,
    seq_source,
    source_weight,
    input_weight,
    gelu_weight,
    decay_gates,
    input_gates,
    channel_params,
    norm_gains,
    output_weight,
    mlp_gate,
    mlp_up,
    mlp_down,
):
    sizes = tuple(lax.axis_size(n) for n in AXES)
    dxn, _, zhn, _, _ = sizes
    group = dxn * 2 * zhn * 2
    dc, zl, mp = (lax.axis_index(n) for n in ("dc", "zl", "mp"))
    slot = dc * 2 + zl
    width = tokens_in.shape[3]
    local = input_weight.shape[1] // 4
    heads = decay_gates.shape[0] // 4
    drows = input_weight.shape[0]
    piece = decay_gates.shape[1]

    tokens, w_ig, w_o, blocks, channels, gains, dm, dout, own, w_g = fetch_first(
        tokens_in[:, 0],
        cotangent[:, 0],
        seq_source,
        source_weight,
        input_weight,
        gelu_weight,
        output_weight,
        decay_gates,
        input_gates,
        channel_params,
        norm_gains,
        mlp_gate,
    )

    n1, mixed, saved = recur_forward(tokens, w_ig, blocks, channels, gains[0:1])
    middle, n2, w_u, w_d = reduce_and_fetch(mixed, w_o, own, gains[1:2], mlp_up, mlp_down)

    hidden, dgm, dup = feed_forward(n2, dm, w_g, w_u, w_d)
    n2, dm = n2.reshape(-1, width), dm.reshape(-1, width)
    dr1, gain_two, do, g_gate, g_down, out_part = reduce_and_return(
        (w_g, w_u, w_d), middle, dout, gains[1:2], dm, hidden, n2, dgm, dup, drows
    )
    gain_two = jnp.sum(gain_two, axis=0)

    dboth, g_blocks, channel_grad, block_out, g_up = recur_backward(
        do, saved, w_o, channels, out_part, middle, n2, dup, drows
    )

    g_gates = jnp.stack(
        [
            jnp.stack(
                [
                    g_blocks[
                        h * BLOCK : (h + 1) * BLOCK,
                        g * local + h * BLOCK : g * local + (h + 1) * BLOCK,
                    ]
                    for h in range(heads)
                ]
            )
            for g in range(2)
        ]
    )
    g_gates = g_gates.reshape(2 * heads, group, piece).transpose(1, 0, 2).reshape(group, -1)
    count = g_gates.shape[1]
    unit = (count + 2047) // 2048 * 16
    g_gates = jnp.pad(g_gates, ((0, 0), (0, unit * 128 - count))).astype(BF)
    grad_tokens, gain_one, g_input, g_gelu, g_output, share_gates = return_last(
        w_ig,
        own,
        dr1,
        gains[0:1],
        do.reshape(-1, width),
        mixed,
        n1,
        dboth,
        g_gates.reshape(group * unit, 128),
        drows,
    )
    gain_one = jnp.sum(gain_one, axis=0)
    g_gates = share_gates.reshape(4, -1)[:, :count].astype(F32).reshape(4, 2, heads, piece)
    g_gates = g_gates.transpose(1, 0, 2, 3).reshape(2, 4 * heads, piece)

    per = 4 * local // group
    mine = channel_grad.reshape(8, group // 4, per).transpose(1, 0, 2)
    mine = jnp.where(
        jnp.arange(4, dtype=jnp.int32)[:, None, None, None] == slot, mine[None], 0.0
    ).reshape(group, 1, 8 * per)
    mine = jnp.where(jnp.arange(2, dtype=jnp.int32)[None, :, None] == mp, mine, 0.0)
    both_gains = jnp.stack([gain_one, gain_two]).reshape(2, group, -1).transpose(1, 0, 2)
    both_gains = jnp.broadcast_to(both_gains.reshape(group, 1, -1), (group, 2, 2 * drows))
    sums = jnp.concatenate([both_gains, mine], axis=2).reshape(2 * group, -1)
    sums = jnp.sum(lax.all_to_all(sums, AXES, 0, 0, tiled=True), axis=0)
    g_gains = sums[: 2 * drows].reshape(2, drows)
    g_channels = sums[2 * drows :].reshape(8, 1, per)
    return (
        block_out[:, None],
        grad_tokens[:, None],
        g_input.astype(F32),
        g_gelu.astype(F32),
        g_gates[0],
        g_gates[1],
        g_channels,
        g_gains,
        g_output.astype(F32),
        g_gate.astype(F32),
        g_up.astype(F32),
        g_down.astype(F32),
    )


def solution(mesh):
    dpn, seqn, mpn = (mesh.shape[n] for n in ("dp", "seq", "mp"))
    fine = Mesh(mesh.devices.reshape(dpn // 2, 2, seqn // 2, 2, mpn), AXES)
    dp, seq = ("dx", "dc"), ("zh", "zl")
    shards = dp + seq
    weights = (
        P(shards, "mp"),
        P(shards, "mp"),
        P("mp", shards),
        P("mp", shards),
        P(None, "mp", shards),
        P(None, shards),
        P("mp", shards),
        P(shards, "mp"),
        P(shards, "mp"),
        P("mp", shards),
    )
    rows = P(None, dp, seq, None)
    return jax.shard_map(
        on_device,
        mesh=fine,
        in_specs=(rows, rows, P(None, dp), P()) + weights,
        out_specs=(rows, rows) + weights,
        check_vma=False,
    )
```

```python
import functools

import jax
import jax.numpy as jnp
import numpy as np
from jax import lax
from jax.experimental import pallas as pl
from jax.experimental.pallas import tpu as pltpu
from jax.sharding import Mesh, PartitionSpec as P

WIDTH = 2560
HEADS = 16
BLOCK = WIDTH // HEADS
EPSILON = 1e-06
DECAY_SCALE = 8.0
AXES = ("dx", "dc", "zh", "zl", "mp")
BF = jnp.bfloat16
F32 = jnp.float32
LANES = 384


def swap_pairs(sizes, partner):
    pairs = []
    for flat in range(int(np.prod(sizes))):
        coords = np.unravel_index(flat, sizes)
        pairs.append((flat, int(np.ravel_multi_index(partner(*map(int, coords)), sizes))))
    return pairs


def gather_blocks(x, axis, dim):
    if lax.axis_size(axis) != 2:
        return lax.all_gather(x, axis, axis=dim, tiled=False)
    here = lax.axis_index(axis)
    other = lax.ppermute(x, axis, [(0, 1), (1, 0)])
    low = jnp.where(here == 0, x, other)
    high = jnp.where(here == 0, other, x)
    return jnp.stack([low, high], axis=dim)


def scatter_blocks(x, axis, dim):
    if lax.axis_size(axis) != 2:
        n = x.shape[dim]
        out = lax.psum_scatter(x.astype(BF), axis, scatter_dimension=dim, tiled=True)
        return lax.squeeze(out, [dim]).astype(F32)
    here = lax.axis_index(axis)
    mine = lax.dynamic_index_in_dim(x, here, dim, keepdims=False)
    theirs = lax.dynamic_index_in_dim(x, 1 - here, dim, keepdims=False)
    got = lax.ppermute(theirs.astype(BF), axis, [(0, 1), (1, 0)])
    return mine.astype(F32) + got.astype(F32)


def fetch_weight(shard, parts):
    rows, cols = shard[0].shape[0], None
    pieces = [s.reshape(rows, parts, -1) for s in shard]
    joined = jnp.concatenate(pieces, axis=2) if len(pieces) > 1 else pieces[0]
    cols = joined.shape[2]
    x = jnp.transpose(joined, (1, 0, 2))
    x = lax.all_to_all(x, ("dc", "zl"), 0, 0, tiled=True)
    x = x.reshape(2, 2, rows, cols)
    x = gather_blocks(x, "zh", 1)
    x = gather_blocks(x, "dx", 0)
    return x.reshape(-1, cols)


def return_grad(grad, rows):
    cols = grad.shape[1]
    dxn, zhn = lax.axis_size("dx"), lax.axis_size("zh")
    g = grad.reshape(dxn, 2, zhn, 2, rows, cols)
    g = scatter_blocks(g, "dx", 0)
    g = scatter_blocks(g, "zh", 1)
    g = g.astype(BF).reshape(4, rows, cols)
    return lax.all_to_all(g, ("dc", "zl"), 0, 0, tiled=True)


class Tokens:
    def __init__(self):
        sizes = tuple(lax.axis_size(n) for n in AXES)
        self.core = swap_pairs(sizes, lambda a, b, c, d, e: (a, 1 - b, c, d, e))
        self.first = swap_pairs(
            sizes, lambda a, b, c, d, e: (a, b, c, d, 1 - e) if b == 0 else (a, b, c, 1 - d, e)
        )
        self.second = swap_pairs(
            sizes, lambda a, b, c, d, e: (a, b, c, 1 - d, e) if b == 0 else (a, b, c, d, 1 - e)
        )
        self.dc, self.zl, self.mp = (lax.axis_index(n) for n in ("dc", "zl", "mp"))

    def order(self, dc):
        mp, zl = self.mp, self.zl
        own = mp * 2 + zl
        by_mp = (1 - mp) * 2 + zl
        by_zl = mp * 2 + 1 - zl
        both = (1 - mp) * 2 + 1 - zl
        one = jnp.where(dc == 0, by_mp, by_zl)
        two = jnp.where(dc == 0, by_zl, by_mp)
        return own, one, two, both

    def gather(self, x):
        rows, width = x.shape
        one = lax.ppermute(x, AXES, self.first)
        two = lax.ppermute(jnp.stack([x, one]), AXES, self.second)
        far = [lax.ppermute(v, AXES, self.core) for v in (x, one, two)]
        out = jnp.zeros((8, rows, width), x.dtype)
        for dc, blocks in (
            (self.dc, (x, one, two[0], two[1])),
            (1 - self.dc, (far[0], far[1], far[2][0], far[2][1])),
        ):
            for at, block in zip(self.order(dc), blocks):
                out = lax.dynamic_update_index_in_dim(out, block, dc * 4 + at, 0)
        return out.reshape(8 * rows, width)

    def scatter(self, x):
        rows, width = x.shape[0] // 8, x.shape[1]
        x = x.reshape(2, 4, rows, width)
        theirs = lax.dynamic_index_in_dim(x, 1 - self.dc, 0, keepdims=False).astype(BF)
        mine = lax.dynamic_index_in_dim(x, self.dc, 0, keepdims=False)
        total = mine.astype(F32) + lax.ppermute(theirs, AXES, self.core).astype(F32)
        own, one, two, both = self.order(self.dc)
        pick = lambda at: lax.dynamic_index_in_dim(total, at, 0, keepdims=False)
        got = lax.ppermute(jnp.stack([pick(two), pick(both)]).astype(BF), AXES, self.second)
        keep_own = pick(own) + got[0].astype(F32)
        keep_one = pick(one) + got[1].astype(F32)
        got = lax.ppermute(keep_one.astype(BF), AXES, self.first)
        return keep_own + got.astype(F32)


MESH = pl.DeviceIdType.MESH
ANY = pl.BlockSpec(memory_space=pl.ANY)
VMEM = pl.BlockSpec(memory_space=pltpu.VMEM)


def flip(index, by):
    return 1 - index if by else index


class Place:
    def __init__(self):
        self.dx, self.dc, self.zh, self.zl, self.mp = (lax.axis_index(n) for n in AXES)

    def peer(self, dx=0, dc=0, zh=0, zl=0, mp=0):
        return (
            flip(self.dx, dx),
            flip(self.dc, dc),
            flip(self.zh, zh),
            flip(self.zl, zl),
            flip(self.mp, mp),
        )

    def block(self, dx=0, dc=0, zh=0, zl=0):
        a, b, c, d, _ = self.peer(dx, dc, zh, zl)
        return ((a * 2 + b) * 2 + c) * 2 + d

    def slot(self, dc=0, zl=0):
        return flip(self.dc, dc) * 2 + flip(self.zl, zl)

    def rows(self, dc=0, mp=0, zl=0):
        return (flip(self.dc, dc) * 2 + flip(self.mp, mp)) * 2 + flip(self.zl, zl)


def greet(peers):
    barrier = pltpu.get_barrier_semaphore()
    for device in peers:
        pl.semaphore_signal(barrier, inc=1, device_id=device, device_id_type=MESH)
    pl.semaphore_wait(barrier, len(peers))


class Links:
    def __init__(self, send, recv, local):
        self.send, self.recv, self.local = send, recv, local
        self.n, self.m = 0, 0
        self.sent, self.copies = [], []

    def pair(self):
        self.n += 1
        return self.n - 1

    def start(self, src, dst, at, device):
        copy = pltpu.make_async_remote_copy(
            src_ref=src,
            dst_ref=dst,
            send_sem=self.send.at[at],
            recv_sem=self.recv.at[at],
            device_id=device,
            device_id_type=MESH,
        )
        copy.start()
        self.sent.append(copy)

    def arrived(self, ref, at):
        pltpu.make_async_copy(ref, ref, self.recv.at[at]).wait()

    def keep(self, src, dst):
        copy = pltpu.make_async_copy(src, dst, self.local.at[self.m])
        self.m += 1
        copy.start()
        return copy

    def finish(self):
        for copy in self.sent:
            copy.wait_send()


FLIPS = [(zh, dc, zl) for zh in (1, 0) for dc in (0, 1) for zl in (0, 1)]


class WeightGather:
    def __init__(self, place, links, source, target, unit):
        self.place, self.links, self.target = place, links, target
        self.at = {f: links.pair() for f in FLIPS}
        self.cross = {(zh, dc): links.pair() for zh in (0, 1) for dc in (0, 1)}
        self.source = source
        self.kept = None

    def begin(self, zhs=(1, 0), dcs=(0, 1)):
        p = self.place
        mine = p.block()
        for f in FLIPS:
            zh, dc, zl = f
            if zh not in zhs or dc not in dcs:
                continue
            src, dst = self.source(p.slot(dc, zl)), self.target(mine, 1)
            if f == (0, 0, 0):
                self.kept = self.links.keep(src, dst)
            else:
                self.links.start(src, dst, self.at[f], p.peer(dc=dc, zh=zh, zl=zl))

    def onward(self, zh, dcs=(0, 1)):
        p = self.place
        for dc in dcs:
            for zl in (0, 1):
                if (zh, dc, zl) == (0, 0, 0):
                    self.kept.wait()
                else:
                    self.links.arrived(
                        self.target(p.block(dc=dc, zh=zh, zl=zl), 1), self.at[zh, dc, zl]
                    )
            two = self.target(p.block(dc=dc, zh=zh) // 2 * 2, 2)
            self.links.start(two, two, self.cross[zh, dc], p.peer(dx=1))

    def end(self):
        p = self.place
        for zh in (0, 1):
            for dc in (0, 1):
                two = self.target(p.block(dx=1, dc=dc, zh=zh) // 2 * 2, 2)
                self.links.arrived(two, self.cross[zh, dc])


def row_blocks(ref, unit, cols=None):
    def target(first, count):
        rows = pl.ds(pl.multiple_of(first * unit, unit), count * unit)
        return ref.at[rows] if cols is None else ref.at[rows, cols]

    return target


def column_blocks(ref, unit):
    return lambda first, count: ref.at[:, pl.ds(pl.multiple_of(first * unit, unit), count * unit)]


def first_kernel(
    weight_ref, source_ref, tok_ref, cot_ref, ig_ref, o_ref, gates_ref, small_ref, gate_ref,
    all_ref, wig_ref, wo_ref, wide_ref, ch_ref, gains_ref, dms_ref, dout_ref, own_ref, wg_ref,
    pieces, smalls, dm, send, recv, local,
):
    p = Place()
    links = Links(send, recv, local)
    drows = ig_ref.shape[1]
    crows = wo_ref.shape[0]
    greet(weight_peers(p))
    gather = TokenGatherTwice(p, links, tok_ref, all_ref)
    w_ig = WeightGather(p, links, lambda j: ig_ref.at[j], row_blocks(wig_ref, drows), drows)
    w_o = WeightGather(
        p,
        links,
        lambda j: o_ref.at[pl.ds(pl.multiple_of(j * crows, 16), crows)],
        column_blocks(wo_ref, o_ref.shape[1]),
        drows,
    )
    unit = gates_ref.shape[1]
    w_g = WeightGather(p, links, lambda j: gates_ref.at[j], row_blocks(pieces, unit), unit)
    w_s = WeightGather(p, links, lambda j: small_ref, row_blocks(smalls, 16), 16)
    w_gate = slot_columns(p, links, gate_ref, wg_ref)
    adjoint = TokenGatherTwice(p, links, dm, dms_ref)
    w_s.begin()
    w_ig.begin((1,))
    w_ig.begin((0,))
    w_g.begin((0,))
    w_o.begin((0,))
    gather.begin()
    own = links.keep(tok_ref.at[p.mp], own_ref)
    scales = [weight_ref[source_ref[m, 0]] for m in range(2)]
    for m in range(2):

        def scale(rows, m=m):
            value = cot_ref[m, rows, :].astype(F32) * scales[m]
            dm[m, rows, :] = value.astype(BF)

            @pl.when(p.mp == m)
            def _():
                dout_ref[rows, :] = value

        chunks(cot_ref.shape[1], scale, 1)
    adjoint.begin()
    w_ig.onward(0)
    w_g.onward(0)
    w_o.onward(0)
    w_s.onward(0)
    w_gate.begin((0,))
    w_o.begin((1,))
    w_g.begin((1,))
    w_ig.onward(1)
    w_gate.begin((1,), (0,))
    w_s.onward(1)
    gather.forward()
    w_o.onward(1)
    w_g.onward(1)
    w_gate.begin((1,), (1,))
    gather.forward_core()
    w_gate.onward(0)
    adjoint.forward()
    w_gate.onward(1, (0,))
    adjoint.forward_core()
    w_s.end()
    count = small_channels(local_channels=crows)
    table = jnp.zeros((8, LANES), F32)
    for k in range(4):
        at = pl.ds(pl.multiple_of((p.slot() * 4 + k) * 16, 16), 16)
        rows = smalls[at, :].astype(F32)[:8]
        rows = jnp.concatenate([rows, jnp.zeros((8, LANES - 128), F32)], axis=1)
        table = table + (pltpu.roll(rows, k * count, 1) if k else rows)
    ch_ref[...] = table
    for k in range(16):
        rows = smalls[k * 16 : (k + 1) * 16, :].astype(F32)
        gains_ref[:, k * 128 : (k + 1) * 128] = rows[8:10]
    w_g.end()
    size = crows // 2
    per = size // 16
    total = jnp.zeros(wide_ref.shape, F32)
    row = lax.broadcasted_iota(jnp.int32, (LANES, pieces.shape[0]), 0)
    column = lax.broadcasted_iota(jnp.int32, (LANES, pieces.shape[0]), 1)
    source = lax.broadcasted_iota(jnp.int32, (LANES, 2 * LANES), 0)
    target = lax.broadcasted_iota(jnp.int32, (LANES, 2 * LANES), 1)
    for h in range(2):
        r = column % 32 - h * 16
        wanted = (r >= 0) & (r < per) & (row == h * size + column // 32 * per + r)
        rows = dot(jnp.where(wanted, 1.0, 0.0).astype(BF), pieces[...], NN, BF)
        gate = target // LANES
        wanted = (source == target - gate * LANES - h * size + gate * size) & (
            (source >= gate * size) & (source < (gate + 1) * size)
        )
        total = total + dot(rows, jnp.where(wanted, 1.0, 0.0).astype(BF), NN)
    wide_ref[...] = total.astype(BF)
    w_gate.onward(1, (1,))
    own.wait()
    gather.end()
    adjoint.end()
    w_gate.end()
    w_ig.end()
    w_o.end()
    links.finish()


def small_channels(local_channels):
    return local_channels // 4


class TokenGatherTwice:
    def __init__(self, place, links, source, target):
        self.place, self.links, self.source, self.target = place, links, source, target
        self.z, self.y = links.pair(), links.pair()
        self.core = {(mp, zl): links.pair() for mp in (0, 1) for zl in (0, 1)}

    def begin(self):
        p = self.place
        self.kept = []
        for mp in (0, 1):
            at = p.rows(mp=mp)
            src = self.source.at[flip(p.mp, mp)]
            if mp == 0:
                self.links.start(src, self.target.at[at], self.z, p.peer(zl=1))
            self.links.start(src, self.target.at[at], self.core[mp, 0], p.peer(dc=1))
            self.kept.append(self.links.keep(src, self.target.at[at]))

    def forward(self):
        p = self.place
        far = self.target.at[p.rows(zl=1)]
        self.links.arrived(far, self.z)
        self.links.start(far, far, self.y, p.peer(mp=1))
        self.links.start(far, far, self.core[0, 1], p.peer(dc=1))

    def forward_core(self):
        p = self.place
        far = self.target.at[p.rows(mp=1, zl=1)]
        self.links.arrived(far, self.y)
        self.links.start(far, far, self.core[1, 1], p.peer(dc=1))

    def end(self):
        p = self.place
        for (mp, zl), at in self.core.items():
            self.links.arrived(self.target.at[p.rows(dc=1, mp=mp, zl=zl)], at)
        for copy in self.kept:
            copy.wait()


class TokenGather:
    def __init__(self, place, links, source, target, span):
        self.place, self.links = place, links
        self.span = pl.ds(*span)
        self.source, self.target = source.at[self.span], target
        self.z, self.y0, self.y1 = links.pair(), links.pair(), links.pair()
        self.core = {(mp, zl): links.pair() for mp in (0, 1) for zl in (0, 1)}

    def block(self, **where):
        return self.target.at[self.place.rows(**where), self.span]

    def begin(self):
        p = self.place
        at = self.block()
        self.links.start(self.source, at, self.z, p.peer(zl=1))
        self.links.start(self.source, at, self.y0, p.peer(mp=1))
        self.links.start(self.source, at, self.core[0, 0], p.peer(dc=1))
        self.kept = self.links.keep(self.source, at)

    def forward(self):
        p = self.place
        far = self.block(zl=1)
        self.links.arrived(far, self.z)
        self.links.start(far, far, self.y1, p.peer(mp=1))
        self.links.start(far, far, self.core[0, 1], p.peer(dc=1))

    def forward_core(self):
        p = self.place
        far = self.block(mp=1)
        self.links.arrived(far, self.y0)
        self.links.start(far, far, self.core[1, 0], p.peer(dc=1))
        far = self.block(mp=1, zl=1)
        self.links.arrived(far, self.y1)
        self.links.start(far, far, self.core[1, 1], p.peer(dc=1))

    def end(self):
        for (mp, zl), at in self.core.items():
            self.links.arrived(self.block(dc=1, mp=mp, zl=zl), at)
        self.kept.wait()


CHUNK = 16


def chunks(count, body, most=11, first=0):
    n = count // CHUNK
    per = max(k for k in range(1, most + 1) if n % k == 0)

    def step(i, carry):
        for k in range(per):
            body(pl.ds(pl.multiple_of(first + (i * per + k) * CHUNK, CHUNK), CHUNK))
        return carry

    if n == per:
        step(0, 0)
    else:
        lax.fori_loop(0, n // per, step, 0)


def halves(rows):
    first = (rows // 2 + CHUNK - 1) // CHUNK * CHUNK
    return [(0, first), (first, rows - first)]


class RowScatter:
    def __init__(self, place, links, source, buffers, parts=None):
        self.place, self.links, self.source = place, links, source
        self.mine, self.from_core, self.from_y, self.from_z, self.out = buffers[:5]
        self.to_core = buffers[5] if len(buffers) > 5 else None
        self.parts = parts or [(0, self.mine.shape[1])]
        self.blocks = [(mp, zl) for mp in (1, 0) for zl in (1, 0)]
        self.kept = {}
        n = range(len(self.parts))
        self.core = {(h, block): links.pair() for h in n for block in self.blocks}
        self.y = {(h, zl): links.pair() for h in n for zl in (1, 0)}
        self.z = {h: links.pair() for h in n}

    def begin(self, mps=(1, 0)):
        p = self.place
        for mp, zl in self.blocks:
            if mp not in mps:
                continue
            i, block = mp * 2 + zl, p.rows(dc=1, mp=mp, zl=zl)
            if self.to_core is None:
                src = self.source.at[block]
            else:
                self.to_core[i] = self.source(block).astype(BF)
                src = self.to_core.at[i]
            for h, part in enumerate(self.parts):
                at = pl.ds(*part)
                self.links.start(
                    src.at[at], self.from_core.at[i, at], self.core[h, (mp, zl)], p.peer(dc=1)
                )
            block = p.rows(mp=mp, zl=zl)
            if self.to_core is None:
                self.kept[mp, zl] = self.links.keep(self.source.at[block], self.mine.at[i])
            else:
                self.mine[i] = self.source(block).astype(BF)

    def ready(self, mp, zl, h):
        i = mp * 2 + zl
        if h == 0 and self.kept:
            self.kept[mp, zl].wait()
        at = pl.ds(*self.parts[h])
        self.links.arrived(self.from_core.at[i, at], self.core[h, (mp, zl)])
        return i

    def across_y(self, h=0):
        p = self.place
        first, count = self.parts[h]
        at = pl.ds(first, count)
        for zl in (1, 0):
            i = self.ready(1, zl, h)

            def add(rows, i=i, zl=zl):
                total = self.mine[i, rows, :].astype(F32) + self.from_core[i, rows, :].astype(F32)
                self.out[zl, rows, :] = total.astype(BF)

            chunks(count, add, first=first)
            self.links.start(
                self.out.at[zl, at], self.from_y.at[zl, at], self.y[h, zl], p.peer(mp=1)
            )

    def across_z(self, h=0):
        p = self.place
        first, count = self.parts[h]
        at = pl.ds(first, count)
        i = self.ready(0, 1, h)
        self.links.arrived(self.from_y.at[1, at], self.y[h, 1])

        def add(rows):
            total = self.mine[i, rows, :].astype(F32) + self.from_core[i, rows, :].astype(F32)
            self.out[2, rows, :] = (total + self.from_y[1, rows, :].astype(F32)).astype(BF)

        chunks(count, add, first=first)
        self.links.start(self.out.at[2, at], self.from_z.at[at], self.z[h], p.peer(zl=1))

    def arrive(self, h=0):
        at = pl.ds(*self.parts[h])
        self.ready(0, 0, h)
        self.links.arrived(self.from_y.at[0, at], self.y[h, 0])
        self.links.arrived(self.from_z.at[at], self.z[h])

    def total(self, rows):
        a = self.mine[0, rows, :].astype(F32) + self.from_core[0, rows, :].astype(F32)
        b = self.from_y[0, rows, :].astype(F32) + self.from_z[rows, :].astype(F32)
        return a + b


def scatter_buffers(rows, width, products=False):
    return [
        pltpu.VMEM((4, rows, width), BF),
        pltpu.VMEM((4, rows, width), BF),
        pltpu.VMEM((2, rows, width), BF),
        pltpu.VMEM((rows, width), BF),
        pltpu.VMEM((3, rows, width), BF),
    ] + ([pltpu.VMEM((4, rows, width), BF)] if products else [])


def group_peers(p):
    return [p.peer(dc=1), p.peer(zl=1), p.peer(mp=1)]


def weight_peers(p):
    return [p.peer(dc=dc, zh=zh, zl=zl) for zh, dc, zl in FLIPS if (zh, dc, zl) != (0, 0, 0)] + [
        p.peer(dx=1),
        p.peer(mp=1),
    ]


def second_kernel(
    mixed_ref, wo_ref, own_ref, gain_ref, up_ref, down_ref,
    mid_ref, all_ref, wu_ref, wd_ref,
    *scratch,
):
    p = Place()
    links = Links(*scratch[-3:])
    normed = scratch[-4]
    rows, channels = own_ref.shape[0], wo_ref.shape[0]
    greet(weight_peers(p))

    def project(b):
        at = pl.ds(pl.multiple_of(b * rows, 16), rows)
        return dot(mixed_ref[at, :channels], wo_ref[...], NN)

    parts = halves(rows)
    scatter = RowScatter(p, links, project, scratch[:6], parts)
    w_u = slot_columns(p, links, up_ref, wu_ref)
    w_d = WeightGather(
        p,
        links,
        lambda j: down_ref.at[pl.ds(pl.multiple_of(j * wd_ref.shape[0], 16), wd_ref.shape[0])],
        column_blocks(wd_ref, down_ref.shape[1]),
        down_ref.shape[1],
    )
    gathers = [TokenGather(p, links, normed, all_ref, part) for part in parts]
    w_u.begin((1,), (0,))
    scatter.begin((1,))
    w_u.begin((0,))
    scatter.across_y(0)
    scatter.across_y(1)
    w_u.begin((1,), (1,))
    scatter.begin((0,))
    w_d.begin((0,))
    w_u.onward(0)

    def normalise(at):
        value = own_ref[at, :].astype(F32) + scatter.total(at)
        mid_ref[at, :] = value
        inv = lax.rsqrt(jnp.mean(value * value, axis=-1, keepdims=True) + EPSILON)
        normed[at, :] = (value * inv * gain_ref[...]).astype(BF)

    def middle(h):
        scatter.arrive(h)
        chunks(parts[h][1], normalise, first=parts[h][0])
        gathers[h].begin()

    scatter.across_z(0)
    w_d.onward(0)
    scatter.across_z(1)
    w_d.begin((1,), (0,))
    middle(0)
    w_u.onward(1, (0,))
    middle(1)
    w_u.onward(1, (1,))
    w_d.begin((1,), (1,))
    gathers[0].forward()
    gathers[1].forward()
    w_d.onward(1, (0,))
    gathers[0].forward_core()
    gathers[1].forward_core()
    w_d.onward(1, (1,))
    for gather in gathers:
        gather.end()
    w_u.end()
    w_d.end()
    links.finish()


def slot_columns(p, links, source, result):
    count = result.shape[1]
    return WeightGather(
        p,
        links,
        lambda j: source.at[:, pl.ds(pl.multiple_of(j * count, 128), count)],
        row_blocks(result, source.shape[0]),
        source.shape[0],
    )


class GradScatter:
    FAR = [(1, 0, 1), (1, 1, 1)], [(1, 0, 0), (1, 1, 0)]
    NEAR = [(0, 0, 1), (0, 1, 1)], [(0, 0, 0), (0, 1, 0)]
    ORDER = FAR[0] + NEAR[0] + FAR[1] + NEAR[1]
    EARLY = FAR[0] + FAR[1] + NEAR[0] + NEAR[1]

    def __init__(self, place, links, left, right, buffers, order=ORDER):
        self.order = order
        self.place, self.links, self.left, self.right = place, links, left, right
        self.to_x, self.from_x, self.to_z, self.from_z, self.sums, self.result = buffers[:6]
        self.columns = buffers[6] if len(buffers) > 6 else None
        self.rows = self.to_x.shape[1]
        self.x = {(zh, dc): links.pair() for zh in (1, 0) for dc in (0, 1)}
        self.z = {dc: links.pair() for dc in (0, 1)}
        self.at = {(dc, zl): links.pair() for dc in (0, 1) for zl in (0, 1)}
        self.count = 0
        self.load()

    def load(self):
        if self.count < 8 and self.columns is not None:
            dx, dc, zh = self.order[self.count]
            first = self.place.block(dx=dx, dc=dc, zh=zh) // 2
            columns = pl.ds(pl.multiple_of(first * self.rows, self.rows), self.rows)
            self.loading = self.links.keep(
                self.left.at[:, columns], self.columns.at[self.count % 2]
            )

    def product(self, dx=0, dc=0, zh=0):
        assert self.order[self.count] == (dx, dc, zh)
        self.loading.wait()
        self.count += 1
        self.load()
        return dot(self.columns[(self.count - 1) % 2], self.right[...], TN)

    def begin(self, zh):
        for dc in (0, 1):
            i = zh * 2 + dc
            self.to_x[i] = self.product(dx=1, dc=dc, zh=zh).astype(BF)
            self.links.start(
                self.to_x.at[i], self.from_x.at[i], self.x[zh, dc], self.place.peer(dx=1)
            )

    def across(self, dc):
        mine = self.product(dc=dc, zh=1)
        self.links.arrived(self.from_x.at[2 + dc], self.x[1, dc])
        self.to_z[dc] = (mine + self.from_x[2 + dc].astype(F32)).astype(BF)
        self.links.start(self.to_z.at[dc], self.from_z.at[dc], self.z[dc], self.place.peer(zh=1))

    def last(self, dc):
        p = self.place
        mine = self.product(dc=dc, zh=0)
        self.links.arrived(self.from_x.at[dc], self.x[0, dc])
        self.links.arrived(self.from_z.at[dc], self.z[dc])
        total = mine + self.from_x[dc].astype(F32) + self.from_z[dc].astype(F32)
        self.sums[dc] = total.astype(BF)
        unit = self.rows // 2
        for zl in (1, 0):
            src = self.sums.at[dc, pl.ds(pl.multiple_of(flip(p.zl, zl) * unit, unit), unit)]
            dst = self.result.at[p.slot()]
            if (dc, zl) == (0, 0):
                self.own = self.links.keep(src, dst)
            else:
                self.links.start(src, dst, self.at[dc, zl], p.peer(dc=dc, zl=zl))

    def end(self):
        p = self.place
        for (dc, zl), at in self.at.items():
            if (dc, zl) == (0, 0):
                self.own.wait()
            else:
                self.links.arrived(self.result.at[p.slot(dc, zl)], at)


class Ready(GradScatter):
    def product(self, dx=0, dc=0, zh=0):
        first = self.place.block(dx=dx, dc=dc, zh=zh) // 2
        return self.left[pl.ds(pl.multiple_of(first * self.rows, self.rows), self.rows), :].astype(
            F32
        )


def grad_buffers(rows, columns, tokens=None):
    return (
        [pltpu.VMEM((n, rows, columns), BF) for n in (4, 4, 2, 2, 2)]
        + [pltpu.VMEM((4, rows // 2, columns), BF)]
        + ([pltpu.VMEM((2, tokens, rows), BF)] if tokens else [])
    )


def norm_back(value, gain, upstream):
    inv = lax.rsqrt(jnp.mean(value * value, axis=-1, keepdims=True) + EPSILON)
    scaled = value * inv
    up = upstream * gain
    inner = jnp.mean(up * scaled, axis=-1, keepdims=True)
    return inv * (up - scaled * inner), upstream * scaled


def fold(rows):
    return rows[:8] + rows[8:]


def third_kernel(
    wg_ref, wu_ref, wd_in, mid_in, dout_in, gain_ref, dm_ref, hidden_ref, n2_ref, dgm_ref,
    dup_ref,
    dr1_ref, gain_out, all_ref, gate_out, down_out, part_out,
    *scratch,
):
    p = Place()
    links = Links(*scratch[-3:])
    do, wd_ref, mid_ref, dout_ref = scratch[-7:-3]
    rows_of = mid_ref.shape[0]
    staged = [
        links.keep(src, dst)
        for src, dst in ((mid_in, mid_ref), (dout_in, dout_ref), (wd_in, wd_ref))
    ]
    greet(weight_peers(p))

    def product(b):
        at = pl.ds(pl.multiple_of(b * rows_of, 16), rows_of)
        return dot(dgm_ref[at, :], wg_ref[...], NT) + dot(dup_ref[at, :], wu_ref[...], NT)

    parts = halves(rows_of)
    scatter = RowScatter(p, links, product, scratch[:6], parts)
    down = GradScatter(p, links, dm_ref, hidden_ref, scratch[6:13])
    gate = GradScatter(p, links, n2_ref, dgm_ref, scratch[13:20])
    gathers = [TokenGather(p, links, do, all_ref, part) for part in parts]
    down.begin(1)
    scatter.begin((1,))
    scatter.across_y(0)
    scatter.across_y(1)
    down.across(0)
    scatter.begin((0,))
    down.across(1)
    gate.begin(1)
    gain_out[...] = jnp.zeros_like(gain_out)
    for copy in staged:
        copy.wait()

    def back(rows):
        part, gain = norm_back(mid_ref[rows, :], gain_ref[...], scatter.total(rows))
        value = dout_ref[rows, :] + part
        dr1_ref[rows, :] = value
        do[rows, :] = value.astype(BF)
        gain_out[...] += fold(gain)

    def middle(h):
        scatter.arrive(h)
        chunks(parts[h][1], back, first=parts[h][0])
        gathers[h].begin()

    scatter.across_z(0)
    down.begin(0)
    gate.across(0)
    scatter.across_z(1)
    middle(0)
    gate.across(1)
    gate.begin(0)
    middle(1)
    gathers[0].forward()
    gathers[1].forward()
    down.last(0)
    down.last(1)
    gathers[0].forward_core()
    gate.last(0)
    out = scratch[0]
    writes = []
    for b in range(8):
        if b >= 4:
            writes[b - 4].wait()
        at = pl.ds(b * rows_of, rows_of)
        out[b % 4] = dot(hidden_ref[at, :], wd_ref[...], NN, BF)
        writes.append(links.keep(out.at[b % 4], part_out.at[b]))
    gathers[1].forward_core()
    gate.last(1)
    for gather in gathers:
        gather.end()
    down.end()
    ff = down.result.shape[2]
    for j in range(4):
        down_out[j * ff : (j + 1) * ff, :] = down.result[j].astype(F32).T.astype(BF)
    gate.end()
    for j in range(4):
        gate_out[:, j * ff : (j + 1) * ff] = gate.result[j]
    for write in writes[4:]:
        write.wait()
    links.finish()


def fourth_kernel(
    wig_ref, own_ref, dr1_ref, gain_ref, do_ref, mixed_ref, n1_ref, dboth_ref, gg_ref,
    dx_ref, gain_out, in_out, gelu_out, out_out, gates_out,
    *scratch,
):
    p = Place()
    links = Links(*scratch[-3:])
    dx_send, dx_recv = scratch[-5:-3]
    greet(weight_peers(p))
    rows_of = own_ref.shape[0]

    def product(b):
        at = pl.ds(pl.multiple_of(b * rows_of, 16), rows_of)
        return dot(dboth_ref[at, :], wig_ref[...], NT)

    parts = halves(rows_of)
    scatter = RowScatter(p, links, product, scratch[:6], parts)
    out = GradScatter(p, links, do_ref, mixed_ref, scratch[6:13])
    wide = GradScatter(p, links, n1_ref, dboth_ref, scratch[13:20])
    gates = Ready(p, links, gg_ref, None, scratch[20:26])
    out.begin(1)
    scatter.begin((1,))
    scatter.across_y(0)
    scatter.across_y(1)
    out.across(0)
    out.across(1)
    wide.begin(1)
    scatter.begin((0,))
    gates.begin(1)
    out.begin(0)
    for g in (wide, gates):
        g.across(0)
        g.across(1)
        g.begin(0)
    gain_out[...] = jnp.zeros_like(gain_out)

    def back(rows):
        value = own_ref[rows, :].astype(F32)
        part, gain = norm_back(value, gain_ref[...], scatter.total(rows))
        total = dr1_ref[rows, :] + part
        dx_ref[p.mp, rows, :] = total
        dx_send[rows, :] = total.astype(BF)
        gain_out[...] += fold(gain)

    sent = []

    def middle(h):
        scatter.arrive(h)
        chunks(parts[h][1], back, first=parts[h][0])
        span, at = pl.ds(*parts[h]), links.pair()
        links.start(dx_send.at[span], dx_recv.at[span], at, p.peer(mp=1))
        sent.append((span, at))

    scatter.across_z(0)
    scatter.across_z(1)
    middle(0)
    for g in (out, gates):
        g.last(0)
        g.last(1)
    middle(1)
    wide.last(0)
    wide.last(1)
    local = out.result.shape[2]
    out.end()
    for j in range(4):
        out_out[j * out_out.shape[0] // 4 : (j + 1) * out_out.shape[0] // 4, :] = (
            out.result[j].astype(F32).T[: out_out.shape[0] // 4].astype(BF)
        )
    gates.end()
    gates_out[...] = gates.result[...]
    wide.end()
    two = wide.result.shape[2]
    left = lax.broadcasted_iota(jnp.int32, (1, two), 1) < two // 2
    for j in (0, 2):
        a, b = (wide.result[j + i].astype(F32) for i in (0, 1))
        span = slice(j * two // 2, (j + 2) * two // 2)
        in_out[:, span] = jnp.where(left, a, pltpu.roll(b, two // 2, 1)).astype(BF)
        gelu_out[:, span] = jnp.where(left, pltpu.roll(a, two // 2, 1), b).astype(BF)
    for span, at in sent:
        links.arrived(dx_recv.at[span], at)
    dx_ref[1 - p.mp] = dx_recv[...].astype(F32)
    links.finish()


def mlp_kernel(
    n2_ref, dm_ref, wg_ref, wu_ref, wd_ref, hidden_ref, dgm_ref, dup_ref, pre, upp, dhm
):
    count, rows, width = n2_ref.shape
    n2 = n2_ref[...].reshape(count * rows, width)
    pre[...] = dot(n2, wg_ref[...], NN)
    upp[...] = dot(n2, wu_ref[...], NN)
    dhm[...] = dot(dm_ref[...].reshape(count * rows, width), wd_ref[...], NT)

    def body(at):
        up, d = upp[at, :], dhm[at, :]
        value, slope = gelu_both(pre[at, :])
        hidden_ref[at, :] = (value * up).astype(BF)
        dgm_ref[at, :] = (d * up * slope).astype(BF)
        dup_ref[at, :] = (d * value).astype(BF)

    chunks(count * rows, body)


def feed_forward(n2, dm, w_g, w_u, w_d):
    blocks, rows, width = n2.shape
    ff = w_d.shape[0]
    if not shape_fits():
        n2, dm = n2.reshape(-1, width), dm.reshape(-1, width)
        pre, d = dot(n2, w_g, NN), dot(dm, w_d, NT)
        gm, up = pre, dot(n2, w_u, NN)
        value, slope = gelu_both(gm)
        return (value * up).astype(BF), (d * up * slope).astype(BF), (d * value).astype(BF)
    two = pl.BlockSpec((2, rows, width), lambda i: (i, 0, 0))
    flat = pl.BlockSpec((2 * rows, ff), lambda i: (i, 0))
    whole = lambda v: pl.BlockSpec(v.shape, lambda i: (0, 0))
    total = blocks * rows
    return pl.pallas_call(
        mlp_kernel,
        name="feed_forward",
        grid=(blocks // 2,),
        in_specs=[two, two, whole(w_g), whole(w_u), whole(w_d)],
        out_specs=[flat] * 3,
        out_shape=[jax.ShapeDtypeStruct((total, ff), BF)] * 3,
        scratch_shapes=[pltpu.VMEM((2 * rows, ff), F32)] * 3,
        compiler_params=pltpu.CompilerParams(vmem_limit_bytes=48 * 1024 * 1024),
        cost_estimate=pl.CostEstimate(
            flops=2 * total * width * ff * 3, bytes_accessed=total * width * 4, transcendentals=0
        ),
    )(n2, dm, w_g, w_u, w_d)


def semaphores(pairs, local):
    return [
        pltpu.SemaphoreType.DMA((pairs,)),
        pltpu.SemaphoreType.DMA((pairs,)),
        pltpu.SemaphoreType.DMA((local,)),
    ]


def run_kernel(body, name, outs, out_specs, in_specs, scratch, ident, args, mib=40):
    return pl.pallas_call(
        body,
        name=name,
        out_shape=[jax.ShapeDtypeStruct(*o) for o in outs],
        in_specs=in_specs,
        out_specs=out_specs,
        scratch_shapes=scratch,
        compiler_params=pltpu.CompilerParams(
            collective_id=ident, has_side_effects=True, vmem_limit_bytes=mib * 1024 * 1024
        ),
    )(*args)


def fetch_first(
    tokens, cotangent, seq_source, source_weight, input_weight, gelu_weight, output_weight,
    decay_gates, input_gates, channel_params, norm_gains, mlp_gate,
):
    args = (
        tokens, cotangent, seq_source, source_weight, input_weight, gelu_weight, output_weight,
        decay_gates, input_gates, channel_params, norm_gains, mlp_gate,
    )
    if not shape_fits():
        return plain_fetch_first(*args)
    rows, width = tokens.shape[1:]
    drows, local = input_weight.shape[0], input_weight.shape[1] // 4
    pairs = [v.reshape(drows, 4, local) for v in (input_weight, gelu_weight)]
    ig = jnp.concatenate(pairs, axis=2).transpose(1, 0, 2)
    per = decay_gates.shape[1] // BLOCK
    gates = [v.reshape(8, per, BLOCK) for v in (decay_gates, input_gates)]
    gates = jnp.concatenate(gates, axis=2)
    gates = jnp.pad(gates, ((0, 0), (0, 16 - per), (0, LANES - 2 * BLOCK))).reshape(4, 32, LANES)
    small = jnp.pad(channel_params[:, 0], ((0, 0), (0, drows - channel_params.shape[2])))
    small = jnp.pad(jnp.concatenate([small, norm_gains], axis=0), ((0, 6), (0, 0)))
    smem = pl.BlockSpec(memory_space=pltpu.SMEM)
    return run_kernel(
        first_kernel,
        "fetch_first",
        [
            ((8, rows, width), BF),
            ((width, 2 * local), BF),
            ((local, width), BF),
            ((LANES, 2 * LANES), BF),
            ((8, LANES), F32),
            ((2, width), F32),
            ((8, rows, width), BF),
            ((rows, width), F32),
            ((rows, width), BF),
            ((width, mlp_gate.shape[1] // 4), BF),
        ],
        [ANY] * 3 + [VMEM] * 3 + [ANY, VMEM, ANY, ANY],
        [smem, smem, ANY, VMEM] + [ANY] * 5,
        [
            pltpu.VMEM((512, LANES), BF),
            pltpu.VMEM((256, 128), BF),
            pltpu.VMEM((2, rows, width), BF),
        ]
        + semaphores(80, 16),
        1,
        (source_weight, seq_source, tokens, cotangent, ig, output_weight, gates, small, mlp_gate),
        61,
    )


def reduce_and_fetch(mixed, w_o, own, gain, mlp_up, mlp_down):
    if not shape_fits():
        return plain_reduce_and_fetch(mixed, w_o, own, gain, mlp_up, mlp_down)
    rows, width = own.shape
    ff = mlp_up.shape[1] // 4
    return run_kernel(
        second_kernel,
        "reduce_and_fetch",
        [((rows, width), F32), ((8, rows, width), BF), ((width, ff), BF), ((ff, width), BF)],
        [VMEM] + [ANY] * 3,
        [VMEM] * 4 + [ANY] * 2,
        scatter_buffers(rows, width, True) + [pltpu.VMEM((rows, width), BF)] + semaphores(64, 16),
        2,
        (mixed, w_o, own, gain, mlp_up, mlp_down),
    )


def reduce_and_return(weights, middle, dout, gain, dm, hidden, n2, dgm, dup, drows):
    if not shape_fits():
        return plain_reduce_and_return(
            weights, middle, dout, gain, dm, hidden, n2, dgm, dup, drows
        )
    rows, width = middle.shape
    ff = hidden.shape[1]
    return run_kernel(
        third_kernel,
        "reduce_and_return",
        [
            ((rows, width), F32),
            ((8, width), F32),
            ((8, rows, width), BF),
            ((drows, 4 * ff), BF),
            ((4 * ff, drows), BF),
            ((8, rows, width), BF),
        ],
        [VMEM, VMEM, ANY] + [VMEM] * 2 + [ANY],
        [VMEM] * 2 + [ANY] * 3 + [VMEM] + [ANY, VMEM] * 2 + [VMEM],
        scatter_buffers(rows, width, True)
        + grad_buffers(2 * drows, ff, 8 * rows) * 2
        + [pltpu.VMEM((rows, width), BF), pltpu.VMEM((ff, width), BF)]
        + [pltpu.VMEM((rows, width), F32)] * 2
        + semaphores(56, 56),
        3,
        (*weights, middle, dout, gain, dm, hidden, n2, dgm, dup),
        61,
    )


def return_last(w_ig, own, dr1, gain, do, mixed, n1, dboth, g_gates, drows):
    if not shape_fits():
        return plain_return_last(w_ig, own, dr1, gain, do, mixed, n1, dboth, g_gates, drows)
    rows, width = own.shape
    local, unit = dboth.shape[1] // 2, g_gates.shape[0] // 16
    return run_kernel(
        fourth_kernel,
        "return_last",
        [
            ((2, rows, width), F32),
            ((8, width), F32),
            ((drows, 4 * local), BF),
            ((drows, 4 * local), BF),
            ((4 * local, drows), BF),
            ((4, unit, 128), BF),
        ],
        [VMEM] * 6,
        [VMEM] * 4 + [ANY, VMEM] * 2 + [VMEM],
        scatter_buffers(rows, width, True)
        + grad_buffers(2 * drows, mixed.shape[1], 8 * rows)
        + grad_buffers(2 * drows, 2 * local, 8 * rows)
        + grad_buffers(2 * unit, 128)
        + [pltpu.VMEM((rows, width), BF)] * 2
        + semaphores(64, 48),
        4,
        (w_ig, own, dr1, gain, do, mixed, n1, dboth, g_gates),
        60,
    )


def shape_fits():
    return all(lax.axis_size(n) == 2 for n in AXES)


def plain_fetch_first(
    tokens, cotangent, seq_source, source_weight, input_weight, gelu_weight, output_weight,
    decay_gates, input_gates, channel_params, norm_gains, mlp_gate,
):
    exchange = Tokens()
    dxn, zhn, mp = lax.axis_size("dx"), lax.axis_size("zh"), exchange.mp
    group = dxn * 2 * zhn * 2
    local = input_weight.shape[1] // 4
    heads, piece = decay_gates.shape[0] // 4, decay_gates.shape[1]
    shards = ("dx", "dc", "zh", "zl")
    own = lax.dynamic_index_in_dim(tokens, mp, 0, keepdims=False)
    sources = jnp.arange(source_weight.shape[0], dtype=jnp.int32)
    scales = jnp.sum(jnp.where(seq_source == sources[None], source_weight[None], 0.0), axis=1)
    douts = cotangent.astype(F32) * scales[:, None, None]
    small = jnp.concatenate([channel_params.reshape(-1), norm_gains.reshape(-1)])
    small = lax.all_to_all(
        jnp.broadcast_to(small[None], (group, small.size)), shards, 0, 0, tiled=True
    )
    nch = channel_params.size
    channels = small[:, :nch].reshape(group, 8, -1).transpose(1, 0, 2).reshape(8, -1)
    slot = exchange.dc * 2 + exchange.zl
    channels = lax.dynamic_slice_in_dim(channels, slot * local, local, 1).astype(F32)
    gains = small[:, nch:].reshape(group, 2, -1).transpose(1, 0, 2).reshape(2, -1).astype(F32)
    gates = jnp.stack([decay_gates, input_gates]).reshape(2, 4, heads, piece)
    gates = gates.transpose(1, 0, 2, 3).reshape(2, 1, 2, 1, 2 * heads * piece)
    gates = jnp.broadcast_to(gates, (2, zhn, 2, dxn, 2 * heads * piece))
    gates = gates.transpose(3, 0, 1, 2, 4).reshape(group, 2 * heads * piece)
    gates = lax.all_to_all(gates, shards, 0, 0, tiled=True)
    gates = gates.reshape(group, 2 * heads, piece).transpose(1, 0, 2)
    gates = gates.reshape(2, heads, BLOCK, BLOCK)
    zero = jnp.zeros((BLOCK, BLOCK), BF)
    blocks = [
        [gates[g, h] if k == h else zero for g in range(2) for k in range(heads)]
        for h in range(heads)
    ]
    return (
        exchange.gather(own).reshape((8,) + own.shape),
        fetch_weight([input_weight, gelu_weight], 4),
        fetch_weight([output_weight.T], 4).T,
        jnp.concatenate([jnp.concatenate(v, axis=1) for v in blocks], axis=0),
        channels,
        gains,
        exchange.gather(lax.dynamic_index_in_dim(douts, mp, 0, keepdims=False).astype(BF)).reshape(
            (8,) + own.shape
        ),
        lax.dynamic_index_in_dim(douts, mp, 0, keepdims=False),
        own,
        fetch_weight([mlp_gate], 4),
    )


def plain_reduce_and_fetch(mixed, w_o, own, gain, mlp_up, mlp_down):
    exchange = Tokens()
    middle = own.astype(F32) + exchange.scatter(dot(mixed, w_o, NN, BF))
    normed = (middle * inverse_rms(middle) * gain).astype(BF)
    return (
        middle,
        exchange.gather(normed).reshape((8,) + own.shape),
        fetch_weight([mlp_up], 4),
        fetch_weight([mlp_down.T], 4).T,
    )


def columns(share, at, count):
    return share[:, :, at : at + count].astype(F32).transpose(1, 0, 2).reshape(-1, 4 * count)


def both_batches(rows):
    mp = lax.axis_index("mp")
    other = lax.ppermute(rows, "mp", [(0, 1), (1, 0)])
    return jnp.stack([jnp.where(mp == 0, rows, other), jnp.where(mp == 0, other, rows)])


def plain_reduce_and_return(weights, middle, dout, gain, dm, hidden, n2, dgm, dup, drows):
    exchange = Tokens()
    w_g, w_u, w_d = weights
    ff = hidden.shape[1]
    total = exchange.scatter((dot(dgm, w_g, NT) + dot(dup, w_u, NT)).astype(BF))
    change, gain_rows = norm_back(middle, gain, total)
    dr1 = dout + change
    gate = return_grad(dot(n2, dgm, TN, BF), drows)
    down = return_grad(dot(dm, hidden, TN, BF), drows)
    return (
        dr1,
        jnp.sum(gain_rows, axis=0, keepdims=True),
        exchange.gather(dr1.astype(BF)).reshape((8,) + dr1.shape),
        columns(gate, 0, ff),
        columns(down, 0, ff).T,
        dot(hidden, w_d, NN, BF).reshape((8,) + dr1.shape),
    )


def plain_return_last(w_ig, own, dr1, gain, do, mixed, n1, dboth, g_gates, drows):
    exchange = Tokens()
    local = dboth.shape[1] // 2
    total = exchange.scatter(dot(dboth, w_ig, NT, BF))
    change, gain_rows = norm_back(own.astype(F32), gain, total)
    group = n1.shape[1] // drows
    wide = return_grad(dot(n1, dboth, TN, BF), drows)
    out = return_grad(dot(do, mixed, TN, BF), drows)
    return (
        both_batches(dr1 + change),
        jnp.sum(gain_rows, axis=0, keepdims=True),
        columns(wide, 0, local),
        columns(wide, local, local),
        columns(out, 0, local).T,
        return_grad(g_gates, g_gates.shape[0] // group),
    )


def scan_body(reverse, a_ref, b_ref, p_ref, h_ref):
    length, width = a_ref.shape[1], a_ref.shape[2]
    row = lax.broadcasted_iota(jnp.int32, (8, width), 0)

    def tile(i, carry):
        ca, ch = carry
        at = (length // 8 - 1 - i if reverse else i) * 8
        at = pl.multiple_of(at, 8)
        a = a_ref[0, pl.ds(at, 8), :]
        b = b_ref[0, pl.ds(at, 8), :]
        for step in (1, 2, 4):
            if reverse:
                inside = row < 8 - step
                shift = 8 - step
            else:
                inside = row >= step
                shift = step
            sa = jnp.where(inside, pltpu.roll(a, shift, 0), 1.0)
            sb = jnp.where(inside, pltpu.roll(b, shift, 0), 0.0)
            b = b + a * sb
            a = a * sa
        h = b + a * ch
        p = a * ca
        h_ref[0, pl.ds(at, 8), :] = h
        p_ref[0, pl.ds(at, 8), :] = p
        last = 0 if reverse else 7
        return p[last : last + 1, :], h[last : last + 1, :]

    lax.fori_loop(
        0,
        length // 8,
        tile,
        (jnp.ones((1, width), F32), jnp.zeros((1, width), F32)),
    )


def local_scan(a, b, reverse):
    segs, length, width = a.shape
    spec = pl.BlockSpec((1, length, width), lambda s: (s, 0, 0))
    return pl.pallas_call(
        lambda *refs: scan_body(reverse, *refs),
        grid=(segs,),
        in_specs=[spec, spec],
        out_specs=[spec, spec],
        out_shape=[jax.ShapeDtypeStruct(a.shape, F32)] * 2,
        cost_estimate=pl.CostEstimate(
            flops=20 * a.size, bytes_accessed=16 * a.size, transcendentals=0
        ),
    )(a, b)


def carried(product, state, reverse):
    count = lax.axis_size("zh")
    if count == 2:
        return lax.ppermute(state, "zh", [(1, 0)] if reverse else [(0, 1)])
    here = lax.axis_index("zh")
    pairs = lax.all_gather(jnp.stack([product, state]), "zh")
    total = jnp.zeros_like(state)
    for k in range(count):
        at = count - 1 - k if reverse else k
        reached = at > here if reverse else at < here
        total = jnp.where(reached, pairs[at, 1] + pairs[at, 0] * total, total)
    return total


def from_behind(x, by):
    count = lax.axis_size("zh")
    return lax.ppermute(
        x, "zh", [(i, i + by) for i in range(count) if 0 <= i + by < count]
    )


def inverse_rms(values):
    return lax.rsqrt(jnp.mean(values * values, axis=-1, keepdims=True) + EPSILON)


def gelu(v):
    return jax.nn.gelu(v, approximate=True)


def gelu_both(v):
    c = 0.7978845608028654
    t = jnp.tanh(c * (v + 0.044715 * v * v * v))
    value = 0.5 * v * (1.0 + t)
    slope = 0.5 * (1.0 + t) + 0.5 * v * (1.0 - t * t) * c * (1.0 + 3 * 0.044715 * v * v)
    return value, slope


def dot(a, b, dims, out=F32):
    r = lax.dot_general(a, b, (dims, ((), ())), preferred_element_type=F32)
    return r.astype(out)


NN = ((1,), (0,))
NT = ((1,), (1,))
TN = ((0,), (0,))


def minus_expm1(v):
    series = 1.0 + v / 8.0
    for k in (7.0, 6.0, 5.0, 4.0, 3.0, 2.0):
        series = 1.0 + v * (1.0 / k) * series
    return jnp.where(v > -0.4, -v * series, 1.0 - jnp.exp(v))


def loop(count, body, unroll=1):
    def step(i, carry):
        body(i)
        return carry

    lax.fori_loop(0, count, step, 0, unroll=unroll)


def tile_scan(a, b, row, reverse):
    for step in (1, 2, 4):
        inside = row < 8 - step if reverse else row >= step
        shift = 8 - step if reverse else step
        sa = jnp.where(inside, pltpu.roll(a, shift, 0), 1.0)
        sb = jnp.where(inside, pltpu.roll(b, shift, 0), 0.0)
        b = b + a * sb
        a = a * sa
    return a, b


def eight(i):
    return pl.multiple_of(i * 8, 8)


def recur_forward_kernel(
    tok_ref, wig_ref, blocks_ref, ch_ref, gain_ref,
    n1_out, xs_out, gy_out, u_out, siga_out, sigi_out, decay_out, states, mixed,
    xs, gy, u, siga, sigi, decay, run, logits, n1, both, halo, ends, inc, tok, sems,
    send, recv, local_sems,
):
    p = Place()
    links = Links(send, recv, local_sems)
    rows, local = tok_ref.shape[1], wig_ref.shape[1] // 2
    zh = p.zh
    greet([p.peer(zh=1)])

    def read(b):
        return pltpu.make_async_copy(tok_ref.at[b], tok.at[b % 2], sems.at[4 + b % 2])

    read(0).start()
    lane = lax.broadcasted_iota(jnp.int32, (1, LANES), 1)
    real = lane < local

    def project(b):
        read(b).wait()

        @pl.when(b < 7)
        def _():
            read(b + 1).start()

        def normalise(at):
            value = tok[b % 2, at, :].astype(F32)
            inv = lax.rsqrt(jnp.mean(value * value, axis=-1, keepdims=True) + EPSILON)
            n1[b % 2, at, :] = (value * inv * gain_ref[...]).astype(BF)

        def write(i, at):
            return pltpu.make_async_copy(n1.at[i], n1_out.at[at], sems.at[i])

        @pl.when(b >= 2)
        def _():
            write(b % 2, b - 2).wait()

        chunks(rows, normalise)
        write(b % 2, b).start()
        both[...] = dot(n1[b % 2], wig_ref[...], NN)
        seg, zl = b // 2, b % 2

        def split(at):
            v = both[at, :]
            xb = jnp.where(real, v[:, :LANES], 0.0).astype(BF).astype(F32)
            xs[seg, pl.ds(pl.multiple_of(8 + zl * rows + at.start, 8), CHUNK), :] = xb
            rest = pltpu.roll(v, v.shape[1] - local, 1)[:, :LANES]
            gy[b, at, :] = jnp.where(real, rest, 0.0)

        chunks(rows, split)

    loop(8, project)
    for b in (6, 7):
        pltpu.make_async_copy(n1.at[b % 2], n1_out.at[b], sems.at[b % 2]).wait()

    def to_partner(src, dst):
        at = links.pair()
        links.start(src, dst, at, p.peer(zh=1))
        return at

    at = to_partner(xs.at[:, pl.ds(2 * rows, 8)], halo)
    kept = [links.keep(gy, gy_out)]
    links.arrived(halo, at)
    row = lax.broadcasted_iota(jnp.int32, (8, LANES), 0)
    soft = ch_ref[0:1, :]

    def head(seg):
        xs[seg, 0:8, :] = jnp.where(zh == 1, halo[seg], 0.0)

    loop(4, head)

    def convolve(b):
        seg, zl = b // 2, b % 2

        def body(at):
            v = xs[seg, pl.ds(pl.multiple_of(zl * rows + at.start, 8), CHUNK + 8), :]
            total = ch_ref[3:4, :] + ch_ref[4:5, :] * v[8:]
            for k in (1, 2, 3):
                total = total + ch_ref[4 + k : 5 + k, :] * pltpu.roll(v, k, 0)[8:]
            u[b, at, :] = total.astype(BF)

        chunks(rows, body)
        logits[b] = dot(u[b], blocks_ref[...], NN)

    loop(8, convolve)

    def tile(i, carry, zl):
        at = pl.ds(pl.multiple_of(i * CHUNK, CHUNK), CHUNK)
        out = []
        for seg in range(4):
            b = seg * 2 + zl
            cp, ch = carry[seg]
            sa = jax.nn.sigmoid(logits[b, at, :LANES] + ch_ref[1:2, :])
            si = jax.nn.sigmoid(logits[b, at, LANES:] + ch_ref[2:3, :])
            log_decay = -DECAY_SCALE * sa * soft
            a = jnp.exp(log_decay)
            drive = jnp.sqrt(minus_expm1(2.0 * log_decay)) * si * u[b, at, :].astype(F32)
            siga[b, at, :] = sa
            sigi[b, at, :] = si
            decay[b, at, :] = a
            for k in range(2):
                pa, h = tile_scan(a[k * 8 : k * 8 + 8], drive[k * 8 : k * 8 + 8], row, False)
                h = h + pa * ch
                pa = pa * cp
                run[b, pl.ds(eight(i * 2 + k), 8), :] = pa
                there = pl.ds(pl.multiple_of(8 + zl * rows + i * CHUNK + k * 8, 8), 8)
                states[seg, there, :] = h
                cp, ch = pa[7:8, :], h[7:8, :]
            out.append((cp, ch))
        return tuple(out)

    kept += [links.keep(xs, xs_out), links.keep(u, u_out)]
    carry = ((jnp.ones((1, LANES), F32), jnp.zeros((1, LANES), F32)),) * 4
    for zl in range(2):
        carry = lax.fori_loop(0, rows // CHUNK, functools.partial(tile, zl=zl), carry)
    ends[...] = jnp.zeros_like(ends)
    for seg in range(4):
        ends[seg : seg + 1, :] = carry[seg][1]
    at = to_partner(ends, inc)
    kept += [links.keep(siga, siga_out), links.keep(sigi, sigi_out), links.keep(decay, decay_out)]
    links.arrived(inc, at)

    def finish(b):
        seg, zl = b // 2, b % 2
        start = jnp.where(zh == 1, inc[pl.ds(seg, 1), :], 0.0)

        @pl.when(zl == 0)
        def _():
            states[seg, 0:8, :] = jnp.broadcast_to(start, (8, LANES))

        def state(at):
            there = pl.ds(pl.multiple_of(8 + zl * rows + at.start, 8), CHUNK)
            h = states[seg, there, :] + run[b, at, :] * start
            states[seg, there, :] = h
            v = gy[b, at, :]
            t = jnp.tanh(0.7978845608028654 * (v + 0.044715 * v * v * v))
            mixed[b, at, :] = (0.5 * v * (1.0 + t) * h).astype(BF)

        chunks(rows, state)

    loop(8, finish)
    for copy in kept:
        copy.wait()
    links.finish()


def recur_backward_kernel(
    do_ref, wo_ref, blocks_ref, ch_ref,
    xs_in, gy, u_in, siga_in, sigi_in, decay_in, states, rows_ref, mid_in, n2_ref, dup_ref,
    dboth_out, gb_out, ch_out, block_out, up_out,
    xs, u, siga, sigi, decay, mid_ref,
    dh, after, dgy, dlog_ref, du, dboth, halo, ends, inc, do, final, sems,
    *scratch,
):
    p = Place()
    links = Links(*scratch[-3:])
    rows, local = do_ref.shape[1], wo_ref.shape[0]
    zh = p.zh
    greet(weight_peers(p))
    scatter = RowScatter(p, links, rows_ref, scratch[:5])
    up = GradScatter(p, links, n2_ref, dup_ref, scratch[5:12], GradScatter.EARLY)

    def read(b):
        return pltpu.make_async_copy(do_ref.at[b], do.at[b % 2], sems.at[4 + b % 2])

    read(0).start()
    kept = {
        name: links.keep(src, dst)
        for name, src, dst in (
            ("decay", decay_in, decay),
            ("siga", siga_in, siga),
            ("sigi", sigi_in, sigi),
            ("u", u_in, u),
            ("xs", xs_in, xs),
            ("mid", mid_in, mid_ref),
        )
    }
    scatter.begin()
    up.begin(1)
    scatter.across_y()
    ch_out[...] = jnp.zeros_like(ch_out)
    gb_out[...] = jnp.zeros_like(gb_out)
    soft = ch_ref[0:1, :]

    def to_partner(src, dst):
        at = links.pair()
        links.start(src, dst, at, p.peer(zh=1))
        return at

    def upstream(b):
        seg, zl = b // 2, b % 2
        dh[b, :, local:] = jnp.zeros((rows, LANES - local), F32)
        read(b).wait()

        @pl.when(b < 7)
        def _():
            read(b + 1).start()

        dh[b, :, :local] = dot(do[b % 2], wo_ref[...], NT)

        def split(at):
            value, slope = gelu_both(gy[b, at, :])
            dz = dh[b, at, :]
            h = states[seg, pl.ds(pl.multiple_of(8 + zl * rows + at.start, 8), CHUNK), :]
            dh[b, at, :] = dz * value
            dgy[b, at, :] = (dz * h * slope).astype(BF)

        chunks(rows, split)

    loop(8, upstream)
    up.begin(0)
    row = lax.broadcasted_iota(jnp.int32, (8, LANES), 0)
    one = jnp.ones((1, LANES), F32)
    ends[...] = jnp.zeros_like(ends)

    def tile(i, carry, zl):
        at = pl.ds(eight(rows // 8 - 1 - i), 8)
        out = []
        for seg in range(4):
            b = seg * 2 + zl
            cp, cg, following = carry[seg]
            a = decay[b, at, :]
            shifted = jnp.where(row == 7, following, pltpu.roll(a, 7, 0))
            pa, g = tile_scan(shifted, dh[b, at, :], row, True)
            g = g + pa * cg
            pa = pa * cp
            dh[b, at, :] = g
            after[b, at, :] = pa
            out.append((pa[0:1, :], g[0:1, :], a[0:1, :]))
        return tuple(out)

    carry = ((one, jnp.zeros((1, LANES), F32), one),) * 4
    kept["decay"].wait()
    for zl in (1, 0):
        carry = lax.fori_loop(0, rows // 8, functools.partial(tile, zl=zl), carry)
    for seg in range(4):
        ends[seg : seg + 1, :] = carry[seg][1] * carry[seg][2]
    at = to_partner(ends, inc)
    links.arrived(inc, at)
    scatter.across_z()
    up.across(0)

    def gradients(b):
        seg, zl = b // 2, b % 2
        later = jnp.where(zh == 0, inc[pl.ds(seg, 1), :], 0.0)

        def body(at):
            window = states[seg, pl.ds(pl.multiple_of(zl * rows + at.start, 8), CHUNK + 8), :]
            previous = pltpu.roll(window, 1, 0)[8:]
            g = dh[b, at, :] + after[b, at, :] * later
            sa, si, a = siga[b, at, :], sigi[b, at, :], decay[b, at, :]
            uf = u[b, at, :].astype(F32)
            root = jnp.sqrt(minus_expm1((-2.0 * DECAY_SCALE) * sa * soft))
            gu = g * uf
            gr = g * root
            d_log = a * (g * previous - gu * si * a / root)
            d_log = jnp.where(real, d_log, 0.0)
            dra = (d_log * (-DECAY_SCALE * soft) * sa * (1.0 - sa)).astype(BF)
            dri = (gr * uf * si * (1.0 - si)).astype(BF)
            du[seg, pl.ds(pl.multiple_of(zl * rows + at.start, 8), CHUNK), :] = gr * si
            dlog_ref[at, :LANES] = dra
            dlog_ref[at, LANES:] = dri
            for k, v in enumerate((d_log * sa, dra.astype(F32), dri.astype(F32))):
                sums[k] = sums[k] + fold(v)

        sums = [jnp.zeros((8, LANES), F32) for _ in range(3)]
        chunks(rows, body)
        for k in range(3):
            ch_out[k] += sums[k]
        d = dlog_ref[...]
        there = pl.ds(pl.multiple_of(zl * rows, 8), rows)
        du[seg, there, :] += dot(d, blocks_ref[...], NT)
        gb_out[...] += dot(u[b], d, TN)

    lane = lax.broadcasted_iota(jnp.int32, (1, LANES), 1)
    real = lane < local
    for name in ("siga", "sigi", "u"):
        kept[name].wait()
    loop(8, gradients)
    at = to_partner(du.at[:, pl.ds(0, 8)], halo)
    up.across(1)

    def write(i, at, src, dst, base):
        return pltpu.make_async_copy(src.at[i], dst.at[at], sems.at[base + i])

    def convolve(i, zl):
        seg = i
        b = i * 2 + zl
        slot = i % 2

        @pl.when(i >= 2)
        def _():
            write(slot, b - 4, dboth, dboth_out, 0).wait()

        def body(at):
            start = pl.multiple_of(zl * rows + at.start, 8)
            v = du[seg, pl.ds(start, CHUNK + 8), :]
            x = xs[seg, pl.ds(start, CHUNK + 8), :]
            here = v[:CHUNK]
            total = ch_ref[4:5, :] * here
            sums[0] = sums[0] + fold(here)
            sums[1] = sums[1] + fold(here * x[8:])
            for k in (1, 2, 3):
                total = total + ch_ref[4 + k : 5 + k, :] * pltpu.roll(v, CHUNK + 8 - k, 0)[:CHUNK]
                sums[1 + k] = sums[1 + k] + fold(here * pltpu.roll(x, k, 0)[8:])
            wide = 2 * local - LANES
            zeros = jnp.zeros((CHUNK, wide), F32)
            left = jnp.concatenate([total, zeros], axis=1)
            right = jnp.concatenate([dgy[b, at, :].astype(F32), zeros], axis=1)
            dboth[slot, at, :] = (left + pltpu.roll(right, local, 1)).astype(BF)

        sums = [jnp.zeros((8, LANES), F32) for _ in range(5)]
        chunks(rows, body)
        for k in range(5):
            ch_out[3 + k] += sums[k]
        write(slot, b, dboth, dboth_out, 0).start()

    def drain(zl):
        for i in (2, 3):
            write(i % 2, i * 2 + zl, dboth, dboth_out, 0).wait()

    kept["xs"].wait()
    kept["mid"].wait()
    loop(4, functools.partial(convolve, zl=0))
    drain(0)
    links.arrived(halo, at)

    def tail(seg):
        du[seg, pl.ds(2 * rows, 8), :] = jnp.where(zh == 0, halo[seg], 0.0)

    loop(4, tail)
    scatter.arrive()

    def add(at):
        final[at, :] = (mid_ref[at, :] + scatter.total(at)).astype(BF)

    chunks(rows, add)
    at = links.pair()
    links.start(final, block_out.at[p.mp], at, p.peer(mp=1))
    own = links.keep(final, block_out.at[p.mp])
    loop(4, functools.partial(convolve, zl=1))
    up.last(0)
    drain(1)
    up.last(1)
    up.end()
    ff = up.result.shape[2]
    for j in range(4):
        up_out[:, j * ff : (j + 1) * ff] = up.result[j]
    own.wait()
    links.arrived(block_out.at[1 - p.mp], at)
    links.finish()


def recur_forward(tokens, w_ig, blocks, channels, gain):
    if not shape_fits():
        return plain_recur_forward(tokens, w_ig, blocks, channels, gain)
    rows, width = tokens.shape[1:]
    local = w_ig.shape[1] // 2
    table = jnp.concatenate([jax.nn.softplus(-channels[0:1]), channels[1:]], axis=0)
    f, h = (8, rows, LANES), (4, 2 * rows + 8, LANES)
    n1, *saved = run_kernel(
        recur_forward_kernel,
        "recur_forward",
        [(tokens.shape, BF), (h, F32), (f, F32), (f, BF)]
        + [(f, F32)] * 3
        + [(h, F32), (f, BF)],
        [ANY] * 7 + [VMEM] * 2,
        [ANY] + [VMEM] * 4,
        [
            pltpu.VMEM(h, F32),
            pltpu.VMEM(f, F32),
            pltpu.VMEM(f, BF),
            pltpu.VMEM(f, F32),
            pltpu.VMEM(f, F32),
            pltpu.VMEM(f, F32),
            pltpu.VMEM(f, F32),
            pltpu.VMEM((8, rows, 2 * LANES), F32),
            pltpu.VMEM((2, rows, width), BF),
            pltpu.VMEM((rows, 2 * local), F32),
            pltpu.VMEM((4, 8, LANES), F32),
            pltpu.VMEM((8, LANES), F32),
            pltpu.VMEM((8, LANES), F32),
            pltpu.VMEM((2, rows, width), BF),
        ]
        + semaphores(6, 2)[:1]
        + semaphores(2, 6),
        5,
        (tokens, w_ig, blocks, table, gain),
        61,
    )
    *saved, mixed = saved
    return n1.reshape(-1, width), mixed.reshape(-1, LANES), (table, blocks, *saved)


def recur_backward(do, saved, w_o, channels, out_part, middle, n2, dup, drows):
    if not shape_fits():
        return plain_recur_backward(do, saved, w_o, channels, out_part, middle, n2, dup, drows)
    ff = dup.shape[1]
    table, wide, xs, gy, u, siga, sigi, decay, states = saved
    rows, width = do.shape[1:]
    local = w_o.shape[0]
    f, h = (8, rows, LANES), (4, 2 * rows + 8, LANES)
    dboth, g_blocks, sums, block_out, g_up = run_kernel(
        recur_backward_kernel,
        "recur_backward",
        [
            ((8, rows, 2 * local), BF),
            ((LANES, 2 * LANES), F32),
            ((8, 8, LANES), F32),
            ((2, rows, width), BF),
            ((drows, 4 * ff), BF),
        ],
        [ANY] + [VMEM] * 2 + [ANY, VMEM],
        [ANY] + [VMEM] * 3 + [ANY, VMEM] + [ANY] * 4 + [VMEM] + [ANY] * 3 + [VMEM],
        [
            pltpu.VMEM(h, F32),
            pltpu.VMEM(f, BF),
            pltpu.VMEM(f, F32),
            pltpu.VMEM(f, F32),
            pltpu.VMEM(f, F32),
            pltpu.VMEM((rows, width), F32),
            pltpu.VMEM(f, F32),
            pltpu.VMEM(f, F32),
            pltpu.VMEM(f, BF),
            pltpu.VMEM((rows, 2 * LANES), BF),
            pltpu.VMEM(h, F32),
            pltpu.VMEM((2, rows, 2 * local), BF),
            pltpu.VMEM((4, 8, LANES), F32),
            pltpu.VMEM((8, LANES), F32),
            pltpu.VMEM((8, LANES), F32),
            pltpu.VMEM((2, rows, width), BF),
            pltpu.VMEM((rows, width), BF),
        ]
        + semaphores(6, 2)[:1]
        + scatter_buffers(rows, width)
        + grad_buffers(2 * drows, ff, 8 * rows)
        + semaphores(32, 32),
        6,
        (do, w_o, wide, table, xs, gy, u, siga, sigi, decay, states)
        + (out_part, middle, n2, dup),
        61,
    )
    sums = jnp.sum(sums, axis=1)[:, :local]
    dlam = sums[0] * DECAY_SCALE * jax.nn.sigmoid(-channels[0, :local])
    g_blocks = jnp.concatenate(
        [g_blocks[:local, g * LANES : g * LANES + local] for g in (0, 1)], axis=1
    )
    return (
        dboth.reshape(-1, 2 * local),
        g_blocks,
        jnp.concatenate([dlam[None], sums[1:]], axis=0),
        block_out,
        g_up,
    )


def plain_recur_forward(tokens, w_ig, blocks, channels, gain):
    length, local, width = tokens.shape[1], w_ig.shape[1] // 2, tokens.shape[2]
    wide = tokens.reshape(-1, width).astype(F32)
    n1 = (wide * inverse_rms(wide) * gain).astype(BF)
    both = dot(n1, w_ig, NN)
    xb = both[:, :local].astype(BF).reshape(4, 2 * length, local)
    gy = both[:, local:].reshape(4, 2 * length, local)
    rim = from_behind(xb[:, -3:], 1)
    padded = jnp.concatenate([rim, xb], axis=1).astype(F32)
    conv = channels[3]
    for k in range(4):
        conv = conv + channels[4 + k] * padded[:, 3 - k : 3 - k + 2 * length]
    u = conv.astype(BF)
    logits = dot(u.reshape(-1, local), blocks, NN).reshape(4, 2 * length, 2 * local)
    sig_a = jax.nn.sigmoid(logits[..., :local] + channels[1])
    sig_i = jax.nn.sigmoid(logits[..., local:] + channels[2])
    log_decay = -DECAY_SCALE * sig_a * jax.nn.softplus(-channels[0])
    decay = jnp.exp(log_decay)
    root = jnp.sqrt(-jnp.expm1(2.0 * log_decay))
    running, state = local_scan(decay, root * sig_i * u.astype(F32), False)
    incoming = carried(running[:, -1], state[:, -1], False)
    states = state + running * incoming[:, None]
    gelu_y, slope_y = gelu_both(gy)
    mixed = (gelu_y * states).astype(BF).reshape(-1, local)
    saved = (blocks, padded, u, sig_a, sig_i, decay, root, running, incoming, states)
    return n1, mixed, saved + (gelu_y, slope_y)


def plain_recur_backward(do, saved, w_o, channels, out_part, middle, n2, dup, drows):
    blocks, padded, u, sig_a, sig_i, decay, root, running, incoming, states = saved[:10]
    gelu_y, slope_y = saved[10:]
    length, local, width = do.shape[1], w_o.shape[0], do.shape[2]
    dz = dot(do.reshape(-1, width), w_o, NT).reshape(4, 2 * length, local)
    dh = dz * gelu_y
    dgy = (dz * states * slope_y).astype(BF)
    ones = jnp.ones_like(decay[:, :1])
    after, adjoint = local_scan(jnp.concatenate([decay[:, 1:], ones], axis=1), dh, True)
    later = carried(running[:, -1], decay[:, 0] * adjoint[:, 0], True)
    adjoint = adjoint + after * later[:, None]
    previous = jnp.concatenate([incoming[:, None], states[:, :-1]], axis=1)
    soft, uf = jax.nn.softplus(-channels[0]), u.astype(F32)
    d_root = adjoint * sig_i * uf
    d_log = adjoint * previous * decay - d_root * decay * decay / root
    dra = (d_log * (-DECAY_SCALE * soft) * sig_a * (1.0 - sig_a)).astype(BF)
    dri = (adjoint * root * uf * sig_i * (1.0 - sig_i)).astype(BF)
    dlam = jnp.sum(d_log * sig_a, axis=(0, 1)) * DECAY_SCALE * jax.nn.sigmoid(-channels[0])
    dlogits = jnp.concatenate([dra, dri], axis=2).reshape(-1, 2 * local)
    g_blocks = dot(u.reshape(-1, local), dlogits, TN)
    du = adjoint * root * sig_i + dot(dlogits, blocks, NT).reshape(4, 2 * length, local)
    zeros = jnp.zeros((4, 3, local), F32)
    spread = jnp.concatenate([zeros, du, zeros], axis=1)
    dpad = jnp.zeros((4, 2 * length + 3, local), F32)
    taps = []
    for k in range(4):
        dpad = dpad + channels[4 + k] * spread[:, k : k + 2 * length + 3]
        taps.append(jnp.sum(du * padded[:, 3 - k : 3 - k + 2 * length], axis=(0, 1)))
    back = from_behind(dpad[:, :3], -1)
    dxb = dpad[:, 3:] + jnp.concatenate(
        [jnp.zeros((4, 2 * length - 3, local), F32), back], axis=1
    )
    dboth = jnp.concatenate([dxb.astype(BF), dgy], axis=2).reshape(-1, 2 * local)
    sums = [jnp.sum(v.astype(F32), axis=(0, 1)) for v in (dra, dri, du)]
    result = (middle + Tokens().scatter(out_part.reshape(-1, width))).astype(BF)
    g_up = columns(return_grad(dot(n2, dup, TN, BF), drows), 0, dup.shape[1])
    small = jnp.stack([dlam] + sums + taps)
    return dboth, g_blocks, small, both_batches(result), g_up


def on_device(
    tokens_in,
    cotangent,
    seq_source,
    source_weight,
    input_weight,
    gelu_weight,
    decay_gates,
    input_gates,
    channel_params,
    norm_gains,
    output_weight,
    mlp_gate,
    mlp_up,
    mlp_down,
):
    sizes = tuple(lax.axis_size(n) for n in AXES)
    dxn, _, zhn, _, _ = sizes
    group = dxn * 2 * zhn * 2
    dc, zl, mp = (lax.axis_index(n) for n in ("dc", "zl", "mp"))
    slot = dc * 2 + zl
    width = tokens_in.shape[3]
    local = input_weight.shape[1] // 4
    heads = decay_gates.shape[0] // 4
    drows = input_weight.shape[0]
    piece = decay_gates.shape[1]

    tokens, w_ig, w_o, blocks, channels, gains, dm, dout, own, w_g = fetch_first(
        tokens_in[:, 0],
        cotangent[:, 0],
        seq_source,
        source_weight,
        input_weight,
        gelu_weight,
        output_weight,
        decay_gates,
        input_gates,
        channel_params,
        norm_gains,
        mlp_gate,
    )

    n1, mixed, saved = recur_forward(tokens, w_ig, blocks, channels, gains[0:1])
    middle, n2, w_u, w_d = reduce_and_fetch(mixed, w_o, own, gains[1:2], mlp_up, mlp_down)

    hidden, dgm, dup = feed_forward(n2, dm, w_g, w_u, w_d)
    n2, dm = n2.reshape(-1, width), dm.reshape(-1, width)
    dr1, gain_two, do, g_gate, g_down, out_part = reduce_and_return(
        (w_g, w_u, w_d), middle, dout, gains[1:2], dm, hidden, n2, dgm, dup, drows
    )
    gain_two = jnp.sum(gain_two, axis=0)

    dboth, g_blocks, channel_grad, block_out, g_up = recur_backward(
        do, saved, w_o, channels, out_part, middle, n2, dup, drows
    )

    g_gates = jnp.stack(
        [
            jnp.stack(
                [
                    g_blocks[
                        h * BLOCK : (h + 1) * BLOCK,
                        g * local + h * BLOCK : g * local + (h + 1) * BLOCK,
                    ]
                    for h in range(heads)
                ]
            )
            for g in range(2)
        ]
    )
    g_gates = g_gates.reshape(2 * heads, group, piece).transpose(1, 0, 2).reshape(group, -1)
    count = g_gates.shape[1]
    unit = (count + 2047) // 2048 * 16
    g_gates = jnp.pad(g_gates, ((0, 0), (0, unit * 128 - count))).astype(BF)
    grad_tokens, gain_one, g_input, g_gelu, g_output, share_gates = return_last(
        w_ig,
        own,
        dr1,
        gains[0:1],
        do.reshape(-1, width),
        mixed,
        n1,
        dboth,
        g_gates.reshape(group * unit, 128),
        drows,
    )
    gain_one = jnp.sum(gain_one, axis=0)
    g_gates = share_gates.reshape(4, -1)[:, :count].astype(F32).reshape(4, 2, heads, piece)
    g_gates = g_gates.transpose(1, 0, 2, 3).reshape(2, 4 * heads, piece)

    per = 4 * local // group
    mine = channel_grad.reshape(8, group // 4, per).transpose(1, 0, 2)
    mine = jnp.where(
        jnp.arange(4, dtype=jnp.int32)[:, None, None, None] == slot, mine[None], 0.0
    ).reshape(group, 1, 8 * per)
    mine = jnp.where(jnp.arange(2, dtype=jnp.int32)[None, :, None] == mp, mine, 0.0)
    both_gains = jnp.stack([gain_one, gain_two]).reshape(2, group, -1).transpose(1, 0, 2)
    both_gains = jnp.broadcast_to(both_gains.reshape(group, 1, -1), (group, 2, 2 * drows))
    sums = jnp.concatenate([both_gains, mine], axis=2).reshape(2 * group, -1)
    sums = jnp.sum(lax.all_to_all(sums, AXES, 0, 0, tiled=True), axis=0)
    g_gains = sums[: 2 * drows].reshape(2, drows)
    g_channels = sums[2 * drows :].reshape(8, 1, per)
    return (
        block_out[:, None],
        grad_tokens[:, None],
        g_input.astype(F32),
        g_gelu.astype(F32),
        g_gates[0],
        g_gates[1],
        g_channels,
        g_gains,
        g_output.astype(F32),
        g_gate.astype(F32),
        g_up.astype(F32),
        g_down.astype(F32),
    )


def solution(mesh):
    dpn, seqn, mpn = (mesh.shape[n] for n in ("dp", "seq", "mp"))
    fine = Mesh(mesh.devices.reshape(dpn // 2, 2, seqn // 2, 2, mpn), AXES)
    dp, seq = ("dx", "dc"), ("zh", "zl")
    shards = dp + seq
    weights = (
        P(shards, "mp"),
        P(shards, "mp"),
        P("mp", shards),
        P("mp", shards),
        P(None, "mp", shards),
        P(None, shards),
        P("mp", shards),
        P(shards, "mp"),
        P(shards, "mp"),
        P("mp", shards),
    )
    rows = P(None, dp, seq, None)
    return jax.shard_map(
        on_device,
        mesh=fine,
        in_specs=(rows, rows, P(None, dp), P()) + weights,
        out_specs=(rows, rows) + weights,
        check_vma=False,
    )
```

```python
import functools

import jax
import jax.numpy as jnp
import numpy as np
from jax import lax
from jax.experimental import pallas as pl
from jax.experimental.pallas import tpu as pltpu
from jax.sharding import Mesh, PartitionSpec as P

WIDTH = 2560
HEADS = 16
BLOCK = WIDTH // HEADS
EPSILON = 1e-06
DECAY_SCALE = 8.0
AXES = ("dx", "dc", "zh", "zl", "mp")
BF = jnp.bfloat16
F32 = jnp.float32
LANES = 384


def swap_pairs(sizes, partner):
    pairs = []
    for flat in range(int(np.prod(sizes))):
        coords = np.unravel_index(flat, sizes)
        pairs.append((flat, int(np.ravel_multi_index(partner(*map(int, coords)), sizes))))
    return pairs


def gather_blocks(x, axis, dim):
    if lax.axis_size(axis) != 2:
        return lax.all_gather(x, axis, axis=dim, tiled=False)
    here = lax.axis_index(axis)
    other = lax.ppermute(x, axis, [(0, 1), (1, 0)])
    low = jnp.where(here == 0, x, other)
    high = jnp.where(here == 0, other, x)
    return jnp.stack([low, high], axis=dim)


def scatter_blocks(x, axis, dim):
    if lax.axis_size(axis) != 2:
        n = x.shape[dim]
        out = lax.psum_scatter(x.astype(BF), axis, scatter_dimension=dim, tiled=True)
        return lax.squeeze(out, [dim]).astype(F32)
    here = lax.axis_index(axis)
    mine = lax.dynamic_index_in_dim(x, here, dim, keepdims=False)
    theirs = lax.dynamic_index_in_dim(x, 1 - here, dim, keepdims=False)
    got = lax.ppermute(theirs.astype(BF), axis, [(0, 1), (1, 0)])
    return mine.astype(F32) + got.astype(F32)


def fetch_weight(shard, parts):
    rows, cols = shard[0].shape[0], None
    pieces = [s.reshape(rows, parts, -1) for s in shard]
    joined = jnp.concatenate(pieces, axis=2) if len(pieces) > 1 else pieces[0]
    cols = joined.shape[2]
    x = jnp.transpose(joined, (1, 0, 2))
    x = lax.all_to_all(x, ("dc", "zl"), 0, 0, tiled=True)
    x = x.reshape(2, 2, rows, cols)
    x = gather_blocks(x, "zh", 1)
    x = gather_blocks(x, "dx", 0)
    return x.reshape(-1, cols)


def return_grad(grad, rows):
    cols = grad.shape[1]
    dxn, zhn = lax.axis_size("dx"), lax.axis_size("zh")
    g = grad.reshape(dxn, 2, zhn, 2, rows, cols)
    g = scatter_blocks(g, "dx", 0)
    g = scatter_blocks(g, "zh", 1)
    g = g.astype(BF).reshape(4, rows, cols)
    return lax.all_to_all(g, ("dc", "zl"), 0, 0, tiled=True)


class Tokens:
    def __init__(self):
        sizes = tuple(lax.axis_size(n) for n in AXES)
        self.core = swap_pairs(sizes, lambda a, b, c, d, e: (a, 1 - b, c, d, e))
        self.first = swap_pairs(
            sizes, lambda a, b, c, d, e: (a, b, c, d, 1 - e) if b == 0 else (a, b, c, 1 - d, e)
        )
        self.second = swap_pairs(
            sizes, lambda a, b, c, d, e: (a, b, c, 1 - d, e) if b == 0 else (a, b, c, d, 1 - e)
        )
        self.dc, self.zl, self.mp = (lax.axis_index(n) for n in ("dc", "zl", "mp"))

    def order(self, dc):
        mp, zl = self.mp, self.zl
        own = mp * 2 + zl
        by_mp = (1 - mp) * 2 + zl
        by_zl = mp * 2 + 1 - zl
        both = (1 - mp) * 2 + 1 - zl
        one = jnp.where(dc == 0, by_mp, by_zl)
        two = jnp.where(dc == 0, by_zl, by_mp)
        return own, one, two, both

    def gather(self, x):
        rows, width = x.shape
        one = lax.ppermute(x, AXES, self.first)
        two = lax.ppermute(jnp.stack([x, one]), AXES, self.second)
        far = [lax.ppermute(v, AXES, self.core) for v in (x, one, two)]
        out = jnp.zeros((8, rows, width), x.dtype)
        for dc, blocks in (
            (self.dc, (x, one, two[0], two[1])),
            (1 - self.dc, (far[0], far[1], far[2][0], far[2][1])),
        ):
            for at, block in zip(self.order(dc), blocks):
                out = lax.dynamic_update_index_in_dim(out, block, dc * 4 + at, 0)
        return out.reshape(8 * rows, width)

    def scatter(self, x):
        rows, width = x.shape[0] // 8, x.shape[1]
        x = x.reshape(2, 4, rows, width)
        theirs = lax.dynamic_index_in_dim(x, 1 - self.dc, 0, keepdims=False).astype(BF)
        mine = lax.dynamic_index_in_dim(x, self.dc, 0, keepdims=False)
        total = mine.astype(F32) + lax.ppermute(theirs, AXES, self.core).astype(F32)
        own, one, two, both = self.order(self.dc)
        pick = lambda at: lax.dynamic_index_in_dim(total, at, 0, keepdims=False)
        got = lax.ppermute(jnp.stack([pick(two), pick(both)]).astype(BF), AXES, self.second)
        keep_own = pick(own) + got[0].astype(F32)
        keep_one = pick(one) + got[1].astype(F32)
        got = lax.ppermute(keep_one.astype(BF), AXES, self.first)
        return keep_own + got.astype(F32)


MESH = pl.DeviceIdType.MESH
ANY = pl.BlockSpec(memory_space=pl.ANY)
VMEM = pl.BlockSpec(memory_space=pltpu.VMEM)


def flip(index, by):
    return 1 - index if by else index


class Place:
    def __init__(self):
        self.dx, self.dc, self.zh, self.zl, self.mp = (lax.axis_index(n) for n in AXES)

    def peer(self, dx=0, dc=0, zh=0, zl=0, mp=0):
        return (
            flip(self.dx, dx),
            flip(self.dc, dc),
            flip(self.zh, zh),
            flip(self.zl, zl),
            flip(self.mp, mp),
        )

    def block(self, dx=0, dc=0, zh=0, zl=0):
        a, b, c, d, _ = self.peer(dx, dc, zh, zl)
        return ((a * 2 + b) * 2 + c) * 2 + d

    def slot(self, dc=0, zl=0):
        return flip(self.dc, dc) * 2 + flip(self.zl, zl)

    def rows(self, dc=0, mp=0, zl=0):
        return (flip(self.dc, dc) * 2 + flip(self.mp, mp)) * 2 + flip(self.zl, zl)


def greet(peers):
    barrier = pltpu.get_barrier_semaphore()
    for device in peers:
        pl.semaphore_signal(barrier, inc=1, device_id=device, device_id_type=MESH)
    pl.semaphore_wait(barrier, len(peers))


class Links:
    def __init__(self, send, recv, local):
        self.send, self.recv, self.local = send, recv, local
        self.n, self.m = 0, 0
        self.sent, self.copies = [], []

    def pair(self):
        self.n += 1
        return self.n - 1

    def start(self, src, dst, at, device):
        copy = pltpu.make_async_remote_copy(
            src_ref=src,
            dst_ref=dst,
            send_sem=self.send.at[at],
            recv_sem=self.recv.at[at],
            device_id=device,
            device_id_type=MESH,
        )
        copy.start()
        self.sent.append(copy)

    def arrived(self, ref, at):
        pltpu.make_async_copy(ref, ref, self.recv.at[at]).wait()

    def keep(self, src, dst):
        copy = pltpu.make_async_copy(src, dst, self.local.at[self.m])
        self.m += 1
        copy.start()
        return copy

    def finish(self):
        for copy in self.sent:
            copy.wait_send()


FLIPS = [(zh, dc, zl) for zh in (1, 0) for dc in (0, 1) for zl in (0, 1)]


class WeightGather:
    def __init__(self, place, links, source, target, unit):
        self.place, self.links, self.target = place, links, target
        self.at = {f: links.pair() for f in FLIPS}
        self.cross = {(zh, dc): links.pair() for zh in (0, 1) for dc in (0, 1)}
        self.source = source
        self.kept = None

    def begin(self, zhs=(1, 0), dcs=(0, 1)):
        p = self.place
        mine = p.block()
        for f in FLIPS:
            zh, dc, zl = f
            if zh not in zhs or dc not in dcs:
                continue
            src, dst = self.source(p.slot(dc, zl)), self.target(mine, 1)
            if f == (0, 0, 0):
                self.kept = self.links.keep(src, dst)
            else:
                self.links.start(src, dst, self.at[f], p.peer(dc=dc, zh=zh, zl=zl))

    def onward(self, zh, dcs=(0, 1)):
        p = self.place
        for dc in dcs:
            for zl in (0, 1):
                if (zh, dc, zl) == (0, 0, 0):
                    self.kept.wait()
                else:
                    self.links.arrived(
                        self.target(p.block(dc=dc, zh=zh, zl=zl), 1), self.at[zh, dc, zl]
                    )
            two = self.target(p.block(dc=dc, zh=zh) // 2 * 2, 2)
            self.links.start(two, two, self.cross[zh, dc], p.peer(dx=1))

    def end(self):
        p = self.place
        for zh in (0, 1):
            for dc in (0, 1):
                two = self.target(p.block(dx=1, dc=dc, zh=zh) // 2 * 2, 2)
                self.links.arrived(two, self.cross[zh, dc])


def row_blocks(ref, unit, cols=None):
    def target(first, count):
        rows = pl.ds(pl.multiple_of(first * unit, unit), count * unit)
        return ref.at[rows] if cols is None else ref.at[rows, cols]

    return target


def column_blocks(ref, unit):
    return lambda first, count: ref.at[:, pl.ds(pl.multiple_of(first * unit, unit), count * unit)]


def first_kernel(
    weight_ref, source_ref, tok_ref, cot_ref, ig_ref, o_ref, gates_ref, small_ref, gate_ref,
    all_ref, wig_ref, wo_ref, wide_ref, ch_ref, gains_ref, dms_ref, dout_ref, own_ref, wg_ref,
    pieces, smalls, dm, send, recv, local,
):
    p = Place()
    links = Links(send, recv, local)
    drows = ig_ref.shape[1]
    crows = wo_ref.shape[0]
    greet(weight_peers(p))
    gather = TokenGatherTwice(p, links, tok_ref, all_ref)
    w_ig = WeightGather(p, links, lambda j: ig_ref.at[j], row_blocks(wig_ref, drows), drows)
    w_o = WeightGather(
        p,
        links,
        lambda j: o_ref.at[pl.ds(pl.multiple_of(j * crows, 16), crows)],
        column_blocks(wo_ref, o_ref.shape[1]),
        drows,
    )
    unit = gates_ref.shape[1]
    w_g = WeightGather(p, links, lambda j: gates_ref.at[j], row_blocks(pieces, unit), unit)
    w_s = WeightGather(p, links, lambda j: small_ref, row_blocks(smalls, 16), 16)
    w_gate = slot_columns(p, links, gate_ref, wg_ref)
    adjoint = TokenGatherTwice(p, links, dm, dms_ref)
    w_s.begin()
    w_ig.begin((1,))
    w_ig.begin((0,))
    w_g.begin((0,))
    w_o.begin((0,))
    gather.begin()
    own = links.keep(tok_ref.at[p.mp], own_ref)
    scales = [weight_ref[source_ref[m, 0]] for m in range(2)]
    for m in range(2):

        def scale(rows, m=m):
            value = cot_ref[m, rows, :].astype(F32) * scales[m]
            dm[m, rows, :] = value.astype(BF)

            @pl.when(p.mp == m)
            def _():
                dout_ref[rows, :] = value

        chunks(cot_ref.shape[1], scale, 1)
    adjoint.begin()
    w_ig.onward(0)
    w_g.onward(0)
    w_o.onward(0)
    w_s.onward(0)
    w_gate.begin((0,))
    w_o.begin((1,))
    w_g.begin((1,))
    w_ig.onward(1)
    w_gate.begin((1,), (0,))
    w_s.onward(1)
    gather.forward()
    w_o.onward(1)
    w_g.onward(1)
    w_gate.begin((1,), (1,))
    gather.forward_core()
    w_gate.onward(0)
    adjoint.forward()
    w_gate.onward(1, (0,))
    adjoint.forward_core()
    w_s.end()
    count = small_channels(local_channels=crows)
    table = jnp.zeros((8, LANES), F32)
    for k in range(4):
        at = pl.ds(pl.multiple_of((p.slot() * 4 + k) * 16, 16), 16)
        rows = smalls[at, :].astype(F32)[:8]
        rows = jnp.concatenate([rows, jnp.zeros((8, LANES - 128), F32)], axis=1)
        table = table + (pltpu.roll(rows, k * count, 1) if k else rows)
    ch_ref[...] = table
    for k in range(16):
        rows = smalls[k * 16 : (k + 1) * 16, :].astype(F32)
        gains_ref[:, k * 128 : (k + 1) * 128] = rows[8:10]
    w_g.end()
    size = crows // 2
    per = size // 16
    total = jnp.zeros(wide_ref.shape, F32)
    row = lax.broadcasted_iota(jnp.int32, (LANES, pieces.shape[0]), 0)
    column = lax.broadcasted_iota(jnp.int32, (LANES, pieces.shape[0]), 1)
    source = lax.broadcasted_iota(jnp.int32, (LANES, 2 * LANES), 0)
    target = lax.broadcasted_iota(jnp.int32, (LANES, 2 * LANES), 1)
    for h in range(2):
        r = column % 32 - h * 16
        wanted = (r >= 0) & (r < per) & (row == h * size + column // 32 * per + r)
        rows = dot(jnp.where(wanted, 1.0, 0.0).astype(BF), pieces[...], NN, BF)
        gate = target // LANES
        wanted = (source == target - gate * LANES - h * size + gate * size) & (
            (source >= gate * size) & (source < (gate + 1) * size)
        )
        total = total + dot(rows, jnp.where(wanted, 1.0, 0.0).astype(BF), NN)
    wide_ref[...] = total.astype(BF)
    w_gate.onward(1, (1,))
    own.wait()
    gather.end()
    adjoint.end()
    w_gate.end()
    w_ig.end()
    w_o.end()
    links.finish()


def small_channels(local_channels):
    return local_channels // 4


class TokenGatherTwice:
    def __init__(self, place, links, source, target):
        self.place, self.links, self.source, self.target = place, links, source, target
        self.z, self.y = links.pair(), links.pair()
        self.core = {(mp, zl): links.pair() for mp in (0, 1) for zl in (0, 1)}

    def begin(self):
        p = self.place
        self.kept = []
        for mp in (0, 1):
            at = p.rows(mp=mp)
            src = self.source.at[flip(p.mp, mp)]
            if mp == 0:
                self.links.start(src, self.target.at[at], self.z, p.peer(zl=1))
            self.links.start(src, self.target.at[at], self.core[mp, 0], p.peer(dc=1))
            self.kept.append(self.links.keep(src, self.target.at[at]))

    def forward(self):
        p = self.place
        far = self.target.at[p.rows(zl=1)]
        self.links.arrived(far, self.z)
        self.links.start(far, far, self.y, p.peer(mp=1))
        self.links.start(far, far, self.core[0, 1], p.peer(dc=1))

    def forward_core(self):
        p = self.place
        far = self.target.at[p.rows(mp=1, zl=1)]
        self.links.arrived(far, self.y)
        self.links.start(far, far, self.core[1, 1], p.peer(dc=1))

    def end(self):
        p = self.place
        for (mp, zl), at in self.core.items():
            self.links.arrived(self.target.at[p.rows(dc=1, mp=mp, zl=zl)], at)
        for copy in self.kept:
            copy.wait()


class TokenGather:
    def __init__(self, place, links, source, target, span):
        self.place, self.links = place, links
        self.span = pl.ds(*span)
        self.source, self.target = source.at[self.span], target
        self.z, self.y0, self.y1 = links.pair(), links.pair(), links.pair()
        self.core = {(mp, zl): links.pair() for mp in (0, 1) for zl in (0, 1)}

    def block(self, **where):
        return self.target.at[self.place.rows(**where), self.span]

    def begin(self):
        p = self.place
        at = self.block()
        self.links.start(self.source, at, self.z, p.peer(zl=1))
        self.links.start(self.source, at, self.y0, p.peer(mp=1))
        self.links.start(self.source, at, self.core[0, 0], p.peer(dc=1))
        self.kept = self.links.keep(self.source, at)

    def forward(self):
        p = self.place
        far = self.block(zl=1)
        self.links.arrived(far, self.z)
        self.links.start(far, far, self.y1, p.peer(mp=1))
        self.links.start(far, far, self.core[0, 1], p.peer(dc=1))

    def forward_core(self):
        p = self.place
        far = self.block(mp=1)
        self.links.arrived(far, self.y0)
        self.links.start(far, far, self.core[1, 0], p.peer(dc=1))
        far = self.block(mp=1, zl=1)
        self.links.arrived(far, self.y1)
        self.links.start(far, far, self.core[1, 1], p.peer(dc=1))

    def end(self):
        for (mp, zl), at in self.core.items():
            self.links.arrived(self.block(dc=1, mp=mp, zl=zl), at)
        self.kept.wait()


CHUNK = 16


def chunks(count, body, most=11, first=0):
    n = count // CHUNK
    per = max(k for k in range(1, most + 1) if n % k == 0)

    def step(i, carry):
        for k in range(per):
            body(pl.ds(pl.multiple_of(first + (i * per + k) * CHUNK, CHUNK), CHUNK))
        return carry

    if n == per:
        step(0, 0)
    else:
        lax.fori_loop(0, n // per, step, 0)


def halves(rows):
    first = (rows // 2 + CHUNK - 1) // CHUNK * CHUNK
    return [(0, first), (first, rows - first)]


class RowScatter:
    def __init__(self, place, links, source, buffers, parts=None):
        self.place, self.links, self.source = place, links, source
        self.mine, self.from_core, self.from_y, self.from_z, self.out = buffers[:5]
        self.to_core = buffers[5] if len(buffers) > 5 else None
        self.parts = parts or [(0, self.mine.shape[1])]
        self.blocks = [(mp, zl) for mp in (1, 0) for zl in (1, 0)]
        self.kept = {}
        n = range(len(self.parts))
        self.core = {(h, block): links.pair() for h in n for block in self.blocks}
        self.y = {(h, zl): links.pair() for h in n for zl in (1, 0)}
        self.z = {h: links.pair() for h in n}

    def begin(self, mps=(1, 0)):
        p = self.place
        for mp, zl in self.blocks:
            if mp not in mps:
                continue
            i, block = mp * 2 + zl, p.rows(dc=1, mp=mp, zl=zl)
            if self.to_core is None:
                src = self.source.at[block]
            else:
                self.to_core[i] = self.source(block).astype(BF)
                src = self.to_core.at[i]
            for h, part in enumerate(self.parts):
                at = pl.ds(*part)
                self.links.start(
                    src.at[at], self.from_core.at[i, at], self.core[h, (mp, zl)], p.peer(dc=1)
                )
            block = p.rows(mp=mp, zl=zl)
            if self.to_core is None:
                self.kept[mp, zl] = self.links.keep(self.source.at[block], self.mine.at[i])
            else:
                self.mine[i] = self.source(block).astype(BF)

    def ready(self, mp, zl, h):
        i = mp * 2 + zl
        if h == 0 and self.kept:
            self.kept[mp, zl].wait()
        at = pl.ds(*self.parts[h])
        self.links.arrived(self.from_core.at[i, at], self.core[h, (mp, zl)])
        return i

    def across_y(self, h=0):
        p = self.place
        first, count = self.parts[h]
        at = pl.ds(first, count)
        for zl in (1, 0):
            i = self.ready(1, zl, h)

            def add(rows, i=i, zl=zl):
                total = self.mine[i, rows, :].astype(F32) + self.from_core[i, rows, :].astype(F32)
                self.out[zl, rows, :] = total.astype(BF)

            chunks(count, add, first=first)
            self.links.start(
                self.out.at[zl, at], self.from_y.at[zl, at], self.y[h, zl], p.peer(mp=1)
            )

    def across_z(self, h=0):
        p = self.place
        first, count = self.parts[h]
        at = pl.ds(first, count)
        i = self.ready(0, 1, h)
        self.links.arrived(self.from_y.at[1, at], self.y[h, 1])

        def add(rows):
            total = self.mine[i, rows, :].astype(F32) + self.from_core[i, rows, :].astype(F32)
            self.out[2, rows, :] = (total + self.from_y[1, rows, :].astype(F32)).astype(BF)

        chunks(count, add, first=first)
        self.links.start(self.out.at[2, at], self.from_z.at[at], self.z[h], p.peer(zl=1))

    def arrive(self, h=0):
        at = pl.ds(*self.parts[h])
        self.ready(0, 0, h)
        self.links.arrived(self.from_y.at[0, at], self.y[h, 0])
        self.links.arrived(self.from_z.at[at], self.z[h])

    def total(self, rows):
        a = self.mine[0, rows, :].astype(F32) + self.from_core[0, rows, :].astype(F32)
        b = self.from_y[0, rows, :].astype(F32) + self.from_z[rows, :].astype(F32)
        return a + b


def scatter_buffers(rows, width, products=False):
    return [
        pltpu.VMEM((4, rows, width), BF),
        pltpu.VMEM((4, rows, width), BF),
        pltpu.VMEM((2, rows, width), BF),
        pltpu.VMEM((rows, width), BF),
        pltpu.VMEM((3, rows, width), BF),
    ] + ([pltpu.VMEM((4, rows, width), BF)] if products else [])


def group_peers(p):
    return [p.peer(dc=1), p.peer(zl=1), p.peer(mp=1)]


def weight_peers(p):
    return [p.peer(dc=dc, zh=zh, zl=zl) for zh, dc, zl in FLIPS if (zh, dc, zl) != (0, 0, 0)] + [
        p.peer(dx=1),
        p.peer(mp=1),
    ]


def second_kernel(
    mixed_ref, wo_ref, own_ref, gain_ref, up_ref, down_ref,
    mid_ref, all_ref, wu_ref, wd_ref,
    *scratch,
):
    p = Place()
    links = Links(*scratch[-3:])
    normed = scratch[-4]
    rows, channels = own_ref.shape[0], wo_ref.shape[0]
    greet(weight_peers(p))

    def project(b):
        at = pl.ds(pl.multiple_of(b * rows, 16), rows)
        return dot(mixed_ref[at, :channels], wo_ref[...], NN)

    parts = halves(rows)
    scatter = RowScatter(p, links, project, scratch[:6], parts)
    w_u = slot_columns(p, links, up_ref, wu_ref)
    w_d = WeightGather(
        p,
        links,
        lambda j: down_ref.at[pl.ds(pl.multiple_of(j * wd_ref.shape[0], 16), wd_ref.shape[0])],
        column_blocks(wd_ref, down_ref.shape[1]),
        down_ref.shape[1],
    )
    gathers = [TokenGather(p, links, normed, all_ref, part) for part in parts]
    w_u.begin((1,), (0,))
    scatter.begin((1,))
    w_u.begin((0,))
    scatter.across_y(0)
    scatter.across_y(1)
    w_u.begin((1,), (1,))
    scatter.begin((0,))
    w_d.begin((0,))
    w_u.onward(0)

    def normalise(at):
        value = own_ref[at, :].astype(F32) + scatter.total(at)
        mid_ref[at, :] = value
        inv = lax.rsqrt(jnp.mean(value * value, axis=-1, keepdims=True) + EPSILON)
        normed[at, :] = (value * inv * gain_ref[...]).astype(BF)

    def middle(h):
        scatter.arrive(h)
        chunks(parts[h][1], normalise, first=parts[h][0])
        gathers[h].begin()

    scatter.across_z(0)
    w_d.onward(0)
    scatter.across_z(1)
    w_d.begin((1,), (0,))
    middle(0)
    w_u.onward(1, (0,))
    middle(1)
    w_u.onward(1, (1,))
    w_d.begin((1,), (1,))
    gathers[0].forward()
    gathers[1].forward()
    w_d.onward(1, (0,))
    gathers[0].forward_core()
    gathers[1].forward_core()
    w_d.onward(1, (1,))
    for gather in gathers:
        gather.end()
    w_u.end()
    w_d.end()
    links.finish()


def slot_columns(p, links, source, result):
    count = result.shape[1]
    return WeightGather(
        p,
        links,
        lambda j: source.at[:, pl.ds(pl.multiple_of(j * count, 128), count)],
        row_blocks(result, source.shape[0]),
        source.shape[0],
    )


class GradScatter:
    FAR = [(1, 0, 1), (1, 1, 1)], [(1, 0, 0), (1, 1, 0)]
    NEAR = [(0, 0, 1), (0, 1, 1)], [(0, 0, 0), (0, 1, 0)]
    ORDER = FAR[0] + NEAR[0] + FAR[1] + NEAR[1]
    EARLY = FAR[0] + FAR[1] + NEAR[0] + NEAR[1]

    def __init__(self, place, links, left, right, buffers, order=ORDER):
        self.order = order
        self.place, self.links, self.left, self.right = place, links, left, right
        self.to_x, self.from_x, self.to_z, self.from_z, self.sums, self.result = buffers[:6]
        self.columns = buffers[6] if len(buffers) > 6 else None
        self.rows = self.to_x.shape[1]
        self.x = {(zh, dc): links.pair() for zh in (1, 0) for dc in (0, 1)}
        self.z = {dc: links.pair() for dc in (0, 1)}
        self.at = {(dc, zl): links.pair() for dc in (0, 1) for zl in (0, 1)}
        self.count = 0
        self.load()

    def load(self):
        if self.count < 8 and self.columns is not None:
            dx, dc, zh = self.order[self.count]
            first = self.place.block(dx=dx, dc=dc, zh=zh) // 2
            columns = pl.ds(pl.multiple_of(first * self.rows, self.rows), self.rows)
            self.loading = self.links.keep(
                self.left.at[:, columns], self.columns.at[self.count % 2]
            )

    def product(self, dx=0, dc=0, zh=0):
        assert self.order[self.count] == (dx, dc, zh)
        self.loading.wait()
        self.count += 1
        self.load()
        return dot(self.columns[(self.count - 1) % 2], self.right[...], TN)

    def begin(self, zh):
        for dc in (0, 1):
            i = zh * 2 + dc
            self.to_x[i] = self.product(dx=1, dc=dc, zh=zh).astype(BF)
            self.links.start(
                self.to_x.at[i], self.from_x.at[i], self.x[zh, dc], self.place.peer(dx=1)
            )

    def across(self, dc):
        mine = self.product(dc=dc, zh=1)
        self.links.arrived(self.from_x.at[2 + dc], self.x[1, dc])
        self.to_z[dc] = (mine + self.from_x[2 + dc].astype(F32)).astype(BF)
        self.links.start(self.to_z.at[dc], self.from_z.at[dc], self.z[dc], self.place.peer(zh=1))

    def last(self, dc):
        p = self.place
        mine = self.product(dc=dc, zh=0)
        self.links.arrived(self.from_x.at[dc], self.x[0, dc])
        self.links.arrived(self.from_z.at[dc], self.z[dc])
        total = mine + self.from_x[dc].astype(F32) + self.from_z[dc].astype(F32)
        self.sums[dc] = total.astype(BF)
        unit = self.rows // 2
        for zl in (1, 0):
            src = self.sums.at[dc, pl.ds(pl.multiple_of(flip(p.zl, zl) * unit, unit), unit)]
            dst = self.result.at[p.slot()]
            if (dc, zl) == (0, 0):
                self.own = self.links.keep(src, dst)
            else:
                self.links.start(src, dst, self.at[dc, zl], p.peer(dc=dc, zl=zl))

    def end(self):
        p = self.place
        for (dc, zl), at in self.at.items():
            if (dc, zl) == (0, 0):
                self.own.wait()
            else:
                self.links.arrived(self.result.at[p.slot(dc, zl)], at)


class Ready(GradScatter):
    def product(self, dx=0, dc=0, zh=0):
        first = self.place.block(dx=dx, dc=dc, zh=zh) // 2
        return self.left[pl.ds(pl.multiple_of(first * self.rows, self.rows), self.rows), :].astype(
            F32
        )


def grad_buffers(rows, columns, tokens=None):
    return (
        [pltpu.VMEM((n, rows, columns), BF) for n in (4, 4, 2, 2, 2)]
        + [pltpu.VMEM((4, rows // 2, columns), BF)]
        + ([pltpu.VMEM((2, tokens, rows), BF)] if tokens else [])
    )


def norm_back(value, gain, upstream):
    inv = lax.rsqrt(jnp.mean(value * value, axis=-1, keepdims=True) + EPSILON)
    scaled = value * inv
    up = upstream * gain
    inner = jnp.mean(up * scaled, axis=-1, keepdims=True)
    return inv * (up - scaled * inner), upstream * scaled


def fold(rows):
    return rows[:8] + rows[8:]


def third_kernel(
    wg_ref, wu_ref, wd_in, mid_in, dout_in, gain_ref, dm_ref, hidden_ref, n2_ref, dgm_ref,
    dup_ref,
    dr1_ref, gain_out, all_ref, gate_out, down_out, part_out,
    *scratch,
):
    p = Place()
    links = Links(*scratch[-3:])
    do, wd_ref, mid_ref, dout_ref = scratch[-7:-3]
    rows_of = mid_ref.shape[0]
    staged = [
        links.keep(src, dst)
        for src, dst in ((mid_in, mid_ref), (dout_in, dout_ref), (wd_in, wd_ref))
    ]
    greet(weight_peers(p))

    def product(b):
        at = pl.ds(pl.multiple_of(b * rows_of, 16), rows_of)
        return dot(dgm_ref[at, :], wg_ref[...], NT) + dot(dup_ref[at, :], wu_ref[...], NT)

    parts = halves(rows_of)
    scatter = RowScatter(p, links, product, scratch[:6], parts)
    down = GradScatter(p, links, dm_ref, hidden_ref, scratch[6:13])
    gate = GradScatter(p, links, n2_ref, dgm_ref, scratch[13:20])
    gathers = [TokenGather(p, links, do, all_ref, part) for part in parts]
    down.begin(1)
    scatter.begin((1,))
    scatter.across_y(0)
    scatter.across_y(1)
    down.across(0)
    scatter.begin((0,))
    down.across(1)
    gate.begin(1)
    gain_out[...] = jnp.zeros_like(gain_out)
    for copy in staged:
        copy.wait()

    def back(rows):
        part, gain = norm_back(mid_ref[rows, :], gain_ref[...], scatter.total(rows))
        value = dout_ref[rows, :] + part
        dr1_ref[rows, :] = value
        do[rows, :] = value.astype(BF)
        gain_out[...] += fold(gain)

    def middle(h):
        scatter.arrive(h)
        chunks(parts[h][1], back, first=parts[h][0])
        gathers[h].begin()

    scatter.across_z(0)
    down.begin(0)
    gate.across(0)
    scatter.across_z(1)
    middle(0)
    gate.across(1)
    gate.begin(0)
    middle(1)
    gathers[0].forward()
    gathers[1].forward()
    down.last(0)
    down.last(1)
    gathers[0].forward_core()
    gate.last(0)
    out = scratch[0]
    writes = []
    for b in range(8):
        if b >= 4:
            writes[b - 4].wait()
        at = pl.ds(b * rows_of, rows_of)
        out[b % 4] = dot(hidden_ref[at, :], wd_ref[...], NN, BF)
        writes.append(links.keep(out.at[b % 4], part_out.at[b]))
    gathers[1].forward_core()
    gate.last(1)
    for gather in gathers:
        gather.end()
    down.end()
    ff = down.result.shape[2]
    for j in range(4):
        down_out[j * ff : (j + 1) * ff, :] = down.result[j].astype(F32).T
    gate.end()
    for j in range(4):
        gate_out[:, j * ff : (j + 1) * ff] = gate.result[j].astype(F32)
    for write in writes[4:]:
        write.wait()
    links.finish()


def fourth_kernel(
    wig_ref, own_ref, dr1_ref, gain_ref, do_ref, mixed_ref, n1_ref, dboth_ref, gg_ref,
    dx_ref, gain_out, in_out, gelu_out, out_out, gates_out,
    *scratch,
):
    p = Place()
    links = Links(*scratch[-3:])
    dx_send, dx_recv = scratch[-5:-3]
    greet(weight_peers(p))
    rows_of = own_ref.shape[0]

    def product(b):
        at = pl.ds(pl.multiple_of(b * rows_of, 16), rows_of)
        return dot(dboth_ref[at, :], wig_ref[...], NT)

    parts = halves(rows_of)
    scatter = RowScatter(p, links, product, scratch[:6], parts)
    out = GradScatter(p, links, do_ref, mixed_ref, scratch[6:13])
    wide = GradScatter(p, links, n1_ref, dboth_ref, scratch[13:20])
    gates = Ready(p, links, gg_ref, None, scratch[20:26])
    out.begin(1)
    scatter.begin((1,))
    scatter.across_y(0)
    scatter.across_y(1)
    out.across(0)
    out.across(1)
    wide.begin(1)
    scatter.begin((0,))
    gates.begin(1)
    out.begin(0)
    for g in (wide, gates):
        g.across(0)
        g.across(1)
        g.begin(0)
    gain_out[...] = jnp.zeros_like(gain_out)

    def back(rows):
        value = own_ref[rows, :].astype(F32)
        part, gain = norm_back(value, gain_ref[...], scatter.total(rows))
        total = dr1_ref[rows, :] + part
        dx_ref[p.mp, rows, :] = total
        dx_send[rows, :] = total.astype(BF)
        gain_out[...] += fold(gain)

    sent = []

    def middle(h):
        scatter.arrive(h)
        chunks(parts[h][1], back, first=parts[h][0])
        span, at = pl.ds(*parts[h]), links.pair()
        links.start(dx_send.at[span], dx_recv.at[span], at, p.peer(mp=1))
        sent.append((span, at))

    scatter.across_z(0)
    scatter.across_z(1)
    middle(0)
    for g in (out, gates):
        g.last(0)
        g.last(1)
    middle(1)
    wide.last(0)
    wide.last(1)
    local = out.result.shape[2]
    out.end()
    for j in range(4):
        out_out[j * out_out.shape[0] // 4 : (j + 1) * out_out.shape[0] // 4, :] = (
            out.result[j].astype(F32).T[: out_out.shape[0] // 4]
        )
    gates.end()
    gates_out[...] = gates.result[...]
    wide.end()
    two = wide.result.shape[2]
    left = lax.broadcasted_iota(jnp.int32, (1, two), 1) < two // 2
    for j in (0, 2):
        a, b = (wide.result[j + i].astype(F32) for i in (0, 1))
        span = slice(j * two // 2, (j + 2) * two // 2)
        in_out[:, span] = jnp.where(left, a, pltpu.roll(b, two // 2, 1))
        gelu_out[:, span] = jnp.where(left, pltpu.roll(a, two // 2, 1), b)
    for span, at in sent:
        links.arrived(dx_recv.at[span], at)
    dx_ref[1 - p.mp] = dx_recv[...].astype(F32)
    links.finish()


def mlp_kernel(
    n2_ref, dm_ref, wg_ref, wu_ref, wd_ref, hidden_ref, dgm_ref, dup_ref, pre, upp, dhm
):
    count, rows, width = n2_ref.shape
    n2 = n2_ref[...].reshape(count * rows, width)
    pre[...] = dot(n2, wg_ref[...], NN)
    upp[...] = dot(n2, wu_ref[...], NN)
    dhm[...] = dot(dm_ref[...].reshape(count * rows, width), wd_ref[...], NT)

    def body(at):
        up, d = upp[at, :], dhm[at, :]
        value, slope = gelu_both(pre[at, :])
        hidden_ref[at, :] = (value * up).astype(BF)
        dgm_ref[at, :] = (d * up * slope).astype(BF)
        dup_ref[at, :] = (d * value).astype(BF)

    chunks(count * rows, body)


def feed_forward(n2, dm, w_g, w_u, w_d):
    blocks, rows, width = n2.shape
    ff = w_d.shape[0]
    if not shape_fits():
        n2, dm = n2.reshape(-1, width), dm.reshape(-1, width)
        pre, d = dot(n2, w_g, NN), dot(dm, w_d, NT)
        gm, up = pre, dot(n2, w_u, NN)
        value, slope = gelu_both(gm)
        return (value * up).astype(BF), (d * up * slope).astype(BF), (d * value).astype(BF)
    two = pl.BlockSpec((2, rows, width), lambda i: (i, 0, 0))
    flat = pl.BlockSpec((2 * rows, ff), lambda i: (i, 0))
    whole = lambda v: pl.BlockSpec(v.shape, lambda i: (0, 0))
    total = blocks * rows
    return pl.pallas_call(
        mlp_kernel,
        name="feed_forward",
        grid=(blocks // 2,),
        in_specs=[two, two, whole(w_g), whole(w_u), whole(w_d)],
        out_specs=[flat] * 3,
        out_shape=[jax.ShapeDtypeStruct((total, ff), BF)] * 3,
        scratch_shapes=[pltpu.VMEM((2 * rows, ff), F32)] * 3,
        compiler_params=pltpu.CompilerParams(vmem_limit_bytes=48 * 1024 * 1024),
        cost_estimate=pl.CostEstimate(
            flops=2 * total * width * ff * 3, bytes_accessed=total * width * 4, transcendentals=0
        ),
    )(n2, dm, w_g, w_u, w_d)


def semaphores(pairs, local):
    return [
        pltpu.SemaphoreType.DMA((pairs,)),
        pltpu.SemaphoreType.DMA((pairs,)),
        pltpu.SemaphoreType.DMA((local,)),
    ]


def run_kernel(body, name, outs, out_specs, in_specs, scratch, ident, args, mib=40):
    return pl.pallas_call(
        body,
        name=name,
        out_shape=[jax.ShapeDtypeStruct(*o) for o in outs],
        in_specs=in_specs,
        out_specs=out_specs,
        scratch_shapes=scratch,
        compiler_params=pltpu.CompilerParams(
            collective_id=ident, has_side_effects=True, vmem_limit_bytes=mib * 1024 * 1024
        ),
    )(*args)


def fetch_first(
    tokens, cotangent, seq_source, source_weight, input_weight, gelu_weight, output_weight,
    decay_gates, input_gates, channel_params, norm_gains, mlp_gate,
):
    args = (
        tokens, cotangent, seq_source, source_weight, input_weight, gelu_weight, output_weight,
        decay_gates, input_gates, channel_params, norm_gains, mlp_gate,
    )
    if not shape_fits():
        return plain_fetch_first(*args)
    rows, width = tokens.shape[1:]
    drows, local = input_weight.shape[0], input_weight.shape[1] // 4
    pairs = [v.reshape(drows, 4, local) for v in (input_weight, gelu_weight)]
    ig = jnp.concatenate(pairs, axis=2).transpose(1, 0, 2)
    per = decay_gates.shape[1] // BLOCK
    gates = [v.reshape(8, per, BLOCK) for v in (decay_gates, input_gates)]
    gates = jnp.concatenate(gates, axis=2)
    gates = jnp.pad(gates, ((0, 0), (0, 16 - per), (0, LANES - 2 * BLOCK))).reshape(4, 32, LANES)
    small = jnp.pad(channel_params[:, 0], ((0, 0), (0, drows - channel_params.shape[2])))
    small = jnp.pad(jnp.concatenate([small, norm_gains], axis=0), ((0, 6), (0, 0)))
    smem = pl.BlockSpec(memory_space=pltpu.SMEM)
    return run_kernel(
        first_kernel,
        "fetch_first",
        [
            ((8, rows, width), BF),
            ((width, 2 * local), BF),
            ((local, width), BF),
            ((LANES, 2 * LANES), BF),
            ((8, LANES), F32),
            ((2, width), F32),
            ((8, rows, width), BF),
            ((rows, width), F32),
            ((rows, width), BF),
            ((width, mlp_gate.shape[1] // 4), BF),
        ],
        [ANY] * 3 + [VMEM] * 3 + [ANY, VMEM, ANY, ANY],
        [smem, smem, ANY, VMEM] + [ANY] * 5,
        [
            pltpu.VMEM((512, LANES), BF),
            pltpu.VMEM((256, 128), BF),
            pltpu.VMEM((2, rows, width), BF),
        ]
        + semaphores(80, 16),
        1,
        (source_weight, seq_source, tokens, cotangent, ig, output_weight, gates, small, mlp_gate),
        61,
    )


def reduce_and_fetch(mixed, w_o, own, gain, mlp_up, mlp_down):
    if not shape_fits():
        return plain_reduce_and_fetch(mixed, w_o, own, gain, mlp_up, mlp_down)
    rows, width = own.shape
    ff = mlp_up.shape[1] // 4
    return run_kernel(
        second_kernel,
        "reduce_and_fetch",
        [((rows, width), F32), ((8, rows, width), BF), ((width, ff), BF), ((ff, width), BF)],
        [VMEM] + [ANY] * 3,
        [VMEM] * 4 + [ANY] * 2,
        scatter_buffers(rows, width, True) + [pltpu.VMEM((rows, width), BF)] + semaphores(64, 16),
        2,
        (mixed, w_o, own, gain, mlp_up, mlp_down),
    )


def reduce_and_return(weights, middle, dout, gain, dm, hidden, n2, dgm, dup, drows):
    if not shape_fits():
        return plain_reduce_and_return(
            weights, middle, dout, gain, dm, hidden, n2, dgm, dup, drows
        )
    rows, width = middle.shape
    ff = hidden.shape[1]
    return run_kernel(
        third_kernel,
        "reduce_and_return",
        [
            ((rows, width), F32),
            ((8, width), F32),
            ((8, rows, width), BF),
            ((drows, 4 * ff), F32),
            ((4 * ff, drows), F32),
            ((8, rows, width), BF),
        ],
        [VMEM, VMEM, ANY] + [VMEM] * 2 + [ANY],
        [VMEM] * 2 + [ANY] * 3 + [VMEM] + [ANY, VMEM] * 2 + [VMEM],
        scatter_buffers(rows, width, True)
        + grad_buffers(2 * drows, ff, 8 * rows) * 2
        + [pltpu.VMEM((rows, width), BF), pltpu.VMEM((ff, width), BF)]
        + [pltpu.VMEM((rows, width), F32)] * 2
        + semaphores(56, 56),
        3,
        (*weights, middle, dout, gain, dm, hidden, n2, dgm, dup),
        61,
    )


def return_last(w_ig, own, dr1, gain, do, mixed, n1, dboth, g_gates, drows):
    if not shape_fits():
        return plain_return_last(w_ig, own, dr1, gain, do, mixed, n1, dboth, g_gates, drows)
    rows, width = own.shape
    local, unit = dboth.shape[1] // 2, g_gates.shape[0] // 16
    return run_kernel(
        fourth_kernel,
        "return_last",
        [
            ((2, rows, width), F32),
            ((8, width), F32),
            ((drows, 4 * local), F32),
            ((drows, 4 * local), F32),
            ((4 * local, drows), F32),
            ((4, unit, 128), BF),
        ],
        [VMEM] * 6,
        [VMEM] * 4 + [ANY, VMEM] * 2 + [VMEM],
        scatter_buffers(rows, width, True)
        + grad_buffers(2 * drows, mixed.shape[1], 8 * rows)
        + grad_buffers(2 * drows, 2 * local, 8 * rows)
        + grad_buffers(2 * unit, 128)
        + [pltpu.VMEM((rows, width), BF)] * 2
        + semaphores(64, 48),
        4,
        (w_ig, own, dr1, gain, do, mixed, n1, dboth, g_gates),
        60,
    )


def shape_fits():
    return all(lax.axis_size(n) == 2 for n in AXES)


def plain_fetch_first(
    tokens, cotangent, seq_source, source_weight, input_weight, gelu_weight, output_weight,
    decay_gates, input_gates, channel_params, norm_gains, mlp_gate,
):
    exchange = Tokens()
    dxn, zhn, mp = lax.axis_size("dx"), lax.axis_size("zh"), exchange.mp
    group = dxn * 2 * zhn * 2
    local = input_weight.shape[1] // 4
    heads, piece = decay_gates.shape[0] // 4, decay_gates.shape[1]
    shards = ("dx", "dc", "zh", "zl")
    own = lax.dynamic_index_in_dim(tokens, mp, 0, keepdims=False)
    sources = jnp.arange(source_weight.shape[0], dtype=jnp.int32)
    scales = jnp.sum(jnp.where(seq_source == sources[None], source_weight[None], 0.0), axis=1)
    douts = cotangent.astype(F32) * scales[:, None, None]
    small = jnp.concatenate([channel_params.reshape(-1), norm_gains.reshape(-1)])
    small = lax.all_to_all(
        jnp.broadcast_to(small[None], (group, small.size)), shards, 0, 0, tiled=True
    )
    nch = channel_params.size
    channels = small[:, :nch].reshape(group, 8, -1).transpose(1, 0, 2).reshape(8, -1)
    slot = exchange.dc * 2 + exchange.zl
    channels = lax.dynamic_slice_in_dim(channels, slot * local, local, 1).astype(F32)
    gains = small[:, nch:].reshape(group, 2, -1).transpose(1, 0, 2).reshape(2, -1).astype(F32)
    gates = jnp.stack([decay_gates, input_gates]).reshape(2, 4, heads, piece)
    gates = gates.transpose(1, 0, 2, 3).reshape(2, 1, 2, 1, 2 * heads * piece)
    gates = jnp.broadcast_to(gates, (2, zhn, 2, dxn, 2 * heads * piece))
    gates = gates.transpose(3, 0, 1, 2, 4).reshape(group, 2 * heads * piece)
    gates = lax.all_to_all(gates, shards, 0, 0, tiled=True)
    gates = gates.reshape(group, 2 * heads, piece).transpose(1, 0, 2)
    gates = gates.reshape(2, heads, BLOCK, BLOCK)
    zero = jnp.zeros((BLOCK, BLOCK), BF)
    blocks = [
        [gates[g, h] if k == h else zero for g in range(2) for k in range(heads)]
        for h in range(heads)
    ]
    return (
        exchange.gather(own).reshape((8,) + own.shape),
        fetch_weight([input_weight, gelu_weight], 4),
        fetch_weight([output_weight.T], 4).T,
        jnp.concatenate([jnp.concatenate(v, axis=1) for v in blocks], axis=0),
        channels,
        gains,
        exchange.gather(lax.dynamic_index_in_dim(douts, mp, 0, keepdims=False).astype(BF)).reshape(
            (8,) + own.shape
        ),
        lax.dynamic_index_in_dim(douts, mp, 0, keepdims=False),
        own,
        fetch_weight([mlp_gate], 4),
    )


def plain_reduce_and_fetch(mixed, w_o, own, gain, mlp_up, mlp_down):
    exchange = Tokens()
    middle = own.astype(F32) + exchange.scatter(dot(mixed, w_o, NN, BF))
    normed = (middle * inverse_rms(middle) * gain).astype(BF)
    return (
        middle,
        exchange.gather(normed).reshape((8,) + own.shape),
        fetch_weight([mlp_up], 4),
        fetch_weight([mlp_down.T], 4).T,
    )


def columns(share, at, count):
    return share[:, :, at : at + count].astype(F32).transpose(1, 0, 2).reshape(-1, 4 * count)


def both_batches(rows):
    mp = lax.axis_index("mp")
    other = lax.ppermute(rows, "mp", [(0, 1), (1, 0)])
    return jnp.stack([jnp.where(mp == 0, rows, other), jnp.where(mp == 0, other, rows)])


def plain_reduce_and_return(weights, middle, dout, gain, dm, hidden, n2, dgm, dup, drows):
    exchange = Tokens()
    w_g, w_u, w_d = weights
    ff = hidden.shape[1]
    total = exchange.scatter((dot(dgm, w_g, NT) + dot(dup, w_u, NT)).astype(BF))
    change, gain_rows = norm_back(middle, gain, total)
    dr1 = dout + change
    gate = return_grad(dot(n2, dgm, TN, BF), drows)
    down = return_grad(dot(dm, hidden, TN, BF), drows)
    return (
        dr1,
        jnp.sum(gain_rows, axis=0, keepdims=True),
        exchange.gather(dr1.astype(BF)).reshape((8,) + dr1.shape),
        columns(gate, 0, ff),
        columns(down, 0, ff).T,
        dot(hidden, w_d, NN, BF).reshape((8,) + dr1.shape),
    )


def plain_return_last(w_ig, own, dr1, gain, do, mixed, n1, dboth, g_gates, drows):
    exchange = Tokens()
    local = dboth.shape[1] // 2
    total = exchange.scatter(dot(dboth, w_ig, NT, BF))
    change, gain_rows = norm_back(own.astype(F32), gain, total)
    group = n1.shape[1] // drows
    wide = return_grad(dot(n1, dboth, TN, BF), drows)
    out = return_grad(dot(do, mixed, TN, BF), drows)
    return (
        both_batches(dr1 + change),
        jnp.sum(gain_rows, axis=0, keepdims=True),
        columns(wide, 0, local),
        columns(wide, local, local),
        columns(out, 0, local).T,
        return_grad(g_gates, g_gates.shape[0] // group),
    )


def scan_body(reverse, a_ref, b_ref, p_ref, h_ref):
    length, width = a_ref.shape[1], a_ref.shape[2]
    row = lax.broadcasted_iota(jnp.int32, (8, width), 0)

    def tile(i, carry):
        ca, ch = carry
        at = (length // 8 - 1 - i if reverse else i) * 8
        at = pl.multiple_of(at, 8)
        a = a_ref[0, pl.ds(at, 8), :]
        b = b_ref[0, pl.ds(at, 8), :]
        for step in (1, 2, 4):
            if reverse:
                inside = row < 8 - step
                shift = 8 - step
            else:
                inside = row >= step
                shift = step
            sa = jnp.where(inside, pltpu.roll(a, shift, 0), 1.0)
            sb = jnp.where(inside, pltpu.roll(b, shift, 0), 0.0)
            b = b + a * sb
            a = a * sa
        h = b + a * ch
        p = a * ca
        h_ref[0, pl.ds(at, 8), :] = h
        p_ref[0, pl.ds(at, 8), :] = p
        last = 0 if reverse else 7
        return p[last : last + 1, :], h[last : last + 1, :]

    lax.fori_loop(
        0,
        length // 8,
        tile,
        (jnp.ones((1, width), F32), jnp.zeros((1, width), F32)),
    )


def local_scan(a, b, reverse):
    segs, length, width = a.shape
    spec = pl.BlockSpec((1, length, width), lambda s: (s, 0, 0))
    return pl.pallas_call(
        lambda *refs: scan_body(reverse, *refs),
        grid=(segs,),
        in_specs=[spec, spec],
        out_specs=[spec, spec],
        out_shape=[jax.ShapeDtypeStruct(a.shape, F32)] * 2,
        cost_estimate=pl.CostEstimate(
            flops=20 * a.size, bytes_accessed=16 * a.size, transcendentals=0
        ),
    )(a, b)


def carried(product, state, reverse):
    count = lax.axis_size("zh")
    if count == 2:
        return lax.ppermute(state, "zh", [(1, 0)] if reverse else [(0, 1)])
    here = lax.axis_index("zh")
    pairs = lax.all_gather(jnp.stack([product, state]), "zh")
    total = jnp.zeros_like(state)
    for k in range(count):
        at = count - 1 - k if reverse else k
        reached = at > here if reverse else at < here
        total = jnp.where(reached, pairs[at, 1] + pairs[at, 0] * total, total)
    return total


def from_behind(x, by):
    count = lax.axis_size("zh")
    return lax.ppermute(
        x, "zh", [(i, i + by) for i in range(count) if 0 <= i + by < count]
    )


def inverse_rms(values):
    return lax.rsqrt(jnp.mean(values * values, axis=-1, keepdims=True) + EPSILON)


def gelu(v):
    return jax.nn.gelu(v, approximate=True)


def gelu_both(v):
    c = 0.7978845608028654
    t = jnp.tanh(c * (v + 0.044715 * v * v * v))
    value = 0.5 * v * (1.0 + t)
    slope = 0.5 * (1.0 + t) + 0.5 * v * (1.0 - t * t) * c * (1.0 + 3 * 0.044715 * v * v)
    return value, slope


def dot(a, b, dims, out=F32):
    r = lax.dot_general(a, b, (dims, ((), ())), preferred_element_type=F32)
    return r.astype(out)


NN = ((1,), (0,))
NT = ((1,), (1,))
TN = ((0,), (0,))


def minus_expm1(v):
    series = 1.0 + v / 8.0
    for k in (7.0, 6.0, 5.0, 4.0, 3.0, 2.0):
        series = 1.0 + v * (1.0 / k) * series
    return jnp.where(v > -0.4, -v * series, 1.0 - jnp.exp(v))


def loop(count, body, unroll=1):
    def step(i, carry):
        body(i)
        return carry

    lax.fori_loop(0, count, step, 0, unroll=unroll)


def tile_scan(a, b, row, reverse):
    for step in (1, 2, 4):
        inside = row < 8 - step if reverse else row >= step
        shift = 8 - step if reverse else step
        sa = jnp.where(inside, pltpu.roll(a, shift, 0), 1.0)
        sb = jnp.where(inside, pltpu.roll(b, shift, 0), 0.0)
        b = b + a * sb
        a = a * sa
    return a, b


def eight(i):
    return pl.multiple_of(i * 8, 8)


def recur_forward_kernel(
    tok_ref, wig_ref, blocks_ref, ch_ref, gain_ref,
    n1_out, xs_out, gy_out, u_out, siga_out, sigi_out, decay_out, states, mixed,
    xs, gy, u, siga, sigi, decay, run, logits, n1, both, halo, ends, inc, tok, sems,
    send, recv, local_sems,
):
    p = Place()
    links = Links(send, recv, local_sems)
    rows, local = tok_ref.shape[1], wig_ref.shape[1] // 2
    zh = p.zh
    greet([p.peer(zh=1)])

    def read(b):
        return pltpu.make_async_copy(tok_ref.at[b], tok.at[b % 2], sems.at[4 + b % 2])

    read(0).start()
    lane = lax.broadcasted_iota(jnp.int32, (1, LANES), 1)
    real = lane < local

    def project(b):
        read(b).wait()

        @pl.when(b < 7)
        def _():
            read(b + 1).start()

        def normalise(at):
            value = tok[b % 2, at, :].astype(F32)
            inv = lax.rsqrt(jnp.mean(value * value, axis=-1, keepdims=True) + EPSILON)
            n1[b % 2, at, :] = (value * inv * gain_ref[...]).astype(BF)

        def write(i, at):
            return pltpu.make_async_copy(n1.at[i], n1_out.at[at], sems.at[i])

        @pl.when(b >= 2)
        def _():
            write(b % 2, b - 2).wait()

        chunks(rows, normalise)
        write(b % 2, b).start()
        both[...] = dot(n1[b % 2], wig_ref[...], NN)
        seg, zl = b // 2, b % 2

        def split(at):
            v = both[at, :]
            xb = jnp.where(real, v[:, :LANES], 0.0).astype(BF).astype(F32)
            xs[seg, pl.ds(pl.multiple_of(8 + zl * rows + at.start, 8), CHUNK), :] = xb
            rest = pltpu.roll(v, v.shape[1] - local, 1)[:, :LANES]
            gy[b, at, :] = jnp.where(real, rest, 0.0)

        chunks(rows, split)

    loop(8, project)
    for b in (6, 7):
        pltpu.make_async_copy(n1.at[b % 2], n1_out.at[b], sems.at[b % 2]).wait()

    def to_partner(src, dst):
        at = links.pair()
        links.start(src, dst, at, p.peer(zh=1))
        return at

    at = to_partner(xs.at[:, pl.ds(2 * rows, 8)], halo)
    kept = [links.keep(gy, gy_out)]
    links.arrived(halo, at)
    row = lax.broadcasted_iota(jnp.int32, (8, LANES), 0)
    soft = ch_ref[0:1, :]

    def head(seg):
        xs[seg, 0:8, :] = jnp.where(zh == 1, halo[seg], 0.0)

    loop(4, head)

    def convolve(b):
        seg, zl = b // 2, b % 2

        def body(at):
            v = xs[seg, pl.ds(pl.multiple_of(zl * rows + at.start, 8), CHUNK + 8), :]
            total = ch_ref[3:4, :] + ch_ref[4:5, :] * v[8:]
            for k in (1, 2, 3):
                total = total + ch_ref[4 + k : 5 + k, :] * pltpu.roll(v, k, 0)[8:]
            u[b, at, :] = total.astype(BF)

        chunks(rows, body)
        logits[b] = dot(u[b], blocks_ref[...], NN)

    loop(8, convolve)

    def tile(i, carry, zl):
        at = pl.ds(pl.multiple_of(i * CHUNK, CHUNK), CHUNK)
        out = []
        for seg in range(4):
            b = seg * 2 + zl
            cp, ch = carry[seg]
            sa = jax.nn.sigmoid(logits[b, at, :LANES] + ch_ref[1:2, :])
            si = jax.nn.sigmoid(logits[b, at, LANES:] + ch_ref[2:3, :])
            log_decay = -DECAY_SCALE * sa * soft
            a = jnp.exp(log_decay)
            drive = jnp.sqrt(minus_expm1(2.0 * log_decay)) * si * u[b, at, :].astype(F32)
            siga[b, at, :] = sa
            sigi[b, at, :] = si
            decay[b, at, :] = a
            for k in range(2):
                pa, h = tile_scan(a[k * 8 : k * 8 + 8], drive[k * 8 : k * 8 + 8], row, False)
                h = h + pa * ch
                pa = pa * cp
                run[b, pl.ds(eight(i * 2 + k), 8), :] = pa
                there = pl.ds(pl.multiple_of(8 + zl * rows + i * CHUNK + k * 8, 8), 8)
                states[seg, there, :] = h
                cp, ch = pa[7:8, :], h[7:8, :]
            out.append((cp, ch))
        return tuple(out)

    kept += [links.keep(xs, xs_out), links.keep(u, u_out)]
    carry = ((jnp.ones((1, LANES), F32), jnp.zeros((1, LANES), F32)),) * 4
    for zl in range(2):
        carry = lax.fori_loop(0, rows // CHUNK, functools.partial(tile, zl=zl), carry)
    ends[...] = jnp.zeros_like(ends)
    for seg in range(4):
        ends[seg : seg + 1, :] = carry[seg][1]
    at = to_partner(ends, inc)
    kept += [links.keep(siga, siga_out), links.keep(sigi, sigi_out), links.keep(decay, decay_out)]
    links.arrived(inc, at)

    def finish(b):
        seg, zl = b // 2, b % 2
        start = jnp.where(zh == 1, inc[pl.ds(seg, 1), :], 0.0)

        @pl.when(zl == 0)
        def _():
            states[seg, 0:8, :] = jnp.broadcast_to(start, (8, LANES))

        def state(at):
            there = pl.ds(pl.multiple_of(8 + zl * rows + at.start, 8), CHUNK)
            h = states[seg, there, :] + run[b, at, :] * start
            states[seg, there, :] = h
            v = gy[b, at, :]
            t = jnp.tanh(0.7978845608028654 * (v + 0.044715 * v * v * v))
            mixed[b, at, :] = (0.5 * v * (1.0 + t) * h).astype(BF)

        chunks(rows, state)

    loop(8, finish)
    for copy in kept:
        copy.wait()
    links.finish()


def recur_backward_kernel(
    do_ref, wo_ref, blocks_ref, ch_ref,
    xs_in, gy, u_in, siga_in, sigi_in, decay_in, states, rows_ref, mid_in, n2_ref, dup_ref,
    dboth_out, gb_out, ch_out, block_out, up_out,
    xs, u, siga, sigi, decay, mid_ref,
    dh, after, dgy, dlog_ref, du, dboth, halo, ends, inc, do, final, sems,
    *scratch,
):
    p = Place()
    links = Links(*scratch[-3:])
    rows, local = do_ref.shape[1], wo_ref.shape[0]
    zh = p.zh
    greet(weight_peers(p))
    scatter = RowScatter(p, links, rows_ref, scratch[:5])
    up = GradScatter(p, links, n2_ref, dup_ref, scratch[5:12], GradScatter.EARLY)

    def read(b):
        return pltpu.make_async_copy(do_ref.at[b], do.at[b % 2], sems.at[4 + b % 2])

    read(0).start()
    kept = {
        name: links.keep(src, dst)
        for name, src, dst in (
            ("decay", decay_in, decay),
            ("siga", siga_in, siga),
            ("sigi", sigi_in, sigi),
            ("u", u_in, u),
            ("xs", xs_in, xs),
            ("mid", mid_in, mid_ref),
        )
    }
    scatter.begin()
    up.begin(1)
    scatter.across_y()
    ch_out[...] = jnp.zeros_like(ch_out)
    gb_out[...] = jnp.zeros_like(gb_out)
    soft = ch_ref[0:1, :]

    def to_partner(src, dst):
        at = links.pair()
        links.start(src, dst, at, p.peer(zh=1))
        return at

    def upstream(b):
        seg, zl = b // 2, b % 2
        dh[b, :, local:] = jnp.zeros((rows, LANES - local), F32)
        read(b).wait()

        @pl.when(b < 7)
        def _():
            read(b + 1).start()

        dh[b, :, :local] = dot(do[b % 2], wo_ref[...], NT)

        def split(at):
            value, slope = gelu_both(gy[b, at, :])
            dz = dh[b, at, :]
            h = states[seg, pl.ds(pl.multiple_of(8 + zl * rows + at.start, 8), CHUNK), :]
            dh[b, at, :] = dz * value
            dgy[b, at, :] = (dz * h * slope).astype(BF)

        chunks(rows, split)

    loop(8, upstream)
    up.begin(0)
    row = lax.broadcasted_iota(jnp.int32, (8, LANES), 0)
    one = jnp.ones((1, LANES), F32)
    ends[...] = jnp.zeros_like(ends)

    def tile(i, carry, zl):
        at = pl.ds(eight(rows // 8 - 1 - i), 8)
        out = []
        for seg in range(4):
            b = seg * 2 + zl
            cp, cg, following = carry[seg]
            a = decay[b, at, :]
            shifted = jnp.where(row == 7, following, pltpu.roll(a, 7, 0))
            pa, g = tile_scan(shifted, dh[b, at, :], row, True)
            g = g + pa * cg
            pa = pa * cp
            dh[b, at, :] = g
            after[b, at, :] = pa
            out.append((pa[0:1, :], g[0:1, :], a[0:1, :]))
        return tuple(out)

    carry = ((one, jnp.zeros((1, LANES), F32), one),) * 4
    kept["decay"].wait()
    for zl in (1, 0):
        carry = lax.fori_loop(0, rows // 8, functools.partial(tile, zl=zl), carry)
    for seg in range(4):
        ends[seg : seg + 1, :] = carry[seg][1] * carry[seg][2]
    at = to_partner(ends, inc)
    links.arrived(inc, at)
    scatter.across_z()
    up.across(0)

    def gradients(b):
        seg, zl = b // 2, b % 2
        later = jnp.where(zh == 0, inc[pl.ds(seg, 1), :], 0.0)

        def body(at):
            window = states[seg, pl.ds(pl.multiple_of(zl * rows + at.start, 8), CHUNK + 8), :]
            previous = pltpu.roll(window, 1, 0)[8:]
            g = dh[b, at, :] + after[b, at, :] * later
            sa, si, a = siga[b, at, :], sigi[b, at, :], decay[b, at, :]
            uf = u[b, at, :].astype(F32)
            root = jnp.sqrt(minus_expm1((-2.0 * DECAY_SCALE) * sa * soft))
            gu = g * uf
            gr = g * root
            d_log = a * (g * previous - gu * si * a / root)
            d_log = jnp.where(real, d_log, 0.0)
            dra = (d_log * (-DECAY_SCALE * soft) * sa * (1.0 - sa)).astype(BF)
            dri = (gr * uf * si * (1.0 - si)).astype(BF)
            du[seg, pl.ds(pl.multiple_of(zl * rows + at.start, 8), CHUNK), :] = gr * si
            dlog_ref[at, :LANES] = dra
            dlog_ref[at, LANES:] = dri
            for k, v in enumerate((d_log * sa, dra.astype(F32), dri.astype(F32))):
                sums[k] = sums[k] + fold(v)

        sums = [jnp.zeros((8, LANES), F32) for _ in range(3)]
        chunks(rows, body)
        for k in range(3):
            ch_out[k] += sums[k]
        d = dlog_ref[...]
        there = pl.ds(pl.multiple_of(zl * rows, 8), rows)
        du[seg, there, :] += dot(d, blocks_ref[...], NT)
        gb_out[...] += dot(u[b], d, TN)

    lane = lax.broadcasted_iota(jnp.int32, (1, LANES), 1)
    real = lane < local
    for name in ("siga", "sigi", "u"):
        kept[name].wait()
    loop(8, gradients)
    at = to_partner(du.at[:, pl.ds(0, 8)], halo)
    up.across(1)

    def write(i, at, src, dst, base):
        return pltpu.make_async_copy(src.at[i], dst.at[at], sems.at[base + i])

    def convolve(i, zl):
        seg = i
        b = i * 2 + zl
        slot = i % 2

        @pl.when(i >= 2)
        def _():
            write(slot, b - 4, dboth, dboth_out, 0).wait()

        def body(at):
            start = pl.multiple_of(zl * rows + at.start, 8)
            v = du[seg, pl.ds(start, CHUNK + 8), :]
            x = xs[seg, pl.ds(start, CHUNK + 8), :]
            here = v[:CHUNK]
            total = ch_ref[4:5, :] * here
            sums[0] = sums[0] + fold(here)
            sums[1] = sums[1] + fold(here * x[8:])
            for k in (1, 2, 3):
                total = total + ch_ref[4 + k : 5 + k, :] * pltpu.roll(v, CHUNK + 8 - k, 0)[:CHUNK]
                sums[1 + k] = sums[1 + k] + fold(here * pltpu.roll(x, k, 0)[8:])
            wide = 2 * local - LANES
            zeros = jnp.zeros((CHUNK, wide), F32)
            left = jnp.concatenate([total, zeros], axis=1)
            right = jnp.concatenate([dgy[b, at, :].astype(F32), zeros], axis=1)
            dboth[slot, at, :] = (left + pltpu.roll(right, local, 1)).astype(BF)

        sums = [jnp.zeros((8, LANES), F32) for _ in range(5)]
        chunks(rows, body)
        for k in range(5):
            ch_out[3 + k] += sums[k]
        write(slot, b, dboth, dboth_out, 0).start()

    def drain(zl):
        for i in (2, 3):
            write(i % 2, i * 2 + zl, dboth, dboth_out, 0).wait()

    kept["xs"].wait()
    kept["mid"].wait()
    loop(4, functools.partial(convolve, zl=0))
    drain(0)
    links.arrived(halo, at)

    def tail(seg):
        du[seg, pl.ds(2 * rows, 8), :] = jnp.where(zh == 0, halo[seg], 0.0)

    loop(4, tail)
    scatter.arrive()

    def add(at):
        final[at, :] = (mid_ref[at, :] + scatter.total(at)).astype(BF)

    chunks(rows, add)
    at = links.pair()
    links.start(final, block_out.at[p.mp], at, p.peer(mp=1))
    own = links.keep(final, block_out.at[p.mp])
    loop(4, functools.partial(convolve, zl=1))
    up.last(0)
    drain(1)
    up.last(1)
    up.end()
    ff = up.result.shape[2]
    for j in range(4):
        up_out[:, j * ff : (j + 1) * ff] = up.result[j].astype(F32)
    own.wait()
    links.arrived(block_out.at[1 - p.mp], at)
    links.finish()


def recur_forward(tokens, w_ig, blocks, channels, gain):
    if not shape_fits():
        return plain_recur_forward(tokens, w_ig, blocks, channels, gain)
    rows, width = tokens.shape[1:]
    local = w_ig.shape[1] // 2
    table = jnp.concatenate([jax.nn.softplus(-channels[0:1]), channels[1:]], axis=0)
    f, h = (8, rows, LANES), (4, 2 * rows + 8, LANES)
    n1, *saved = run_kernel(
        recur_forward_kernel,
        "recur_forward",
        [(tokens.shape, BF), (h, F32), (f, F32), (f, BF)]
        + [(f, F32)] * 3
        + [(h, F32), (f, BF)],
        [ANY] * 7 + [VMEM] * 2,
        [ANY] + [VMEM] * 4,
        [
            pltpu.VMEM(h, F32),
            pltpu.VMEM(f, F32),
            pltpu.VMEM(f, BF),
            pltpu.VMEM(f, F32),
            pltpu.VMEM(f, F32),
            pltpu.VMEM(f, F32),
            pltpu.VMEM(f, F32),
            pltpu.VMEM((8, rows, 2 * LANES), F32),
            pltpu.VMEM((2, rows, width), BF),
            pltpu.VMEM((rows, 2 * local), F32),
            pltpu.VMEM((4, 8, LANES), F32),
            pltpu.VMEM((8, LANES), F32),
            pltpu.VMEM((8, LANES), F32),
            pltpu.VMEM((2, rows, width), BF),
        ]
        + semaphores(6, 2)[:1]
        + semaphores(2, 6),
        5,
        (tokens, w_ig, blocks, table, gain),
        61,
    )
    *saved, mixed = saved
    return n1.reshape(-1, width), mixed.reshape(-1, LANES), (table, blocks, *saved)


def recur_backward(do, saved, w_o, channels, out_part, middle, n2, dup, drows):
    if not shape_fits():
        return plain_recur_backward(do, saved, w_o, channels, out_part, middle, n2, dup, drows)
    ff = dup.shape[1]
    table, wide, xs, gy, u, siga, sigi, decay, states = saved
    rows, width = do.shape[1:]
    local = w_o.shape[0]
    f, h = (8, rows, LANES), (4, 2 * rows + 8, LANES)
    dboth, g_blocks, sums, block_out, g_up = run_kernel(
        recur_backward_kernel,
        "recur_backward",
        [
            ((8, rows, 2 * local), BF),
            ((LANES, 2 * LANES), F32),
            ((8, 8, LANES), F32),
            ((2, rows, width), BF),
            ((drows, 4 * ff), F32),
        ],
        [ANY] + [VMEM] * 2 + [ANY, VMEM],
        [ANY] + [VMEM] * 3 + [ANY, VMEM] + [ANY] * 4 + [VMEM] + [ANY] * 3 + [VMEM],
        [
            pltpu.VMEM(h, F32),
            pltpu.VMEM(f, BF),
            pltpu.VMEM(f, F32),
            pltpu.VMEM(f, F32),
            pltpu.VMEM(f, F32),
            pltpu.VMEM((rows, width), F32),
            pltpu.VMEM(f, F32),
            pltpu.VMEM(f, F32),
            pltpu.VMEM(f, BF),
            pltpu.VMEM((rows, 2 * LANES), BF),
            pltpu.VMEM(h, F32),
            pltpu.VMEM((2, rows, 2 * local), BF),
            pltpu.VMEM((4, 8, LANES), F32),
            pltpu.VMEM((8, LANES), F32),
            pltpu.VMEM((8, LANES), F32),
            pltpu.VMEM((2, rows, width), BF),
            pltpu.VMEM((rows, width), BF),
        ]
        + semaphores(6, 2)[:1]
        + scatter_buffers(rows, width)
        + grad_buffers(2 * drows, ff, 8 * rows)
        + semaphores(32, 32),
        6,
        (do, w_o, wide, table, xs, gy, u, siga, sigi, decay, states)
        + (out_part, middle, n2, dup),
        61,
    )
    sums = jnp.sum(sums, axis=1)[:, :local]
    dlam = sums[0] * DECAY_SCALE * jax.nn.sigmoid(-channels[0, :local])
    g_blocks = jnp.concatenate(
        [g_blocks[:local, g * LANES : g * LANES + local] for g in (0, 1)], axis=1
    )
    return (
        dboth.reshape(-1, 2 * local),
        g_blocks,
        jnp.concatenate([dlam[None], sums[1:]], axis=0),
        block_out,
        g_up,
    )


def plain_recur_forward(tokens, w_ig, blocks, channels, gain):
    length, local, width = tokens.shape[1], w_ig.shape[1] // 2, tokens.shape[2]
    wide = tokens.reshape(-1, width).astype(F32)
    n1 = (wide * inverse_rms(wide) * gain).astype(BF)
    both = dot(n1, w_ig, NN)
    xb = both[:, :local].astype(BF).reshape(4, 2 * length, local)
    gy = both[:, local:].reshape(4, 2 * length, local)
    rim = from_behind(xb[:, -3:], 1)
    padded = jnp.concatenate([rim, xb], axis=1).astype(F32)
    conv = channels[3]
    for k in range(4):
        conv = conv + channels[4 + k] * padded[:, 3 - k : 3 - k + 2 * length]
    u = conv.astype(BF)
    logits = dot(u.reshape(-1, local), blocks, NN).reshape(4, 2 * length, 2 * local)
    sig_a = jax.nn.sigmoid(logits[..., :local] + channels[1])
    sig_i = jax.nn.sigmoid(logits[..., local:] + channels[2])
    log_decay = -DECAY_SCALE * sig_a * jax.nn.softplus(-channels[0])
    decay = jnp.exp(log_decay)
    root = jnp.sqrt(-jnp.expm1(2.0 * log_decay))
    running, state = local_scan(decay, root * sig_i * u.astype(F32), False)
    incoming = carried(running[:, -1], state[:, -1], False)
    states = state + running * incoming[:, None]
    gelu_y, slope_y = gelu_both(gy)
    mixed = (gelu_y * states).astype(BF).reshape(-1, local)
    saved = (blocks, padded, u, sig_a, sig_i, decay, root, running, incoming, states)
    return n1, mixed, saved + (gelu_y, slope_y)


def plain_recur_backward(do, saved, w_o, channels, out_part, middle, n2, dup, drows):
    blocks, padded, u, sig_a, sig_i, decay, root, running, incoming, states = saved[:10]
    gelu_y, slope_y = saved[10:]
    length, local, width = do.shape[1], w_o.shape[0], do.shape[2]
    dz = dot(do.reshape(-1, width), w_o, NT).reshape(4, 2 * length, local)
    dh = dz * gelu_y
    dgy = (dz * states * slope_y).astype(BF)
    ones = jnp.ones_like(decay[:, :1])
    after, adjoint = local_scan(jnp.concatenate([decay[:, 1:], ones], axis=1), dh, True)
    later = carried(running[:, -1], decay[:, 0] * adjoint[:, 0], True)
    adjoint = adjoint + after * later[:, None]
    previous = jnp.concatenate([incoming[:, None], states[:, :-1]], axis=1)
    soft, uf = jax.nn.softplus(-channels[0]), u.astype(F32)
    d_root = adjoint * sig_i * uf
    d_log = adjoint * previous * decay - d_root * decay * decay / root
    dra = (d_log * (-DECAY_SCALE * soft) * sig_a * (1.0 - sig_a)).astype(BF)
    dri = (adjoint * root * uf * sig_i * (1.0 - sig_i)).astype(BF)
    dlam = jnp.sum(d_log * sig_a, axis=(0, 1)) * DECAY_SCALE * jax.nn.sigmoid(-channels[0])
    dlogits = jnp.concatenate([dra, dri], axis=2).reshape(-1, 2 * local)
    g_blocks = dot(u.reshape(-1, local), dlogits, TN)
    du = adjoint * root * sig_i + dot(dlogits, blocks, NT).reshape(4, 2 * length, local)
    zeros = jnp.zeros((4, 3, local), F32)
    spread = jnp.concatenate([zeros, du, zeros], axis=1)
    dpad = jnp.zeros((4, 2 * length + 3, local), F32)
    taps = []
    for k in range(4):
        dpad = dpad + channels[4 + k] * spread[:, k : k + 2 * length + 3]
        taps.append(jnp.sum(du * padded[:, 3 - k : 3 - k + 2 * length], axis=(0, 1)))
    back = from_behind(dpad[:, :3], -1)
    dxb = dpad[:, 3:] + jnp.concatenate(
        [jnp.zeros((4, 2 * length - 3, local), F32), back], axis=1
    )
    dboth = jnp.concatenate([dxb.astype(BF), dgy], axis=2).reshape(-1, 2 * local)
    sums = [jnp.sum(v.astype(F32), axis=(0, 1)) for v in (dra, dri, du)]
    result = (middle + Tokens().scatter(out_part.reshape(-1, width))).astype(BF)
    g_up = columns(return_grad(dot(n2, dup, TN, BF), drows), 0, dup.shape[1])
    small = jnp.stack([dlam] + sums + taps)
    return dboth, g_blocks, small, both_batches(result), g_up


def on_device(
    tokens_in,
    cotangent,
    seq_source,
    source_weight,
    input_weight,
    gelu_weight,
    decay_gates,
    input_gates,
    channel_params,
    norm_gains,
    output_weight,
    mlp_gate,
    mlp_up,
    mlp_down,
):
    sizes = tuple(lax.axis_size(n) for n in AXES)
    dxn, _, zhn, _, _ = sizes
    group = dxn * 2 * zhn * 2
    dc, zl, mp = (lax.axis_index(n) for n in ("dc", "zl", "mp"))
    slot = dc * 2 + zl
    width = tokens_in.shape[3]
    local = input_weight.shape[1] // 4
    heads = decay_gates.shape[0] // 4
    drows = input_weight.shape[0]
    piece = decay_gates.shape[1]

    tokens, w_ig, w_o, blocks, channels, gains, dm, dout, own, w_g = fetch_first(
        tokens_in[:, 0],
        cotangent[:, 0],
        seq_source,
        source_weight,
        input_weight,
        gelu_weight,
        output_weight,
        decay_gates,
        input_gates,
        channel_params,
        norm_gains,
        mlp_gate,
    )

    n1, mixed, saved = recur_forward(tokens, w_ig, blocks, channels, gains[0:1])
    middle, n2, w_u, w_d = reduce_and_fetch(mixed, w_o, own, gains[1:2], mlp_up, mlp_down)

    hidden, dgm, dup = feed_forward(n2, dm, w_g, w_u, w_d)
    n2, dm = n2.reshape(-1, width), dm.reshape(-1, width)
    dr1, gain_two, do, g_gate, g_down, out_part = reduce_and_return(
        (w_g, w_u, w_d), middle, dout, gains[1:2], dm, hidden, n2, dgm, dup, drows
    )
    gain_two = jnp.sum(gain_two, axis=0)

    dboth, g_blocks, channel_grad, block_out, g_up = recur_backward(
        do, saved, w_o, channels, out_part, middle, n2, dup, drows
    )

    g_gates = jnp.stack(
        [
            jnp.stack(
                [
                    g_blocks[
                        h * BLOCK : (h + 1) * BLOCK,
                        g * local + h * BLOCK : g * local + (h + 1) * BLOCK,
                    ]
                    for h in range(heads)
                ]
            )
            for g in range(2)
        ]
    )
    g_gates = g_gates.reshape(2 * heads, group, piece).transpose(1, 0, 2).reshape(group, -1)
    count = g_gates.shape[1]
    unit = (count + 2047) // 2048 * 16
    g_gates = jnp.pad(g_gates, ((0, 0), (0, unit * 128 - count))).astype(BF)
    grad_tokens, gain_one, g_input, g_gelu, g_output, share_gates = return_last(
        w_ig,
        own,
        dr1,
        gains[0:1],
        do.reshape(-1, width),
        mixed,
        n1,
        dboth,
        g_gates.reshape(group * unit, 128),
        drows,
    )
    gain_one = jnp.sum(gain_one, axis=0)
    g_gates = share_gates.reshape(4, -1)[:, :count].astype(F32).reshape(4, 2, heads, piece)
    g_gates = g_gates.transpose(1, 0, 2, 3).reshape(2, 4 * heads, piece)

    per = 4 * local // group
    mine = channel_grad.reshape(8, group // 4, per).transpose(1, 0, 2)
    mine = jnp.where(
        jnp.arange(4, dtype=jnp.int32)[:, None, None, None] == slot, mine[None], 0.0
    ).reshape(group, 1, 8 * per)
    mine = jnp.where(jnp.arange(2, dtype=jnp.int32)[None, :, None] == mp, mine, 0.0)
    both_gains = jnp.stack([gain_one, gain_two]).reshape(2, group, -1).transpose(1, 0, 2)
    both_gains = jnp.broadcast_to(both_gains.reshape(group, 1, -1), (group, 2, 2 * drows))
    sums = jnp.concatenate([both_gains, mine], axis=2).reshape(2 * group, -1)
    sums = jnp.sum(lax.all_to_all(sums, AXES, 0, 0, tiled=True), axis=0)
    g_gains = sums[: 2 * drows].reshape(2, drows)
    g_channels = sums[2 * drows :].reshape(8, 1, per)
    return (
        block_out[:, None],
        grad_tokens[:, None],
        g_input,
        g_gelu,
        g_gates[0],
        g_gates[1],
        g_channels,
        g_gains,
        g_output,
        g_gate,
        g_up,
        g_down,
    )


def solution(mesh):
    dpn, seqn, mpn = (mesh.shape[n] for n in ("dp", "seq", "mp"))
    fine = Mesh(mesh.devices.reshape(dpn // 2, 2, seqn // 2, 2, mpn), AXES)
    dp, seq = ("dx", "dc"), ("zh", "zl")
    shards = dp + seq
    weights = (
        P(shards, "mp"),
        P(shards, "mp"),
        P("mp", shards),
        P("mp", shards),
        P(None, "mp", shards),
        P(None, shards),
        P("mp", shards),
        P(shards, "mp"),
        P(shards, "mp"),
        P("mp", shards),
    )
    rows = P(None, dp, seq, None)
    return jax.shard_map(
        on_device,
        mesh=fine,
        in_specs=(rows, rows, P(None, dp), P()) + weights,
        out_specs=(rows, rows) + weights,
        check_vma=False,
    )
```
